32 devices in a mesh: row: 8 (over y, x, core), pair: 4 (over z).
Axes of the slice: x: 2, y: 2, z: 4, core: 2. Of those that a mesh axis runs over, the one named last changes fastest.
Arguments:
- basis: float32 [2048, 1024], P('row', 'pair'), may hold values from -48 to 48
Outputs:
- rotated: float32 [2048, 1024], P('row', 'pair')
The draws below stay inside these ranges and needn't reach their ends.
All inputs are finite; a program needn't handle non-finite values.
Results may differ from the reference program's by a relative error of at most 0.0003.
Values sent between devices are 32-bit elements; how exact they have to be, the bound alone decides.
No kernel may reach another device: no remote copies, remote signals or barrier semaphores. Data moves between devices by JAX's collectives and lax.ppermute only.
A program may use at most 64 MiB of HBM per device.

```python
import jax
import jax.numpy as jnp
import numpy as np
from jax import lax

BLK = 128
ROUNDS = 4
JSTEPS = 6
ROWS = 2048
COLS = 1024


def draw_basis(key, part):
    key = jax.random.fold_in(key, 7)
    key_noise, key_shared, key_weight, key_scale = jax.random.split(key, 4)
    noise = jnp.clip(jax.random.normal(key_noise, (ROWS, COLS), jnp.float32), -4.0, 4.0)
    shared = jnp.clip(jax.random.normal(key_shared, (ROWS, 16), jnp.float32), -4.0, 4.0)
    weights = jax.random.uniform(key_weight, (COLS,), jnp.float32, 0.6, 1.2)
    scales = jnp.exp(jax.random.uniform(key_scale, (COLS,), jnp.float32, jnp.log(0.3), jnp.log(3.0)))
    common = jnp.tile(shared, (1, COLS // 16))
    return scales[None, :] * (0.7 * noise + weights[None, :] * common)


def setup_inputs(seed: int = 0) -> dict:
    streams_of = jax.random.split(jax.random.key(seed), 2)
    basis = draw_basis(jax.random.fold_in(streams_of[1], 71), 0)
    return {"basis": basis}


def tournament_order(pair_count):
    ordering = np.zeros(2 * pair_count, dtype=np.int64)
    ordering[0] = 0
    ordering[2] = 1
    for slot in range(2, pair_count):
        ordering[2 * slot] = 2 * (slot - 1)
    for slot in range(pair_count - 1):
        ordering[2 * slot + 1] = 2 * (slot + 1) + 1
    ordering[2 * pair_count - 1] = 2 * (pair_count - 1)
    return ordering

def turn_rows(matrix, cosine, sine_part):
    grouped = matrix.reshape(cosine.shape[0], 2, matrix.shape[1])
    upper_rows = grouped[:, 0]
    lower_rows = grouped[:, 1]
    first_new = cosine[:, None] * upper_rows + sine_part[:, None] * lower_rows
    second_new = cosine[:, None] * lower_rows - sine_part[:, None] * upper_rows
    return jnp.stack((first_new, second_new), axis=1).reshape(matrix.shape)

def jacobi_angle(diag_even, diag_odd, coupling):
    spread = diag_even - diag_odd
    radius = jnp.sqrt(spread * spread + 4.0 * coupling * coupling)
    widened = radius + jnp.abs(spread)
    larger = jnp.sqrt(widened / (2.0 * radius))
    smaller = coupling / (radius * larger)
    forward = spread >= 0.0
    cosine = jnp.where(forward, larger, jnp.abs(smaller))
    sine_part = jnp.where(forward, smaller, jnp.sign(coupling) * larger)
    return (cosine, sine_part)

def jacobi_turns(gram_mat):
    width = gram_mat.shape[0]
    halves = width // 2
    ordering = tournament_order(halves)
    tracked = np.arange(width)
    rotation = jnp.eye(width, dtype=gram_mat.dtype)
    for step_index in range(JSTEPS):
        grouped = gram_mat.reshape(halves, 2, halves, 2)
        diag_even = jnp.diagonal(grouped[:, 0, :, 0])
        diag_odd = jnp.diagonal(grouped[:, 1, :, 1])
        coupling = jnp.diagonal(grouped[:, 0, :, 1])
        cosine, sine_part = jacobi_angle(diag_even, diag_odd, coupling)
        gram_mat = turn_rows(gram_mat, cosine, sine_part)
        gram_mat = turn_rows(gram_mat.T, cosine, sine_part).T
        rotation = turn_rows(rotation.T, cosine, sine_part).T
        gram_mat = gram_mat[ordering][:, ordering]
        rotation = rotation[:, ordering]
        tracked = tracked[ordering]
    inverse = np.argsort(tracked)
    return (rotation[:, inverse], gram_mat[inverse][:, inverse])

def reference(basis):
    hp = lax.Precision.HIGHEST
    pair_count = basis.shape[1] // (2 * BLK)
    blocks = jnp.transpose(basis.reshape(ROWS, 2 * pair_count, BLK), (1, 0, 2))
    ordering = tournament_order(pair_count)

    def one_pair(slab_rows):
        gram_mat = lax.dot_general(slab_rows, slab_rows, (((0,), (0,)), ((), ())), precision=hp)
        rotation, turned = jacobi_turns(gram_mat)
        return jnp.dot(slab_rows, rotation, precision=hp)
    for round_index in range(ROUNDS):
        pairs = blocks.reshape(pair_count, 2, ROWS, BLK).transpose(0, 2, 1, 3).reshape(pair_count, ROWS, 2 * BLK)
        turned_pairs = lax.map(one_pair, pairs)
        blocks = turned_pairs.reshape(pair_count, ROWS, 2, BLK).transpose(0, 2, 1, 3).reshape(2 * pair_count, ROWS, BLK)
        blocks = blocks[ordering]
    return jnp.transpose(blocks, (1, 0, 2)).reshape(ROWS, 2 * pair_count * BLK)
```

```python
import functools

import jax
import jax.numpy as jnp
import numpy as np
from jax import lax
from jax.experimental import pallas as pl
from jax.experimental.pallas import tpu as pltpu
from jax.sharding import PartitionSpec as P

ROUNDS = 4
JSTEPS = 6
REACH = 2 * (JSTEPS - 1) + 1
DIAGS = 16


def tournament_order(pair_count):
    ordering = np.zeros(2 * pair_count, dtype=np.int64)
    ordering[0] = 0
    ordering[2] = 1
    for slot in range(2, pair_count):
        ordering[2 * slot] = 2 * (slot - 1)
    for slot in range(pair_count - 1):
        ordering[2 * slot + 1] = 2 * (slot + 1) + 1
    ordering[2 * pair_count - 1] = 2 * (pair_count - 1)
    return ordering


def host_of(pair, pair_total, round_index):
    if round_index % 2 == 0 or pair == 0:
        return pair
    return min(pair + 1, pair_total - 1) if pair % 2 else pair - 1


def moves(pair_total):
    ordering = tournament_order(pair_total)
    plans = []
    for round_index in range(ROUNDS):
        sends, sends_first, gets_first = [], set(), set()
        for pair in range(pair_total):
            target = host_of(pair, pair_total, round_index + 1)
            for place in (0, 1):
                old = int(ordering[2 * pair + place])
                source = host_of(old // 2, pair_total, round_index)
                if source == target:
                    continue
                sends.append((source, target))
                if old % 2 == 0:
                    sends_first.add(source)
                if place == 0:
                    gets_first.add(target)
        assert len({s for s, _ in sends}) == len(sends) == len({t for _, t in sends})
        plans.append((sends, sends_first, gets_first))
    return plans


def among(members):
    here = lax.axis_index("pair")
    return functools.reduce(
        jnp.logical_or, [here == member for member in sorted(members)], here < 0
    )


def left(x, by):
    width = x.shape[1]
    return pltpu.roll(x, (width - by) % width, 1) if by % width else x


def right(x, by):
    width = x.shape[1]
    return pltpu.roll(x, by % width, 1) if by % width else x


def down(x, by):
    return pltpu.roll(x, by % x.shape[0], 0)


def lanes_of(x):
    return lax.broadcasted_iota(jnp.int32, x.shape, 1)


def split_pair(first, second):
    half = first.shape[1] // 2
    low = lanes_of(first) < half
    even = jnp.where(low, first, right(second, half))
    odd = jnp.where(low, right(first, half), second)
    return even, odd


def join_pair(even, odd):
    half = even.shape[1] // 2
    low = lanes_of(even) < half
    return jnp.where(low, even, right(odd, half)), jnp.where(low, right(even, half), odd)


def separator(width, back):
    rows = lax.broadcasted_iota(jnp.int32, (width, width), 0)
    cols = lax.broadcasted_iota(jnp.int32, (width, width), 1)
    if back:
        rows, cols = cols, rows
    half = width // 2
    source = jnp.where(cols < half, 2 * cols, 2 * (cols - half) + 1)
    return jnp.where(rows == source, 1.0, 0.0).astype(jnp.float32)


def reorder(block, table):
    return jnp.dot(
        block, table, precision=lax.Precision.HIGHEST, preferred_element_type=jnp.float32
    )


def store_bands(even, odd, band_ref):
    rows = even.shape[0]
    sums = [[None] * 4 for _ in range(REACH)]
    for start in range(0, rows, 8):
        e, o = even[start : start + 8], odd[start : start + 8]
        for d in range(REACH):
            e_near, o_near = right(e, d), right(o, d)
            parts = (e_near * e, e_near * o, o_near * e, o_near * o)
            for q in range(4):
                if d == 0 and q == 2:
                    continue
                sums[d][q] = parts[q] if start == 0 else sums[d][q] + parts[q]
    sums[0][2] = sums[0][1]
    for q in range(4):
        for d in range(REACH):
            band_ref[q, d : d + 1, :] = jnp.sum(sums[d][q], axis=0, keepdims=True)
        band_ref[q, REACH:, :] = jnp.zeros((DIAGS - REACH, even.shape[1]), jnp.float32)


def open_kernel(basis_ref, even_ref, odd_ref, band_ref):
    width = basis_ref.shape[1] // 2
    table = separator(width, False)
    first = reorder(basis_ref[:, :width], table)
    second = reorder(basis_ref[:, width:], table)
    even, odd = split_pair(first, second)
    even_ref[...] = even
    odd_ref[...] = odd
    store_bands(even, odd, band_ref)


def pair_kernel(gets_first, kept_ref, came_ref, even_ref, odd_ref, band_ref):
    flag = among(gets_first)
    kept, came = kept_ref[...], came_ref[...]
    even, odd = split_pair(jnp.where(flag, came, kept), jnp.where(flag, kept, came))
    even_ref[...] = even
    odd_ref[...] = odd
    store_bands(even, odd, band_ref)


def jacobi_angle(diag_even, diag_odd, coupling):
    spread = diag_even - diag_odd
    radius = jnp.sqrt(spread * spread + 4.0 * coupling * coupling)
    widened = radius + jnp.abs(spread)
    larger = jnp.sqrt(widened / (2.0 * radius))
    smaller = coupling / (radius * larger)
    forward = spread >= 0.0
    sign = jnp.where(coupling > 0.0, 1.0, jnp.where(coupling < 0.0, -1.0, 0.0))
    cosine = jnp.where(forward, larger, jnp.abs(smaller))
    sine_part = jnp.where(forward, smaller, sign * larger)
    return cosine, sine_part


def turn_bands(ee, eo, oe, oo, cosine, sine):
    cl, sl = jnp.broadcast_to(cosine, ee.shape), jnp.broadcast_to(sine, ee.shape)
    ck = pltpu.roll(cl, 0, 1, stride=1, stride_axis=0)
    sk = pltpu.roll(sl, 0, 1, stride=1, stride_axis=0)
    ee, oe = ck * ee + sk * oe, ck * oe - sk * ee
    eo, oo = ck * eo + sk * oo, ck * oo - sk * eo
    ee, eo = cl * ee + sl * eo, cl * eo - sl * ee
    oe, oo = cl * oe + sl * oo, cl * oo - sl * oe
    return ee, eo, oe, oo


def move_bands(ee, eo, oe, oo):
    lane = lanes_of(ee)
    diag = lax.broadcasted_iota(jnp.int32, ee.shape, 0)
    last = lane == ee.shape[1] - 1
    first, second = lane == diag, lane == diag + 1
    on, next_on = diag == 0, diag == 1

    ee_new = right(ee, 1)
    ee_new = jnp.where(second, right(jnp.where(on, oo, oe), 1), ee_new)
    near = jnp.where(next_on, down(eo, 1), down(ee, 1))
    ee_new = jnp.where(first, jnp.where(on, ee, right(near, 1)), ee_new)

    eo_new = left(down(eo, -2), 1)
    eo_new = jnp.where(second, left(down(oo, -2), 1), eo_new)
    eo_new = jnp.where(first, left(down(eo, -1), 1), eo_new)
    eo_new = jnp.where(last, down(ee, -1), eo_new)

    oo_new = jnp.where(last, jnp.where(on, ee, down(oe, 1)), left(oo, 1))

    oe_new = right(down(oe, 2), 1)
    oe_new = jnp.where(next_on, jnp.where(first, oo, eo), oe_new)
    oe_new = jnp.where(on, eo_new, oe_new)
    return ee_new, eo_new, oe_new, oo_new


def move_columns(even, odd):
    lane = lanes_of(even)
    first, last = lane == 0, lane == even.shape[1] - 1
    even_new = jnp.where(first, even, right(jnp.where(first, odd, even), 1))
    odd_new = jnp.where(last, even, left(odd, 1))
    return even_new, odd_new


def move_columns_back(even, odd):
    lane = lanes_of(even)
    first, last = lane == 0, lane == even.shape[1] - 1
    back = left(even, 1)
    even_old = jnp.where(first, even, jnp.where(last, odd, back))
    odd_old = jnp.where(first, back, right(odd, 1))
    return even_old, odd_old


def turn_kernel(sends_first, is_last, even_ref, odd_ref, *refs):
    *band_refs, kept_ref, sent_ref = refs
    bands = [ref[...] for ref in band_refs]
    while len(bands) > 1:
        bands = [bands[i] + bands[i + 1] for i in range(0, len(bands), 2)]
    ee, eo, oe, oo = (bands[0][q] for q in range(4))
    even, odd = even_ref[...], odd_ref[...]
    for step in range(JSTEPS):
        cosine, sine = jacobi_angle(ee[0:1], oo[0:1], eo[0:1])
        even, odd = cosine * even + sine * odd, cosine * odd - sine * even
        if step < JSTEPS - 1:
            ee, eo, oe, oo = move_bands(*turn_bands(ee, eo, oe, oo, cosine, sine))
            even, odd = move_columns(even, odd)
    for step in range(JSTEPS - 1):
        even, odd = move_columns_back(even, odd)
    first, second = join_pair(even, odd)
    if is_last:
        table = separator(first.shape[1], True)
        first, second = reorder(first, table), reorder(second, table)
    flag = among(sends_first)
    kept_ref[...] = jnp.where(flag, second, first)
    sent_ref[...] = jnp.where(flag, first, second)


def exchange_groups(x, axis):
    size = lax.axis_size(axis)
    bits = [1 << b for b in range(size.bit_length() - 1)]
    groups = [bits[:1]] + [bits[i : i + 2] for i in range(1, len(bits), 2)]
    arrays = [x]
    for group in groups:
        while len(arrays) > 1:
            arrays = [arrays[i] + arrays[i + 1] for i in range(0, len(arrays), 2)]
        x = arrays[0]
        masks = [group[0]] if len(group) == 1 else [group[0], group[1], group[0] | group[1]]
        arrays = [x] + [
            lax.ppermute(x, axis, [(i, i ^ mask) for i in range(size)]) for mask in masks
        ]
    return arrays


def call(kernel, shapes, *args):
    out = [jax.ShapeDtypeStruct(shape, jnp.float32) for shape in shapes]
    return pl.pallas_call(
        kernel,
        out_shape=out,
        compiler_params=pltpu.CompilerParams(vmem_limit_bytes=32 * 1024 * 1024),
    )(*args)


def per_device(basis):
    rows, cols = basis.shape
    width = cols // 2
    column = (rows, width)
    band = (4, DIAGS, width)
    plans = moves(lax.axis_size("pair"))
    even, odd, partial = call(open_kernel, (column, column, band), basis)
    for round_index, (sends, sends_first, gets_first) in enumerate(plans):
        is_last = round_index == ROUNDS - 1
        arrays = exchange_groups(partial, "row")
        kept, sent = call(
            functools.partial(turn_kernel, sends_first, is_last),
            (column, column),
            even,
            odd,
            *arrays,
        )
        came = lax.ppermute(sent, "pair", sends)
        if not is_last:
            even, odd, partial = call(
                functools.partial(pair_kernel, gets_first), (column, column, band), kept, came
            )
    flag = among(gets_first)
    first = jnp.where(flag, came, kept)
    second = jnp.where(flag, kept, came)
    return jnp.concatenate((first, second), axis=1)


def solution(mesh):
    return jax.shard_map(
        per_device,
        mesh=mesh,
        in_specs=(P("row", "pair"),),
        out_specs=P("row", "pair"),
        check_vma=False,
    )
```

```python
import functools

import jax
import jax.numpy as jnp
import numpy as np
from jax import lax
from jax.experimental import pallas as pl
from jax.experimental.pallas import tpu as pltpu
from jax.sharding import PartitionSpec as P

ROUNDS = 4
JSTEPS = 6
REACH = 2 * (JSTEPS - 1) + 1
DIAGS = 16
FAR_REACH = 6 * (JSTEPS - 1) - 1
FAR_DIAGS = 32
WINDOW = 32
NEAR = 16


def tournament_order(pair_count):
    ordering = np.zeros(2 * pair_count, dtype=np.int64)
    ordering[0] = 0
    ordering[2] = 1
    for slot in range(2, pair_count):
        ordering[2 * slot] = 2 * (slot - 1)
    for slot in range(pair_count - 1):
        ordering[2 * slot + 1] = 2 * (slot + 1) + 1
    ordering[2 * pair_count - 1] = 2 * (pair_count - 1)
    return ordering


def host_of(pair, pair_total, round_index):
    if round_index % 2 == 0 or pair == 0:
        return pair
    return min(pair + 1, pair_total - 1) if pair % 2 else pair - 1


def moves(pair_total):
    ordering = tournament_order(pair_total)
    plans = []
    for round_index in range(ROUNDS):
        sends, sends_first, gets_first = [], set(), set()
        for pair in range(pair_total):
            target = host_of(pair, pair_total, round_index + 1)
            for place in (0, 1):
                old = int(ordering[2 * pair + place])
                source = host_of(old // 2, pair_total, round_index)
                if source == target:
                    continue
                sends.append((source, target))
                if old % 2 == 0:
                    sends_first.add(source)
                if place == 0:
                    gets_first.add(target)
        assert len({s for s, _ in sends}) == len(sends) == len({t for _, t in sends})
        plans.append((sends, sends_first, gets_first))
    return plans


def fused_moves(pair_total):
    ordering = tournament_order(pair_total)
    before, last = ROUNDS - 3, ROUNDS - 1
    needs, edges, seconds = {}, [], ({}, {})
    for pair in range(pair_total):
        here = host_of(pair, pair_total, last)
        needs[here] = []
        for place in (0, 1):
            source = int(ordering[2 * pair + place])
            seconds[place][here] = source % 2
            for half in (0, 1):
                old = int(ordering[2 * (source // 2) + half])
                there = host_of(old // 2, pair_total, before)
                needs[here].append((there, old % 2))
                if there != here:
                    edges.append((there, old % 2, here))
    turn, left_over = {}, list(edges)
    while left_over:
        edge, by_target = left_over[0], True
        number = 0
        while edge is not None:
            turn[edge] = number
            left_over.remove(edge)
            key = 2 if by_target else 0
            edge = next((e for e in left_over if e[key] == edge[key]), None)
            by_target, number = not by_target, 1 - number
    sends = [[(e[0], e[2]) for e in edges if turn[e] == i] for i in (0, 1)]
    for chosen in sends:
        assert len({a for a, _ in chosen}) == len({b for _, b in chosen}) == pair_total
    sends_first = {e[0] for e in edges if turn[e] == 0 and e[1] == 0}
    picks = []
    for slot in range(4):
        pick = {}
        for here in range(pair_total):
            there, half = needs[here][slot]
            if there == here:
                pick[here] = 0 if (half == 0) == (here in sends_first) else 1
            else:
                pick[here] = 2 + turn[(there, half, here)]
        picks.append(pick)
    is_second = [{h for h, place in table.items() if place} for table in seconds]
    return sends, sends_first, picks, is_second


def choose(pick, arrays):
    chosen = arrays[0]
    for number in range(1, len(arrays)):
        members = {here for here, value in pick.items() if value == number}
        if members:
            chosen = jnp.where(among(members), arrays[number], chosen)
    return chosen


def among(members):
    here = lax.axis_index("pair")
    return functools.reduce(
        jnp.logical_or, [here == member for member in sorted(members)], here < 0
    )


def left(x, by):
    width = x.shape[1]
    return pltpu.roll(x, (width - by) % width, 1) if by % width else x


def right(x, by):
    width = x.shape[1]
    return pltpu.roll(x, by % width, 1) if by % width else x


def down(x, by):
    return pltpu.roll(x, by % x.shape[0], 0)


def lanes_of(x):
    return lax.broadcasted_iota(jnp.int32, x.shape, 1)


def split_pair(first, second):
    half = first.shape[1] // 2
    low = lanes_of(first) < half
    even = jnp.where(low, first, right(second, half))
    odd = jnp.where(low, right(first, half), second)
    return even, odd


def join_pair(even, odd):
    half = even.shape[1] // 2
    low = lanes_of(even) < half
    return jnp.where(low, even, right(odd, half)), jnp.where(low, right(even, half), odd)


def separator(width, back):
    rows = lax.broadcasted_iota(jnp.int32, (width, width), 0)
    cols = lax.broadcasted_iota(jnp.int32, (width, width), 1)
    if back:
        rows, cols = cols, rows
    half = width // 2
    source = jnp.where(cols < half, 2 * cols, 2 * (cols - half) + 1)
    return jnp.where(rows == source, 1.0, 0.0).astype(jnp.float32)


def reorder(block, table):
    return jnp.dot(
        block, table, precision=lax.Precision.HIGHEST, preferred_element_type=jnp.float32
    )


def store_bands(even, odd, band_ref, reach, diags, base=0):
    rows, width = even.shape
    for d in range(reach):
        sums = [None] * 4
        for start in range(0, rows, 8):
            e, o = even[start : start + 8], odd[start : start + 8]
            e_near, o_near = right(e, d), right(o, d)
            parts = (e_near * e, e_near * o, o_near * e if d else None, o_near * o)
            for q in range(4):
                if parts[q] is not None:
                    sums[q] = parts[q] if start == 0 else sums[q] + parts[q]
        if d == 0:
            sums[2] = sums[1]
        for q in range(4):
            row = base + q * diags + d
            band_ref[row : row + 1, :] = jnp.sum(sums[q], axis=0, keepdims=True)
    for q in range(4):
        band_ref[base + q * diags + reach : base + (q + 1) * diags, :] = jnp.zeros(
            (diags - reach, width), jnp.float32
        )


def open_kernel(basis_ref, even_ref, odd_ref, band_ref):
    width = basis_ref.shape[1] // 2
    table = separator(width, False)
    first = reorder(basis_ref[:, :width], table)
    second = reorder(basis_ref[:, width:], table)
    even, odd = split_pair(first, second)
    even_ref[...] = even
    odd_ref[...] = odd
    store_bands(even, odd, band_ref, REACH, DIAGS)


def pair_kernel(gets_first, kept_ref, came_ref, even_ref, odd_ref, band_ref):
    flag = among(gets_first)
    kept, came = kept_ref[...], came_ref[...]
    even, odd = split_pair(jnp.where(flag, came, kept), jnp.where(flag, kept, came))
    even_ref[...] = even
    odd_ref[...] = odd
    store_bands(even, odd, band_ref, REACH, DIAGS)


def jacobi_angle(diag_even, diag_odd, coupling):
    spread = diag_even - diag_odd
    radius = jnp.sqrt(spread * spread + 4.0 * coupling * coupling)
    widened = radius + jnp.abs(spread)
    larger = jnp.sqrt(widened / (2.0 * radius))
    smaller = coupling / (radius * larger)
    forward = spread >= 0.0
    sign = jnp.where(coupling > 0.0, 1.0, jnp.where(coupling < 0.0, -1.0, 0.0))
    cosine = jnp.where(forward, larger, jnp.abs(smaller))
    sine_part = jnp.where(forward, smaller, sign * larger)
    return cosine, sine_part


def turn_bands(ee, eo, oe, oo, cosine, sine):
    cl, sl = jnp.broadcast_to(cosine, ee.shape), jnp.broadcast_to(sine, ee.shape)
    ck = pltpu.roll(cl, 0, 1, stride=1, stride_axis=0)
    sk = pltpu.roll(sl, 0, 1, stride=1, stride_axis=0)
    ee, oe = ck * ee + sk * oe, ck * oe - sk * ee
    eo, oo = ck * eo + sk * oo, ck * oo - sk * eo
    ee, eo = cl * ee + sl * eo, cl * eo - sl * ee
    oe, oo = cl * oe + sl * oo, cl * oo - sl * oe
    return ee, eo, oe, oo


def move_bands(ee, eo, oe, oo):
    lane = lanes_of(ee)
    diag = lax.broadcasted_iota(jnp.int32, ee.shape, 0)
    last = lane == ee.shape[1] - 1
    first, second = lane == diag, lane == diag + 1
    on, next_on = diag == 0, diag == 1

    ee_new = right(ee, 1)
    ee_new = jnp.where(second, right(jnp.where(on, oo, oe), 1), ee_new)
    near = jnp.where(next_on, down(eo, 1), down(ee, 1))
    ee_new = jnp.where(first, jnp.where(on, ee, right(near, 1)), ee_new)

    eo_new = left(down(eo, -2), 1)
    eo_new = jnp.where(second, left(down(oo, -2), 1), eo_new)
    eo_new = jnp.where(first, left(down(eo, -1), 1), eo_new)
    eo_new = jnp.where(last, down(ee, -1), eo_new)

    oo_new = jnp.where(last, jnp.where(on, ee, down(oe, 1)), left(oo, 1))

    oe_new = right(down(oe, 2), 1)
    oe_new = jnp.where(next_on, jnp.where(first, oo, eo), oe_new)
    oe_new = jnp.where(on, eo_new, oe_new)
    return ee_new, eo_new, oe_new, oo_new


def move_bands_back(ee, eo, oe, oo):
    lane = lanes_of(ee)
    diag = lax.broadcasted_iota(jnp.int32, ee.shape, 0)
    last, first = lane == ee.shape[1] - 1, lane == diag
    on, next_on = diag == 0, diag == 1
    ee_left, oe_left = left(ee, 1), left(down(oe, -2), 1)
    ee_far, eo_far = left(down(ee, -1), 1), right(down(eo, 2), 1)

    ee_old = jnp.where(first, jnp.where(on, ee, ee_far), ee_left)
    ee_old = jnp.where(last, jnp.where(on, oo, down(eo, 1)), ee_old)

    eo_old = jnp.where(on, oe_left, jnp.where(next_on, oe, eo_far))
    eo_old = jnp.where(first, jnp.where(on, ee_far, right(down(eo, 1), 1)), eo_old)
    eo_old = jnp.where(jnp.logical_and(last, on), down(oo, -1), eo_old)

    oe_old = jnp.where(first, ee_left, oe_left)
    oe_old = jnp.where(last, down(oo, -1), oe_old)
    oe_old = jnp.where(on, eo_old, oe_old)

    near = jnp.where(on, ee_left, jnp.where(next_on, oe, eo_far))
    oo_old = jnp.where(first, near, right(oo, 1))
    return ee_old, eo_old, oe_old, oo_old


def move_columns(even, odd):
    lane = lanes_of(even)
    first, last = lane == 0, lane == even.shape[1] - 1
    even_new = jnp.where(first, even, right(jnp.where(first, odd, even), 1))
    odd_new = jnp.where(last, even, left(odd, 1))
    return even_new, odd_new


def move_columns_back(even, odd):
    lane = lanes_of(even)
    first, last = lane == 0, lane == even.shape[1] - 1
    back = left(even, 1)
    even_old = jnp.where(first, even, jnp.where(last, odd, back))
    odd_old = jnp.where(first, back, right(odd, 1))
    return even_old, odd_old


def angles_of(bands, carried):
    angles = []
    for step in range(JSTEPS):
        ee, eo, oe, oo = bands
        cosine, sine = jacobi_angle(ee[0:1], oo[0:1], eo[0:1])
        angles.append((cosine, sine))
        if carried or step < JSTEPS - 1:
            bands = turn_bands(ee, eo, oe, oo, cosine, sine)
        if step < JSTEPS - 1:
            bands = move_bands(*bands)
    if carried:
        for step in range(JSTEPS - 1):
            bands = move_bands_back(*bands)
    return angles, bands


def turn_columns(even, odd, angles):
    for step, (cosine, sine) in enumerate(angles):
        even, odd = cosine * even + sine * odd, cosine * odd - sine * even
        if step < JSTEPS - 1:
            even, odd = move_columns(even, odd)
    for step in range(JSTEPS - 1):
        even, odd = move_columns_back(even, odd)
    return even, odd


def turn_kernel(sends_first, even_ref, odd_ref, *refs):
    *band_refs, kept_ref, sent_ref = refs
    bands = [ref[...] for ref in band_refs]
    while len(bands) > 1:
        bands = [bands[i] + bands[i + 1] for i in range(0, len(bands), 2)]
    bands = [bands[0][q * DIAGS : (q + 1) * DIAGS] for q in range(4)]
    angles, _ = angles_of(bands, False)
    first, second = join_pair(*turn_columns(even_ref[...], odd_ref[...], angles))
    flag = among(sends_first)
    kept_ref[...] = jnp.where(flag, second, first)
    sent_ref[...] = jnp.where(flag, first, second)


def near_starts(width):
    half = width // 2
    reach = REACH - 1
    return (half - 2 * reach, width - WINDOW), (0, half - reach)


def cross_partial(x_even, x_odd, y_even, y_odd, x_second, y_second):
    rows, width = x_even.shape
    x_starts, y_starts = near_starts(width)
    lane = lanes_of(x_even)

    def window(even, odd, flag, starts):
        at_zero = jnp.where(flag, left(even, starts[1]), left(even, starts[0]))
        at_next = jnp.where(flag, left(odd, starts[1] - WINDOW), left(odd, starts[0] - WINDOW))
        return jnp.where(lane < WINDOW, at_zero, jnp.where(lane < 2 * WINDOW, at_next, 0.0))

    corner = lax.dot_general(
        window(y_even, y_odd, y_second, y_starts),
        window(x_even, x_odd, x_second, x_starts),
        (((0,), (0,)), ((), ())),
        precision=lax.Precision.HIGHEST,
        preferred_element_type=jnp.float32,
    )
    low = lax.broadcasted_iota(jnp.int32, (WINDOW, width), 1) < 2 * WINDOW
    return jnp.where(low, corner[:WINDOW], right(corner[WINDOW : 2 * WINDOW], 2 * WINDOW))


def spread(packed, place, flag, starts):
    at = place * WINDOW
    return jnp.where(flag, right(packed, starts[1] - at), right(packed, starts[0] - at))


def cross_bands(corner, x_angles, y_angles, x_second, y_second):
    width = corner.shape[1]
    half = width // 2
    x_starts, y_starts = near_starts(width)
    even = jnp.concatenate([spread(corner, p, x_second, x_starts) for p in (0, 2)], axis=0)
    odd = jnp.concatenate([spread(corner, p, x_second, x_starts) for p in (1, 3)], axis=0)
    even, odd = turn_columns(even, odd, x_angles)
    stacked = jnp.concatenate((even, odd), axis=0)
    ends = jnp.where(x_second, left(stacked, width - NEAR), left(stacked, half - NEAR))
    ends = jnp.transpose(ends)[:NEAR]
    even = jnp.concatenate([spread(ends, p, y_second, y_starts) for p in (0, 2)], axis=0)
    odd = jnp.concatenate([spread(ends, p, y_second, y_starts) for p in (1, 3)], axis=0)
    even, odd = turn_columns(even, odd, y_angles)
    even = jnp.where(y_second, even, right(even, half))
    odd = jnp.where(y_second, odd, right(odd, half))
    quadrants = (even[:NEAR], odd[:NEAR], even[NEAR:], odd[NEAR:])
    offset = lanes_of(ends) - lax.broadcasted_iota(jnp.int32, ends.shape, 0) - (half - NEAR)
    diag = lax.broadcasted_iota(jnp.int32, (DIAGS, width), 0)
    bands = [jnp.zeros((DIAGS, width), jnp.float32) for _ in quadrants]
    for d in range(1, REACH):
        here = offset == d
        for q, quadrant in enumerate(quadrants):
            line = jnp.sum(jnp.where(here, quadrant, 0.0), axis=0, keepdims=True)
            bands[q] = jnp.where(diag == d, line, bands[q])
    return bands


def fused_open(picks, is_second, kept_ref, sent_ref, came0_ref, came1_ref, *refs):
    *column_refs, mine_ref, other_ref, parts = refs
    arrays = [ref[...] for ref in (sent_ref, kept_ref, came0_ref, came1_ref)]
    blocks = [choose(pick, arrays) for pick in picks]
    columns = split_pair(*blocks[:2]) + split_pair(*blocks[2:])
    for ref, value in zip(column_refs, columns):
        ref[...] = value
    corner = cross_partial(*columns, among(is_second[0]), among(is_second[1]))
    for i in (0, 1):
        store_bands(*columns[2 * i : 2 * i + 2], parts.at[i], FAR_REACH, FAR_DIAGS)
        parts[i, 4 * FAR_DIAGS :, :] = corner[i * NEAR : (i + 1) * NEAR]
    odd_core = lax.axis_index("row") % 2
    mine_ref[...] = parts[odd_core]
    other_ref[...] = parts[1 - odd_core]


def fused_turn(x_even, x_odd, y_even, y_odd, x_part, y_part, x_second, y_second):
    half = x_even.shape[1] // 2

    def quadrants(part):
        return [part[q * FAR_DIAGS : (q + 1) * FAR_DIAGS] for q in range(4)]

    x_angles, x_bands = angles_of(quadrants(x_part), True)
    y_angles, y_bands = angles_of(quadrants(y_part), True)
    corner = jnp.concatenate((x_part[4 * FAR_DIAGS :], y_part[4 * FAR_DIAGS :]), axis=0)
    middle = cross_bands(corner, x_angles, y_angles, x_second, y_second)

    def first_half(x):
        return jnp.where(x_second, right(x, half), x)

    def second_half(y):
        return jnp.where(y_second, y, right(y, half))

    lane = lanes_of(middle[0])
    diag = lax.broadcasted_iota(jnp.int32, middle[0].shape, 0)
    bands = [
        jnp.where(
            lane < half,
            first_half(x_bands[q][:DIAGS]),
            jnp.where(lane - diag < half, middle[q], second_half(y_bands[q][:DIAGS])),
        )
        for q in range(4)
    ]
    x_turned = turn_columns(x_even, x_odd, x_angles)
    y_turned = turn_columns(y_even, y_odd, y_angles)
    low = lanes_of(x_even) < half
    even, odd = (
        jnp.where(low, first_half(x), second_half(y)) for x, y in zip(x_turned, y_turned)
    )
    angles, _ = angles_of(bands, False)
    return join_pair(*turn_columns(even, odd, angles))


def fused_kernel(is_second, sends_first, *refs):
    *column_refs, mine_ref, other_ref, kept_ref, sent_ref = refs
    mine, other = mine_ref[...], other_ref[...]
    odd_core = lax.axis_index("row") % 2 == 1
    parts = jnp.where(odd_core, other, mine), jnp.where(odd_core, mine, other)
    first, second = fused_turn(
        *(ref[...] for ref in column_refs),
        *parts,
        among(is_second[0]),
        among(is_second[1]),
    )
    table = separator(first.shape[1], True)
    first, second = reorder(first, table), reorder(second, table)
    flag = among(sends_first)
    kept_ref[...] = jnp.where(flag, second, first)
    sent_ref[...] = jnp.where(flag, first, second)


def pair_sums(arrays):
    while len(arrays) > 1:
        arrays = [arrays[i] + arrays[i + 1] for i in range(0, len(arrays), 2)]
    return arrays[0]


def swap(x, axis, mask):
    return lax.ppermute(x, axis, [(i, i ^ mask) for i in range(lax.axis_size(axis))])


def exchange_groups(x, axis, first_bit=0):
    count = lax.axis_size(axis).bit_length() - 1
    bits = [1 << b for b in range(count)]
    groups = [bits[:1]] + [bits[i : i + 2] for i in range(1, count, 2)]
    arrays = [x]
    for group in groups[first_bit:]:
        x = pair_sums(arrays)
        masks = [group[0]] if len(group) == 1 else [group[0], group[1], group[0] | group[1]]
        arrays = [x] + [swap(x, axis, mask) for mask in masks]
    return arrays


def call(kernel, shapes, *args, scratch=()):
    out = [jax.ShapeDtypeStruct(shape, jnp.float32) for shape in shapes]
    return pl.pallas_call(
        kernel,
        out_shape=out,
        scratch_shapes=[pltpu.VMEM(shape, jnp.float32) for shape in scratch],
        compiler_params=pltpu.CompilerParams(vmem_limit_bytes=32 * 1024 * 1024),
    )(*args)


def per_device(basis):
    rows, cols = basis.shape
    width = cols // 2
    pair_total = lax.axis_size("pair")
    column = (rows, width)
    band = (4 * DIAGS, width)
    part = (4 * FAR_DIAGS + NEAR, width)
    plans = moves(pair_total)
    fused_sends, fused_first, picks, is_second = fused_moves(pair_total)
    even, odd, partial = call(open_kernel, (column, column, band), basis)
    for round_index in range(ROUNDS - 2):
        sends, sends_first, gets_first = plans[round_index]
        ahead = round_index == ROUNDS - 3
        arrays = exchange_groups(partial, "row")
        turn = functools.partial(turn_kernel, fused_first if ahead else sends_first)
        kept, sent = call(turn, (column, column), even, odd, *arrays)
        if not ahead:
            came = lax.ppermute(sent, "pair", sends)
            opening = functools.partial(pair_kernel, gets_first)
            even, odd, partial = call(opening, (column, column, band), kept, came)
    came = [lax.ppermute(x, "pair", s) for x, s in zip((sent, kept), fused_sends)]
    *columns, mine, other = call(
        functools.partial(fused_open, picks, is_second),
        (column,) * 4 + (part,) * 2,
        kept,
        sent,
        *came,
        scratch=((2,) + part,),
    )
    mine = pair_sums(exchange_groups(mine + swap(other, "row", 1), "row", 1))
    other = swap(mine, "row", 1)
    sends, sends_first, gets_first = plans[-1]
    kept, sent = call(
        functools.partial(fused_kernel, is_second, sends_first),
        (column, column),
        *columns,
        mine,
        other,
    )
    came = lax.ppermute(sent, "pair", sends)
    flag = among(gets_first)
    first = jnp.where(flag, came, kept)
    second = jnp.where(flag, kept, came)
    return jnp.concatenate((first, second), axis=1)


def solution(mesh):
    return jax.shard_map(
        per_device,
        mesh=mesh,
        in_specs=(P("row", "pair"),),
        out_specs=P("row", "pair"),
        check_vma=False,
    )
```

```python
import functools

import jax
import jax.numpy as jnp
import numpy as np
from jax import lax
from jax.experimental import pallas as pl
from jax.experimental.pallas import tpu as pltpu
from jax.sharding import PartitionSpec as P

ROUNDS = 4
JSTEPS = 6
REACH = 2 * (JSTEPS - 1) + 1
DIAGS = 16
FAR_REACH = 6 * (JSTEPS - 1) - 1
FAR_DIAGS = 32
WINDOW = 32
NEAR = 16


def tournament_order(pair_count):
    ordering = np.zeros(2 * pair_count, dtype=np.int64)
    ordering[0] = 0
    ordering[2] = 1
    for slot in range(2, pair_count):
        ordering[2 * slot] = 2 * (slot - 1)
    for slot in range(pair_count - 1):
        ordering[2 * slot + 1] = 2 * (slot + 1) + 1
    ordering[2 * pair_count - 1] = 2 * (pair_count - 1)
    return ordering


def host_of(pair, pair_total, round_index):
    if round_index % 2 == 0 or pair == 0:
        return pair
    return min(pair + 1, pair_total - 1) if pair % 2 else pair - 1


def moves(pair_total):
    ordering = tournament_order(pair_total)
    plans = []
    for round_index in range(ROUNDS):
        sends, sends_first, gets_first = [], set(), set()
        for pair in range(pair_total):
            target = host_of(pair, pair_total, round_index + 1)
            for place in (0, 1):
                old = int(ordering[2 * pair + place])
                source = host_of(old // 2, pair_total, round_index)
                if source == target:
                    continue
                sends.append((source, target))
                if old % 2 == 0:
                    sends_first.add(source)
                if place == 0:
                    gets_first.add(target)
        assert len({s for s, _ in sends}) == len(sends) == len({t for _, t in sends})
        plans.append((sends, sends_first, gets_first))
    return plans


def fused_moves(pair_total):
    ordering = tournament_order(pair_total)
    before, last = ROUNDS - 3, ROUNDS - 1
    needs, edges, seconds = {}, [], ({}, {})
    for pair in range(pair_total):
        here = host_of(pair, pair_total, last)
        needs[here] = []
        for place in (0, 1):
            source = int(ordering[2 * pair + place])
            seconds[place][here] = source % 2
            for half in (0, 1):
                old = int(ordering[2 * (source // 2) + half])
                there = host_of(old // 2, pair_total, before)
                needs[here].append((there, old % 2))
                if there != here:
                    edges.append((there, old % 2, here))
    turn, left_over = {}, list(edges)
    while left_over:
        edge, by_target = left_over[0], True
        number = 0
        while edge is not None:
            turn[edge] = number
            left_over.remove(edge)
            key = 2 if by_target else 0
            edge = next((e for e in left_over if e[key] == edge[key]), None)
            by_target, number = not by_target, 1 - number
    sends = [[(e[0], e[2]) for e in edges if turn[e] == i] for i in (0, 1)]
    for chosen in sends:
        assert len({a for a, _ in chosen}) == len({b for _, b in chosen}) == pair_total
    sends_first = {e[0] for e in edges if turn[e] == 0 and e[1] == 0}
    picks = []
    for slot in range(4):
        pick = {}
        for here in range(pair_total):
            there, half = needs[here][slot]
            if there == here:
                pick[here] = 0 if (half == 0) == (here in sends_first) else 1
            else:
                pick[here] = 2 + turn[(there, half, here)]
        picks.append(pick)
    is_second = [{h for h, place in table.items() if place} for table in seconds]
    return sends, sends_first, picks, is_second


def choose(pick, arrays):
    chosen = arrays[0]
    for number in range(1, len(arrays)):
        members = {here for here, value in pick.items() if value == number}
        if members:
            chosen = jnp.where(among(members), arrays[number], chosen)
    return chosen


def among(members):
    here = lax.axis_index("pair")
    return functools.reduce(
        jnp.logical_or, [here == member for member in sorted(members)], here < 0
    )


def left(x, by):
    width = x.shape[1]
    return pltpu.roll(x, (width - by) % width, 1) if by % width else x


def right(x, by):
    width = x.shape[1]
    return pltpu.roll(x, by % width, 1) if by % width else x


def down(x, by):
    return pltpu.roll(x, by % x.shape[0], 0)


def lanes_of(x):
    return lax.broadcasted_iota(jnp.int32, x.shape, 1)


def split_pair(first, second):
    half = first.shape[1] // 2
    low = lanes_of(first) < half
    even = jnp.where(low, first, right(second, half))
    odd = jnp.where(low, right(first, half), second)
    return even, odd


def join_pair(even, odd):
    half = even.shape[1] // 2
    low = lanes_of(even) < half
    return jnp.where(low, even, right(odd, half)), jnp.where(low, right(even, half), odd)


def separator(width, back):
    rows = lax.broadcasted_iota(jnp.int32, (width, width), 0)
    cols = lax.broadcasted_iota(jnp.int32, (width, width), 1)
    if back:
        rows, cols = cols, rows
    half = width // 2
    source = jnp.where(cols < half, 2 * cols, 2 * (cols - half) + 1)
    return jnp.where(rows == source, 1.0, 0.0).astype(jnp.float32)


def reorder(block, table):
    return jnp.dot(
        block, table, precision=lax.Precision.HIGHEST, preferred_element_type=jnp.float32
    )


def store_bands(even, odd, band_ref, reach, diags, base=0):
    rows, width = even.shape
    for d in range(reach):
        sums = [None] * 4
        for start in range(0, rows, 8):
            e, o = even[start : start + 8], odd[start : start + 8]
            e_near, o_near = right(e, d), right(o, d)
            parts = (e_near * e, e_near * o, o_near * e if d else None, o_near * o)
            for q in range(4):
                if parts[q] is not None:
                    sums[q] = parts[q] if start == 0 else sums[q] + parts[q]
        if d == 0:
            sums[2] = sums[1]
        for q in range(4):
            row = base + q * diags + d
            band_ref[row : row + 1, :] = jnp.sum(sums[q], axis=0, keepdims=True)
    for q in range(4):
        band_ref[base + q * diags + reach : base + (q + 1) * diags, :] = jnp.zeros(
            (diags - reach, width), jnp.float32
        )


def backwards(x):
    return jnp.take_along_axis(x, x.shape[1] - 1 - lanes_of(x), axis=1)


def dense_bands(even, odd, diags):
    width = even.shape[1]
    gram = lax.dot_general(
        jnp.concatenate((even, odd), axis=1),
        jnp.concatenate((backwards(even), backwards(odd)), axis=1),
        (((0,), (0,)), ((), ())),
        precision=lax.Precision.HIGHEST,
        preferred_element_type=jnp.float32,
    )
    bands = []
    for near in (0, width):
        for far in (0, width):
            quadrant = gram[far : far + width, near : near + width]
            aligned = pltpu.roll(quadrant, 1, 1, stride=1, stride_axis=0)
            bands.append(jnp.transpose(aligned)[:diags])
    return bands


def open_kernel(basis_ref, even_ref, odd_ref, band_ref):
    width = basis_ref.shape[1] // 2
    table = separator(width, False)
    first = reorder(basis_ref[:, :width], table)
    second = reorder(basis_ref[:, width:], table)
    even, odd = split_pair(first, second)
    even_ref[...] = even
    odd_ref[...] = odd
    store_bands(even, odd, band_ref, REACH, DIAGS)


def pair_kernel(gets_first, kept_ref, came_ref, even_ref, odd_ref, band_ref):
    flag = among(gets_first)
    kept, came = kept_ref[...], came_ref[...]
    even, odd = split_pair(jnp.where(flag, came, kept), jnp.where(flag, kept, came))
    even_ref[...] = even
    odd_ref[...] = odd
    store_bands(even, odd, band_ref, REACH, DIAGS)


def jacobi_angle(diag_even, diag_odd, coupling):
    spread = diag_even - diag_odd
    square = spread * spread + 4.0 * coupling * coupling
    inverse = lax.rsqrt(square)
    larger_square = (square * inverse + jnp.abs(spread)) * (0.5 * inverse)
    larger_inverse = lax.rsqrt(larger_square)
    larger = larger_square * larger_inverse
    smaller = coupling * inverse * larger_inverse
    forward = spread >= 0.0
    sign = jnp.where(coupling > 0.0, 1.0, jnp.where(coupling < 0.0, -1.0, 0.0))
    cosine = jnp.where(forward, larger, jnp.abs(smaller))
    sine_part = jnp.where(forward, smaller, sign * larger)
    return cosine, sine_part


def turn_bands(ee, eo, oe, oo, cosine, sine):
    cl, sl = jnp.broadcast_to(cosine, ee.shape), jnp.broadcast_to(sine, ee.shape)
    ck = pltpu.roll(cl, 0, 1, stride=1, stride_axis=0)
    sk = pltpu.roll(sl, 0, 1, stride=1, stride_axis=0)
    ee, oe = ck * ee + sk * oe, ck * oe - sk * ee
    eo, oo = ck * eo + sk * oo, ck * oo - sk * eo
    ee, eo = cl * ee + sl * eo, cl * eo - sl * ee
    oe, oo = cl * oe + sl * oo, cl * oo - sl * oe
    return ee, eo, oe, oo


def move_bands(ee, eo, oe, oo):
    lane = lanes_of(ee)
    diag = lax.broadcasted_iota(jnp.int32, ee.shape, 0)
    last = lane == ee.shape[1] - 1
    first, second = lane == diag, lane == diag + 1
    on, next_on = diag == 0, diag == 1

    ee_new = right(ee, 1)
    ee_new = jnp.where(second, right(jnp.where(on, oo, oe), 1), ee_new)
    near = jnp.where(next_on, down(eo, 1), down(ee, 1))
    ee_new = jnp.where(first, jnp.where(on, ee, right(near, 1)), ee_new)

    eo_new = left(down(eo, -2), 1)
    eo_new = jnp.where(second, left(down(oo, -2), 1), eo_new)
    eo_new = jnp.where(first, left(down(eo, -1), 1), eo_new)
    eo_new = jnp.where(last, down(ee, -1), eo_new)

    oo_new = jnp.where(last, jnp.where(on, ee, down(oe, 1)), left(oo, 1))

    oe_new = right(down(oe, 2), 1)
    oe_new = jnp.where(next_on, jnp.where(first, oo, eo), oe_new)
    oe_new = jnp.where(on, eo_new, oe_new)
    return ee_new, eo_new, oe_new, oo_new


def move_bands_back(ee, eo, oe, oo):
    lane = lanes_of(ee)
    diag = lax.broadcasted_iota(jnp.int32, ee.shape, 0)
    last, first = lane == ee.shape[1] - 1, lane == diag
    on, next_on = diag == 0, diag == 1
    ee_left, oe_left = left(ee, 1), left(down(oe, -2), 1)
    ee_far, eo_far = left(down(ee, -1), 1), right(down(eo, 2), 1)

    ee_old = jnp.where(first, jnp.where(on, ee, ee_far), ee_left)
    ee_old = jnp.where(last, jnp.where(on, oo, down(eo, 1)), ee_old)

    eo_old = jnp.where(on, oe_left, jnp.where(next_on, oe, eo_far))
    eo_old = jnp.where(first, jnp.where(on, ee_far, right(down(eo, 1), 1)), eo_old)
    eo_old = jnp.where(jnp.logical_and(last, on), down(oo, -1), eo_old)

    oe_old = jnp.where(first, ee_left, oe_left)
    oe_old = jnp.where(last, down(oo, -1), oe_old)
    oe_old = jnp.where(on, eo_old, oe_old)

    near = jnp.where(on, ee_left, jnp.where(next_on, oe, eo_far))
    oo_old = jnp.where(first, near, right(oo, 1))
    return ee_old, eo_old, oe_old, oo_old


def move_columns(even, odd):
    lane = lanes_of(even)
    first, last = lane == 0, lane == even.shape[1] - 1
    even_new = jnp.where(first, even, right(jnp.where(first, odd, even), 1))
    odd_new = jnp.where(last, even, left(odd, 1))
    return even_new, odd_new


def columns_home(even, odd):
    lane = lanes_of(even)
    by, end = JSTEPS - 1, even.shape[1] - 1
    mixed = jnp.where(jnp.logical_and(lane >= 1, lane <= by), right(odd, by + 1), even)
    source = jnp.where(lane <= end - by, lane + by, end + 1 - lane)
    even_home = jnp.take_along_axis(mixed, jnp.where(lane == 0, 0, source), axis=1)
    mixed = jnp.where(lane > end - by, left(even, by + 1), odd)
    source = jnp.where(lane >= by, lane - by, end - lane)
    odd_home = jnp.take_along_axis(mixed, source, axis=1)
    return even_home, odd_home


def trim(bands, reach):
    rows = min(bands[0].shape[0], -(-(reach + 1) // 8) * 8)
    return [band[:rows] for band in bands]


def angles_of(bands, carried):
    angles = []
    ahead = 2 * (JSTEPS - 1)
    kept = 2 * ahead if carried else 0
    for step in range(JSTEPS):
        ee, eo, oe, oo = trim(bands, kept + ahead - 2 * step)
        cosine, sine = jacobi_angle(ee[0:1], oo[0:1], eo[0:1])
        angles.append((cosine, sine))
        bands = ee, eo, oe, oo
        if carried or step < JSTEPS - 1:
            bands = turn_bands(ee, eo, oe, oo, cosine, sine)
        if step < JSTEPS - 1:
            bands = move_bands(*bands)
    if carried:
        for step in range(JSTEPS - 1):
            bands = move_bands_back(*trim(bands, kept - 2 * step))
    return angles, bands


def turn_columns(even, odd, angles):
    for step, (cosine, sine) in enumerate(angles):
        even, odd = cosine * even + sine * odd, cosine * odd - sine * even
        if step < JSTEPS - 1:
            even, odd = move_columns(even, odd)
    return columns_home(even, odd)


def turn_kernel(sends_first, even_ref, odd_ref, *refs):
    *band_refs, kept_ref, sent_ref = refs
    bands = [ref[...] for ref in band_refs]
    while len(bands) > 1:
        bands = [bands[i] + bands[i + 1] for i in range(0, len(bands), 2)]
    bands = [bands[0][q * DIAGS : (q + 1) * DIAGS] for q in range(4)]
    angles, _ = angles_of(bands, False)
    first, second = join_pair(*turn_columns(even_ref[...], odd_ref[...], angles))
    flag = among(sends_first)
    kept_ref[...] = jnp.where(flag, second, first)
    sent_ref[...] = jnp.where(flag, first, second)


def near_starts(width):
    half = width // 2
    reach = REACH - 1
    return (half - 2 * reach, width - WINDOW), (0, half - reach)


def cross_partial(x_even, x_odd, y_even, y_odd, x_second, y_second):
    rows, width = x_even.shape
    x_starts, y_starts = near_starts(width)
    lane = lanes_of(x_even)

    def window(even, odd, flag, starts):
        at_zero = jnp.where(flag, left(even, starts[1]), left(even, starts[0]))
        at_next = jnp.where(flag, left(odd, starts[1] - WINDOW), left(odd, starts[0] - WINDOW))
        return jnp.where(lane < WINDOW, at_zero, jnp.where(lane < 2 * WINDOW, at_next, 0.0))

    corner = lax.dot_general(
        window(y_even, y_odd, y_second, y_starts),
        window(x_even, x_odd, x_second, x_starts),
        (((0,), (0,)), ((), ())),
        precision=lax.Precision.HIGHEST,
        preferred_element_type=jnp.float32,
    )
    low = lax.broadcasted_iota(jnp.int32, (WINDOW, width), 1) < 2 * WINDOW
    return jnp.where(low, corner[:WINDOW], right(corner[WINDOW : 2 * WINDOW], 2 * WINDOW))


def spread(packed, place, flag, starts):
    at = place * WINDOW
    return jnp.where(flag, right(packed, starts[1] - at), right(packed, starts[0] - at))


def cross_bands(corner, x_angles, y_angles, x_second, y_second):
    width = corner.shape[1]
    half = width // 2
    x_starts, y_starts = near_starts(width)
    even = jnp.concatenate([spread(corner, p, x_second, x_starts) for p in (0, 2)], axis=0)
    odd = jnp.concatenate([spread(corner, p, x_second, x_starts) for p in (1, 3)], axis=0)
    even, odd = turn_columns(even, odd, x_angles)
    stacked = jnp.concatenate((even, odd), axis=0)
    ends = jnp.where(x_second, left(stacked, width - NEAR), left(stacked, half - NEAR))
    ends = jnp.transpose(ends)[:NEAR]
    even = jnp.concatenate([spread(ends, p, y_second, y_starts) for p in (0, 2)], axis=0)
    odd = jnp.concatenate([spread(ends, p, y_second, y_starts) for p in (1, 3)], axis=0)
    even, odd = turn_columns(even, odd, y_angles)
    even = jnp.where(y_second, even, right(even, half))
    odd = jnp.where(y_second, odd, right(odd, half))
    quadrants = (even[:NEAR], odd[:NEAR], even[NEAR:], odd[NEAR:])
    offset = lanes_of(ends) - lax.broadcasted_iota(jnp.int32, ends.shape, 0) - (half - NEAR)
    diag = lax.broadcasted_iota(jnp.int32, (DIAGS, width), 0)
    bands = [jnp.zeros((DIAGS, width), jnp.float32) for _ in quadrants]
    for d in range(1, REACH):
        here = offset == d
        for q, quadrant in enumerate(quadrants):
            line = jnp.sum(jnp.where(here, quadrant, 0.0), axis=0, keepdims=True)
            bands[q] = jnp.where(diag == d, line, bands[q])
    return bands


def fused_open(picks, is_second, kept_ref, sent_ref, came0_ref, came1_ref, *refs):
    *column_refs, mine_ref, other_ref, parts = refs
    arrays = [ref[...] for ref in (sent_ref, kept_ref, came0_ref, came1_ref)]
    blocks = [choose(pick, arrays) for pick in picks]
    columns = split_pair(*blocks[:2]) + split_pair(*blocks[2:])
    for ref, value in zip(column_refs, columns):
        ref[...] = value
    corner = cross_partial(*columns, among(is_second[0]), among(is_second[1]))
    for i in (0, 1):
        for q, band in enumerate(dense_bands(*columns[2 * i : 2 * i + 2], FAR_DIAGS)):
            parts[i, q * FAR_DIAGS : (q + 1) * FAR_DIAGS, :] = band
        parts[i, 4 * FAR_DIAGS :, :] = corner[i * NEAR : (i + 1) * NEAR]
    odd_core = lax.axis_index("row") % 2
    mine_ref[...] = parts[odd_core]
    other_ref[...] = parts[1 - odd_core]


def fused_turn(x_even, x_odd, y_even, y_odd, x_part, y_part, x_second, y_second):
    half = x_even.shape[1] // 2

    def quadrants(part):
        return [part[q * FAR_DIAGS : (q + 1) * FAR_DIAGS] for q in range(4)]

    x_angles, x_bands = angles_of(quadrants(x_part), True)
    y_angles, y_bands = angles_of(quadrants(y_part), True)
    corner = jnp.concatenate((x_part[4 * FAR_DIAGS :], y_part[4 * FAR_DIAGS :]), axis=0)
    middle = cross_bands(corner, x_angles, y_angles, x_second, y_second)

    def first_half(x):
        return jnp.where(x_second, right(x, half), x)

    def second_half(y):
        return jnp.where(y_second, y, right(y, half))

    lane = lanes_of(middle[0])
    diag = lax.broadcasted_iota(jnp.int32, middle[0].shape, 0)
    bands = [
        jnp.where(
            lane < half,
            first_half(x_bands[q][:DIAGS]),
            jnp.where(lane - diag < half, middle[q], second_half(y_bands[q][:DIAGS])),
        )
        for q in range(4)
    ]
    x_turned = turn_columns(x_even, x_odd, x_angles)
    y_turned = turn_columns(y_even, y_odd, y_angles)
    low = lanes_of(x_even) < half
    even, odd = (
        jnp.where(low, first_half(x), second_half(y)) for x, y in zip(x_turned, y_turned)
    )
    angles, _ = angles_of(bands, False)
    return join_pair(*turn_columns(even, odd, angles))


def fused_kernel(is_second, sends_first, *refs):
    *column_refs, mine_ref, other_ref, kept_ref, sent_ref = refs
    mine, other = mine_ref[...], other_ref[...]
    odd_core = lax.axis_index("row") % 2 == 1
    parts = jnp.where(odd_core, other, mine), jnp.where(odd_core, mine, other)
    first, second = fused_turn(
        *(ref[...] for ref in column_refs),
        *parts,
        among(is_second[0]),
        among(is_second[1]),
    )
    table = separator(first.shape[1], True)
    first, second = reorder(first, table), reorder(second, table)
    flag = among(sends_first)
    kept_ref[...] = jnp.where(flag, second, first)
    sent_ref[...] = jnp.where(flag, first, second)


def pair_sums(arrays):
    while len(arrays) > 1:
        arrays = [arrays[i] + arrays[i + 1] for i in range(0, len(arrays), 2)]
    return arrays[0]


def swap(x, axis, mask):
    return lax.ppermute(x, axis, [(i, i ^ mask) for i in range(lax.axis_size(axis))])


def exchange_groups(x, axis, first_bit=0):
    count = lax.axis_size(axis).bit_length() - 1
    bits = [1 << b for b in range(count)]
    groups = [bits[:1]] + [bits[i : i + 2] for i in range(1, count, 2)]
    arrays = [x]
    for group in groups[first_bit:]:
        x = pair_sums(arrays)
        masks = [group[0]] if len(group) == 1 else [group[0], group[1], group[0] | group[1]]
        arrays = [x] + [swap(x, axis, mask) for mask in masks]
    return arrays


def call(kernel, shapes, *args, scratch=()):
    out = [jax.ShapeDtypeStruct(shape, jnp.float32) for shape in shapes]
    return pl.pallas_call(
        kernel,
        out_shape=out,
        scratch_shapes=[pltpu.VMEM(shape, jnp.float32) for shape in scratch],
        compiler_params=pltpu.CompilerParams(vmem_limit_bytes=32 * 1024 * 1024),
    )(*args)


def per_device(basis):
    rows, cols = basis.shape
    width = cols // 2
    pair_total = lax.axis_size("pair")
    column = (rows, width)
    band = (4 * DIAGS, width)
    part = (4 * FAR_DIAGS + NEAR, width)
    plans = moves(pair_total)
    fused_sends, fused_first, picks, is_second = fused_moves(pair_total)
    even, odd, partial = call(open_kernel, (column, column, band), basis)
    for round_index in range(ROUNDS - 2):
        sends, sends_first, gets_first = plans[round_index]
        ahead = round_index == ROUNDS - 3
        arrays = exchange_groups(partial, "row")
        turn = functools.partial(turn_kernel, fused_first if ahead else sends_first)
        kept, sent = call(turn, (column, column), even, odd, *arrays)
        if not ahead:
            came = lax.ppermute(sent, "pair", sends)
            opening = functools.partial(pair_kernel, gets_first)
            even, odd, partial = call(opening, (column, column, band), kept, came)
    came = [lax.ppermute(x, "pair", s) for x, s in zip((sent, kept), fused_sends)]
    *columns, mine, other = call(
        functools.partial(fused_open, picks, is_second),
        (column,) * 4 + (part,) * 2,
        kept,
        sent,
        *came,
        scratch=((2,) + part,),
    )
    mine = pair_sums(exchange_groups(mine + swap(other, "row", 1), "row", 1))
    other = swap(mine, "row", 1)
    sends, sends_first, gets_first = plans[-1]
    kept, sent = call(
        functools.partial(fused_kernel, is_second, sends_first),
        (column, column),
        *columns,
        mine,
        other,
    )
    came = lax.ppermute(sent, "pair", sends)
    flag = among(gets_first)
    first = jnp.where(flag, came, kept)
    second = jnp.where(flag, kept, came)
    return jnp.concatenate((first, second), axis=1)


def solution(mesh):
    return jax.shard_map(
        per_device,
        mesh=mesh,
        in_specs=(P("row", "pair"),),
        out_specs=P("row", "pair"),
        check_vma=False,
    )
```

```python
import functools

import jax
import jax.numpy as jnp
import numpy as np
from jax import lax
from jax.experimental import pallas as pl
from jax.experimental.pallas import tpu as pltpu
from jax.sharding import PartitionSpec as P

ROUNDS = 4
JSTEPS = 6
REACH = 2 * (JSTEPS - 1) + 1
DIAGS = 16
FAR_DIAGS = 32
WINDOW = 32
NEAR = 16


def tournament_order(pair_count):
    ordering = np.zeros(2 * pair_count, dtype=np.int64)
    ordering[0] = 0
    ordering[2] = 1
    for slot in range(2, pair_count):
        ordering[2 * slot] = 2 * (slot - 1)
    for slot in range(pair_count - 1):
        ordering[2 * slot + 1] = 2 * (slot + 1) + 1
    ordering[2 * pair_count - 1] = 2 * (pair_count - 1)
    return ordering


def host_of(pair, pair_total, round_index):
    if round_index % 2 == 0 or pair == 0:
        return pair
    return min(pair + 1, pair_total - 1) if pair % 2 else pair - 1


def moves(pair_total):
    ordering = tournament_order(pair_total)
    plans = []
    for round_index in range(ROUNDS):
        sends, sends_first, gets_first = [], set(), set()
        for pair in range(pair_total):
            target = host_of(pair, pair_total, round_index + 1)
            for place in (0, 1):
                old = int(ordering[2 * pair + place])
                source = host_of(old // 2, pair_total, round_index)
                if source == target:
                    continue
                sends.append((source, target))
                if old % 2 == 0:
                    sends_first.add(source)
                if place == 0:
                    gets_first.add(target)
        assert len({s for s, _ in sends}) == len(sends) == len({t for _, t in sends})
        plans.append((sends, sends_first, gets_first))
    return plans


def fused_moves(pair_total):
    ordering = tournament_order(pair_total)
    before, last = ROUNDS - 3, ROUNDS - 1
    needs, edges, seconds = {}, [], ({}, {})
    for pair in range(pair_total):
        here = host_of(pair, pair_total, last)
        needs[here] = []
        for place in (0, 1):
            source = int(ordering[2 * pair + place])
            seconds[place][here] = source % 2
            for half in (0, 1):
                old = int(ordering[2 * (source // 2) + half])
                there = host_of(old // 2, pair_total, before)
                needs[here].append((there, old % 2))
                if there != here:
                    edges.append((there, old % 2, here))
    turn, left_over = {}, list(edges)
    while left_over:
        source, _, target = left_over[0]
        start = source
        while True:
            for number, one, other in ((0, source, target), (1, target, source)):
                edge = next(e for e in left_over if (e[0], e[2]) == (one, other))
                turn[edge] = number
                left_over.remove(edge)
            if target == start:
                break
            ahead = [e[2] for e in left_over if e[0] == target]
            source, target = target, ahead[0]
    sends = [[(e[0], e[2]) for e in edges if turn[e] == i] for i in (0, 1)]
    for chosen in sends:
        assert len({a for a, _ in chosen}) == len({b for _, b in chosen}) == pair_total
    sends_first = {e[0] for e in edges if turn[e] == 0 and e[1] == 0}
    picks = []
    for slot in range(4):
        pick = {}
        for here in range(pair_total):
            there, half = needs[here][slot]
            if there == here:
                pick[here] = 0 if (half == 0) == (here in sends_first) else 1
            else:
                pick[here] = 2 + turn[(there, half, here)]
        picks.append(pick)
    is_second = [{h for h, place in table.items() if place} for table in seconds]
    return sends, sends_first, picks, is_second


def choose(pick, arrays):
    chosen = arrays[0]
    for number in range(1, len(arrays)):
        members = {here for here, value in pick.items() if value == number}
        if members:
            chosen = jnp.where(among(members), arrays[number], chosen)
    return chosen


def among(members):
    here = lax.axis_index("pair")
    return functools.reduce(
        jnp.logical_or, [here == member for member in sorted(members)], here < 0
    )


def left(x, by):
    width = x.shape[1]
    return pltpu.roll(x, (width - by) % width, 1) if by % width else x


def right(x, by):
    width = x.shape[1]
    return pltpu.roll(x, by % width, 1) if by % width else x


def down(x, by):
    return pltpu.roll(x, by % x.shape[0], 0)


def lanes_of(x):
    return lax.broadcasted_iota(jnp.int32, x.shape, 1)


def split_pair(first, second):
    half = first.shape[1] // 2
    low = lanes_of(first) < half
    even = jnp.where(low, first, right(second, half))
    odd = jnp.where(low, right(first, half), second)
    return even, odd


def join_pair(even, odd):
    half = even.shape[1] // 2
    low = lanes_of(even) < half
    return jnp.where(low, even, right(odd, half)), jnp.where(low, right(even, half), odd)


def separator(width, back):
    rows = lax.broadcasted_iota(jnp.int32, (width, width), 0)
    cols = lax.broadcasted_iota(jnp.int32, (width, width), 1)
    if back:
        rows, cols = cols, rows
    half = width // 2
    source = jnp.where(cols < half, 2 * cols, 2 * (cols - half) + 1)
    return jnp.where(rows == source, 1.0, 0.0).astype(jnp.float32)


def reorder(block, table):
    return jnp.dot(
        block, table, precision=lax.Precision.HIGHEST, preferred_element_type=jnp.float32
    )


def backwards(x):
    return jnp.take_along_axis(x, x.shape[1] - 1 - lanes_of(x), axis=1)


def dense_bands(even, odd, diags):
    width = even.shape[1]
    gram = lax.dot_general(
        jnp.concatenate((even, odd), axis=1),
        jnp.concatenate((backwards(even), backwards(odd)), axis=1),
        (((0,), (0,)), ((), ())),
        precision=lax.Precision.HIGHEST,
        preferred_element_type=jnp.float32,
    )
    bands = []
    for near in (0, width):
        for far in (0, width):
            quadrant = gram[far : far + width, near : near + width]
            aligned = pltpu.roll(quadrant, 1, 1, stride=1, stride_axis=0)
            bands.append(jnp.transpose(aligned)[:diags])
    return bands


def store_bands(even, odd, band_ref):
    for q, band in enumerate(dense_bands(even, odd, DIAGS)):
        band_ref[q * DIAGS : (q + 1) * DIAGS, :] = band


def open_kernel(basis_ref, even_ref, odd_ref, band_ref):
    width = basis_ref.shape[1] // 2
    table = separator(width, False)
    first = reorder(basis_ref[:, :width], table)
    second = reorder(basis_ref[:, width:], table)
    even, odd = split_pair(first, second)
    even_ref[...] = even
    odd_ref[...] = odd
    store_bands(even, odd, band_ref)


def pair_kernel(gets_first, kept_ref, came_ref, even_ref, odd_ref, band_ref):
    flag = among(gets_first)
    kept, came = kept_ref[...], came_ref[...]
    even, odd = split_pair(jnp.where(flag, came, kept), jnp.where(flag, kept, came))
    even_ref[...] = even
    odd_ref[...] = odd
    store_bands(even, odd, band_ref)


def jacobi_angle(diag_even, diag_odd, coupling):
    spread = diag_even - diag_odd
    square = spread * spread + 4.0 * coupling * coupling
    inverse = lax.rsqrt(square)
    larger_square = (square * inverse + jnp.abs(spread)) * (0.5 * inverse)
    larger_inverse = lax.rsqrt(larger_square)
    larger = larger_square * larger_inverse
    smaller = coupling * inverse * larger_inverse
    forward = spread >= 0.0
    sign = jnp.where(coupling > 0.0, 1.0, jnp.where(coupling < 0.0, -1.0, 0.0))
    cosine = jnp.where(forward, larger, jnp.abs(smaller))
    sine_part = jnp.where(forward, smaller, sign * larger)
    return cosine, sine_part


def turn_bands(ee, eo, oe, oo, cosine, sine):
    cl, sl = jnp.broadcast_to(cosine, ee.shape), jnp.broadcast_to(sine, ee.shape)
    ck = pltpu.roll(cl, 0, 1, stride=1, stride_axis=0)
    sk = pltpu.roll(sl, 0, 1, stride=1, stride_axis=0)
    ee, oe = ck * ee + sk * oe, ck * oe - sk * ee
    eo, oo = ck * eo + sk * oo, ck * oo - sk * eo
    ee, eo = cl * ee + sl * eo, cl * eo - sl * ee
    oe, oo = cl * oe + sl * oo, cl * oo - sl * oe
    return ee, eo, oe, oo


def move_bands(ee, eo, oe, oo):
    lane = lanes_of(ee)
    diag = lax.broadcasted_iota(jnp.int32, ee.shape, 0)
    last = lane == ee.shape[1] - 1
    on, next_on = diag == 0, diag == 1

    near = down(jnp.where(on, eo, ee), 1)
    turned = jnp.where(on, oo, oe)
    mixed = jnp.where(lane == diag, turned, jnp.where(lane == diag - 1, near, ee))
    ee_new = jnp.where(jnp.logical_and(on, lane == 0), ee, right(mixed, 1))

    far = down(jnp.where(last, ee, eo), -1)
    mixed = down(jnp.where(lane == diag, oo, eo), -2)
    mixed = left(jnp.where(lane == diag + 1, far, mixed), 1)
    eo_new = jnp.where(last, far, mixed)

    oo_new = jnp.where(last, jnp.where(on, ee, down(oe, 1)), left(oo, 1))

    oe_new = right(down(oe, 2), 1)
    oe_new = jnp.where(next_on, jnp.where(lane == diag, oo, eo), oe_new)
    oe_new = jnp.where(on, eo_new, oe_new)
    return ee_new, eo_new, oe_new, oo_new


def move_bands_back(ee, eo, oe, oo):
    lane = lanes_of(ee)
    diag = lax.broadcasted_iota(jnp.int32, ee.shape, 0)
    last, first = lane == ee.shape[1] - 1, lane == diag
    on, next_on = diag == 0, diag == 1
    ahead, behind = lane == diag + 1, lane == diag - 1
    eo_down, oo_up = down(eo, 1), down(oo, -1)
    eo_twice = down(eo, 2)

    ee_left = left(jnp.where(ahead, down(ee, -1), ee), 1)
    ee_old = jnp.where(jnp.logical_and(first, on), ee, ee_left)
    ee_old = jnp.where(last, jnp.where(on, oo, eo_down), ee_old)

    oe_left = left(jnp.where(jnp.logical_and(ahead, diag > 0), ee, down(oe, -2)), 1)
    eo_far = right(jnp.where(behind, eo_down, eo_twice), 1)
    eo_old = jnp.where(on, jnp.where(last, oo_up, oe_left), eo_far)
    eo_old = jnp.where(jnp.logical_and(next_on, lane > 1), oe, eo_old)
    eo_old = jnp.where(jnp.logical_and(on, first), ee_left, eo_old)

    oe_old = jnp.where(on, eo_old, jnp.where(last, oo_up, oe_left))

    oo_old = right(jnp.where(behind, eo_twice, oo), 1)
    oo_old = jnp.where(jnp.logical_and(next_on, first), oe, oo_old)
    oo_old = jnp.where(jnp.logical_and(on, first), left(ee, 1), oo_old)
    return ee_old, eo_old, oe_old, oo_old


def move_columns(even, odd):
    lane = lanes_of(even)
    first, last = lane == 0, lane == even.shape[1] - 1
    even_new = jnp.where(first, even, right(jnp.where(first, odd, even), 1))
    odd_new = jnp.where(last, even, left(odd, 1))
    return even_new, odd_new


def columns_home(even, odd):
    lane = lanes_of(even)
    by, end = JSTEPS - 1, even.shape[1] - 1
    mixed = jnp.where(jnp.logical_and(lane >= 1, lane <= by), right(odd, by + 1), even)
    source = jnp.where(lane <= end - by, lane + by, end + 1 - lane)
    even_home = jnp.take_along_axis(mixed, jnp.where(lane == 0, 0, source), axis=1)
    mixed = jnp.where(lane > end - by, left(even, by + 1), odd)
    source = jnp.where(lane >= by, lane - by, end - lane)
    odd_home = jnp.take_along_axis(mixed, source, axis=1)
    return even_home, odd_home


def trim(bands, reach):
    rows = min(bands[0].shape[0], -(-(reach + 1) // 8) * 8)
    return [band[:rows] for band in bands]


def angles_of(bands, carried):
    angles = []
    ahead = 2 * (JSTEPS - 1)
    kept = 2 * ahead if carried else 0
    for step in range(JSTEPS):
        ee, eo, oe, oo = trim(bands, kept + ahead - 2 * step)
        cosine, sine = jacobi_angle(ee[0:1], oo[0:1], eo[0:1])
        angles.append((cosine, sine))
        bands = ee, eo, oe, oo
        if carried or step < JSTEPS - 1:
            bands = turn_bands(ee, eo, oe, oo, cosine, sine)
        if step < JSTEPS - 1:
            bands = move_bands(*bands)
    if carried:
        for step in range(JSTEPS - 1):
            bands = move_bands_back(*trim(bands, kept - 2 * step))
    return angles, bands


def turn_columns(even, odd, angles):
    for step, (cosine, sine) in enumerate(angles):
        even, odd = cosine * even + sine * odd, cosine * odd - sine * even
        if step < JSTEPS - 1:
            even, odd = move_columns(even, odd)
    return columns_home(even, odd)


def turn_kernel(sends_first, even_ref, odd_ref, *refs):
    *band_refs, kept_ref, sent_ref = refs
    bands = [ref[...] for ref in band_refs]
    while len(bands) > 1:
        bands = [bands[i] + bands[i + 1] for i in range(0, len(bands), 2)]
    bands = [bands[0][q * DIAGS : (q + 1) * DIAGS] for q in range(4)]
    angles, _ = angles_of(bands, False)
    first, second = join_pair(*turn_columns(even_ref[...], odd_ref[...], angles))
    flag = among(sends_first)
    kept_ref[...] = jnp.where(flag, second, first)
    sent_ref[...] = jnp.where(flag, first, second)


def near_starts(width):
    half = width // 2
    reach = REACH - 1
    return (half - 2 * reach, width - WINDOW), (0, half - reach)


def cross_partial(x_even, x_odd, y_even, y_odd, x_second, y_second):
    rows, width = x_even.shape
    x_starts, y_starts = near_starts(width)
    lane = lanes_of(x_even)

    def window(even, odd, flag, starts):
        at_zero = jnp.where(flag, left(even, starts[1]), left(even, starts[0]))
        at_next = jnp.where(flag, left(odd, starts[1] - WINDOW), left(odd, starts[0] - WINDOW))
        return jnp.where(lane < WINDOW, at_zero, jnp.where(lane < 2 * WINDOW, at_next, 0.0))

    corner = lax.dot_general(
        window(y_even, y_odd, y_second, y_starts),
        window(x_even, x_odd, x_second, x_starts),
        (((0,), (0,)), ((), ())),
        precision=lax.Precision.HIGHEST,
        preferred_element_type=jnp.float32,
    )
    low = lax.broadcasted_iota(jnp.int32, (WINDOW, width), 1) < 2 * WINDOW
    return jnp.where(low, corner[:WINDOW], right(corner[WINDOW : 2 * WINDOW], 2 * WINDOW))


def spread(packed, place, flag, starts):
    at = place * WINDOW
    return jnp.where(flag, right(packed, starts[1] - at), right(packed, starts[0] - at))


def cross_bands(corner, x_angles, y_angles, x_second, y_second):
    width = corner.shape[1]
    half = width // 2
    x_starts, y_starts = near_starts(width)
    even = jnp.concatenate([spread(corner, p, x_second, x_starts) for p in (0, 2)], axis=0)
    odd = jnp.concatenate([spread(corner, p, x_second, x_starts) for p in (1, 3)], axis=0)
    even, odd = turn_columns(even, odd, x_angles)
    stacked = jnp.concatenate((even, odd), axis=0)
    ends = jnp.where(x_second, left(stacked, width - NEAR), left(stacked, half - NEAR))
    ends = jnp.transpose(ends)[:NEAR]
    even = jnp.concatenate([spread(ends, p, y_second, y_starts) for p in (0, 2)], axis=0)
    odd = jnp.concatenate([spread(ends, p, y_second, y_starts) for p in (1, 3)], axis=0)
    even, odd = turn_columns(even, odd, y_angles)
    even = jnp.where(y_second, even, right(even, half))
    odd = jnp.where(y_second, odd, right(odd, half))
    quadrants = (even[:NEAR], odd[:NEAR], even[NEAR:], odd[NEAR:])
    offset = lanes_of(ends) - lax.broadcasted_iota(jnp.int32, ends.shape, 0) - (half - NEAR)
    diag = lax.broadcasted_iota(jnp.int32, (DIAGS, width), 0)
    bands = [jnp.zeros((DIAGS, width), jnp.float32) for _ in quadrants]
    for d in range(1, REACH):
        here = offset == d
        for q, quadrant in enumerate(quadrants):
            line = jnp.sum(jnp.where(here, quadrant, 0.0), axis=0, keepdims=True)
            bands[q] = jnp.where(diag == d, line, bands[q])
    return bands


def fused_open(picks, is_second, kept_ref, sent_ref, came0_ref, came1_ref, *refs):
    *column_refs, mine_ref, other_ref, parts = refs
    arrays = [ref[...] for ref in (sent_ref, kept_ref, came0_ref, came1_ref)]
    blocks = [choose(pick, arrays) for pick in picks]
    columns = split_pair(*blocks[:2]) + split_pair(*blocks[2:])
    for ref, value in zip(column_refs, columns):
        ref[...] = value
    corner = cross_partial(*columns, among(is_second[0]), among(is_second[1]))
    for i in (0, 1):
        for q, band in enumerate(dense_bands(*columns[2 * i : 2 * i + 2], FAR_DIAGS)):
            parts[i, q * FAR_DIAGS : (q + 1) * FAR_DIAGS, :] = band
        parts[i, 4 * FAR_DIAGS :, :] = corner[i * NEAR : (i + 1) * NEAR]
    odd_core = lax.axis_index("row") % 2
    mine_ref[...] = parts[odd_core]
    other_ref[...] = parts[1 - odd_core]


def fused_turn(x_even, x_odd, y_even, y_odd, x_part, y_part, x_second, y_second):
    half = x_even.shape[1] // 2

    def quadrants(part):
        return [part[q * FAR_DIAGS : (q + 1) * FAR_DIAGS] for q in range(4)]

    x_angles, x_bands = angles_of(quadrants(x_part), True)
    y_angles, y_bands = angles_of(quadrants(y_part), True)
    corner = jnp.concatenate((x_part[4 * FAR_DIAGS :], y_part[4 * FAR_DIAGS :]), axis=0)
    middle = cross_bands(corner, x_angles, y_angles, x_second, y_second)

    def first_half(x):
        return jnp.where(x_second, right(x, half), x)

    def second_half(y):
        return jnp.where(y_second, y, right(y, half))

    lane = lanes_of(middle[0])
    diag = lax.broadcasted_iota(jnp.int32, middle[0].shape, 0)
    bands = [
        jnp.where(
            lane < half,
            first_half(x_bands[q][:DIAGS]),
            jnp.where(lane - diag < half, middle[q], second_half(y_bands[q][:DIAGS])),
        )
        for q in range(4)
    ]
    x_turned = turn_columns(x_even, x_odd, x_angles)
    y_turned = turn_columns(y_even, y_odd, y_angles)
    low = lanes_of(x_even) < half
    even, odd = (
        jnp.where(low, first_half(x), second_half(y)) for x, y in zip(x_turned, y_turned)
    )
    angles, _ = angles_of(bands, False)
    return join_pair(*turn_columns(even, odd, angles))


def fused_kernel(is_second, sends_first, *refs):
    *column_refs, mine_ref, other_ref, kept_ref, sent_ref = refs
    mine, other = mine_ref[...], other_ref[...]
    odd_core = lax.axis_index("row") % 2 == 1
    parts = jnp.where(odd_core, other, mine), jnp.where(odd_core, mine, other)
    first, second = fused_turn(
        *(ref[...] for ref in column_refs),
        *parts,
        among(is_second[0]),
        among(is_second[1]),
    )
    table = separator(first.shape[1], True)
    first, second = reorder(first, table), reorder(second, table)
    flag = among(sends_first)
    kept_ref[...] = jnp.where(flag, second, first)
    sent_ref[...] = jnp.where(flag, first, second)


def pair_sums(arrays):
    while len(arrays) > 1:
        arrays = [arrays[i] + arrays[i + 1] for i in range(0, len(arrays), 2)]
    return arrays[0]


def swap(x, axis, mask):
    return lax.ppermute(x, axis, [(i, i ^ mask) for i in range(lax.axis_size(axis))])


def exchange_groups(x, axis, first_bit=0):
    count = lax.axis_size(axis).bit_length() - 1
    bits = [1 << b for b in range(count)]
    groups = [bits[:1]] + [bits[i : i + 2] for i in range(1, count, 2)]
    arrays = [x]
    for group in groups[first_bit:]:
        x = pair_sums(arrays)
        masks = [group[0]] if len(group) == 1 else [group[0], group[1], group[0] | group[1]]
        arrays = [x] + [swap(x, axis, mask) for mask in masks]
    return arrays


def call(kernel, shapes, *args, scratch=()):
    out = [jax.ShapeDtypeStruct(shape, jnp.float32) for shape in shapes]
    return pl.pallas_call(
        kernel,
        out_shape=out,
        scratch_shapes=[pltpu.VMEM(shape, jnp.float32) for shape in scratch],
        compiler_params=pltpu.CompilerParams(vmem_limit_bytes=32 * 1024 * 1024),
    )(*args)


def per_device(basis):
    rows, cols = basis.shape
    width = cols // 2
    pair_total = lax.axis_size("pair")
    column = (rows, width)
    band = (4 * DIAGS, width)
    part = (4 * FAR_DIAGS + NEAR, width)
    plans = moves(pair_total)
    fused_sends, fused_first, picks, is_second = fused_moves(pair_total)
    even, odd, partial = call(open_kernel, (column, column, band), basis)
    for round_index in range(ROUNDS - 2):
        sends, sends_first, gets_first = plans[round_index]
        ahead = round_index == ROUNDS - 3
        arrays = exchange_groups(partial, "row")
        turn = functools.partial(turn_kernel, fused_first if ahead else sends_first)
        kept, sent = call(turn, (column, column), even, odd, *arrays)
        if not ahead:
            came = lax.ppermute(sent, "pair", sends)
            opening = functools.partial(pair_kernel, gets_first)
            even, odd, partial = call(opening, (column, column, band), kept, came)
    came = [lax.ppermute(x, "pair", s) for x, s in zip((sent, kept), fused_sends)]
    *columns, mine, other = call(
        functools.partial(fused_open, picks, is_second),
        (column,) * 4 + (part,) * 2,
        kept,
        sent,
        *came,
        scratch=((2,) + part,),
    )
    mine = pair_sums(exchange_groups(mine + swap(other, "row", 1), "row", 1))
    other = swap(mine, "row", 1)
    sends, sends_first, gets_first = plans[-1]
    kept, sent = call(
        functools.partial(fused_kernel, is_second, sends_first),
        (column, column),
        *columns,
        mine,
        other,
    )
    came = lax.ppermute(sent, "pair", sends)
    flag = among(gets_first)
    first = jnp.where(flag, came, kept)
    second = jnp.where(flag, kept, came)
    return jnp.concatenate((first, second), axis=1)


def solution(mesh):
    return jax.shard_map(
        per_device,
        mesh=mesh,
        in_specs=(P("row", "pair"),),
        out_specs=P("row", "pair"),
        check_vma=False,
    )
```

```python
import functools

import jax
import jax.numpy as jnp
import numpy as np
from jax import lax
from jax.experimental import pallas as pl
from jax.experimental.pallas import tpu as pltpu
from jax.sharding import PartitionSpec as P

ROUNDS = 4
JSTEPS = 6
REACH = 2 * (JSTEPS - 1) + 1
DIAGS = 16
FAR_DIAGS = 32
WINDOW = 32
NEAR = 16


def tournament_order(pair_count):
    ordering = np.zeros(2 * pair_count, dtype=np.int64)
    ordering[0] = 0
    ordering[2] = 1
    for slot in range(2, pair_count):
        ordering[2 * slot] = 2 * (slot - 1)
    for slot in range(pair_count - 1):
        ordering[2 * slot + 1] = 2 * (slot + 1) + 1
    ordering[2 * pair_count - 1] = 2 * (pair_count - 1)
    return ordering


def host_of(pair, pair_total, round_index):
    if round_index % 2 == 0 or pair == 0:
        return pair
    return min(pair + 1, pair_total - 1) if pair % 2 else pair - 1


def moves(pair_total):
    ordering = tournament_order(pair_total)
    plans = []
    for round_index in range(ROUNDS):
        sends, sends_first, gets_first = [], set(), set()
        for pair in range(pair_total):
            target = host_of(pair, pair_total, round_index + 1)
            for place in (0, 1):
                old = int(ordering[2 * pair + place])
                source = host_of(old // 2, pair_total, round_index)
                if source == target:
                    continue
                sends.append((source, target))
                if old % 2 == 0:
                    sends_first.add(source)
                if place == 0:
                    gets_first.add(target)
        assert len({s for s, _ in sends}) == len(sends) == len({t for _, t in sends})
        plans.append((sends, sends_first, gets_first))
    return plans


def fused_moves(pair_total):
    ordering = tournament_order(pair_total)
    before, last = ROUNDS - 3, ROUNDS - 1
    needs, edges, seconds = {}, [], ({}, {})
    for pair in range(pair_total):
        here = host_of(pair, pair_total, last)
        needs[here] = []
        for place in (0, 1):
            source = int(ordering[2 * pair + place])
            seconds[place][here] = source % 2
            for half in (0, 1):
                old = int(ordering[2 * (source // 2) + half])
                there = host_of(old // 2, pair_total, before)
                needs[here].append((there, old % 2))
                if there != here:
                    edges.append((there, old % 2, here))
    turn, left_over = {}, list(edges)
    while left_over:
        source, _, target = left_over[0]
        start = source
        while True:
            for number, one, other in ((0, source, target), (1, target, source)):
                edge = next(e for e in left_over if (e[0], e[2]) == (one, other))
                turn[edge] = number
                left_over.remove(edge)
            if target == start:
                break
            ahead = [e[2] for e in left_over if e[0] == target]
            source, target = target, ahead[0]
    sends = [[(e[0], e[2]) for e in edges if turn[e] == i] for i in (0, 1)]
    for chosen in sends:
        assert len({a for a, _ in chosen}) == len({b for _, b in chosen}) == pair_total
    sends_first = {e[0] for e in edges if turn[e] == 0 and e[1] == 0}
    picks = []
    for slot in range(4):
        pick = {}
        for here in range(pair_total):
            there, half = needs[here][slot]
            if there == here:
                pick[here] = 0 if (half == 0) == (here in sends_first) else 1
            else:
                pick[here] = 2 + turn[(there, half, here)]
        picks.append(pick)
    is_second = [{h for h, place in table.items() if place} for table in seconds]
    return sends, sends_first, picks, is_second


def choose(pick, arrays):
    chosen = arrays[0]
    for number in range(1, len(arrays)):
        members = {here for here, value in pick.items() if value == number}
        if members:
            chosen = jnp.where(among(members), arrays[number], chosen)
    return chosen


def among(members):
    here = lax.axis_index("pair")
    return functools.reduce(
        jnp.logical_or, [here == member for member in sorted(members)], here < 0
    )


def left(x, by):
    width = x.shape[1]
    return pltpu.roll(x, (width - by) % width, 1) if by % width else x


def right(x, by):
    width = x.shape[1]
    return pltpu.roll(x, by % width, 1) if by % width else x


def down(x, by):
    return pltpu.roll(x, by % x.shape[0], 0)


def lanes_of(x):
    return lax.broadcasted_iota(jnp.int32, x.shape, 1)


def split_pair(first, second):
    half = first.shape[1] // 2
    low = lanes_of(first) < half
    even = jnp.where(low, first, right(second, half))
    odd = jnp.where(low, right(first, half), second)
    return even, odd


def join_pair(even, odd):
    half = even.shape[1] // 2
    low = lanes_of(even) < half
    return jnp.where(low, even, right(odd, half)), jnp.where(low, right(even, half), odd)


def take_lanes(x, source):
    return jnp.take_along_axis(x, jnp.broadcast_to(source, x.shape), axis=1)


def line_lanes(x):
    return lax.broadcasted_iota(jnp.int32, (1, x.shape[1]), 1)


def separate(first, second):
    lane = line_lanes(first)
    half = first.shape[1] // 2
    low = lane < half
    source = 2 * jnp.where(low, lane, lane - half)
    return tuple(
        jnp.where(low, take_lanes(first, source + odd), take_lanes(second, source + odd))
        for odd in (0, 1)
    )


def backwards(x):
    return jnp.take_along_axis(x, x.shape[1] - 1 - lanes_of(x), axis=1)


def dense_bands(even, odd, diags):
    width = even.shape[1]
    gram = lax.dot_general(
        jnp.concatenate((even, odd), axis=1),
        jnp.concatenate((backwards(even), backwards(odd)), axis=1),
        (((0,), (0,)), ((), ())),
        precision=lax.Precision.HIGHEST,
        preferred_element_type=jnp.float32,
    )
    bands = []
    for near in (0, width):
        for far in (0, width):
            quadrant = gram[far : far + width, near : near + width]
            aligned = pltpu.roll(quadrant, 1, 1, stride=1, stride_axis=0)
            bands.append(jnp.transpose(aligned)[:diags])
    return bands


def store_bands(even, odd, band_ref, diags):
    for q, band in enumerate(dense_bands(even, odd, diags)):
        band_ref[q * diags : (q + 1) * diags, :] = band


def open_kernel(basis_ref, even_ref, odd_ref, band_ref):
    width = basis_ref.shape[1] // 2
    even, odd = separate(basis_ref[:, :width], basis_ref[:, width:])
    even_ref[...] = even
    odd_ref[...] = odd
    store_bands(even, odd, band_ref, DIAGS)


def pair_kernel(gets_first, kept_ref, came_ref, even_ref, odd_ref, band_ref):
    flag = among(gets_first)
    kept, came = kept_ref[...], came_ref[...]
    even, odd = split_pair(jnp.where(flag, came, kept), jnp.where(flag, kept, came))
    even_ref[...] = even
    odd_ref[...] = odd
    store_bands(even, odd, band_ref, DIAGS)


def jacobi_angle(diag_even, diag_odd, coupling):
    spread = diag_even - diag_odd
    square = spread * spread + 4.0 * coupling * coupling
    inverse = lax.rsqrt(square)
    larger_square = (square * inverse + jnp.abs(spread)) * (0.5 * inverse)
    larger_inverse = lax.rsqrt(larger_square)
    larger = larger_square * larger_inverse
    smaller = coupling * inverse * larger_inverse
    forward = spread >= 0.0
    sign = jnp.where(coupling > 0.0, 1.0, jnp.where(coupling < 0.0, -1.0, 0.0))
    cosine = jnp.where(forward, larger, jnp.abs(smaller))
    sine_part = jnp.where(forward, smaller, sign * larger)
    return cosine, sine_part


def turn_bands(ee, eo, oe, oo, cosine, sine):
    cl, sl = jnp.broadcast_to(cosine, ee.shape), jnp.broadcast_to(sine, ee.shape)
    ck = pltpu.roll(cl, 0, 1, stride=1, stride_axis=0)
    sk = pltpu.roll(sl, 0, 1, stride=1, stride_axis=0)
    ee, oe = ck * ee + sk * oe, ck * oe - sk * ee
    eo, oo = ck * eo + sk * oo, ck * oo - sk * eo
    ee, eo = cl * ee + sl * eo, cl * eo - sl * ee
    oe, oo = cl * oe + sl * oo, cl * oo - sl * oe
    return ee, eo, oe, oo


def move_bands(ee, eo, oe, oo):
    lane = lanes_of(ee)
    diag = lax.broadcasted_iota(jnp.int32, ee.shape, 0)
    last = lane == ee.shape[1] - 1
    on, next_on = diag == 0, diag == 1

    near = down(jnp.where(on, eo, ee), 1)
    turned = jnp.where(on, oo, oe)
    mixed = jnp.where(lane == diag, turned, jnp.where(lane == diag - 1, near, ee))
    ee_new = jnp.where(jnp.logical_and(on, lane == 0), ee, right(mixed, 1))

    far = down(jnp.where(last, ee, eo), -1)
    mixed = down(jnp.where(lane == diag, oo, eo), -2)
    mixed = left(jnp.where(lane == diag + 1, far, mixed), 1)
    eo_new = jnp.where(last, far, mixed)

    oo_new = jnp.where(last, jnp.where(on, ee, down(oe, 1)), left(oo, 1))

    oe_new = right(down(oe, 2), 1)
    oe_new = jnp.where(next_on, jnp.where(lane == diag, oo, eo), oe_new)
    oe_new = jnp.where(on, eo_new, oe_new)
    return ee_new, eo_new, oe_new, oo_new


def move_bands_back(ee, eo, oe, oo):
    lane = lanes_of(ee)
    diag = lax.broadcasted_iota(jnp.int32, ee.shape, 0)
    last, first = lane == ee.shape[1] - 1, lane == diag
    on, next_on = diag == 0, diag == 1
    ahead, behind = lane == diag + 1, lane == diag - 1
    eo_down, oo_up = down(eo, 1), down(oo, -1)
    eo_twice = down(eo, 2)

    ee_left = left(jnp.where(ahead, down(ee, -1), ee), 1)
    ee_old = jnp.where(jnp.logical_and(first, on), ee, ee_left)
    ee_old = jnp.where(last, jnp.where(on, oo, eo_down), ee_old)

    oe_left = left(jnp.where(jnp.logical_and(ahead, diag > 0), ee, down(oe, -2)), 1)
    eo_far = right(jnp.where(behind, eo_down, eo_twice), 1)
    eo_old = jnp.where(on, jnp.where(last, oo_up, oe_left), eo_far)
    eo_old = jnp.where(jnp.logical_and(next_on, lane > 1), oe, eo_old)
    eo_old = jnp.where(jnp.logical_and(on, first), ee_left, eo_old)

    oe_old = jnp.where(on, eo_old, jnp.where(last, oo_up, oe_left))

    oo_old = right(jnp.where(behind, eo_twice, oo), 1)
    oo_old = jnp.where(jnp.logical_and(next_on, first), oe, oo_old)
    oo_old = jnp.where(jnp.logical_and(on, first), left(ee, 1), oo_old)
    return ee_old, eo_old, oe_old, oo_old


def move_columns(even, odd):
    lane = lanes_of(even)
    first, last = lane == 0, lane == even.shape[1] - 1
    even_new = jnp.where(first, even, right(jnp.where(first, odd, even), 1))
    odd_new = jnp.where(last, even, left(odd, 1))
    return even_new, odd_new


def home_sources(even, odd):
    lane = line_lanes(even)
    by, end = JSTEPS - 1, even.shape[1] - 1
    entered = jnp.logical_and(lane >= 1, lane <= by)
    mixed_even = jnp.where(entered, right(odd, by + 1), even)
    mixed_odd = jnp.where(lane > end - by, left(even, by + 1), odd)

    def even_source(place):
        moved = jnp.where(place <= end - by, place + by, end + 1 - place)
        return jnp.where(place == 0, 0, moved)

    def odd_source(place):
        return jnp.where(place >= by, place - by, end - place)

    return (mixed_even, even_source), (mixed_odd, odd_source)


def columns_home(even, odd, shifted=None):
    lane = line_lanes(even)
    if shifted is not None:
        half = even.shape[1] // 2
        lane = jnp.where(shifted, jnp.where(lane < half, lane + half, lane - half), lane)
    return tuple(take_lanes(x, source(lane)) for x, source in home_sources(even, odd))


def blocks_home(even, odd):
    lane = line_lanes(even)
    (even, even_source), (odd, odd_source) = home_sources(even, odd)
    blocks = []
    for block in (0, 1):
        place = block * (even.shape[1] // 2) + lane // 2
        from_even, from_odd = (
            take_lanes(x, source(place)) for x, source in ((even, even_source), (odd, odd_source))
        )
        blocks.append(jnp.where(lane % 2 == 0, from_even, from_odd))
    return blocks


def trim(bands, reach):
    rows = min(bands[0].shape[0], -(-(reach + 1) // 8) * 8)
    return [band[:rows] for band in bands]


def angles_of(bands, carried):
    angles = []
    ahead = 2 * (JSTEPS - 1)
    kept = 2 * ahead if carried else 0
    for step in range(JSTEPS):
        ee, eo, oe, oo = trim(bands, kept + ahead - 2 * step)
        cosine, sine = jacobi_angle(ee[0:1], oo[0:1], eo[0:1])
        angles.append((cosine, sine))
        bands = ee, eo, oe, oo
        if carried or step < JSTEPS - 1:
            bands = turn_bands(ee, eo, oe, oo, cosine, sine)
        if step < JSTEPS - 1:
            bands = move_bands(*bands)
    if carried:
        for step in range(JSTEPS - 1):
            bands = move_bands_back(*trim(bands, kept - 2 * step))
    return angles, bands


def turned(even, odd, angles):
    for step, (cosine, sine) in enumerate(angles):
        even, odd = cosine * even + sine * odd, cosine * odd - sine * even
        if step < JSTEPS - 1:
            even, odd = move_columns(even, odd)
    return even, odd


def turn_columns(even, odd, angles, shifted=None):
    return columns_home(*turned(even, odd, angles), shifted)


def turn_kernel(sends_first, even_ref, odd_ref, *refs):
    *band_refs, kept_ref, sent_ref = refs
    bands = [ref[...] for ref in band_refs]
    band = pair_sums(bands)
    bands = [band[q * DIAGS : (q + 1) * DIAGS] for q in range(4)]
    angles, _ = angles_of(bands, False)
    first, second = join_pair(*turn_columns(even_ref[...], odd_ref[...], angles))
    flag = among(sends_first)
    kept_ref[...] = jnp.where(flag, second, first)
    sent_ref[...] = jnp.where(flag, first, second)


def near_starts(width):
    half = width // 2
    reach = REACH - 1
    return (half - 2 * reach, width - WINDOW), (0, half - reach)


def cross_partial(x_even, x_odd, y_even, y_odd, x_second, y_second):
    rows, width = x_even.shape
    x_starts, y_starts = near_starts(width)
    lane = lanes_of(x_even)

    def window(even, odd, flag, starts):
        at_zero = jnp.where(flag, left(even, starts[1]), left(even, starts[0]))
        at_next = jnp.where(flag, left(odd, starts[1] - WINDOW), left(odd, starts[0] - WINDOW))
        return jnp.where(lane < WINDOW, at_zero, jnp.where(lane < 2 * WINDOW, at_next, 0.0))

    corner = lax.dot_general(
        window(y_even, y_odd, y_second, y_starts),
        window(x_even, x_odd, x_second, x_starts),
        (((0,), (0,)), ((), ())),
        precision=lax.Precision.HIGHEST,
        preferred_element_type=jnp.float32,
    )
    low = lax.broadcasted_iota(jnp.int32, (WINDOW, width), 1) < 2 * WINDOW
    return jnp.where(low, corner[:WINDOW], right(corner[WINDOW : 2 * WINDOW], 2 * WINDOW))


def spread(packed, place, flag, starts):
    at = place * WINDOW
    return jnp.where(flag, right(packed, starts[1] - at), right(packed, starts[0] - at))


def cross_bands(corner, x_angles, y_angles, x_second, y_second):
    width = corner.shape[1]
    half = width // 2
    x_starts, y_starts = near_starts(width)
    even = jnp.concatenate([spread(corner, p, x_second, x_starts) for p in (0, 2)], axis=0)
    odd = jnp.concatenate([spread(corner, p, x_second, x_starts) for p in (1, 3)], axis=0)
    even, odd = turn_columns(even, odd, x_angles)
    stacked = jnp.concatenate((even, odd), axis=0)
    ends = jnp.where(x_second, left(stacked, width - NEAR), left(stacked, half - NEAR))
    ends = jnp.transpose(ends)[:NEAR]
    even = jnp.concatenate([spread(ends, p, y_second, y_starts) for p in (0, 2)], axis=0)
    odd = jnp.concatenate([spread(ends, p, y_second, y_starts) for p in (1, 3)], axis=0)
    even, odd = turn_columns(even, odd, y_angles)
    even = jnp.where(y_second, even, right(even, half))
    odd = jnp.where(y_second, odd, right(odd, half))
    quadrants = (even[:NEAR], odd[:NEAR], even[NEAR:], odd[NEAR:])
    offset = lanes_of(ends) - lax.broadcasted_iota(jnp.int32, ends.shape, 0) - (half - NEAR)
    diag = lax.broadcasted_iota(jnp.int32, (DIAGS, width), 0)
    bands = [jnp.zeros((DIAGS, width), jnp.float32) for _ in quadrants]
    for d in range(1, REACH):
        here = offset == d
        for q, quadrant in enumerate(quadrants):
            line = jnp.sum(jnp.where(here, quadrant, 0.0), axis=0, keepdims=True)
            bands[q] = jnp.where(diag == d, line, bands[q])
    return bands


def halves_swapped(is_second):
    return among(is_second[0]), jnp.logical_not(among(is_second[1]))


def on_odd_core():
    return lax.axis_index("row") % 2 == 1


def fused_open(picks, is_second, kept_ref, sent_ref, came0_ref, came1_ref, *refs):
    *column_refs, corner_ref, other_ref = refs
    arrays = [ref[...] for ref in (sent_ref, kept_ref, came0_ref, came1_ref)]
    blocks = [choose(pick, arrays) for pick in picks]
    x, y = split_pair(*blocks[:2]), split_pair(*blocks[2:])
    corner = cross_partial(*x, *y, among(is_second[0]), among(is_second[1]))
    flag = on_odd_core()
    mine = [jnp.where(flag, b, a) for a, b in zip(x, y)]
    theirs = [jnp.where(flag, a, b) for a, b in zip(x, y)]
    for ref, value in zip(column_refs, mine + theirs):
        ref[...] = value
    corner_ref[...] = jnp.where(flag, corner[NEAR:], corner[:NEAR])
    store_bands(*theirs, other_ref, FAR_DIAGS)
    other_ref[4 * FAR_DIAGS :, :] = jnp.where(flag, corner[:NEAR], corner[NEAR:])


def bands_kernel(even_ref, odd_ref, corner_ref, part_ref):
    store_bands(even_ref[...], odd_ref[...], part_ref, FAR_DIAGS)
    part_ref[4 * FAR_DIAGS :, :] = corner_ref[...]


def angles_kernel(*refs):
    *part_refs, found_ref = refs
    part = pair_sums([ref[...] for ref in part_refs])
    quadrants = [part[q * FAR_DIAGS : (q + 1) * FAR_DIAGS] for q in range(4)]
    angles, bands = angles_of(quadrants, True)
    for step, pair in enumerate(angles):
        for i in (0, 1):
            found_ref[2 * step + i : 2 * step + i + 1, :] = pair[i]
    spare = NEAR - 2 * JSTEPS
    found_ref[2 * JSTEPS : NEAR, :] = jnp.zeros((spare, part.shape[1]), jnp.float32)
    for q in range(4):
        found_ref[NEAR + q * DIAGS : NEAR + (q + 1) * DIAGS, :] = bands[q][:DIAGS]
    found_ref[NEAR + 4 * DIAGS :, :] = part[4 * FAR_DIAGS :]


def angles_in(found):
    return [(found[2 * i : 2 * i + 1], found[2 * i + 1 : 2 * i + 2]) for i in range(JSTEPS)]


def columns_kernel(is_second, even_ref, odd_ref, found_ref, *out_refs):
    x_swapped, y_swapped = halves_swapped(is_second)
    flag = on_odd_core()
    swapped = jnp.logical_or(
        jnp.logical_and(flag, y_swapped), jnp.logical_and(jnp.logical_not(flag), x_swapped)
    )
    columns = turn_columns(even_ref[...], odd_ref[...], angles_in(found_ref[...]), swapped)
    for ref, value in zip(out_refs, columns):
        ref[...] = value


def last_bands(x_found, y_found, x_second, y_second):
    corner = jnp.concatenate((x_found[NEAR + 4 * DIAGS :], y_found[NEAR + 4 * DIAGS :]), axis=0)
    middle = cross_bands(corner, angles_in(x_found), angles_in(y_found), x_second, y_second)
    half = corner.shape[1] // 2
    lane = lanes_of(middle[0])
    diag = lax.broadcasted_iota(jnp.int32, middle[0].shape, 0)
    bands = []
    for q in range(4):
        rows = slice(NEAR + q * DIAGS, NEAR + (q + 1) * DIAGS)
        x, y = x_found[rows], y_found[rows]
        x = jnp.where(x_second, right(x, half), x)
        y = jnp.where(y_second, y, right(y, half))
        crossing = jnp.where(lane - diag < half, middle[q], y)
        bands.append(jnp.where(lane < half, x, crossing))
    return bands


def last_kernel(is_second, sends_first, *refs):
    mine_even, mine_odd, even_ref, odd_ref, found_ref, other_ref, kept_ref, sent_ref = refs
    found, other = found_ref[...], other_ref[...]
    flag = on_odd_core()
    x_found, y_found = jnp.where(flag, other, found), jnp.where(flag, found, other)
    bands = last_bands(x_found, y_found, among(is_second[0]), among(is_second[1]))
    x_swapped, y_swapped = halves_swapped(is_second)
    swapped = jnp.logical_or(
        jnp.logical_and(flag, x_swapped), jnp.logical_and(jnp.logical_not(flag), y_swapped)
    )
    theirs = turn_columns(even_ref[...], odd_ref[...], angles_in(other), swapped)
    low = line_lanes(found) < found.shape[1] // 2
    from_mine = jnp.logical_xor(low, flag)
    even = jnp.where(from_mine, mine_even[...], theirs[0])
    odd = jnp.where(from_mine, mine_odd[...], theirs[1])
    angles, _ = angles_of(bands, False)
    first, second = blocks_home(*turned(even, odd, angles))
    flag = among(sends_first)
    kept_ref[...] = jnp.where(flag, second, first)
    sent_ref[...] = jnp.where(flag, first, second)


def pair_sums(arrays):
    while len(arrays) > 1:
        arrays = [arrays[i] + arrays[i + 1] for i in range(0, len(arrays), 2)]
    return arrays[0]


def swap(x, axis, mask):
    return lax.ppermute(x, axis, [(i, i ^ mask) for i in range(lax.axis_size(axis))])


def exchange_groups(x, axis, first_bit=0):
    count = lax.axis_size(axis).bit_length() - 1
    bits = [1 << b for b in range(count)]
    groups = [bits[:1]] + [bits[i : i + 2] for i in range(1, count, 2)]
    arrays = [x]
    for group in groups[first_bit:]:
        x = pair_sums(arrays)
        masks = [group[0]] if len(group) == 1 else [group[0], group[1], group[0] | group[1]]
        arrays = [x] + [swap(x, axis, mask) for mask in masks]
    return arrays


def call(kernel, shapes, *args):
    out = [jax.ShapeDtypeStruct(shape, jnp.float32) for shape in shapes]
    return pl.pallas_call(
        kernel,
        out_shape=out,
        compiler_params=pltpu.CompilerParams(vmem_limit_bytes=32 * 1024 * 1024),
    )(*args)


def per_device(basis):
    rows, cols = basis.shape
    width = cols // 2
    pair_total = lax.axis_size("pair")
    column = (rows, width)
    band = (4 * DIAGS, width)
    part = (4 * FAR_DIAGS + NEAR, width)
    plans = moves(pair_total)
    fused_sends, fused_first, picks, is_second = fused_moves(pair_total)
    even, odd, partial = call(open_kernel, (column, column, band), basis)
    for round_index in range(ROUNDS - 2):
        sends, sends_first, gets_first = plans[round_index]
        ahead = round_index == ROUNDS - 3
        arrays = exchange_groups(partial, "row")
        turn = functools.partial(turn_kernel, fused_first if ahead else sends_first)
        kept, sent = call(turn, (column, column), even, odd, *arrays)
        if not ahead:
            came = lax.ppermute(sent, "pair", sends)
            opening = functools.partial(pair_kernel, gets_first)
            even, odd, partial = call(opening, (column, column, band), kept, came)
    came = [lax.ppermute(x, "pair", s) for x, s in zip((sent, kept), fused_sends)]
    *columns, corner, other = call(
        functools.partial(fused_open, picks, is_second),
        (column,) * 4 + ((NEAR, width), part),
        kept,
        sent,
        *came,
    )
    other = swap(other, "row", 1)
    (mine,) = call(bands_kernel, (part,), *columns[:2], corner)
    (found,) = call(
        angles_kernel, ((2 * NEAR + 4 * DIAGS, width),), *exchange_groups(mine + other, "row", 1)
    )
    other = swap(found, "row", 1)
    turn = functools.partial(columns_kernel, is_second)
    columns[:2] = call(turn, (column, column), *columns[:2], found)
    sends, sends_first, gets_first = plans[-1]
    last = functools.partial(last_kernel, is_second, sends_first)
    kept, sent = call(last, (column, column), *columns, found, other)
    came = lax.ppermute(sent, "pair", sends)
    flag = among(gets_first)
    first = jnp.where(flag, came, kept)
    second = jnp.where(flag, kept, came)
    return jnp.concatenate((first, second), axis=1)


def solution(mesh):
    return jax.shard_map(
        per_device,
        mesh=mesh,
        in_specs=(P("row", "pair"),),
        out_specs=P("row", "pair"),
        check_vma=False,
    )
```

```python
import functools

import jax
import jax.numpy as jnp
import numpy as np
from jax import lax
from jax.experimental import pallas as pl
from jax.experimental.pallas import tpu as pltpu
from jax.sharding import PartitionSpec as P

ROUNDS = 4
JSTEPS = 6
REACH = 2 * (JSTEPS - 1) + 1
DIAGS = 16
FAR_DIAGS = 32
WINDOW = 32
NEAR = 16
STRIP = 16


def tournament_order(pair_count):
    ordering = np.zeros(2 * pair_count, dtype=np.int64)
    ordering[0] = 0
    ordering[2] = 1
    for slot in range(2, pair_count):
        ordering[2 * slot] = 2 * (slot - 1)
    for slot in range(pair_count - 1):
        ordering[2 * slot + 1] = 2 * (slot + 1) + 1
    ordering[2 * pair_count - 1] = 2 * (pair_count - 1)
    return ordering


def host_of(pair, pair_total, round_index):
    if round_index % 2 == 0 or pair == 0:
        return pair
    return min(pair + 1, pair_total - 1) if pair % 2 else pair - 1


def last_moves(pair_total):
    ordering = tournament_order(pair_total)
    sends, sends_first, gets_first = [], set(), set()
    for pair in range(pair_total):
        target = host_of(pair, pair_total, ROUNDS)
        for place in (0, 1):
            old = int(ordering[2 * pair + place])
            source = host_of(old // 2, pair_total, ROUNDS - 1)
            if source == target:
                continue
            sends.append((source, target))
            if old % 2 == 0:
                sends_first.add(source)
            if place == 0:
                gets_first.add(target)
    assert len({s for s, _ in sends}) == len(sends) == len({t for _, t in sends})
    return sends, sends_first, gets_first


def first_moves(pair_total):
    ordering = tournament_order(pair_total)
    sends, sends_second, gets_second, own_second = [], set(), set(), set()
    seconds = (set(), set())
    for pair in range(pair_total):
        here = host_of(pair, pair_total, 1)
        for place in (0, 1):
            old = int(ordering[2 * pair + place])
            if old % 2:
                seconds[place].add(here)
            if old // 2 == here:
                if place:
                    own_second.add(here)
                continue
            sends.append((old // 2, here))
            if old % 2:
                sends_second.add(old // 2)
                gets_second.add(here)
    assert len({s for s, _ in sends}) == len(sends) == len({t for _, t in sends})
    return sends, sends_second, gets_second, own_second, seconds


def fused_moves(pair_total):
    ordering = tournament_order(pair_total)
    before, last = ROUNDS - 3, ROUNDS - 1
    needs, edges, seconds = {}, [], ({}, {})
    for pair in range(pair_total):
        here = host_of(pair, pair_total, last)
        needs[here] = []
        for place in (0, 1):
            source = int(ordering[2 * pair + place])
            seconds[place][here] = source % 2
            for half in (0, 1):
                old = int(ordering[2 * (source // 2) + half])
                there = host_of(old // 2, pair_total, before)
                needs[here].append((there, old % 2))
                if there != here:
                    edges.append((there, old % 2, here))
    turn, left_over = {}, list(edges)
    while left_over:
        source, _, target = left_over[0]
        start = source
        while True:
            for number, one, other in ((0, source, target), (1, target, source)):
                edge = next(e for e in left_over if (e[0], e[2]) == (one, other))
                turn[edge] = number
                left_over.remove(edge)
            if target == start:
                break
            ahead = [e[2] for e in left_over if e[0] == target]
            source, target = target, ahead[0]
    sends = [[(e[0], e[2]) for e in edges if turn[e] == i] for i in (0, 1)]
    for chosen in sends:
        assert len({a for a, _ in chosen}) == len({b for _, b in chosen}) == pair_total
    sends_first = {e[0] for e in edges if turn[e] == 0 and e[1] == 0}
    picks = []
    for slot in range(4):
        pick = {}
        for here in range(pair_total):
            there, half = needs[here][slot]
            if there == here:
                pick[here] = 0 if (half == 0) == (here in sends_first) else 1
            else:
                pick[here] = 2 + turn[(there, half, here)]
        picks.append(pick)
    is_second = [{h for h, place in table.items() if place} for table in seconds]
    return sends, sends_first, picks, is_second


def choose(pick, arrays):
    chosen = arrays[0]
    for number in range(1, len(arrays)):
        members = {here for here, value in pick.items() if value == number}
        if members:
            chosen = jnp.where(among(members), arrays[number], chosen)
    return chosen


def among(members):
    here = lax.axis_index("pair")
    return functools.reduce(
        jnp.logical_or, [here == member for member in sorted(members)], here < 0
    )


def left(x, by):
    width = x.shape[1]
    return pltpu.roll(x, (width - by) % width, 1) if by % width else x


def right(x, by):
    width = x.shape[1]
    return pltpu.roll(x, by % width, 1) if by % width else x


def down(x, by):
    return pltpu.roll(x, by % x.shape[0], 0)


def lanes_of(x):
    return lax.broadcasted_iota(jnp.int32, x.shape, 1)


def split_pair(first, second):
    half = first.shape[1] // 2
    low = lanes_of(first) < half
    even = jnp.where(low, first, right(second, half))
    odd = jnp.where(low, right(first, half), second)
    return even, odd


def join_pair(even, odd):
    half = even.shape[1] // 2
    low = lanes_of(even) < half
    return jnp.where(low, even, right(odd, half)), jnp.where(low, right(even, half), odd)


def take_lanes(x, source):
    return jnp.take_along_axis(x, jnp.broadcast_to(source, x.shape), axis=1)


def line_lanes(x):
    return lax.broadcasted_iota(jnp.int32, (1, x.shape[1]), 1)


def separate(first, second):
    lane = line_lanes(first)
    half = first.shape[1] // 2
    low = lane < half
    source = 2 * jnp.where(low, lane, lane - half)
    return tuple(
        jnp.where(low, take_lanes(first, source + odd), take_lanes(second, source + odd))
        for odd in (0, 1)
    )


def backwards(x):
    return jnp.take_along_axis(x, x.shape[1] - 1 - lanes_of(x), axis=1)


def dense_bands(even, odd, diags):
    width = even.shape[1]
    gram = lax.dot_general(
        jnp.concatenate((even, odd), axis=1),
        jnp.concatenate((backwards(even), backwards(odd)), axis=1),
        (((0,), (0,)), ((), ())),
        precision=lax.Precision.HIGHEST,
        preferred_element_type=jnp.float32,
    )
    bands = []
    for near in (0, width):
        for far in (0, width):
            quadrant = gram[far : far + width, near : near + width]
            aligned = pltpu.roll(quadrant, 1, 1, stride=1, stride_axis=0)
            bands.append(jnp.transpose(aligned)[:diags])
    return bands


def store_bands(even, odd, band_ref, diags):
    for q, band in enumerate(dense_bands(even, odd, diags)):
        band_ref[q * diags : (q + 1) * diags, :] = band


def open_kernel(sends_second, basis_ref, even_ref, odd_ref, payload_ref):
    rows, cols = basis_ref.shape
    width = cols // 2
    half = width // 2
    even, odd = separate(basis_ref[:, :width], basis_ref[:, width:])
    even_ref[...] = even
    odd_ref[...] = odd
    flag = among(sends_second)
    even, odd = (jnp.where(flag, left(x, half - STRIP), x) for x in (even, odd))
    payload_ref[:rows] = jnp.where(line_lanes(even) < half, even, right(odd, half))
    group = rows * 2 * STRIP // width
    strips = jnp.zeros((group, width), jnp.float32)
    for i in range(rows // group):
        for j, x in enumerate((even, odd)):
            start = (2 * i + j) * STRIP
            lane = line_lanes(x)
            here = jnp.logical_and(lane >= start, lane < start + STRIP)
            strips = jnp.where(here, left(x[i * group : (i + 1) * group], half - start), strips)
    payload_ref[rows:] = strips


def unpacked(payload, rows, second):
    width = payload.shape[1]
    half = width // 2
    lane = line_lanes(payload)
    main, strips = payload[:rows], payload[rows:]
    group = strips.shape[0]
    columns = []
    for j, x in enumerate((main, left(main, half))):
        ends = [right(strips, half - (2 * i + j) * STRIP) for i in range(rows // group)]
        x = jnp.where(lane < half, x, jnp.where(lane < half + STRIP, jnp.concatenate(ends), 0.0))
        columns.append(jnp.where(second, right(x, half - STRIP), x))
    return columns


def jacobi_angle(diag_even, diag_odd, coupling):
    spread = diag_even - diag_odd
    square = spread * spread + 4.0 * coupling * coupling
    inverse = lax.rsqrt(square)
    larger_square = (square * inverse + jnp.abs(spread)) * (0.5 * inverse)
    larger_inverse = lax.rsqrt(larger_square)
    larger = larger_square * larger_inverse
    smaller = coupling * inverse * larger_inverse
    forward = spread >= 0.0
    sign = jnp.where(coupling > 0.0, 1.0, jnp.where(coupling < 0.0, -1.0, 0.0))
    cosine = jnp.where(forward, larger, jnp.abs(smaller))
    sine_part = jnp.where(forward, smaller, sign * larger)
    return cosine, sine_part


def turn_bands(ee, eo, oe, oo, cosine, sine):
    cl, sl = jnp.broadcast_to(cosine, ee.shape), jnp.broadcast_to(sine, ee.shape)
    ck = pltpu.roll(cl, 0, 1, stride=1, stride_axis=0)
    sk = pltpu.roll(sl, 0, 1, stride=1, stride_axis=0)
    ee, oe = ck * ee + sk * oe, ck * oe - sk * ee
    eo, oo = ck * eo + sk * oo, ck * oo - sk * eo
    ee, eo = cl * ee + sl * eo, cl * eo - sl * ee
    oe, oo = cl * oe + sl * oo, cl * oo - sl * oe
    return ee, eo, oe, oo


def move_bands(ee, eo, oe, oo):
    lane = lanes_of(ee)
    diag = lax.broadcasted_iota(jnp.int32, ee.shape, 0)
    last = lane == ee.shape[1] - 1
    on, next_on = diag == 0, diag == 1

    near = down(jnp.where(on, eo, ee), 1)
    turned = jnp.where(on, oo, oe)
    mixed = jnp.where(lane == diag, turned, jnp.where(lane == diag - 1, near, ee))
    ee_new = jnp.where(jnp.logical_and(on, lane == 0), ee, right(mixed, 1))

    far = down(jnp.where(last, ee, eo), -1)
    mixed = down(jnp.where(lane == diag, oo, eo), -2)
    mixed = left(jnp.where(lane == diag + 1, far, mixed), 1)
    eo_new = jnp.where(last, far, mixed)

    oo_new = jnp.where(last, jnp.where(on, ee, down(oe, 1)), left(oo, 1))

    oe_new = right(down(oe, 2), 1)
    oe_new = jnp.where(next_on, jnp.where(lane == diag, oo, eo), oe_new)
    oe_new = jnp.where(on, eo_new, oe_new)
    return ee_new, eo_new, oe_new, oo_new


def move_bands_back(ee, eo, oe, oo):
    lane = lanes_of(ee)
    diag = lax.broadcasted_iota(jnp.int32, ee.shape, 0)
    last, first = lane == ee.shape[1] - 1, lane == diag
    on, next_on = diag == 0, diag == 1
    ahead, behind = lane == diag + 1, lane == diag - 1
    eo_down, oo_up = down(eo, 1), down(oo, -1)
    eo_twice = down(eo, 2)

    ee_left = left(jnp.where(ahead, down(ee, -1), ee), 1)
    ee_old = jnp.where(jnp.logical_and(first, on), ee, ee_left)
    ee_old = jnp.where(last, jnp.where(on, oo, eo_down), ee_old)

    oe_left = left(jnp.where(jnp.logical_and(ahead, diag > 0), ee, down(oe, -2)), 1)
    eo_far = right(jnp.where(behind, eo_down, eo_twice), 1)
    eo_old = jnp.where(on, jnp.where(last, oo_up, oe_left), eo_far)
    eo_old = jnp.where(jnp.logical_and(next_on, lane > 1), oe, eo_old)
    eo_old = jnp.where(jnp.logical_and(on, first), ee_left, eo_old)

    oe_old = jnp.where(on, eo_old, jnp.where(last, oo_up, oe_left))

    oo_old = right(jnp.where(behind, eo_twice, oo), 1)
    oo_old = jnp.where(jnp.logical_and(next_on, first), oe, oo_old)
    oo_old = jnp.where(jnp.logical_and(on, first), left(ee, 1), oo_old)
    return ee_old, eo_old, oe_old, oo_old


def move_columns(even, odd):
    lane = lanes_of(even)
    first, last = lane == 0, lane == even.shape[1] - 1
    even_new = jnp.where(first, even, right(jnp.where(first, odd, even), 1))
    odd_new = jnp.where(last, even, left(odd, 1))
    return even_new, odd_new


def home_sources(even, odd):
    lane = line_lanes(even)
    by, end = JSTEPS - 1, even.shape[1] - 1
    entered = jnp.logical_and(lane >= 1, lane <= by)
    mixed_even = jnp.where(entered, right(odd, by + 1), even)
    mixed_odd = jnp.where(lane > end - by, left(even, by + 1), odd)

    def even_source(place):
        moved = jnp.where(place <= end - by, place + by, end + 1 - place)
        return jnp.where(place == 0, 0, moved)

    def odd_source(place):
        return jnp.where(place >= by, place - by, end - place)

    return (mixed_even, even_source), (mixed_odd, odd_source)


def columns_home(even, odd, shifted=None):
    lane = line_lanes(even)
    if shifted is not None:
        half = even.shape[1] // 2
        lane = jnp.where(shifted, jnp.where(lane < half, lane + half, lane - half), lane)
    return tuple(take_lanes(x, source(lane)) for x, source in home_sources(even, odd))


def blocks_home(even, odd):
    lane = line_lanes(even)
    (even, even_source), (odd, odd_source) = home_sources(even, odd)
    blocks = []
    for block in (0, 1):
        place = block * (even.shape[1] // 2) + lane // 2
        from_even, from_odd = (
            take_lanes(x, source(place)) for x, source in ((even, even_source), (odd, odd_source))
        )
        blocks.append(jnp.where(lane % 2 == 0, from_even, from_odd))
    return blocks


def trim(bands, reach):
    rows = min(bands[0].shape[0], -(-(reach + 1) // 8) * 8)
    return [band[:rows] for band in bands]


def angles_of(bands, carried):
    angles = []
    ahead = 2 * (JSTEPS - 1)
    kept = 2 * ahead if carried else 0
    for step in range(JSTEPS):
        ee, eo, oe, oo = trim(bands, kept + ahead - 2 * step)
        cosine, sine = jacobi_angle(ee[0:1], oo[0:1], eo[0:1])
        angles.append((cosine, sine))
        bands = ee, eo, oe, oo
        if carried or step < JSTEPS - 1:
            bands = turn_bands(ee, eo, oe, oo, cosine, sine)
        if step < JSTEPS - 1:
            bands = move_bands(*bands)
    if carried:
        for step in range(JSTEPS - 1):
            bands = move_bands_back(*trim(bands, kept - 2 * step))
    return angles, bands


def turned(even, odd, angles):
    for step, (cosine, sine) in enumerate(angles):
        even, odd = cosine * even + sine * odd, cosine * odd - sine * even
        if step < JSTEPS - 1:
            even, odd = move_columns(even, odd)
    return even, odd


def turn_columns(even, odd, angles, shifted=None):
    return columns_home(*turned(even, odd, angles), shifted)


def near_starts(width):
    half = width // 2
    reach = REACH - 1
    return (half - 2 * reach, width - WINDOW), (0, half - reach)


def cross_partial(x_even, x_odd, y_even, y_odd, x_second, y_second):
    rows, width = x_even.shape
    x_starts, y_starts = near_starts(width)
    lane = lanes_of(x_even)

    def window(even, odd, flag, starts):
        at_zero = jnp.where(flag, left(even, starts[1]), left(even, starts[0]))
        at_next = jnp.where(flag, left(odd, starts[1] - WINDOW), left(odd, starts[0] - WINDOW))
        return jnp.where(lane < WINDOW, at_zero, jnp.where(lane < 2 * WINDOW, at_next, 0.0))

    corner = lax.dot_general(
        window(y_even, y_odd, y_second, y_starts),
        window(x_even, x_odd, x_second, x_starts),
        (((0,), (0,)), ((), ())),
        precision=lax.Precision.HIGHEST,
        preferred_element_type=jnp.float32,
    )
    low = lax.broadcasted_iota(jnp.int32, (WINDOW, width), 1) < 2 * WINDOW
    return jnp.where(low, corner[:WINDOW], right(corner[WINDOW : 2 * WINDOW], 2 * WINDOW))


def spread(packed, place, flag, starts):
    at = place * WINDOW
    return jnp.where(flag, right(packed, starts[1] - at), right(packed, starts[0] - at))


def cross_bands(corner, x_angles, y_angles, x_second, y_second):
    width = corner.shape[1]
    half = width // 2
    x_starts, y_starts = near_starts(width)
    even = jnp.concatenate([spread(corner, p, x_second, x_starts) for p in (0, 2)], axis=0)
    odd = jnp.concatenate([spread(corner, p, x_second, x_starts) for p in (1, 3)], axis=0)
    even, odd = turn_columns(even, odd, x_angles)
    stacked = jnp.concatenate((even, odd), axis=0)
    ends = jnp.where(x_second, left(stacked, width - NEAR), left(stacked, half - NEAR))
    ends = jnp.transpose(ends)[:NEAR]
    even = jnp.concatenate([spread(ends, p, y_second, y_starts) for p in (0, 2)], axis=0)
    odd = jnp.concatenate([spread(ends, p, y_second, y_starts) for p in (1, 3)], axis=0)
    even, odd = turn_columns(even, odd, y_angles)
    even = jnp.where(y_second, even, right(even, half))
    odd = jnp.where(y_second, odd, right(odd, half))
    quadrants = (even[:NEAR], odd[:NEAR], even[NEAR:], odd[NEAR:])
    offset = lanes_of(ends) - lax.broadcasted_iota(jnp.int32, ends.shape, 0) - (half - NEAR)
    diag = lax.broadcasted_iota(jnp.int32, (DIAGS, width), 0)
    bands = [jnp.zeros((DIAGS, width), jnp.float32) for _ in quadrants]
    for d in range(1, REACH):
        here = offset == d
        for q, quadrant in enumerate(quadrants):
            line = jnp.sum(jnp.where(here, quadrant, 0.0), axis=0, keepdims=True)
            bands[q] = jnp.where(diag == d, line, bands[q])
    return bands


def either(flag, one, other):
    return jnp.logical_or(jnp.logical_and(flag, one), jnp.logical_and(jnp.logical_not(flag), other))


def halves_swapped(is_second):
    return among(is_second[0]), jnp.logical_not(among(is_second[1]))


def on_odd_core():
    return lax.axis_index("row") % 2 == 1


def far_starts(width):
    return REACH - 1, width // 2


def pack_far(bands, flag):
    width = bands[0].shape[1]
    half, count = width // 2, (FAR_DIAGS - DIAGS) // 2
    lane = line_lanes(bands[0])
    packed = []
    for band in bands:
        one, two = band[DIAGS : DIAGS + count], band[DIAGS + count :]
        one, two = (
            jnp.where(flag, left(x, far_starts(width)[1] - at), left(x, far_starts(width)[0] - at))
            for x, at in ((one, 0), (two, half))
        )
        packed.append(jnp.concatenate((band[:DIAGS], jnp.where(lane < half, one, two)), axis=0))
    return packed


def unpack_far(packed, flag):
    width = packed.shape[1]
    half = width // 2
    parts = [packed[:DIAGS]]
    for at in (0, half):
        starts = [start - at for start in far_starts(width)]
        x = packed[DIAGS:]
        parts.append(jnp.where(flag, right(x, starts[1]), right(x, starts[0])))
    return jnp.concatenate(parts, axis=0)


PACKED = DIAGS + (FAR_DIAGS - DIAGS) // 2


def store_part(even, odd, corner, flag, part_ref):
    bands = pack_far(dense_bands(even, odd, FAR_DIAGS), flag)
    for q, band in enumerate(bands):
        part_ref[q * PACKED : (q + 1) * PACKED, :] = band
    part_ref[4 * PACKED :, :] = corner


def open_pairs(is_second, x, y, column_refs, corner_ref, other_ref):
    x_second, y_second = among(is_second[0]), among(is_second[1])
    corner = cross_partial(*x, *y, x_second, y_second)
    flag = on_odd_core()
    mine = [jnp.where(flag, b, a) for a, b in zip(x, y)]
    theirs = [jnp.where(flag, a, b) for a, b in zip(x, y)]
    for ref, value in zip(column_refs, mine + theirs):
        ref[...] = value
    corner_ref[...] = jnp.where(flag, corner[NEAR:], corner[:NEAR])
    store_part(
        *theirs,
        jnp.where(flag, corner[:NEAR], corner[NEAR:]),
        either(flag, x_second, y_second),
        other_ref,
    )


def first_open(own_second, gets_second, is_second, even_ref, odd_ref, payload_ref, *refs):
    *column_refs, corner_ref, other_ref = refs
    own = even_ref[...], odd_ref[...]
    came = unpacked(payload_ref[...], own[0].shape[0], among(gets_second))
    flag = among(own_second)
    x = [jnp.where(flag, b, a) for a, b in zip(own, came)]
    y = [jnp.where(flag, a, b) for a, b in zip(own, came)]
    open_pairs(is_second, x, y, column_refs, corner_ref, other_ref)


def fused_open(picks, is_second, kept_ref, sent_ref, came0_ref, came1_ref, *refs):
    *column_refs, corner_ref, other_ref = refs
    arrays = [ref[...] for ref in (sent_ref, kept_ref, came0_ref, came1_ref)]
    blocks = [choose(pick, arrays) for pick in picks]
    x, y = split_pair(*blocks[:2]), split_pair(*blocks[2:])
    open_pairs(is_second, x, y, column_refs, corner_ref, other_ref)


def own_second_flag(is_second):
    return either(on_odd_core(), among(is_second[1]), among(is_second[0]))


def bands_kernel(is_second, even_ref, odd_ref, corner_ref, part_ref):
    flag = own_second_flag(is_second)
    store_part(even_ref[...], odd_ref[...], corner_ref[...], flag, part_ref)


def angles_kernel(is_second, *refs):
    *part_refs, found_ref = refs
    part = pair_sums([ref[...] for ref in part_refs])
    flag = own_second_flag(is_second)
    quadrants = [unpack_far(part[q * PACKED : (q + 1) * PACKED], flag) for q in range(4)]
    angles, bands = angles_of(quadrants, True)
    for step, pair in enumerate(angles):
        for i in (0, 1):
            found_ref[2 * step + i : 2 * step + i + 1, :] = pair[i]
    spare = NEAR - 2 * JSTEPS
    found_ref[2 * JSTEPS : NEAR, :] = jnp.zeros((spare, part.shape[1]), jnp.float32)
    for q in range(4):
        found_ref[NEAR + q * DIAGS : NEAR + (q + 1) * DIAGS, :] = bands[q][:DIAGS]
    found_ref[NEAR + 4 * DIAGS :, :] = part[4 * PACKED :]


def angles_in(found):
    return [(found[2 * i : 2 * i + 1], found[2 * i + 1 : 2 * i + 2]) for i in range(JSTEPS)]


def columns_kernel(is_second, even_ref, odd_ref, found_ref, *out_refs):
    x_swapped, y_swapped = halves_swapped(is_second)
    swapped = either(on_odd_core(), y_swapped, x_swapped)
    columns = turn_columns(even_ref[...], odd_ref[...], angles_in(found_ref[...]), swapped)
    for ref, value in zip(out_refs, columns):
        ref[...] = value


def next_bands(x_found, y_found, x_second, y_second):
    corner = jnp.concatenate((x_found[NEAR + 4 * DIAGS :], y_found[NEAR + 4 * DIAGS :]), axis=0)
    middle = cross_bands(corner, angles_in(x_found), angles_in(y_found), x_second, y_second)
    half = corner.shape[1] // 2
    lane = lanes_of(middle[0])
    diag = lax.broadcasted_iota(jnp.int32, middle[0].shape, 0)
    bands = []
    for q in range(4):
        rows = slice(NEAR + q * DIAGS, NEAR + (q + 1) * DIAGS)
        x, y = x_found[rows], y_found[rows]
        x = jnp.where(x_second, right(x, half), x)
        y = jnp.where(y_second, y, right(y, half))
        crossing = jnp.where(lane - diag < half, middle[q], y)
        bands.append(jnp.where(lane < half, x, crossing))
    return bands


def next_kernel(is_second, sends_first, in_order, *refs):
    mine_even, mine_odd, even_ref, odd_ref, found_ref, other_ref, kept_ref, sent_ref = refs
    found, other = found_ref[...], other_ref[...]
    flag = on_odd_core()
    x_found, y_found = jnp.where(flag, other, found), jnp.where(flag, found, other)
    bands = next_bands(x_found, y_found, among(is_second[0]), among(is_second[1]))
    x_swapped, y_swapped = halves_swapped(is_second)
    swapped = either(flag, x_swapped, y_swapped)
    theirs = turn_columns(even_ref[...], odd_ref[...], angles_in(other), swapped)
    low = line_lanes(found) < found.shape[1] // 2
    from_mine = jnp.logical_xor(low, flag)
    even = jnp.where(from_mine, mine_even[...], theirs[0])
    odd = jnp.where(from_mine, mine_odd[...], theirs[1])
    angles, _ = angles_of(bands, False)
    even, odd = turned(even, odd, angles)
    first, second = blocks_home(even, odd) if in_order else join_pair(*columns_home(even, odd))
    flag = among(sends_first)
    kept_ref[...] = jnp.where(flag, second, first)
    sent_ref[...] = jnp.where(flag, first, second)


def pair_sums(arrays):
    while len(arrays) > 1:
        arrays = [arrays[i] + arrays[i + 1] for i in range(0, len(arrays), 2)]
    return arrays[0]


def swap(x, axis, mask):
    return lax.ppermute(x, axis, [(i, i ^ mask) for i in range(lax.axis_size(axis))])


def exchange_groups(x, axis, first_bit=0):
    count = lax.axis_size(axis).bit_length() - 1
    bits = [1 << b for b in range(count)]
    groups = [bits[:1]] + [bits[i : i + 2] for i in range(1, count, 2)]
    arrays = [x]
    for group in groups[first_bit:]:
        x = pair_sums(arrays)
        masks = [group[0]] if len(group) == 1 else [group[0], group[1], group[0] | group[1]]
        arrays = [x] + [swap(x, axis, mask) for mask in masks]
    return arrays


def call(kernel, shapes, *args):
    out = [jax.ShapeDtypeStruct(shape, jnp.float32) for shape in shapes]
    return pl.pallas_call(
        kernel,
        out_shape=out,
        compiler_params=pltpu.CompilerParams(vmem_limit_bytes=32 * 1024 * 1024),
    )(*args)


def two_rounds(opened, is_second, sends_first, in_order):
    *columns, corner, other = opened
    column, width = columns[0].shape, columns[0].shape[1]
    other = swap(other, "row", 1)
    bands = functools.partial(bands_kernel, is_second)
    (mine,) = call(bands, (other.shape,), *columns[:2], corner)
    (found,) = call(
        functools.partial(angles_kernel, is_second),
        ((2 * NEAR + 4 * DIAGS, width),),
        *exchange_groups(mine + other, "row", 1),
    )
    other = swap(found, "row", 1)
    turn = functools.partial(columns_kernel, is_second)
    columns[:2] = call(turn, (column, column), *columns[:2], found)
    turn = functools.partial(next_kernel, is_second, sends_first, in_order)
    return call(turn, (column, column), *columns, found, other)


def per_device(basis):
    rows, cols = basis.shape
    width = cols // 2
    pair_total = lax.axis_size("pair")
    column = (rows, width)
    opened = (column,) * 4 + ((NEAR, width), (4 * PACKED + NEAR, width))
    payload = (rows + rows * 2 * STRIP // width, width)

    sends, sends_second, gets_second, own_second, is_second = first_moves(pair_total)
    opening = functools.partial(open_kernel, sends_second)
    even, odd, sent = call(opening, (column, column, payload), basis)
    came = lax.ppermute(sent, "pair", sends)
    opening = functools.partial(first_open, own_second, gets_second, is_second)
    arrays = call(opening, opened, even, odd, came)
    sends, sends_first, picks, next_second = fused_moves(pair_total)
    kept, sent = two_rounds(arrays, is_second, sends_first, False)

    came = [lax.ppermute(x, "pair", s) for x, s in zip((sent, kept), sends)]
    opening = functools.partial(fused_open, picks, next_second)
    arrays = call(opening, opened, kept, sent, *came)
    sends, sends_first, gets_first = last_moves(pair_total)
    kept, sent = two_rounds(arrays, next_second, sends_first, True)

    came = lax.ppermute(sent, "pair", sends)
    flag = among(gets_first)
    first = jnp.where(flag, came, kept)
    second = jnp.where(flag, kept, came)
    return jnp.concatenate((first, second), axis=1)


def solution(mesh):
    return jax.shard_map(
        per_device,
        mesh=mesh,
        in_specs=(P("row", "pair"),),
        out_specs=P("row", "pair"),
        check_vma=False,
    )
```

```python
import functools

import jax
import jax.numpy as jnp
import numpy as np
from jax import lax
from jax.experimental import pallas as pl
from jax.experimental.pallas import tpu as pltpu
from jax.sharding import PartitionSpec as P

ROUNDS = 4
JSTEPS = 6
REACH = 2 * (JSTEPS - 1) + 1
DIAGS = 16
FAR_DIAGS = 32
WINDOW = 32
NEAR = 16
STRIP = 16


def tournament_order(pair_count):
    ordering = np.zeros(2 * pair_count, dtype=np.int64)
    ordering[0] = 0
    ordering[2] = 1
    for slot in range(2, pair_count):
        ordering[2 * slot] = 2 * (slot - 1)
    for slot in range(pair_count - 1):
        ordering[2 * slot + 1] = 2 * (slot + 1) + 1
    ordering[2 * pair_count - 1] = 2 * (pair_count - 1)
    return ordering


def host_of(pair, pair_total, round_index):
    if round_index % 2 == 0 or pair == 0:
        return pair
    return min(pair + 1, pair_total - 1) if pair % 2 else pair - 1


def last_moves(pair_total):
    ordering = tournament_order(pair_total)
    sends, sends_first, gets_first = [], set(), set()
    for pair in range(pair_total):
        target = host_of(pair, pair_total, ROUNDS)
        for place in (0, 1):
            old = int(ordering[2 * pair + place])
            source = host_of(old // 2, pair_total, ROUNDS - 1)
            if source == target:
                continue
            sends.append((source, target))
            if old % 2 == 0:
                sends_first.add(source)
            if place == 0:
                gets_first.add(target)
    assert len({s for s, _ in sends}) == len(sends) == len({t for _, t in sends})
    return sends, sends_first, gets_first


def first_moves(pair_total):
    ordering = tournament_order(pair_total)
    sends, sends_second, gets_second, own_second = [], set(), set(), set()
    seconds = (set(), set())
    for pair in range(pair_total):
        here = host_of(pair, pair_total, 1)
        for place in (0, 1):
            old = int(ordering[2 * pair + place])
            if old % 2:
                seconds[place].add(here)
            if old // 2 == here:
                if place:
                    own_second.add(here)
                continue
            sends.append((old // 2, here))
            if old % 2:
                sends_second.add(old // 2)
                gets_second.add(here)
    assert len({s for s, _ in sends}) == len(sends) == len({t for _, t in sends})
    return sends, sends_second, gets_second, own_second, seconds


def fused_moves(pair_total):
    ordering = tournament_order(pair_total)
    before, last = ROUNDS - 3, ROUNDS - 1
    needs, edges, seconds = {}, [], ({}, {})
    for pair in range(pair_total):
        here = host_of(pair, pair_total, last)
        needs[here] = []
        for place in (0, 1):
            source = int(ordering[2 * pair + place])
            seconds[place][here] = source % 2
            for half in (0, 1):
                old = int(ordering[2 * (source // 2) + half])
                there = host_of(old // 2, pair_total, before)
                needs[here].append((there, old % 2))
                if there != here:
                    edges.append((there, old % 2, here))
    turn, left_over = {}, list(edges)
    while left_over:
        source, _, target = left_over[0]
        start = source
        while True:
            for number, one, other in ((0, source, target), (1, target, source)):
                edge = next(e for e in left_over if (e[0], e[2]) == (one, other))
                turn[edge] = number
                left_over.remove(edge)
            if target == start:
                break
            ahead = [e[2] for e in left_over if e[0] == target]
            source, target = target, ahead[0]
    sends = [[(e[0], e[2]) for e in edges if turn[e] == i] for i in (0, 1)]
    for chosen in sends:
        assert len({a for a, _ in chosen}) == len({b for _, b in chosen}) == pair_total
    sends_first = {e[0] for e in edges if turn[e] == 0 and e[1] == 0}
    picks = []
    for slot in range(4):
        pick = {}
        for here in range(pair_total):
            there, half = needs[here][slot]
            if there == here:
                pick[here] = 0 if (half == 0) == (here in sends_first) else 1
            else:
                pick[here] = 2 + turn[(there, half, here)]
        picks.append(pick)
    is_second = [{h for h, place in table.items() if place} for table in seconds]
    return sends, sends_first, picks, is_second


def choose(pick, arrays):
    chosen = arrays[0]
    for number in range(1, len(arrays)):
        members = {here for here, value in pick.items() if value == number}
        if members:
            chosen = jnp.where(among(members), arrays[number], chosen)
    return chosen


def among(members):
    here = lax.axis_index("pair")
    return functools.reduce(
        jnp.logical_or, [here == member for member in sorted(members)], here < 0
    )


def left(x, by):
    width = x.shape[1]
    return pltpu.roll(x, (width - by) % width, 1) if by % width else x


def right(x, by):
    width = x.shape[1]
    return pltpu.roll(x, by % width, 1) if by % width else x


def down(x, by):
    return pltpu.roll(x, by % x.shape[0], 0)


def lanes_of(x):
    return lax.broadcasted_iota(jnp.int32, x.shape, 1)


def split_pair(first, second):
    half = first.shape[1] // 2
    low = lanes_of(first) < half
    even = jnp.where(low, first, right(second, half))
    odd = jnp.where(low, right(first, half), second)
    return even, odd


def join_pair(even, odd):
    half = even.shape[1] // 2
    low = lanes_of(even) < half
    return jnp.where(low, even, right(odd, half)), jnp.where(low, right(even, half), odd)


def take_lanes(x, source):
    return jnp.take_along_axis(x, jnp.broadcast_to(source, x.shape), axis=1)


def line_lanes(x):
    return lax.broadcasted_iota(jnp.int32, (1, x.shape[1]), 1)


def separate(first, second):
    lane = line_lanes(first)
    half = first.shape[1] // 2
    low = lane < half
    source = 2 * jnp.where(low, lane, lane - half)
    return tuple(
        jnp.where(low, take_lanes(first, source + odd), take_lanes(second, source + odd))
        for odd in (0, 1)
    )


def backwards(x):
    return jnp.take_along_axis(x, x.shape[1] - 1 - lanes_of(x), axis=1)


def dense_bands(even, odd, diags):
    width = even.shape[1]
    gram = lax.dot_general(
        jnp.concatenate((even, odd), axis=1),
        jnp.concatenate((backwards(even), backwards(odd)), axis=1),
        (((0,), (0,)), ((), ())),
        precision=lax.Precision.HIGHEST,
        preferred_element_type=jnp.float32,
    )
    bands = []
    for near in (0, width):
        for far in (0, width):
            quadrant = gram[far : far + width, near : near + width]
            aligned = pltpu.roll(quadrant, 1, 1, stride=1, stride_axis=0)
            bands.append(jnp.transpose(aligned)[:diags])
    return bands


def store_bands(even, odd, band_ref, diags):
    for q, band in enumerate(dense_bands(even, odd, diags)):
        band_ref[q * diags : (q + 1) * diags, :] = band


def open_kernel(sends_second, basis_ref, even_ref, odd_ref, payload_ref):
    rows, cols = basis_ref.shape
    width = cols // 2
    half = width // 2
    even, odd = separate(basis_ref[:, :width], basis_ref[:, width:])
    even_ref[...] = even
    odd_ref[...] = odd
    flag = among(sends_second)
    even, odd = (jnp.where(flag, left(x, half - STRIP), x) for x in (even, odd))
    payload_ref[:rows] = jnp.where(line_lanes(even) < half, even, right(odd, half))
    group = rows * 2 * STRIP // width
    strips = jnp.zeros((group, width), jnp.float32)
    for i in range(rows // group):
        for j, x in enumerate((even, odd)):
            start = (2 * i + j) * STRIP
            lane = line_lanes(x)
            here = jnp.logical_and(lane >= start, lane < start + STRIP)
            strips = jnp.where(here, left(x[i * group : (i + 1) * group], half - start), strips)
    payload_ref[rows:] = strips


def unpacked(payload, rows, second):
    width = payload.shape[1]
    half = width // 2
    lane = line_lanes(payload)
    main, strips = payload[:rows], payload[rows:]
    group = strips.shape[0]
    columns = []
    for j, x in enumerate((main, left(main, half))):
        ends = [right(strips, half - (2 * i + j) * STRIP) for i in range(rows // group)]
        x = jnp.where(lane < half, x, jnp.where(lane < half + STRIP, jnp.concatenate(ends), 0.0))
        columns.append(jnp.where(second, right(x, half - STRIP), x))
    return columns


def jacobi_angle(diag_even, diag_odd, coupling):
    spread = diag_even - diag_odd
    square = spread * spread + 4.0 * coupling * coupling
    inverse = lax.rsqrt(square)
    larger_square = (square * inverse + jnp.abs(spread)) * (0.5 * inverse)
    larger_inverse = lax.rsqrt(larger_square)
    larger = larger_square * larger_inverse
    smaller = coupling * inverse * larger_inverse
    forward = spread >= 0.0
    sign = jnp.where(coupling > 0.0, 1.0, jnp.where(coupling < 0.0, -1.0, 0.0))
    cosine = jnp.where(forward, larger, jnp.abs(smaller))
    sine_part = jnp.where(forward, smaller, sign * larger)
    return cosine, sine_part


def turn_bands(ee, eo, oe, oo, cosine, sine):
    cl, sl = jnp.broadcast_to(cosine, ee.shape), jnp.broadcast_to(sine, ee.shape)
    ck = pltpu.roll(cl, 0, 1, stride=1, stride_axis=0)
    sk = pltpu.roll(sl, 0, 1, stride=1, stride_axis=0)
    ee, oe = ck * ee + sk * oe, ck * oe - sk * ee
    eo, oo = ck * eo + sk * oo, ck * oo - sk * eo
    ee, eo = cl * ee + sl * eo, cl * eo - sl * ee
    oe, oo = cl * oe + sl * oo, cl * oo - sl * oe
    return ee, eo, oe, oo


def move_bands(ee, eo, oe, oo):
    lane = lanes_of(ee)
    diag = lax.broadcasted_iota(jnp.int32, ee.shape, 0)
    last = lane == ee.shape[1] - 1
    on, next_on = diag == 0, diag == 1

    near = down(jnp.where(on, eo, ee), 1)
    turned = jnp.where(on, oo, oe)
    mixed = jnp.where(lane == diag, turned, jnp.where(lane == diag - 1, near, ee))
    ee_new = jnp.where(jnp.logical_and(on, lane == 0), ee, right(mixed, 1))

    far = down(jnp.where(last, ee, eo), -1)
    mixed = down(jnp.where(lane == diag, oo, eo), -2)
    mixed = left(jnp.where(lane == diag + 1, far, mixed), 1)
    eo_new = jnp.where(last, far, mixed)

    oo_new = jnp.where(last, jnp.where(on, ee, down(oe, 1)), left(oo, 1))

    oe_new = right(down(oe, 2), 1)
    oe_new = jnp.where(next_on, jnp.where(lane == diag, oo, eo), oe_new)
    oe_new = jnp.where(on, eo_new, oe_new)
    return ee_new, eo_new, oe_new, oo_new


def move_bands_back(ee, eo, oe, oo):
    lane = lanes_of(ee)
    diag = lax.broadcasted_iota(jnp.int32, ee.shape, 0)
    last, first = lane == ee.shape[1] - 1, lane == diag
    on, next_on = diag == 0, diag == 1
    ahead, behind = lane == diag + 1, lane == diag - 1
    eo_down, oo_up = down(eo, 1), down(oo, -1)
    eo_twice = down(eo, 2)

    ee_left = left(jnp.where(ahead, down(ee, -1), ee), 1)
    ee_old = jnp.where(jnp.logical_and(first, on), ee, ee_left)
    ee_old = jnp.where(last, jnp.where(on, oo, eo_down), ee_old)

    oe_left = left(jnp.where(jnp.logical_and(ahead, diag > 0), ee, down(oe, -2)), 1)
    eo_far = right(jnp.where(behind, eo_down, eo_twice), 1)
    eo_old = jnp.where(on, jnp.where(last, oo_up, oe_left), eo_far)
    eo_old = jnp.where(jnp.logical_and(next_on, lane > 1), oe, eo_old)
    eo_old = jnp.where(jnp.logical_and(on, first), ee_left, eo_old)

    oe_old = jnp.where(on, eo_old, jnp.where(last, oo_up, oe_left))

    oo_old = right(jnp.where(behind, eo_twice, oo), 1)
    oo_old = jnp.where(jnp.logical_and(next_on, first), oe, oo_old)
    oo_old = jnp.where(jnp.logical_and(on, first), left(ee, 1), oo_old)
    return ee_old, eo_old, oe_old, oo_old


def move_columns(even, odd):
    lane = lanes_of(even)
    first, last = lane == 0, lane == even.shape[1] - 1
    even_new = jnp.where(first, even, right(jnp.where(first, odd, even), 1))
    odd_new = jnp.where(last, even, left(odd, 1))
    return even_new, odd_new


def home_sources(even, odd):
    lane = line_lanes(even)
    by, end = JSTEPS - 1, even.shape[1] - 1
    entered = jnp.logical_and(lane >= 1, lane <= by)
    mixed_even = jnp.where(entered, right(odd, by + 1), even)
    mixed_odd = jnp.where(lane > end - by, left(even, by + 1), odd)

    def even_source(place):
        moved = jnp.where(place <= end - by, place + by, end + 1 - place)
        return jnp.where(place == 0, 0, moved)

    def odd_source(place):
        return jnp.where(place >= by, place - by, end - place)

    return (mixed_even, even_source), (mixed_odd, odd_source)


def columns_home(even, odd, shifted=None):
    lane = line_lanes(even)
    if shifted is not None:
        half = even.shape[1] // 2
        lane = jnp.where(shifted, jnp.where(lane < half, lane + half, lane - half), lane)
    return tuple(take_lanes(x, source(lane)) for x, source in home_sources(even, odd))


def blocks_home(even, odd):
    lane = line_lanes(even)
    (even, even_source), (odd, odd_source) = home_sources(even, odd)
    blocks = []
    for block in (0, 1):
        place = block * (even.shape[1] // 2) + lane // 2
        from_even, from_odd = (
            take_lanes(x, source(place)) for x, source in ((even, even_source), (odd, odd_source))
        )
        blocks.append(jnp.where(lane % 2 == 0, from_even, from_odd))
    return blocks


def trim(bands, reach):
    rows = min(bands[0].shape[0], -(-(reach + 1) // 8) * 8)
    return [band[:rows] for band in bands]


def angles_of(bands, carried):
    angles = []
    ahead = 2 * (JSTEPS - 1)
    kept = 2 * ahead if carried else 0
    for step in range(JSTEPS):
        ee, eo, oe, oo = trim(bands, kept + ahead - 2 * step)
        cosine, sine = jacobi_angle(ee[0:1], oo[0:1], eo[0:1])
        angles.append((cosine, sine))
        bands = ee, eo, oe, oo
        if carried or step < JSTEPS - 1:
            bands = turn_bands(ee, eo, oe, oo, cosine, sine)
        if step < JSTEPS - 1:
            bands = move_bands(*bands)
    if carried:
        for step in range(JSTEPS - 1):
            bands = move_bands_back(*trim(bands, kept - 2 * step))
    return angles, bands


def turned(even, odd, angles):
    for step, (cosine, sine) in enumerate(angles):
        even, odd = cosine * even + sine * odd, cosine * odd - sine * even
        if step < JSTEPS - 1:
            even, odd = move_columns(even, odd)
    return even, odd


def turn_columns(even, odd, angles, shifted=None):
    return columns_home(*turned(even, odd, angles), shifted)


def near_starts(width):
    half = width // 2
    reach = REACH - 1
    return (half - 2 * reach, width - WINDOW), (0, half - reach)


def cross_partial(x_even, x_odd, y_even, y_odd, x_second, y_second):
    rows, width = x_even.shape
    x_starts, y_starts = near_starts(width)
    lane = lanes_of(x_even)

    def window(even, odd, flag, starts):
        at_zero = jnp.where(flag, left(even, starts[1]), left(even, starts[0]))
        at_next = jnp.where(flag, left(odd, starts[1] - WINDOW), left(odd, starts[0] - WINDOW))
        return jnp.where(lane < WINDOW, at_zero, jnp.where(lane < 2 * WINDOW, at_next, 0.0))

    corner = lax.dot_general(
        window(y_even, y_odd, y_second, y_starts),
        window(x_even, x_odd, x_second, x_starts),
        (((0,), (0,)), ((), ())),
        precision=lax.Precision.HIGHEST,
        preferred_element_type=jnp.float32,
    )
    low = lax.broadcasted_iota(jnp.int32, (WINDOW, width), 1) < 2 * WINDOW
    return jnp.where(low, corner[:WINDOW], right(corner[WINDOW : 2 * WINDOW], 2 * WINDOW))


def own_rotation(angles, second, swapped, first_pair):
    width = angles[0][0].shape[1]
    half = width // 2
    x_starts, y_starts = near_starts(width)
    starts = [jnp.where(first_pair, x, y) for x, y in zip(x_starts, y_starts)]
    shape = (2 * WINDOW, width)
    row = lax.broadcasted_iota(jnp.int32, shape, 0)
    lane = lax.broadcasted_iota(jnp.int32, shape, 1) - jnp.where(second, starts[1], starts[0])
    even, odd = (
        jnp.where(jnp.logical_and(row == lane + at, row // WINDOW == at // WINDOW), 1.0, 0.0)
        for at in (0, WINDOW)
    )
    even, odd = turn_columns(even, odd, angles, swapped)
    low = lax.broadcasted_iota(jnp.int32, shape, 1) < half
    return jnp.where(jnp.logical_xor(low, first_pair), right(odd, half), even)


def cross_bands(packed, x_rotation, y_rotation):
    width = packed.shape[1]
    half = width // 2
    corner = jnp.concatenate((packed[:, :half], right(packed, half)[:, :half]), axis=0)
    highest = dict(precision=lax.Precision.HIGHEST, preferred_element_type=jnp.float32)
    turned_x = jnp.dot(corner, x_rotation, **highest)
    ends = lax.dot_general(turned_x, y_rotation, (((0,), (0,)), ((), ())), **highest)
    even, odd = ends[half - NEAR : half], ends[width - NEAR :]
    quadrants = (even, right(even, half), odd, right(odd, half))
    offset = lanes_of(even) - lax.broadcasted_iota(jnp.int32, even.shape, 0) - (half - NEAR)
    diag = lax.broadcasted_iota(jnp.int32, (DIAGS, width), 0)
    bands = [jnp.zeros((DIAGS, width), jnp.float32) for _ in quadrants]
    for d in range(1, REACH):
        here = offset == d
        for q, quadrant in enumerate(quadrants):
            line = jnp.sum(jnp.where(here, quadrant, 0.0), axis=0, keepdims=True)
            bands[q] = jnp.where(diag == d, line, bands[q])
    return bands


def either(flag, one, other):
    return jnp.logical_or(jnp.logical_and(flag, one), jnp.logical_and(jnp.logical_not(flag), other))


def halves_swapped(is_second):
    return among(is_second[0]), jnp.logical_not(among(is_second[1]))


def on_odd_core():
    return lax.axis_index("row") % 2 == 1


def far_starts(width):
    return REACH - 1, width // 2


def pack_far(bands, flag):
    width = bands[0].shape[1]
    half, count = width // 2, (FAR_DIAGS - DIAGS) // 2
    lane = line_lanes(bands[0])
    packed = []
    for band in bands:
        one, two = band[DIAGS : DIAGS + count], band[DIAGS + count :]
        one, two = (
            jnp.where(flag, left(x, far_starts(width)[1] - at), left(x, far_starts(width)[0] - at))
            for x, at in ((one, 0), (two, half))
        )
        packed.append(jnp.concatenate((band[:DIAGS], jnp.where(lane < half, one, two)), axis=0))
    return packed


def unpack_far(packed, flag):
    width = packed.shape[1]
    half = width // 2
    parts = [packed[:DIAGS]]
    for at in (0, half):
        starts = [start - at for start in far_starts(width)]
        x = packed[DIAGS:]
        parts.append(jnp.where(flag, right(x, starts[1]), right(x, starts[0])))
    return jnp.concatenate(parts, axis=0)


PACKED = DIAGS + (FAR_DIAGS - DIAGS) // 2


def store_part(even, odd, corner, flag, part_ref):
    bands = pack_far(dense_bands(even, odd, FAR_DIAGS), flag)
    for q, band in enumerate(bands):
        part_ref[q * PACKED : (q + 1) * PACKED, :] = band
    part_ref[4 * PACKED :, :] = corner


def open_pairs(is_second, x, y, column_refs, corner_ref, other_ref):
    x_second, y_second = among(is_second[0]), among(is_second[1])
    corner = cross_partial(*x, *y, x_second, y_second)
    flag = on_odd_core()
    mine = [jnp.where(flag, b, a) for a, b in zip(x, y)]
    theirs = [jnp.where(flag, a, b) for a, b in zip(x, y)]
    for ref, value in zip(column_refs, mine + theirs):
        ref[...] = value
    corner_ref[...] = jnp.where(flag, corner[NEAR:], corner[:NEAR])
    store_part(
        *theirs,
        jnp.where(flag, corner[:NEAR], corner[NEAR:]),
        either(flag, x_second, y_second),
        other_ref,
    )


def first_open(own_second, gets_second, is_second, even_ref, odd_ref, payload_ref, *refs):
    *column_refs, corner_ref, other_ref = refs
    own = even_ref[...], odd_ref[...]
    came = unpacked(payload_ref[...], own[0].shape[0], among(gets_second))
    flag = among(own_second)
    x = [jnp.where(flag, b, a) for a, b in zip(own, came)]
    y = [jnp.where(flag, a, b) for a, b in zip(own, came)]
    open_pairs(is_second, x, y, column_refs, corner_ref, other_ref)


def fused_open(picks, is_second, kept_ref, sent_ref, came0_ref, came1_ref, *refs):
    *column_refs, corner_ref, other_ref = refs
    arrays = [ref[...] for ref in (sent_ref, kept_ref, came0_ref, came1_ref)]
    blocks = [choose(pick, arrays) for pick in picks]
    x, y = split_pair(*blocks[:2]), split_pair(*blocks[2:])
    open_pairs(is_second, x, y, column_refs, corner_ref, other_ref)


def swapped_flag(is_second):
    x_swapped, y_swapped = halves_swapped(is_second)
    return either(on_odd_core(), y_swapped, x_swapped)


def own_second_flag(is_second):
    return either(on_odd_core(), among(is_second[1]), among(is_second[0]))


def bands_kernel(is_second, even_ref, odd_ref, corner_ref, part_ref):
    flag = own_second_flag(is_second)
    store_part(even_ref[...], odd_ref[...], corner_ref[...], flag, part_ref)


def angles_kernel(is_second, *refs):
    *part_refs, found_ref = refs
    part = pair_sums([ref[...] for ref in part_refs])
    flag = own_second_flag(is_second)
    quadrants = [unpack_far(part[q * PACKED : (q + 1) * PACKED], flag) for q in range(4)]
    angles, bands = angles_of(quadrants, True)
    for step, pair in enumerate(angles):
        for i in (0, 1):
            found_ref[2 * step + i : 2 * step + i + 1, :] = pair[i]
    spare = NEAR - 2 * JSTEPS
    found_ref[2 * JSTEPS : NEAR, :] = jnp.zeros((spare, part.shape[1]), jnp.float32)
    for q in range(4):
        found_ref[NEAR + q * DIAGS : NEAR + (q + 1) * DIAGS, :] = bands[q][:DIAGS]
    found_ref[CORNER:ROTATION, :] = part[4 * PACKED :]
    first_pair = jnp.logical_not(on_odd_core())
    found_ref[ROTATION:, :] = own_rotation(angles, flag, swapped_flag(is_second), first_pair)


CORNER = NEAR + 4 * DIAGS
ROTATION = CORNER + NEAR
FOUND = ROTATION + 2 * WINDOW


def angles_in(found):
    return [(found[2 * i : 2 * i + 1], found[2 * i + 1 : 2 * i + 2]) for i in range(JSTEPS)]


def columns_kernel(is_second, even_ref, odd_ref, found_ref, *out_refs):
    angles = angles_in(found_ref[...])
    columns = turn_columns(even_ref[...], odd_ref[...], angles, swapped_flag(is_second))
    for ref, value in zip(out_refs, columns):
        ref[...] = value


def next_bands(x_found, y_found, x_second, y_second):
    corner = jnp.concatenate((x_found[CORNER:ROTATION], y_found[CORNER:ROTATION]), axis=0)
    middle = cross_bands(corner, x_found[ROTATION:], y_found[ROTATION:])
    half = corner.shape[1] // 2
    lane = lanes_of(middle[0])
    diag = lax.broadcasted_iota(jnp.int32, middle[0].shape, 0)
    bands = []
    for q in range(4):
        rows = slice(NEAR + q * DIAGS, NEAR + (q + 1) * DIAGS)
        x, y = x_found[rows], y_found[rows]
        x = jnp.where(x_second, right(x, half), x)
        y = jnp.where(y_second, y, right(y, half))
        crossing = jnp.where(lane - diag < half, middle[q], y)
        bands.append(jnp.where(lane < half, x, crossing))
    return bands


def next_kernel(is_second, sends_first, in_order, *refs):
    mine_even, mine_odd, even_ref, odd_ref, found_ref, other_ref, kept_ref, sent_ref = refs
    found, other = found_ref[...], other_ref[...]
    flag = on_odd_core()
    x_found, y_found = jnp.where(flag, other, found), jnp.where(flag, found, other)
    bands = next_bands(x_found, y_found, among(is_second[0]), among(is_second[1]))
    x_swapped, y_swapped = halves_swapped(is_second)
    swapped = either(flag, x_swapped, y_swapped)
    theirs = turn_columns(even_ref[...], odd_ref[...], angles_in(other), swapped)
    low = line_lanes(found) < found.shape[1] // 2
    from_mine = jnp.logical_xor(low, flag)
    even = jnp.where(from_mine, mine_even[...], theirs[0])
    odd = jnp.where(from_mine, mine_odd[...], theirs[1])
    angles, _ = angles_of(bands, False)
    even, odd = turned(even, odd, angles)
    first, second = blocks_home(even, odd) if in_order else join_pair(*columns_home(even, odd))
    flag = among(sends_first)
    kept_ref[...] = jnp.where(flag, second, first)
    sent_ref[...] = jnp.where(flag, first, second)


def pair_sums(arrays):
    while len(arrays) > 1:
        arrays = [arrays[i] + arrays[i + 1] for i in range(0, len(arrays), 2)]
    return arrays[0]


def swap(x, axis, mask):
    return lax.ppermute(x, axis, [(i, i ^ mask) for i in range(lax.axis_size(axis))])


def exchange_groups(x, axis, first_bit=0):
    count = lax.axis_size(axis).bit_length() - 1
    bits = [1 << b for b in range(count)]
    groups = [bits[:1]] + [bits[i : i + 2] for i in range(1, count, 2)]
    arrays = [x]
    for group in groups[first_bit:]:
        x = pair_sums(arrays)
        masks = [group[0]] if len(group) == 1 else [group[0], group[1], group[0] | group[1]]
        arrays = [x] + [swap(x, axis, mask) for mask in masks]
    return arrays


def call(kernel, shapes, *args):
    out = [jax.ShapeDtypeStruct(shape, jnp.float32) for shape in shapes]
    return pl.pallas_call(
        kernel,
        out_shape=out,
        compiler_params=pltpu.CompilerParams(vmem_limit_bytes=32 * 1024 * 1024),
    )(*args)


def two_rounds(opened, is_second, sends_first, in_order):
    *columns, corner, other = opened
    column, width = columns[0].shape, columns[0].shape[1]
    other = swap(other, "row", 1)
    bands = functools.partial(bands_kernel, is_second)
    (mine,) = call(bands, (other.shape,), *columns[:2], corner)
    (found,) = call(
        functools.partial(angles_kernel, is_second),
        ((FOUND, width),),
        *exchange_groups(mine + other, "row", 1),
    )
    other = swap(found, "row", 1)
    turn = functools.partial(columns_kernel, is_second)
    columns[:2] = call(turn, (column, column), *columns[:2], found)
    turn = functools.partial(next_kernel, is_second, sends_first, in_order)
    return call(turn, (column, column), *columns, found, other)


def per_device(basis):
    rows, cols = basis.shape
    width = cols // 2
    pair_total = lax.axis_size("pair")
    column = (rows, width)
    opened = (column,) * 4 + ((NEAR, width), (4 * PACKED + NEAR, width))
    payload = (rows + rows * 2 * STRIP // width, width)

    sends, sends_second, gets_second, own_second, is_second = first_moves(pair_total)
    opening = functools.partial(open_kernel, sends_second)
    even, odd, sent = call(opening, (column, column, payload), basis)
    came = lax.ppermute(sent, "pair", sends)
    opening = functools.partial(first_open, own_second, gets_second, is_second)
    arrays = call(opening, opened, even, odd, came)
    sends, sends_first, picks, next_second = fused_moves(pair_total)
    kept, sent = two_rounds(arrays, is_second, sends_first, False)

    came = [lax.ppermute(x, "pair", s) for x, s in zip((sent, kept), sends)]
    opening = functools.partial(fused_open, picks, next_second)
    arrays = call(opening, opened, kept, sent, *came)
    sends, sends_first, gets_first = last_moves(pair_total)
    kept, sent = two_rounds(arrays, next_second, sends_first, True)

    came = lax.ppermute(sent, "pair", sends)
    flag = among(gets_first)
    first = jnp.where(flag, came, kept)
    second = jnp.where(flag, kept, came)
    return jnp.concatenate((first, second), axis=1)


def solution(mesh):
    return jax.shard_map(
        per_device,
        mesh=mesh,
        in_specs=(P("row", "pair"),),
        out_specs=P("row", "pair"),
        check_vma=False,
    )
```

```python
import functools

import jax
import jax.numpy as jnp
import numpy as np
from jax import lax
from jax.experimental import pallas as pl
from jax.experimental.pallas import tpu as pltpu
from jax.sharding import PartitionSpec as P

ROUNDS = 4
JSTEPS = 6
REACH = 2 * (JSTEPS - 1) + 1
DIAGS = 16
FAR_DIAGS = 32
WINDOW = 32
NEAR = 16
STRIP = 16


def tournament_order(pair_count):
    ordering = np.zeros(2 * pair_count, dtype=np.int64)
    ordering[0] = 0
    ordering[2] = 1
    for slot in range(2, pair_count):
        ordering[2 * slot] = 2 * (slot - 1)
    for slot in range(pair_count - 1):
        ordering[2 * slot + 1] = 2 * (slot + 1) + 1
    ordering[2 * pair_count - 1] = 2 * (pair_count - 1)
    return ordering


def host_of(pair, pair_total, round_index):
    if round_index % 2 == 0 or pair == 0:
        return pair
    return min(pair + 1, pair_total - 1) if pair % 2 else pair - 1


def last_moves(pair_total):
    ordering = tournament_order(pair_total)
    sends, sends_first, gets_first = [], set(), set()
    for pair in range(pair_total):
        target = host_of(pair, pair_total, ROUNDS)
        for place in (0, 1):
            old = int(ordering[2 * pair + place])
            source = host_of(old // 2, pair_total, ROUNDS - 1)
            if source == target:
                continue
            sends.append((source, target))
            if old % 2 == 0:
                sends_first.add(source)
            if place == 0:
                gets_first.add(target)
    assert len({s for s, _ in sends}) == len(sends) == len({t for _, t in sends})
    return sends, sends_first, gets_first


def first_moves(pair_total):
    ordering = tournament_order(pair_total)
    sends, sends_second, gets_second, own_second = [], set(), set(), set()
    seconds = (set(), set())
    for pair in range(pair_total):
        here = host_of(pair, pair_total, 1)
        for place in (0, 1):
            old = int(ordering[2 * pair + place])
            if old % 2:
                seconds[place].add(here)
            if old // 2 == here:
                if place:
                    own_second.add(here)
                continue
            sends.append((old // 2, here))
            if old % 2:
                sends_second.add(old // 2)
                gets_second.add(here)
    assert len({s for s, _ in sends}) == len(sends) == len({t for _, t in sends})
    return sends, sends_second, gets_second, own_second, seconds


def fused_moves(pair_total):
    ordering = tournament_order(pair_total)
    before, last = ROUNDS - 3, ROUNDS - 1
    needs, edges, seconds = {}, [], ({}, {})
    for pair in range(pair_total):
        here = host_of(pair, pair_total, last)
        needs[here] = []
        for place in (0, 1):
            source = int(ordering[2 * pair + place])
            seconds[place][here] = source % 2
            for half in (0, 1):
                old = int(ordering[2 * (source // 2) + half])
                there = host_of(old // 2, pair_total, before)
                needs[here].append((there, old % 2))
                if there != here:
                    edges.append((there, old % 2, here))
    turn, left_over = {}, list(edges)
    while left_over:
        source, _, target = left_over[0]
        start = source
        while True:
            for number, one, other in ((0, source, target), (1, target, source)):
                edge = next(e for e in left_over if (e[0], e[2]) == (one, other))
                turn[edge] = number
                left_over.remove(edge)
            if target == start:
                break
            ahead = [e[2] for e in left_over if e[0] == target]
            source, target = target, ahead[0]
    sends = [[(e[0], e[2]) for e in edges if turn[e] == i] for i in (0, 1)]
    for chosen in sends:
        assert len({a for a, _ in chosen}) == len({b for _, b in chosen}) == pair_total
    sends_first = {e[0] for e in edges if turn[e] == 0 and e[1] == 0}
    picks = []
    for slot in range(4):
        pick = {}
        for here in range(pair_total):
            there, half = needs[here][slot]
            if there == here:
                pick[here] = 0 if (half == 0) == (here in sends_first) else 1
            else:
                pick[here] = 2 + turn[(there, half, here)]
        picks.append(pick)
    is_second = [{h for h, place in table.items() if place} for table in seconds]
    return sends, sends_first, picks, is_second


def choose(pick, arrays):
    chosen = arrays[0]
    for number in range(1, len(arrays)):
        members = {here for here, value in pick.items() if value == number}
        if members:
            chosen = jnp.where(among(members), arrays[number], chosen)
    return chosen


def among(members):
    here = lax.axis_index("pair")
    return functools.reduce(
        jnp.logical_or, [here == member for member in sorted(members)], here < 0
    )


def left(x, by):
    width = x.shape[1]
    return pltpu.roll(x, (width - by) % width, 1) if by % width else x


def right(x, by):
    width = x.shape[1]
    return pltpu.roll(x, by % width, 1) if by % width else x


def down(x, by):
    return pltpu.roll(x, by % x.shape[0], 0)


def lanes_of(x):
    return lax.broadcasted_iota(jnp.int32, x.shape, 1)


def split_pair(first, second):
    half = first.shape[1] // 2
    low = lanes_of(first) < half
    even = jnp.where(low, first, right(second, half))
    odd = jnp.where(low, right(first, half), second)
    return even, odd


def take_lanes(x, source):
    if x.shape[0] == 1:
        return take_lanes(jnp.broadcast_to(x, (8, x.shape[1])), source)[:1]
    return jnp.take_along_axis(x, jnp.broadcast_to(source, x.shape), axis=1)


def line_lanes(x):
    return lax.broadcasted_iota(jnp.int32, (1, x.shape[1]), 1)


def separate(first, second):
    lane = line_lanes(first)
    half = first.shape[1] // 2
    low = lane < half
    source = 2 * jnp.where(low, lane, lane - half)
    return tuple(
        jnp.where(low, take_lanes(first, source + odd), take_lanes(second, source + odd))
        for odd in (0, 1)
    )


def backwards(x):
    return jnp.take_along_axis(x, x.shape[1] - 1 - lanes_of(x), axis=1)


def dense_bands(even, odd, diags):
    width = even.shape[1]
    gram = lax.dot_general(
        jnp.concatenate((even, odd), axis=1),
        jnp.concatenate((backwards(even), backwards(odd)), axis=1),
        (((0,), (0,)), ((), ())),
        precision=lax.Precision.HIGHEST,
        preferred_element_type=jnp.float32,
    )
    bands = []
    for near in (0, width):
        for far in (0, width):
            quadrant = gram[far : far + width, near : near + width]
            aligned = pltpu.roll(quadrant, 1, 1, stride=1, stride_axis=0)
            bands.append(jnp.transpose(aligned)[:diags])
    return bands


def store_bands(even, odd, band_ref, diags):
    for q, band in enumerate(dense_bands(even, odd, diags)):
        band_ref[q * diags : (q + 1) * diags, :] = band


def open_kernel(sends_second, basis_ref, even_ref, odd_ref, payload_ref):
    rows, cols = basis_ref.shape
    width = cols // 2
    half = width // 2
    even, odd = separate(basis_ref[:, :width], basis_ref[:, width:])
    even_ref[...] = even
    odd_ref[...] = odd
    flag = among(sends_second)
    even, odd = (jnp.where(flag, left(x, half - STRIP), x) for x in (even, odd))
    payload_ref[:rows] = jnp.where(line_lanes(even) < half, even, right(odd, half))
    group = rows * 2 * STRIP // width
    strips = jnp.zeros((group, width), jnp.float32)
    for i in range(rows // group):
        for j, x in enumerate((even, odd)):
            start = (2 * i + j) * STRIP
            lane = line_lanes(x)
            here = jnp.logical_and(lane >= start, lane < start + STRIP)
            strips = jnp.where(here, left(x[i * group : (i + 1) * group], half - start), strips)
    payload_ref[rows:] = strips


def unpacked(payload, rows, second):
    width = payload.shape[1]
    half = width // 2
    lane = line_lanes(payload)
    main, strips = payload[:rows], payload[rows:]
    group = strips.shape[0]
    columns = []
    for j, x in enumerate((main, left(main, half))):
        ends = [right(strips, half - (2 * i + j) * STRIP) for i in range(rows // group)]
        x = jnp.where(lane < half, x, jnp.where(lane < half + STRIP, jnp.concatenate(ends), 0.0))
        columns.append(jnp.where(second, right(x, half - STRIP), x))
    return columns


def jacobi_angle(diag_even, diag_odd, coupling):
    spread = diag_even - diag_odd
    square = spread * spread + 4.0 * coupling * coupling
    inverse = lax.rsqrt(square)
    larger_square = (square * inverse + jnp.abs(spread)) * (0.5 * inverse)
    larger_inverse = lax.rsqrt(larger_square)
    larger = larger_square * larger_inverse
    smaller = coupling * inverse * larger_inverse
    forward = spread >= 0.0
    sign = jnp.where(coupling > 0.0, 1.0, jnp.where(coupling < 0.0, -1.0, 0.0))
    cosine = jnp.where(forward, larger, jnp.abs(smaller))
    sine_part = jnp.where(forward, smaller, sign * larger)
    return cosine, sine_part


def turn_bands(ee, eo, oe, oo, cosine, sine):
    cl, sl = jnp.broadcast_to(cosine, ee.shape), jnp.broadcast_to(sine, ee.shape)
    ck = pltpu.roll(cl, 0, 1, stride=1, stride_axis=0)
    sk = pltpu.roll(sl, 0, 1, stride=1, stride_axis=0)
    ee, oe = ck * ee + sk * oe, ck * oe - sk * ee
    eo, oo = ck * eo + sk * oo, ck * oo - sk * eo
    ee, eo = cl * ee + sl * eo, cl * eo - sl * ee
    oe, oo = cl * oe + sl * oo, cl * oo - sl * oe
    return ee, eo, oe, oo


def step_bands(ee, eo, oe, oo, cosine, sine):
    lane = lanes_of(ee)
    diag = lax.broadcasted_iota(jnp.int32, ee.shape, 0)
    last = lane == ee.shape[1] - 1
    on, next_on = diag == 0, diag == 1

    def slanted(x, by):
        if by >= 0:
            return pltpu.roll(x, by, 1, stride=1, stride_axis=0)
        return jnp.where(on, left(x, -by), down(slanted(x, 0), -by))

    def rotated(by, wanted):
        cl, sl = (jnp.broadcast_to(x, ee.shape) for x in (cosine, sine))
        ck, sk = (slanted(x, by) for x in (cl, sl))
        cl, sl, a, b, c, d = (right(x, by) for x in (cl, sl, ee, eo, oe, oo))
        a, c = ck * a + sk * c, ck * c - sk * a
        b, d = ck * b + sk * d, ck * d - sk * b
        found = {"ee": (a, b), "eo": (b, a), "oe": (c, d), "oo": (d, c)}
        return [
            cl * one + sl * two if name in ("ee", "oe") else cl * one - sl * two
            for name, (one, two) in found.items()
            if name in wanted
        ]

    ee_0, eo_0, oe_0, oo_0 = rotated(0, ("ee", "eo", "oe", "oo"))
    ee_r, eo_r, oe_r, oo_r = rotated(1, ("ee", "eo", "oe", "oo"))
    eo_l, oo_l = rotated(-1, ("eo", "oo"))

    near = down(jnp.where(on, eo_r, ee_r), 1)
    turned = jnp.where(on, oo_r, oe_r)
    ee_new = jnp.where(lane == diag + 1, turned, jnp.where(lane == diag, near, ee_r))
    ee_new = jnp.where(jnp.logical_and(on, lane == 0), ee_0, ee_new)

    eo_new = down(jnp.where(lane == diag - 1, oo_l, eo_l), -2)
    eo_new = jnp.where(lane == diag, down(eo_l, -1), eo_new)
    eo_new = jnp.where(last, down(ee_0, -1), eo_new)

    oo_new = jnp.where(last, jnp.where(on, ee_0, down(oe_0, 1)), oo_l)

    oe_new = down(oe_r, 2)
    oe_new = jnp.where(next_on, jnp.where(lane == diag, oo_0, eo_0), oe_new)
    oe_new = jnp.where(on, eo_new, oe_new)
    return ee_new, eo_new, oe_new, oo_new


def move_bands(ee, eo, oe, oo):
    lane = lanes_of(ee)
    diag = lax.broadcasted_iota(jnp.int32, ee.shape, 0)
    last = lane == ee.shape[1] - 1
    on, next_on = diag == 0, diag == 1

    near = down(jnp.where(on, eo, ee), 1)
    turned = jnp.where(on, oo, oe)
    mixed = jnp.where(lane == diag, turned, jnp.where(lane == diag - 1, near, ee))
    ee_new = jnp.where(jnp.logical_and(on, lane == 0), ee, right(mixed, 1))

    far = down(jnp.where(last, ee, eo), -1)
    mixed = down(jnp.where(lane == diag, oo, eo), -2)
    mixed = left(jnp.where(lane == diag + 1, far, mixed), 1)
    eo_new = jnp.where(last, far, mixed)

    oo_new = jnp.where(last, jnp.where(on, ee, down(oe, 1)), left(oo, 1))

    oe_new = right(down(oe, 2), 1)
    oe_new = jnp.where(next_on, jnp.where(lane == diag, oo, eo), oe_new)
    oe_new = jnp.where(on, eo_new, oe_new)
    return ee_new, eo_new, oe_new, oo_new


def move_bands_back(ee, eo, oe, oo):
    lane = lanes_of(ee)
    diag = lax.broadcasted_iota(jnp.int32, ee.shape, 0)
    last, first = lane == ee.shape[1] - 1, lane == diag
    on, next_on = diag == 0, diag == 1
    ahead, behind = lane == diag + 1, lane == diag - 1
    eo_down, oo_up = down(eo, 1), down(oo, -1)
    eo_twice = down(eo, 2)

    ee_left = left(jnp.where(ahead, down(ee, -1), ee), 1)
    ee_old = jnp.where(jnp.logical_and(first, on), ee, ee_left)
    ee_old = jnp.where(last, jnp.where(on, oo, eo_down), ee_old)

    oe_left = left(jnp.where(jnp.logical_and(ahead, diag > 0), ee, down(oe, -2)), 1)
    eo_far = right(jnp.where(behind, eo_down, eo_twice), 1)
    eo_old = jnp.where(on, jnp.where(last, oo_up, oe_left), eo_far)
    eo_old = jnp.where(jnp.logical_and(next_on, lane > 1), oe, eo_old)
    eo_old = jnp.where(jnp.logical_and(on, first), ee_left, eo_old)

    oe_old = jnp.where(on, eo_old, jnp.where(last, oo_up, oe_left))

    oo_old = right(jnp.where(behind, eo_twice, oo), 1)
    oo_old = jnp.where(jnp.logical_and(next_on, first), oe, oo_old)
    oo_old = jnp.where(jnp.logical_and(on, first), left(ee, 1), oo_old)
    return ee_old, eo_old, oe_old, oo_old


def move_columns(even, odd):
    lane = lanes_of(even)
    first, last = lane == 0, lane == even.shape[1] - 1
    even_new = jnp.where(first, even, right(jnp.where(first, odd, even), 1))
    odd_new = jnp.where(last, even, left(odd, 1))
    return even_new, odd_new


def in_pair(even, shifted=None):
    lane = line_lanes(even)
    if shifted is not None:
        half = even.shape[1] // 2
        lane = jnp.where(shifted, jnp.where(lane < half, lane + half, lane - half), lane)
    return (lane < 0, lane), (lane >= 0, lane)


def in_blocks(even):
    lane, half = line_lanes(even), even.shape[1] // 2
    place = jnp.where(lane < half, lane, lane - half)
    return (lane >= half, place), (lane >= half, place + half)


def in_order(even):
    lane, half = line_lanes(even), even.shape[1] // 2
    return (lane % 2 == 1, lane // 2), (lane % 2 == 1, lane // 2 + half)


def turn_to(layout, even, odd, angles):
    for cosine, sine in angles[:-1]:
        even, odd = cosine * even + sine * odd, cosine * odd - sine * even
        even, odd = move_columns(even, odd)
    by, end = JSTEPS - 1, even.shape[1] - 1
    results = []
    for is_odd, place in layout:
        stayed = place <= end - by
        from_even = jnp.where(stayed, place + by, 2 * end + 1 - by - place)
        from_even = jnp.where(place == 0, 0, from_even)
        source = jnp.where(is_odd, jnp.abs(place - by), from_even)
        is_even = jnp.logical_or(
            jnp.logical_and(is_odd, place < by),
            jnp.logical_and(jnp.logical_not(is_odd), stayed),
        )
        cosine, sine = (take_lanes(x, source) for x in angles[-1])
        by_even = jnp.where(is_even, cosine, -sine)
        by_odd = jnp.where(is_even, sine, cosine)
        results.append(by_even * take_lanes(even, source) + by_odd * take_lanes(odd, source))
    return results


def trim(bands, reach):
    rows = min(bands[0].shape[0], -(-(reach + 1) // 8) * 8)
    return [band[:rows] for band in bands]


def angles_of(bands):
    angles = []
    for step in range(JSTEPS):
        ee, eo, oe, oo = bands = trim(bands, 2 * (JSTEPS - 1 - step))
        angles.append(jacobi_angle(ee[0:1], oo[0:1], eo[0:1]))
        if step < JSTEPS - 1:
            bands = step_bands(*bands, *angles[-1])
    return angles


def carried(bands, angles):
    ahead = 2 * (JSTEPS - 1)
    for step, (cosine, sine) in enumerate(angles):
        bands = turn_bands(*trim(bands, 3 * ahead - 2 * step), cosine, sine)
        if step < JSTEPS - 1:
            bands = move_bands(*bands)
    for step in range(JSTEPS - 1):
        bands = move_bands_back(*trim(bands, 2 * (ahead - step)))
    return bands


def near_starts(width):
    half = width // 2
    reach = REACH - 1
    return (half - 2 * reach, width - WINDOW), (0, half - reach)


def cross_partial(x_even, x_odd, y_even, y_odd, x_second, y_second):
    rows, width = x_even.shape
    x_starts, y_starts = near_starts(width)
    lane = lanes_of(x_even)

    def window(even, odd, flag, starts):
        start = jnp.where(flag, starts[1], starts[0])
        at_zero = pltpu.roll(even, width - start, 1)
        at_next = pltpu.roll(odd, (width - start + WINDOW) % width, 1)
        return jnp.where(lane < WINDOW, at_zero, jnp.where(lane < 2 * WINDOW, at_next, 0.0))

    corner = lax.dot_general(
        window(y_even, y_odd, y_second, y_starts),
        window(x_even, x_odd, x_second, x_starts),
        (((0,), (0,)), ((), ())),
        precision=lax.Precision.HIGHEST,
        preferred_element_type=jnp.float32,
    )
    low = lax.broadcasted_iota(jnp.int32, (WINDOW, width), 1) < 2 * WINDOW
    return jnp.where(low, corner[:WINDOW], right(corner[WINDOW : 2 * WINDOW], 2 * WINDOW))


def own_rotation(angles, second, swapped, first_pair):
    width = angles[0][0].shape[1]
    half = width // 2
    x_starts, y_starts = near_starts(width)
    starts = [jnp.where(first_pair, x, y) for x, y in zip(x_starts, y_starts)]
    shape = (2 * WINDOW, width)
    row = lax.broadcasted_iota(jnp.int32, shape, 0)
    lane = lax.broadcasted_iota(jnp.int32, shape, 1) - jnp.where(second, starts[1], starts[0])
    even, odd = (
        jnp.where(jnp.logical_and(row == lane + at, row // WINDOW == at // WINDOW), 1.0, 0.0)
        for at in (0, WINDOW)
    )
    even, odd = turn_to(in_pair(even, swapped), even, odd, angles)
    low = lax.broadcasted_iota(jnp.int32, shape, 1) < half
    return jnp.where(jnp.logical_xor(low, first_pair), right(odd, half), even)


def cross_bands(packed, x_rotation, y_rotation):
    width = packed.shape[1]
    half = width // 2
    corner = jnp.concatenate((packed[:, :half], right(packed, half)[:, :half]), axis=0)
    highest = dict(precision=lax.Precision.HIGHEST, preferred_element_type=jnp.float32)
    turned_x = jnp.dot(corner, x_rotation, **highest)
    ends = lax.dot_general(turned_x, y_rotation, (((0,), (0,)), ((), ())), **highest)
    even, odd = ends[half - NEAR : half], ends[width - NEAR :]
    quadrants = (even, right(even, half), odd, right(odd, half))
    offset = lanes_of(even) - lax.broadcasted_iota(jnp.int32, even.shape, 0) - (half - NEAR)
    diag = lax.broadcasted_iota(jnp.int32, (DIAGS, width), 0)
    bands = [jnp.zeros((DIAGS, width), jnp.float32) for _ in quadrants]
    for d in range(1, REACH):
        here = offset == d
        for q, quadrant in enumerate(quadrants):
            line = jnp.sum(jnp.where(here, quadrant, 0.0), axis=0, keepdims=True)
            bands[q] = jnp.where(diag == d, line, bands[q])
    return bands


def either(flag, one, other):
    return jnp.logical_or(jnp.logical_and(flag, one), jnp.logical_and(jnp.logical_not(flag), other))


def halves_swapped(is_second):
    return among(is_second[0]), jnp.logical_not(among(is_second[1]))


def on_odd_core():
    return lax.axis_index("row") % 2 == 1


def far_starts(width):
    return REACH - 1, width // 2


def pack_far(bands, flag):
    width = bands[0].shape[1]
    half, count = width // 2, (FAR_DIAGS - DIAGS) // 2
    lane = line_lanes(bands[0])
    packed = []
    for band in bands:
        one, two = band[DIAGS : DIAGS + count], band[DIAGS + count :]
        one, two = (
            jnp.where(flag, left(x, far_starts(width)[1] - at), left(x, far_starts(width)[0] - at))
            for x, at in ((one, 0), (two, half))
        )
        packed.append(jnp.concatenate((band[:DIAGS], jnp.where(lane < half, one, two)), axis=0))
    return packed


def unpack_far(packed, flag):
    width = packed.shape[1]
    half = width // 2
    parts = [packed[:DIAGS]]
    for at in (0, half):
        starts = [start - at for start in far_starts(width)]
        x = packed[DIAGS:]
        parts.append(jnp.where(flag, right(x, starts[1]), right(x, starts[0])))
    return jnp.concatenate(parts, axis=0)


PACKED = DIAGS + (FAR_DIAGS - DIAGS) // 2


def store_part(even, odd, corner, flag, part_ref):
    bands = pack_far(dense_bands(even, odd, FAR_DIAGS), flag)
    for q, band in enumerate(bands):
        part_ref[q * PACKED : (q + 1) * PACKED, :] = band
    part_ref[4 * PACKED :, :] = corner


def open_pairs(is_second, x, y, column_refs, corner_ref, other_ref):
    x_second, y_second = among(is_second[0]), among(is_second[1])
    corner = cross_partial(*x, *y, x_second, y_second)
    flag = on_odd_core()
    mine = [jnp.where(flag, b, a) for a, b in zip(x, y)]
    theirs = [jnp.where(flag, a, b) for a, b in zip(x, y)]
    for ref, value in zip(column_refs, mine + theirs):
        ref[...] = value
    corner_ref[...] = jnp.where(flag, corner[NEAR:], corner[:NEAR])
    store_part(
        *theirs,
        jnp.where(flag, corner[:NEAR], corner[NEAR:]),
        either(flag, x_second, y_second),
        other_ref,
    )


def first_open(own_second, gets_second, is_second, even_ref, odd_ref, payload_ref, *refs):
    *column_refs, corner_ref, other_ref = refs
    own = even_ref[...], odd_ref[...]
    came = unpacked(payload_ref[...], own[0].shape[0], among(gets_second))
    flag = among(own_second)
    x = [jnp.where(flag, b, a) for a, b in zip(own, came)]
    y = [jnp.where(flag, a, b) for a, b in zip(own, came)]
    open_pairs(is_second, x, y, column_refs, corner_ref, other_ref)


def fused_open(picks, is_second, kept_ref, sent_ref, came0_ref, came1_ref, *refs):
    *column_refs, corner_ref, other_ref = refs
    arrays = [ref[...] for ref in (sent_ref, kept_ref, came0_ref, came1_ref)]
    blocks = [choose(pick, arrays) for pick in picks]
    x, y = split_pair(*blocks[:2]), split_pair(*blocks[2:])
    open_pairs(is_second, x, y, column_refs, corner_ref, other_ref)


def swapped_flag(is_second):
    x_swapped, y_swapped = halves_swapped(is_second)
    return either(on_odd_core(), y_swapped, x_swapped)


def own_second_flag(is_second):
    return either(on_odd_core(), among(is_second[1]), among(is_second[0]))


def bands_kernel(is_second, even_ref, odd_ref, corner_ref, part_ref):
    flag = own_second_flag(is_second)
    store_part(even_ref[...], odd_ref[...], corner_ref[...], flag, part_ref)


def angles_kernel(is_second, *refs):
    *part_refs, found_ref = refs
    part = pair_sums([ref[...] for ref in part_refs])
    flag = own_second_flag(is_second)
    quadrants = [unpack_far(part[q * PACKED : (q + 1) * PACKED], flag) for q in range(4)]
    angles = angles_of(quadrants)
    bands = carried(quadrants, angles)
    for step, pair in enumerate(angles):
        for i in (0, 1):
            found_ref[2 * step + i : 2 * step + i + 1, :] = pair[i]
    spare = NEAR - 2 * JSTEPS
    found_ref[2 * JSTEPS : NEAR, :] = jnp.zeros((spare, part.shape[1]), jnp.float32)
    for q in range(4):
        found_ref[NEAR + q * DIAGS : NEAR + (q + 1) * DIAGS, :] = bands[q][:DIAGS]
    found_ref[CORNER:ROTATION, :] = part[4 * PACKED :]
    first_pair = jnp.logical_not(on_odd_core())
    found_ref[ROTATION:, :] = own_rotation(angles, flag, swapped_flag(is_second), first_pair)


CORNER = NEAR + 4 * DIAGS
ROTATION = CORNER + NEAR
FOUND = ROTATION + 2 * WINDOW


def angles_in(found):
    return [(found[2 * i : 2 * i + 1], found[2 * i + 1 : 2 * i + 2]) for i in range(JSTEPS)]


def columns_kernel(is_second, even_ref, odd_ref, found_ref, *out_refs):
    angles = angles_in(found_ref[...])
    layout = in_pair(even_ref, swapped_flag(is_second))
    columns = turn_to(layout, even_ref[...], odd_ref[...], angles)
    for ref, value in zip(out_refs, columns):
        ref[...] = value


def next_bands(x_found, y_found, x_second, y_second):
    corner = jnp.concatenate((x_found[CORNER:ROTATION], y_found[CORNER:ROTATION]), axis=0)
    middle = cross_bands(corner, x_found[ROTATION:], y_found[ROTATION:])
    half = corner.shape[1] // 2
    lane = lanes_of(middle[0])
    diag = lax.broadcasted_iota(jnp.int32, middle[0].shape, 0)
    bands = []
    for q in range(4):
        rows = slice(NEAR + q * DIAGS, NEAR + (q + 1) * DIAGS)
        x, y = x_found[rows], y_found[rows]
        x = jnp.where(x_second, right(x, half), x)
        y = jnp.where(y_second, y, right(y, half))
        crossing = jnp.where(lane - diag < half, middle[q], y)
        bands.append(jnp.where(lane < half, x, crossing))
    return bands


def next_kernel(is_second, sends_first, layout_of, *refs):
    mine_even, mine_odd, even_ref, odd_ref, found_ref, other_ref, kept_ref, sent_ref = refs
    found, other = found_ref[...], other_ref[...]
    flag = on_odd_core()
    x_found, y_found = jnp.where(flag, other, found), jnp.where(flag, found, other)
    bands = next_bands(x_found, y_found, among(is_second[0]), among(is_second[1]))
    x_swapped, y_swapped = halves_swapped(is_second)
    swapped = either(flag, x_swapped, y_swapped)
    layout = in_pair(even_ref, swapped)
    theirs = turn_to(layout, even_ref[...], odd_ref[...], angles_in(other))
    low = line_lanes(found) < found.shape[1] // 2
    from_mine = jnp.logical_xor(low, flag)
    even = jnp.where(from_mine, mine_even[...], theirs[0])
    odd = jnp.where(from_mine, mine_odd[...], theirs[1])
    angles = angles_of(bands)
    first, second = turn_to(layout_of(even), even, odd, angles)
    flag = among(sends_first)
    kept_ref[...] = jnp.where(flag, second, first)
    sent_ref[...] = jnp.where(flag, first, second)


def pair_sums(arrays):
    while len(arrays) > 1:
        arrays = [arrays[i] + arrays[i + 1] for i in range(0, len(arrays), 2)]
    return arrays[0]


def swap(x, axis, mask):
    return lax.ppermute(x, axis, [(i, i ^ mask) for i in range(lax.axis_size(axis))])


def exchange_groups(x, axis, first_bit=0):
    count = lax.axis_size(axis).bit_length() - 1
    bits = [1 << b for b in range(count)]
    groups = [bits[:1]] + [bits[i : i + 2] for i in range(1, count, 2)]
    arrays = [x]
    for group in groups[first_bit:]:
        x = pair_sums(arrays)
        masks = [group[0]] if len(group) == 1 else [group[0], group[1], group[0] | group[1]]
        arrays = [x] + [swap(x, axis, mask) for mask in masks]
    return arrays


def call(kernel, shapes, *args):
    out = [jax.ShapeDtypeStruct(shape, jnp.float32) for shape in shapes]
    return pl.pallas_call(
        kernel,
        out_shape=out,
        compiler_params=pltpu.CompilerParams(vmem_limit_bytes=32 * 1024 * 1024),
    )(*args)


def two_rounds(opened, is_second, sends_first, layout_of):
    *columns, corner, other = opened
    column, width = columns[0].shape, columns[0].shape[1]
    other = swap(other, "row", 1)
    bands = functools.partial(bands_kernel, is_second)
    (mine,) = call(bands, (other.shape,), *columns[:2], corner)
    (found,) = call(
        functools.partial(angles_kernel, is_second),
        ((FOUND, width),),
        *exchange_groups(mine + other, "row", 1),
    )
    other = swap(found, "row", 1)
    turn = functools.partial(columns_kernel, is_second)
    columns[:2] = call(turn, (column, column), *columns[:2], found)
    turn = functools.partial(next_kernel, is_second, sends_first, layout_of)
    return call(turn, (column, column), *columns, found, other)


def per_device(basis):
    rows, cols = basis.shape
    width = cols // 2
    pair_total = lax.axis_size("pair")
    column = (rows, width)
    opened = (column,) * 4 + ((NEAR, width), (4 * PACKED + NEAR, width))
    payload = (rows + rows * 2 * STRIP // width, width)

    sends, sends_second, gets_second, own_second, is_second = first_moves(pair_total)
    opening = functools.partial(open_kernel, sends_second)
    even, odd, sent = call(opening, (column, column, payload), basis)
    came = lax.ppermute(sent, "pair", sends)
    opening = functools.partial(first_open, own_second, gets_second, is_second)
    arrays = call(opening, opened, even, odd, came)
    sends, sends_first, picks, next_second = fused_moves(pair_total)
    kept, sent = two_rounds(arrays, is_second, sends_first, in_blocks)

    came = [lax.ppermute(x, "pair", s) for x, s in zip((sent, kept), sends)]
    opening = functools.partial(fused_open, picks, next_second)
    arrays = call(opening, opened, kept, sent, *came)
    sends, sends_first, gets_first = last_moves(pair_total)
    kept, sent = two_rounds(arrays, next_second, sends_first, in_order)

    came = lax.ppermute(sent, "pair", sends)
    flag = among(gets_first)
    first = jnp.where(flag, came, kept)
    second = jnp.where(flag, kept, came)
    return jnp.concatenate((first, second), axis=1)


def solution(mesh):
    return jax.shard_map(
        per_device,
        mesh=mesh,
        in_specs=(P("row", "pair"),),
        out_specs=P("row", "pair"),
        check_vma=False,
    )
```

```python
import functools

import jax
import jax.numpy as jnp
import numpy as np
from jax import lax
from jax.experimental import pallas as pl
from jax.experimental.pallas import tpu as pltpu
from jax.sharding import PartitionSpec as P

ROUNDS = 4
JSTEPS = 6
REACH = 2 * (JSTEPS - 1) + 1
DIAGS = 16
FAR_DIAGS = 32
WINDOW = 32
NEAR = 16
STRIP = 16


def tournament_order(pair_count):
    ordering = np.zeros(2 * pair_count, dtype=np.int64)
    ordering[0] = 0
    ordering[2] = 1
    for slot in range(2, pair_count):
        ordering[2 * slot] = 2 * (slot - 1)
    for slot in range(pair_count - 1):
        ordering[2 * slot + 1] = 2 * (slot + 1) + 1
    ordering[2 * pair_count - 1] = 2 * (pair_count - 1)
    return ordering


def host_of(pair, pair_total, round_index):
    if round_index % 2 == 0 or pair == 0:
        return pair
    return min(pair + 1, pair_total - 1) if pair % 2 else pair - 1


def last_moves(pair_total):
    ordering = tournament_order(pair_total)
    sends, sends_first, gets_first = [], set(), set()
    for pair in range(pair_total):
        target = host_of(pair, pair_total, ROUNDS)
        for place in (0, 1):
            old = int(ordering[2 * pair + place])
            source = host_of(old // 2, pair_total, ROUNDS - 1)
            if source == target:
                continue
            sends.append((source, target))
            if old % 2 == 0:
                sends_first.add(source)
            if place == 0:
                gets_first.add(target)
    assert len({s for s, _ in sends}) == len(sends) == len({t for _, t in sends})
    return sends, sends_first, gets_first


def first_moves(pair_total):
    ordering = tournament_order(pair_total)
    sends, sends_second, gets_second, own_second = [], set(), set(), set()
    seconds = (set(), set())
    for pair in range(pair_total):
        here = host_of(pair, pair_total, 1)
        for place in (0, 1):
            old = int(ordering[2 * pair + place])
            if old % 2:
                seconds[place].add(here)
            if old // 2 == here:
                if place:
                    own_second.add(here)
                continue
            sends.append((old // 2, here))
            if old % 2:
                sends_second.add(old // 2)
                gets_second.add(here)
    assert len({s for s, _ in sends}) == len(sends) == len({t for _, t in sends})
    return sends, sends_second, gets_second, own_second, seconds


def fused_moves(pair_total):
    ordering = tournament_order(pair_total)
    before, last = ROUNDS - 3, ROUNDS - 1
    needs, edges, seconds = {}, [], ({}, {})
    for pair in range(pair_total):
        here = host_of(pair, pair_total, last)
        needs[here] = []
        for place in (0, 1):
            source = int(ordering[2 * pair + place])
            seconds[place][here] = source % 2
            for half in (0, 1):
                old = int(ordering[2 * (source // 2) + half])
                there = host_of(old // 2, pair_total, before)
                needs[here].append((there, old % 2))
                if there != here:
                    edges.append((there, old % 2, here))
    turn, left_over = {}, list(edges)
    while left_over:
        start = source = min(e[0] for e in left_over)
        target, number = min(e[2] for e in left_over if e[0] == source), 0
        while True:
            for one, other in ((source, target), (target, source)):
                edge = next(e for e in left_over if (e[0], e[2]) == (one, other))
                turn[edge] = number
                left_over.remove(edge)
            if target == start:
                break
            source, number = target, 1 - number
            target = next(e[2] for e in left_over if e[0] == source)
    sends = [[(e[0], e[2]) for e in edges if turn[e] == i] for i in (0, 1)]
    for chosen in sends:
        assert len({a for a, _ in chosen}) == len({b for _, b in chosen}) == pair_total
    sends_first = {e[0] for e in edges if turn[e] == 0 and e[1] == 0}
    picks = []
    for slot in range(4):
        pick = {}
        for here in range(pair_total):
            there, half = needs[here][slot]
            if there == here:
                pick[here] = 0 if (half == 0) == (here in sends_first) else 1
            else:
                pick[here] = 2 + turn[(there, half, here)]
        picks.append(pick)
    is_second = [{h for h, place in table.items() if place} for table in seconds]
    return sends, sends_first, picks, is_second


def choose(pick, arrays):
    chosen = arrays[0]
    for number in range(1, len(arrays)):
        members = {here for here, value in pick.items() if value == number}
        if members:
            chosen = jnp.where(among(members), arrays[number], chosen)
    return chosen


def among(members):
    here = lax.axis_index("pair")
    return functools.reduce(
        jnp.logical_or, [here == member for member in sorted(members)], here < 0
    )


def left(x, by):
    width = x.shape[1]
    return pltpu.roll(x, (width - by) % width, 1) if by % width else x


def right(x, by):
    width = x.shape[1]
    return pltpu.roll(x, by % width, 1) if by % width else x


def down(x, by):
    return pltpu.roll(x, by % x.shape[0], 0)


def lanes_of(x):
    return lax.broadcasted_iota(jnp.int32, x.shape, 1)


def split_pair(first, second):
    half = first.shape[1] // 2
    low = lanes_of(first) < half
    even = jnp.where(low, first, right(second, half))
    odd = jnp.where(low, right(first, half), second)
    return even, odd


def take_lanes(x, source):
    if x.shape[0] == 1:
        return take_lanes(jnp.broadcast_to(x, (8, x.shape[1])), source)[:1]
    return jnp.take_along_axis(x, jnp.broadcast_to(source, x.shape), axis=1)


def line_lanes(x):
    return lax.broadcasted_iota(jnp.int32, (1, x.shape[1]), 1)


def separate(first, second):
    lane = line_lanes(first)
    half = first.shape[1] // 2
    low = lane < half
    source = 2 * jnp.where(low, lane, lane - half)
    return tuple(
        jnp.where(low, take_lanes(first, source + odd), take_lanes(second, source + odd))
        for odd in (0, 1)
    )


def backwards(x):
    return jnp.take_along_axis(x, x.shape[1] - 1 - lanes_of(x), axis=1)


def dense_bands(even, odd, diags):
    width = even.shape[1]
    gram = lax.dot_general(
        jnp.concatenate((even, odd), axis=1),
        jnp.concatenate((backwards(even), backwards(odd)), axis=1),
        (((0,), (0,)), ((), ())),
        precision=lax.Precision.HIGHEST,
        preferred_element_type=jnp.float32,
    )
    bands = []
    for near in (0, width):
        for far in (0, width):
            quadrant = gram[far : far + width, near : near + width]
            aligned = pltpu.roll(quadrant, 1, 1, stride=1, stride_axis=0)
            bands.append(jnp.transpose(aligned)[:diags])
    return bands


def store_bands(even, odd, band_ref, diags):
    for q, band in enumerate(dense_bands(even, odd, diags)):
        band_ref[q * diags : (q + 1) * diags, :] = band


def open_kernel(sends_second, basis_ref, even_ref, odd_ref, payload_ref):
    rows, cols = basis_ref.shape
    width = cols // 2
    half = width // 2
    even, odd = separate(basis_ref[:, :width], basis_ref[:, width:])
    even_ref[...] = even
    odd_ref[...] = odd
    flag = among(sends_second)
    even, odd = (jnp.where(flag, left(x, half - STRIP), x) for x in (even, odd))
    payload_ref[:rows] = jnp.where(line_lanes(even) < half, even, right(odd, half))
    group = rows * 2 * STRIP // width
    strips = jnp.zeros((group, width), jnp.float32)
    for i in range(rows // group):
        for j, x in enumerate((even, odd)):
            start = (2 * i + j) * STRIP
            lane = line_lanes(x)
            here = jnp.logical_and(lane >= start, lane < start + STRIP)
            strips = jnp.where(here, left(x[i * group : (i + 1) * group], half - start), strips)
    payload_ref[rows:] = strips


def unpacked(payload, rows, second):
    width = payload.shape[1]
    half = width // 2
    lane = line_lanes(payload)
    main, strips = payload[:rows], payload[rows:]
    group = strips.shape[0]
    columns = []
    for j, x in enumerate((main, left(main, half))):
        ends = [right(strips, half - (2 * i + j) * STRIP) for i in range(rows // group)]
        x = jnp.where(lane < half, x, jnp.where(lane < half + STRIP, jnp.concatenate(ends), 0.0))
        columns.append(jnp.where(second, right(x, half - STRIP), x))
    return columns


def jacobi_angle(diag_even, diag_odd, coupling):
    spread = diag_even - diag_odd
    square = spread * spread + 4.0 * coupling * coupling
    inverse = lax.rsqrt(square)
    larger_square = (square * inverse + jnp.abs(spread)) * (0.5 * inverse)
    larger_inverse = lax.rsqrt(larger_square)
    larger = larger_square * larger_inverse
    smaller = coupling * inverse * larger_inverse
    forward = spread >= 0.0
    sign = jnp.where(coupling > 0.0, 1.0, jnp.where(coupling < 0.0, -1.0, 0.0))
    cosine = jnp.where(forward, larger, jnp.abs(smaller))
    sine_part = jnp.where(forward, smaller, sign * larger)
    return cosine, sine_part


def turn_bands(ee, eo, oe, oo, cosine, sine):
    cl, sl = jnp.broadcast_to(cosine, ee.shape), jnp.broadcast_to(sine, ee.shape)
    ck = pltpu.roll(cl, 0, 1, stride=1, stride_axis=0)
    sk = pltpu.roll(sl, 0, 1, stride=1, stride_axis=0)
    ee, oe = ck * ee + sk * oe, ck * oe - sk * ee
    eo, oo = ck * eo + sk * oo, ck * oo - sk * eo
    ee, eo = cl * ee + sl * eo, cl * eo - sl * ee
    oe, oo = cl * oe + sl * oo, cl * oo - sl * oe
    return ee, eo, oe, oo


def step_bands(ee, eo, oe, oo, cosine, sine):
    lane = lanes_of(ee)
    diag = lax.broadcasted_iota(jnp.int32, ee.shape, 0)
    last = lane == ee.shape[1] - 1
    on, next_on = diag == 0, diag == 1

    def slanted(x, by):
        if by >= 0:
            return pltpu.roll(x, by, 1, stride=1, stride_axis=0)
        return jnp.where(on, left(x, -by), down(slanted(x, 0), -by))

    def rotated(by, wanted):
        cl, sl = (jnp.broadcast_to(x, ee.shape) for x in (cosine, sine))
        ck, sk = (slanted(x, by) for x in (cl, sl))
        cl, sl, a, b, c, d = (right(x, by) for x in (cl, sl, ee, eo, oe, oo))
        a, c = ck * a + sk * c, ck * c - sk * a
        b, d = ck * b + sk * d, ck * d - sk * b
        found = {"ee": (a, b), "eo": (b, a), "oe": (c, d), "oo": (d, c)}
        return [
            cl * one + sl * two if name in ("ee", "oe") else cl * one - sl * two
            for name, (one, two) in found.items()
            if name in wanted
        ]

    ee_0, eo_0, oe_0, oo_0 = rotated(0, ("ee", "eo", "oe", "oo"))
    ee_r, eo_r, oe_r, oo_r = rotated(1, ("ee", "eo", "oe", "oo"))
    eo_l, oo_l = rotated(-1, ("eo", "oo"))

    near = down(jnp.where(on, eo_r, ee_r), 1)
    turned = jnp.where(on, oo_r, oe_r)
    ee_new = jnp.where(lane == diag + 1, turned, jnp.where(lane == diag, near, ee_r))
    ee_new = jnp.where(jnp.logical_and(on, lane == 0), ee_0, ee_new)

    eo_new = down(jnp.where(lane == diag - 1, oo_l, eo_l), -2)
    eo_new = jnp.where(lane == diag, down(eo_l, -1), eo_new)
    eo_new = jnp.where(last, down(ee_0, -1), eo_new)

    oo_new = jnp.where(last, jnp.where(on, ee_0, down(oe_0, 1)), oo_l)

    oe_new = down(oe_r, 2)
    oe_new = jnp.where(next_on, jnp.where(lane == diag, oo_0, eo_0), oe_new)
    oe_new = jnp.where(on, eo_new, oe_new)
    return ee_new, eo_new, oe_new, oo_new


def move_bands(ee, eo, oe, oo):
    lane = lanes_of(ee)
    diag = lax.broadcasted_iota(jnp.int32, ee.shape, 0)
    last = lane == ee.shape[1] - 1
    on, next_on = diag == 0, diag == 1

    near = down(jnp.where(on, eo, ee), 1)
    turned = jnp.where(on, oo, oe)
    mixed = jnp.where(lane == diag, turned, jnp.where(lane == diag - 1, near, ee))
    ee_new = jnp.where(jnp.logical_and(on, lane == 0), ee, right(mixed, 1))

    far = down(jnp.where(last, ee, eo), -1)
    mixed = down(jnp.where(lane == diag, oo, eo), -2)
    mixed = left(jnp.where(lane == diag + 1, far, mixed), 1)
    eo_new = jnp.where(last, far, mixed)

    oo_new = jnp.where(last, jnp.where(on, ee, down(oe, 1)), left(oo, 1))

    oe_new = right(down(oe, 2), 1)
    oe_new = jnp.where(next_on, jnp.where(lane == diag, oo, eo), oe_new)
    oe_new = jnp.where(on, eo_new, oe_new)
    return ee_new, eo_new, oe_new, oo_new


def move_bands_back(ee, eo, oe, oo):
    lane = lanes_of(ee)
    diag = lax.broadcasted_iota(jnp.int32, ee.shape, 0)
    last, first = lane == ee.shape[1] - 1, lane == diag
    on, next_on = diag == 0, diag == 1
    ahead, behind = lane == diag + 1, lane == diag - 1
    eo_down, oo_up = down(eo, 1), down(oo, -1)
    eo_twice = down(eo, 2)

    ee_left = left(jnp.where(ahead, down(ee, -1), ee), 1)
    ee_old = jnp.where(jnp.logical_and(first, on), ee, ee_left)
    ee_old = jnp.where(last, jnp.where(on, oo, eo_down), ee_old)

    oe_left = left(jnp.where(jnp.logical_and(ahead, diag > 0), ee, down(oe, -2)), 1)
    eo_far = right(jnp.where(behind, eo_down, eo_twice), 1)
    eo_old = jnp.where(on, jnp.where(last, oo_up, oe_left), eo_far)
    eo_old = jnp.where(jnp.logical_and(next_on, lane > 1), oe, eo_old)
    eo_old = jnp.where(jnp.logical_and(on, first), ee_left, eo_old)

    oe_old = jnp.where(on, eo_old, jnp.where(last, oo_up, oe_left))

    oo_old = right(jnp.where(behind, eo_twice, oo), 1)
    oo_old = jnp.where(jnp.logical_and(next_on, first), oe, oo_old)
    oo_old = jnp.where(jnp.logical_and(on, first), left(ee, 1), oo_old)
    return ee_old, eo_old, oe_old, oo_old


def move_columns(even, odd):
    lane = lanes_of(even)
    first, last = lane == 0, lane == even.shape[1] - 1
    even_new = jnp.where(first, even, right(jnp.where(first, odd, even), 1))
    odd_new = jnp.where(last, even, left(odd, 1))
    return even_new, odd_new


def in_pair(even, shifted=None):
    lane = line_lanes(even)
    if shifted is not None:
        half = even.shape[1] // 2
        lane = jnp.where(shifted, jnp.where(lane < half, lane + half, lane - half), lane)
    return (lane < 0, lane), (lane >= 0, lane)


def in_blocks(even):
    lane, half = line_lanes(even), even.shape[1] // 2
    place = jnp.where(lane < half, lane, lane - half)
    return (lane >= half, place), (lane >= half, place + half)


def in_order(even):
    lane, half = line_lanes(even), even.shape[1] // 2
    return (lane % 2 == 1, lane // 2), (lane % 2 == 1, lane // 2 + half)


def turn_to(layout, even, odd, angles):
    for cosine, sine in angles[:-1]:
        even, odd = cosine * even + sine * odd, cosine * odd - sine * even
        even, odd = move_columns(even, odd)
    by, end = JSTEPS - 1, even.shape[1] - 1
    results = []
    for is_odd, place in layout:
        stayed = place <= end - by
        from_even = jnp.where(stayed, place + by, 2 * end + 1 - by - place)
        from_even = jnp.where(place == 0, 0, from_even)
        source = jnp.where(is_odd, jnp.abs(place - by), from_even)
        is_even = jnp.logical_or(
            jnp.logical_and(is_odd, place < by),
            jnp.logical_and(jnp.logical_not(is_odd), stayed),
        )
        cosine, sine = (take_lanes(x, source) for x in angles[-1])
        by_even = jnp.where(is_even, cosine, -sine)
        by_odd = jnp.where(is_even, sine, cosine)
        results.append(by_even * take_lanes(even, source) + by_odd * take_lanes(odd, source))
    return results


def trim(bands, reach):
    rows = min(bands[0].shape[0], -(-(reach + 1) // 8) * 8)
    return [band[:rows] for band in bands]


def angles_of(bands):
    angles = []
    for step in range(JSTEPS):
        ee, eo, oe, oo = bands = trim(bands, 2 * (JSTEPS - 1 - step))
        angles.append(jacobi_angle(ee[0:1], oo[0:1], eo[0:1]))
        if step < JSTEPS - 1:
            bands = step_bands(*bands, *angles[-1])
    return angles


def carried(bands, angles):
    ahead = 2 * (JSTEPS - 1)
    for step, (cosine, sine) in enumerate(angles):
        bands = turn_bands(*trim(bands, 3 * ahead - 2 * step), cosine, sine)
        if step < JSTEPS - 1:
            bands = move_bands(*bands)
    for step in range(JSTEPS - 1):
        bands = move_bands_back(*trim(bands, 2 * (ahead - step)))
    return bands


def near_starts(width):
    half = width // 2
    reach = REACH - 1
    return (half - 2 * reach, width - WINDOW), (0, half - reach)


def cross_partial(x_even, x_odd, y_even, y_odd, x_second, y_second):
    rows, width = x_even.shape
    x_starts, y_starts = near_starts(width)
    lane = lanes_of(x_even)

    def window(even, odd, flag, starts):
        start = jnp.where(flag, starts[1], starts[0])
        at_zero = pltpu.roll(even, width - start, 1)
        at_next = pltpu.roll(odd, (width - start + WINDOW) % width, 1)
        return jnp.where(lane < WINDOW, at_zero, jnp.where(lane < 2 * WINDOW, at_next, 0.0))

    corner = lax.dot_general(
        window(y_even, y_odd, y_second, y_starts),
        window(x_even, x_odd, x_second, x_starts),
        (((0,), (0,)), ((), ())),
        precision=lax.Precision.HIGHEST,
        preferred_element_type=jnp.float32,
    )
    low = lax.broadcasted_iota(jnp.int32, (WINDOW, width), 1) < 2 * WINDOW
    return jnp.where(low, corner[:WINDOW], right(corner[WINDOW : 2 * WINDOW], 2 * WINDOW))


def own_rotation(angles, second, swapped, first_pair):
    width = angles[0][0].shape[1]
    half = width // 2
    x_starts, y_starts = near_starts(width)
    starts = [jnp.where(first_pair, x, y) for x, y in zip(x_starts, y_starts)]
    shape = (2 * WINDOW, width)
    row = lax.broadcasted_iota(jnp.int32, shape, 0)
    lane = lax.broadcasted_iota(jnp.int32, shape, 1) - jnp.where(second, starts[1], starts[0])
    even, odd = (
        jnp.where(jnp.logical_and(row == lane + at, row // WINDOW == at // WINDOW), 1.0, 0.0)
        for at in (0, WINDOW)
    )
    even, odd = turn_to(in_pair(even, swapped), even, odd, angles)
    low = lax.broadcasted_iota(jnp.int32, shape, 1) < half
    return jnp.where(jnp.logical_xor(low, first_pair), right(odd, half), even)


def cross_bands(packed, x_rotation, y_rotation):
    width = packed.shape[1]
    half = width // 2
    corner = jnp.concatenate((packed[:, :half], right(packed, half)[:, :half]), axis=0)
    highest = dict(precision=lax.Precision.HIGHEST, preferred_element_type=jnp.float32)
    turned_x = jnp.dot(corner, x_rotation, **highest)
    ends = lax.dot_general(turned_x, y_rotation, (((0,), (0,)), ((), ())), **highest)
    even, odd = ends[half - NEAR : half], ends[width - NEAR :]
    quadrants = (even, right(even, half), odd, right(odd, half))
    offset = lanes_of(even) - lax.broadcasted_iota(jnp.int32, even.shape, 0) - (half - NEAR)
    diag = lax.broadcasted_iota(jnp.int32, (DIAGS, width), 0)
    bands = [jnp.zeros((DIAGS, width), jnp.float32) for _ in quadrants]
    for d in range(1, REACH):
        here = offset == d
        for q, quadrant in enumerate(quadrants):
            line = jnp.sum(jnp.where(here, quadrant, 0.0), axis=0, keepdims=True)
            bands[q] = jnp.where(diag == d, line, bands[q])
    return bands


def either(flag, one, other):
    return jnp.logical_or(jnp.logical_and(flag, one), jnp.logical_and(jnp.logical_not(flag), other))


def halves_swapped(is_second):
    return among(is_second[0]), jnp.logical_not(among(is_second[1]))


def on_odd_core():
    return lax.axis_index("row") % 2 == 1


def far_starts(width):
    return REACH - 1, width // 2


def pack_far(bands, flag):
    width = bands[0].shape[1]
    half, count = width // 2, (FAR_DIAGS - DIAGS) // 2
    lane = line_lanes(bands[0])
    packed = []
    for band in bands:
        one, two = band[DIAGS : DIAGS + count], band[DIAGS + count :]
        one, two = (
            jnp.where(flag, left(x, far_starts(width)[1] - at), left(x, far_starts(width)[0] - at))
            for x, at in ((one, 0), (two, half))
        )
        packed.append(jnp.concatenate((band[:DIAGS], jnp.where(lane < half, one, two)), axis=0))
    return packed


def unpack_far(packed, flag):
    width = packed.shape[1]
    half = width // 2
    parts = [packed[:DIAGS]]
    for at in (0, half):
        starts = [start - at for start in far_starts(width)]
        x = packed[DIAGS:]
        parts.append(jnp.where(flag, right(x, starts[1]), right(x, starts[0])))
    return jnp.concatenate(parts, axis=0)


PACKED = DIAGS + (FAR_DIAGS - DIAGS) // 2


def store_part(even, odd, corner, flag, part_ref):
    bands = pack_far(dense_bands(even, odd, FAR_DIAGS), flag)
    for q, band in enumerate(bands):
        part_ref[q * PACKED : (q + 1) * PACKED, :] = band
    part_ref[4 * PACKED :, :] = corner


def open_pairs(is_second, x, y, column_refs, corner_ref, other_ref):
    x_second, y_second = among(is_second[0]), among(is_second[1])
    corner = cross_partial(*x, *y, x_second, y_second)
    flag = on_odd_core()
    mine = [jnp.where(flag, b, a) for a, b in zip(x, y)]
    theirs = [jnp.where(flag, a, b) for a, b in zip(x, y)]
    for ref, value in zip(column_refs, mine + theirs):
        ref[...] = value
    corner_ref[...] = jnp.where(flag, corner[NEAR:], corner[:NEAR])
    store_part(
        *theirs,
        jnp.where(flag, corner[:NEAR], corner[NEAR:]),
        either(flag, x_second, y_second),
        other_ref,
    )


def first_open(own_second, gets_second, is_second, even_ref, odd_ref, payload_ref, *refs):
    *column_refs, corner_ref, other_ref = refs
    own = even_ref[...], odd_ref[...]
    came = unpacked(payload_ref[...], own[0].shape[0], among(gets_second))
    flag = among(own_second)
    x = [jnp.where(flag, b, a) for a, b in zip(own, came)]
    y = [jnp.where(flag, a, b) for a, b in zip(own, came)]
    open_pairs(is_second, x, y, column_refs, corner_ref, other_ref)


def fused_open(picks, is_second, kept_ref, sent_ref, came0_ref, came1_ref, *refs):
    *column_refs, corner_ref, other_ref = refs
    arrays = [ref[...] for ref in (sent_ref, kept_ref, came0_ref, came1_ref)]
    blocks = [choose(pick, arrays) for pick in picks]
    x, y = split_pair(*blocks[:2]), split_pair(*blocks[2:])
    open_pairs(is_second, x, y, column_refs, corner_ref, other_ref)


def swapped_flag(is_second):
    x_swapped, y_swapped = halves_swapped(is_second)
    return either(on_odd_core(), y_swapped, x_swapped)


def own_second_flag(is_second):
    return either(on_odd_core(), among(is_second[1]), among(is_second[0]))


def bands_kernel(is_second, even_ref, odd_ref, corner_ref, part_ref):
    flag = own_second_flag(is_second)
    store_part(even_ref[...], odd_ref[...], corner_ref[...], flag, part_ref)


def angles_kernel(is_second, *refs):
    *part_refs, found_ref = refs
    part = pair_sums([ref[...] for ref in part_refs])
    flag = own_second_flag(is_second)
    quadrants = [unpack_far(part[q * PACKED : (q + 1) * PACKED], flag) for q in range(4)]
    angles = angles_of(quadrants)
    bands = carried(quadrants, angles)
    for step, pair in enumerate(angles):
        for i in (0, 1):
            found_ref[2 * step + i : 2 * step + i + 1, :] = pair[i]
    spare = NEAR - 2 * JSTEPS
    found_ref[2 * JSTEPS : NEAR, :] = jnp.zeros((spare, part.shape[1]), jnp.float32)
    for q in range(4):
        found_ref[NEAR + q * DIAGS : NEAR + (q + 1) * DIAGS, :] = bands[q][:DIAGS]
    found_ref[CORNER:ROTATION, :] = part[4 * PACKED :]
    first_pair = jnp.logical_not(on_odd_core())
    found_ref[ROTATION:, :] = own_rotation(angles, flag, swapped_flag(is_second), first_pair)


CORNER = NEAR + 4 * DIAGS
ROTATION = CORNER + NEAR
FOUND = ROTATION + 2 * WINDOW


def angles_in(found):
    return [(found[2 * i : 2 * i + 1], found[2 * i + 1 : 2 * i + 2]) for i in range(JSTEPS)]


def columns_kernel(is_second, even_ref, odd_ref, found_ref, *out_refs):
    angles = angles_in(found_ref[...])
    layout = in_pair(even_ref, swapped_flag(is_second))
    columns = turn_to(layout, even_ref[...], odd_ref[...], angles)
    for ref, value in zip(out_refs, columns):
        ref[...] = value


def next_bands(x_found, y_found, x_second, y_second):
    corner = jnp.concatenate((x_found[CORNER:ROTATION], y_found[CORNER:ROTATION]), axis=0)
    middle = cross_bands(corner, x_found[ROTATION:], y_found[ROTATION:])
    half = corner.shape[1] // 2
    lane = lanes_of(middle[0])
    diag = lax.broadcasted_iota(jnp.int32, middle[0].shape, 0)
    bands = []
    for q in range(4):
        rows = slice(NEAR + q * DIAGS, NEAR + (q + 1) * DIAGS)
        x, y = x_found[rows], y_found[rows]
        x = jnp.where(x_second, right(x, half), x)
        y = jnp.where(y_second, y, right(y, half))
        crossing = jnp.where(lane - diag < half, middle[q], y)
        bands.append(jnp.where(lane < half, x, crossing))
    return bands


def next_kernel(is_second, sends_first, layout_of, *refs):
    mine_even, mine_odd, even_ref, odd_ref, found_ref, other_ref, kept_ref, sent_ref = refs
    found, other = found_ref[...], other_ref[...]
    flag = on_odd_core()
    x_found, y_found = jnp.where(flag, other, found), jnp.where(flag, found, other)
    bands = next_bands(x_found, y_found, among(is_second[0]), among(is_second[1]))
    x_swapped, y_swapped = halves_swapped(is_second)
    swapped = either(flag, x_swapped, y_swapped)
    layout = in_pair(even_ref, swapped)
    theirs = turn_to(layout, even_ref[...], odd_ref[...], angles_in(other))
    low = line_lanes(found) < found.shape[1] // 2
    from_mine = jnp.logical_xor(low, flag)
    even = jnp.where(from_mine, mine_even[...], theirs[0])
    odd = jnp.where(from_mine, mine_odd[...], theirs[1])
    angles = angles_of(bands)
    first, second = turn_to(layout_of(even), even, odd, angles)
    flag = among(sends_first)
    kept_ref[...] = jnp.where(flag, second, first)
    sent_ref[...] = jnp.where(flag, first, second)


def pair_sums(arrays):
    while len(arrays) > 1:
        arrays = [arrays[i] + arrays[i + 1] for i in range(0, len(arrays), 2)]
    return arrays[0]


def swap(x, axis, mask):
    return lax.ppermute(x, axis, [(i, i ^ mask) for i in range(lax.axis_size(axis))])


def exchange_groups(x, axis, first_bit=0):
    count = lax.axis_size(axis).bit_length() - 1
    bits = [1 << b for b in range(count)]
    groups = [bits[:1]] + [bits[i : i + 2] for i in range(1, count, 2)]
    arrays = [x]
    for group in groups[first_bit:]:
        x = pair_sums(arrays)
        masks = [group[0]] if len(group) == 1 else [group[0], group[1], group[0] | group[1]]
        arrays = [x] + [swap(x, axis, mask) for mask in masks]
    return arrays


def call(kernel, shapes, *args):
    out = [jax.ShapeDtypeStruct(shape, jnp.float32) for shape in shapes]
    return pl.pallas_call(
        kernel,
        out_shape=out,
        compiler_params=pltpu.CompilerParams(vmem_limit_bytes=32 * 1024 * 1024),
    )(*args)


def two_rounds(opened, is_second, sends_first, layout_of):
    *columns, corner, other = opened
    column, width = columns[0].shape, columns[0].shape[1]
    other = swap(other, "row", 1)
    bands = functools.partial(bands_kernel, is_second)
    (mine,) = call(bands, (other.shape,), *columns[:2], corner)
    (found,) = call(
        functools.partial(angles_kernel, is_second),
        ((FOUND, width),),
        *exchange_groups(mine + other, "row", 1),
    )
    other = swap(found, "row", 1)
    turn = functools.partial(columns_kernel, is_second)
    columns[:2] = call(turn, (column, column), *columns[:2], found)
    turn = functools.partial(next_kernel, is_second, sends_first, layout_of)
    return call(turn, (column, column), *columns, found, other)


def per_device(basis):
    rows, cols = basis.shape
    width = cols // 2
    pair_total = lax.axis_size("pair")
    column = (rows, width)
    opened = (column,) * 4 + ((NEAR, width), (4 * PACKED + NEAR, width))
    payload = (rows + rows * 2 * STRIP // width, width)

    sends, sends_second, gets_second, own_second, is_second = first_moves(pair_total)
    opening = functools.partial(open_kernel, sends_second)
    even, odd, sent = call(opening, (column, column, payload), basis)
    came = lax.ppermute(sent, "pair", sends)
    opening = functools.partial(first_open, own_second, gets_second, is_second)
    arrays = call(opening, opened, even, odd, came)
    sends, sends_first, picks, next_second = fused_moves(pair_total)
    kept, sent = two_rounds(arrays, is_second, sends_first, in_blocks)

    came = [lax.ppermute(x, "pair", s) for x, s in zip((sent, kept), sends)]
    opening = functools.partial(fused_open, picks, next_second)
    arrays = call(opening, opened, kept, sent, *came)
    sends, sends_first, gets_first = last_moves(pair_total)
    kept, sent = two_rounds(arrays, next_second, sends_first, in_order)

    came = lax.ppermute(sent, "pair", sends)
    flag = among(gets_first)
    first = jnp.where(flag, came, kept)
    second = jnp.where(flag, kept, came)
    return jnp.concatenate((first, second), axis=1)


def solution(mesh):
    return jax.shard_map(
        per_device,
        mesh=mesh,
        in_specs=(P("row", "pair"),),
        out_specs=P("row", "pair"),
        check_vma=False,
    )
```

```python
import functools

import jax
import jax.numpy as jnp
import numpy as np
from jax import lax
from jax.experimental import pallas as pl
from jax.experimental.pallas import tpu as pltpu
from jax.sharding import PartitionSpec as P

ROUNDS = 4
JSTEPS = 6
REACH = 2 * (JSTEPS - 1) + 1
DIAGS = 16
FAR_DIAGS = 32
WINDOW = 32
NEAR = 16
STRIP = 16


def tournament_order(pair_count):
    ordering = np.zeros(2 * pair_count, dtype=np.int64)
    ordering[0] = 0
    ordering[2] = 1
    for slot in range(2, pair_count):
        ordering[2 * slot] = 2 * (slot - 1)
    for slot in range(pair_count - 1):
        ordering[2 * slot + 1] = 2 * (slot + 1) + 1
    ordering[2 * pair_count - 1] = 2 * (pair_count - 1)
    return ordering


def host_of(pair, pair_total, round_index):
    if round_index % 2 == 0 or pair == 0:
        return pair
    return min(pair + 1, pair_total - 1) if pair % 2 else pair - 1


def last_moves(pair_total):
    ordering = tournament_order(pair_total)
    sends, sends_first, gets_first = [], set(), set()
    for pair in range(pair_total):
        target = host_of(pair, pair_total, ROUNDS)
        for place in (0, 1):
            old = int(ordering[2 * pair + place])
            source = host_of(old // 2, pair_total, ROUNDS - 1)
            if source == target:
                continue
            sends.append((source, target))
            if old % 2 == 0:
                sends_first.add(source)
            if place == 0:
                gets_first.add(target)
    assert len({s for s, _ in sends}) == len(sends) == len({t for _, t in sends})
    return sends, sends_first, gets_first


def first_moves(pair_total):
    ordering = tournament_order(pair_total)
    sends, sends_second, gets_second, own_second = [], set(), set(), set()
    seconds = (set(), set())
    for pair in range(pair_total):
        here = host_of(pair, pair_total, 1)
        for place in (0, 1):
            old = int(ordering[2 * pair + place])
            if old % 2:
                seconds[place].add(here)
            if old // 2 == here:
                if place:
                    own_second.add(here)
                continue
            sends.append((old // 2, here))
            if old % 2:
                sends_second.add(old // 2)
                gets_second.add(here)
    assert len({s for s, _ in sends}) == len(sends) == len({t for _, t in sends})
    return sends, sends_second, gets_second, own_second, seconds


def fused_moves(pair_total):
    ordering = tournament_order(pair_total)
    before, last = ROUNDS - 3, ROUNDS - 1
    needs, edges, seconds = {}, [], ({}, {})
    for pair in range(pair_total):
        here = host_of(pair, pair_total, last)
        needs[here] = []
        for place in (0, 1):
            source = int(ordering[2 * pair + place])
            seconds[place][here] = source % 2
            for half in (0, 1):
                old = int(ordering[2 * (source // 2) + half])
                there = host_of(old // 2, pair_total, before)
                needs[here].append((there, old % 2))
                if there != here:
                    edges.append((there, old % 2, here))
    turn, left_over = {}, list(edges)
    while left_over:
        source, _, target = left_over[0]
        start = source
        while True:
            for number, one, other in ((1, source, target), (0, target, source)):
                edge = next(e for e in left_over if (e[0], e[2]) == (one, other))
                turn[edge] = number
                left_over.remove(edge)
            if target == start:
                break
            ahead = [e[2] for e in left_over if e[0] == target]
            source, target = target, ahead[0]
    sends = [[(e[0], e[2]) for e in edges if turn[e] == i] for i in (0, 1)]
    for chosen in sends:
        assert len({a for a, _ in chosen}) == len({b for _, b in chosen}) == pair_total
    sends_first = {e[0] for e in edges if turn[e] == 0 and e[1] == 0}
    picks = []
    for slot in range(4):
        pick = {}
        for here in range(pair_total):
            there, half = needs[here][slot]
            if there == here:
                pick[here] = 0 if (half == 0) == (here in sends_first) else 1
            else:
                pick[here] = 2 + turn[(there, half, here)]
        picks.append(pick)
    is_second = [{h for h, place in table.items() if place} for table in seconds]
    return sends, sends_first, picks, is_second


def choose(pick, arrays):
    chosen = arrays[0]
    for number in range(1, len(arrays)):
        members = {here for here, value in pick.items() if value == number}
        if members:
            chosen = jnp.where(among(members), arrays[number], chosen)
    return chosen


def among(members):
    here = lax.axis_index("pair")
    return functools.reduce(
        jnp.logical_or, [here == member for member in sorted(members)], here < 0
    )


def left(x, by):
    width = x.shape[1]
    return pltpu.roll(x, (width - by) % width, 1) if by % width else x


def right(x, by):
    width = x.shape[1]
    return pltpu.roll(x, by % width, 1) if by % width else x


def down(x, by):
    return pltpu.roll(x, by % x.shape[0], 0)


def lanes_of(x):
    return lax.broadcasted_iota(jnp.int32, x.shape, 1)


def split_pair(first, second):
    half = first.shape[1] // 2
    low = lanes_of(first) < half
    even = jnp.where(low, first, right(second, half))
    odd = jnp.where(low, right(first, half), second)
    return even, odd


def take_lanes(x, source):
    if x.shape[0] == 1:
        return take_lanes(jnp.broadcast_to(x, (8, x.shape[1])), source)[:1]
    return jnp.take_along_axis(x, jnp.broadcast_to(source, x.shape), axis=1)


def line_lanes(x):
    return lax.broadcasted_iota(jnp.int32, (1, x.shape[1]), 1)


def separate(first, second):
    lane = line_lanes(first)
    half = first.shape[1] // 2
    low = lane < half
    source = 2 * jnp.where(low, lane, lane - half)
    return tuple(
        jnp.where(low, take_lanes(first, source + odd), take_lanes(second, source + odd))
        for odd in (0, 1)
    )


def backwards(x):
    return jnp.take_along_axis(x, x.shape[1] - 1 - lanes_of(x), axis=1)


def dense_bands(even, odd, diags):
    width = even.shape[1]
    gram = lax.dot_general(
        jnp.concatenate((even, odd), axis=1),
        jnp.concatenate((backwards(even), backwards(odd)), axis=1),
        (((0,), (0,)), ((), ())),
        precision=lax.Precision.HIGHEST,
        preferred_element_type=jnp.float32,
    )
    bands = []
    for near in (0, width):
        for far in (0, width):
            quadrant = gram[far : far + width, near : near + width]
            aligned = pltpu.roll(quadrant, 1, 1, stride=1, stride_axis=0)
            bands.append(jnp.transpose(aligned)[:diags])
    return bands


def store_bands(even, odd, band_ref, diags):
    for q, band in enumerate(dense_bands(even, odd, diags)):
        band_ref[q * diags : (q + 1) * diags, :] = band


def open_kernel(sends_second, basis_ref, even_ref, odd_ref, payload_ref):
    rows, cols = basis_ref.shape
    width = cols // 2
    half = width // 2
    even, odd = separate(basis_ref[:, :width], basis_ref[:, width:])
    even_ref[...] = even
    odd_ref[...] = odd
    flag = among(sends_second)
    even, odd = (jnp.where(flag, left(x, half - STRIP), x) for x in (even, odd))
    payload_ref[:rows] = jnp.where(line_lanes(even) < half, even, right(odd, half))
    group = rows * 2 * STRIP // width
    strips = jnp.zeros((group, width), jnp.float32)
    for i in range(rows // group):
        for j, x in enumerate((even, odd)):
            start = (2 * i + j) * STRIP
            lane = line_lanes(x)
            here = jnp.logical_and(lane >= start, lane < start + STRIP)
            strips = jnp.where(here, left(x[i * group : (i + 1) * group], half - start), strips)
    payload_ref[rows:] = strips


def unpacked(payload, rows, second):
    width = payload.shape[1]
    half = width // 2
    lane = line_lanes(payload)
    main, strips = payload[:rows], payload[rows:]
    group = strips.shape[0]
    columns = []
    for j, x in enumerate((main, left(main, half))):
        ends = [right(strips, half - (2 * i + j) * STRIP) for i in range(rows // group)]
        x = jnp.where(lane < half, x, jnp.where(lane < half + STRIP, jnp.concatenate(ends), 0.0))
        columns.append(jnp.where(second, right(x, half - STRIP), x))
    return columns


def jacobi_angle(diag_even, diag_odd, coupling):
    spread = diag_even - diag_odd
    square = spread * spread + 4.0 * coupling * coupling
    inverse = lax.rsqrt(square)
    larger_square = (square * inverse + jnp.abs(spread)) * (0.5 * inverse)
    larger_inverse = lax.rsqrt(larger_square)
    larger = larger_square * larger_inverse
    smaller = coupling * inverse * larger_inverse
    forward = spread >= 0.0
    sign = jnp.where(coupling > 0.0, 1.0, jnp.where(coupling < 0.0, -1.0, 0.0))
    cosine = jnp.where(forward, larger, jnp.abs(smaller))
    sine_part = jnp.where(forward, smaller, sign * larger)
    return cosine, sine_part


def turn_bands(ee, eo, oe, oo, cosine, sine):
    cl, sl = jnp.broadcast_to(cosine, ee.shape), jnp.broadcast_to(sine, ee.shape)
    ck = pltpu.roll(cl, 0, 1, stride=1, stride_axis=0)
    sk = pltpu.roll(sl, 0, 1, stride=1, stride_axis=0)
    ee, oe = ck * ee + sk * oe, ck * oe - sk * ee
    eo, oo = ck * eo + sk * oo, ck * oo - sk * eo
    ee, eo = cl * ee + sl * eo, cl * eo - sl * ee
    oe, oo = cl * oe + sl * oo, cl * oo - sl * oe
    return ee, eo, oe, oo


def step_bands(ee, eo, oe, oo, cosine, sine):
    lane = lanes_of(ee)
    diag = lax.broadcasted_iota(jnp.int32, ee.shape, 0)
    last = lane == ee.shape[1] - 1
    on, next_on = diag == 0, diag == 1

    def slanted(x, by):
        if by >= 0:
            return pltpu.roll(x, by, 1, stride=1, stride_axis=0)
        return jnp.where(on, left(x, -by), down(slanted(x, 0), -by))

    def rotated(by, wanted):
        cl, sl = (jnp.broadcast_to(x, ee.shape) for x in (cosine, sine))
        ck, sk = (slanted(x, by) for x in (cl, sl))
        cl, sl, a, b, c, d = (right(x, by) for x in (cl, sl, ee, eo, oe, oo))
        a, c = ck * a + sk * c, ck * c - sk * a
        b, d = ck * b + sk * d, ck * d - sk * b
        found = {"ee": (a, b), "eo": (b, a), "oe": (c, d), "oo": (d, c)}
        return [
            cl * one + sl * two if name in ("ee", "oe") else cl * one - sl * two
            for name, (one, two) in found.items()
            if name in wanted
        ]

    ee_0, eo_0, oe_0, oo_0 = rotated(0, ("ee", "eo", "oe", "oo"))
    ee_r, eo_r, oe_r, oo_r = rotated(1, ("ee", "eo", "oe", "oo"))
    eo_l, oo_l = rotated(-1, ("eo", "oo"))

    near = down(jnp.where(on, eo_r, ee_r), 1)
    turned = jnp.where(on, oo_r, oe_r)
    ee_new = jnp.where(lane == diag + 1, turned, jnp.where(lane == diag, near, ee_r))
    ee_new = jnp.where(jnp.logical_and(on, lane == 0), ee_0, ee_new)

    eo_new = down(jnp.where(lane == diag - 1, oo_l, eo_l), -2)
    eo_new = jnp.where(lane == diag, down(eo_l, -1), eo_new)
    eo_new = jnp.where(last, down(ee_0, -1), eo_new)

    oo_new = jnp.where(last, jnp.where(on, ee_0, down(oe_0, 1)), oo_l)

    oe_new = down(oe_r, 2)
    oe_new = jnp.where(next_on, jnp.where(lane == diag, oo_0, eo_0), oe_new)
    oe_new = jnp.where(on, eo_new, oe_new)
    return ee_new, eo_new, oe_new, oo_new


def move_bands(ee, eo, oe, oo):
    lane = lanes_of(ee)
    diag = lax.broadcasted_iota(jnp.int32, ee.shape, 0)
    last = lane == ee.shape[1] - 1
    on, next_on = diag == 0, diag == 1

    near = down(jnp.where(on, eo, ee), 1)
    turned = jnp.where(on, oo, oe)
    mixed = jnp.where(lane == diag, turned, jnp.where(lane == diag - 1, near, ee))
    ee_new = jnp.where(jnp.logical_and(on, lane == 0), ee, right(mixed, 1))

    far = down(jnp.where(last, ee, eo), -1)
    mixed = down(jnp.where(lane == diag, oo, eo), -2)
    mixed = left(jnp.where(lane == diag + 1, far, mixed), 1)
    eo_new = jnp.where(last, far, mixed)

    oo_new = jnp.where(last, jnp.where(on, ee, down(oe, 1)), left(oo, 1))

    oe_new = right(down(oe, 2), 1)
    oe_new = jnp.where(next_on, jnp.where(lane == diag, oo, eo), oe_new)
    oe_new = jnp.where(on, eo_new, oe_new)
    return ee_new, eo_new, oe_new, oo_new


def move_bands_back(ee, eo, oe, oo):
    lane = lanes_of(ee)
    diag = lax.broadcasted_iota(jnp.int32, ee.shape, 0)
    last, first = lane == ee.shape[1] - 1, lane == diag
    on, next_on = diag == 0, diag == 1
    ahead, behind = lane == diag + 1, lane == diag - 1
    eo_down, oo_up = down(eo, 1), down(oo, -1)
    eo_twice = down(eo, 2)

    ee_left = left(jnp.where(ahead, down(ee, -1), ee), 1)
    ee_old = jnp.where(jnp.logical_and(first, on), ee, ee_left)
    ee_old = jnp.where(last, jnp.where(on, oo, eo_down), ee_old)

    oe_left = left(jnp.where(jnp.logical_and(ahead, diag > 0), ee, down(oe, -2)), 1)
    eo_far = right(jnp.where(behind, eo_down, eo_twice), 1)
    eo_old = jnp.where(on, jnp.where(last, oo_up, oe_left), eo_far)
    eo_old = jnp.where(jnp.logical_and(next_on, lane > 1), oe, eo_old)
    eo_old = jnp.where(jnp.logical_and(on, first), ee_left, eo_old)

    oe_old = jnp.where(on, eo_old, jnp.where(last, oo_up, oe_left))

    oo_old = right(jnp.where(behind, eo_twice, oo), 1)
    oo_old = jnp.where(jnp.logical_and(next_on, first), oe, oo_old)
    oo_old = jnp.where(jnp.logical_and(on, first), left(ee, 1), oo_old)
    return ee_old, eo_old, oe_old, oo_old


def move_columns(even, odd):
    lane = lanes_of(even)
    first, last = lane == 0, lane == even.shape[1] - 1
    even_new = jnp.where(first, even, right(jnp.where(first, odd, even), 1))
    odd_new = jnp.where(last, even, left(odd, 1))
    return even_new, odd_new


def in_pair(even, shifted=None):
    lane = line_lanes(even)
    if shifted is not None:
        half = even.shape[1] // 2
        lane = jnp.where(shifted, jnp.where(lane < half, lane + half, lane - half), lane)
    return (lane < 0, lane), (lane >= 0, lane)


def in_blocks(even):
    lane, half = line_lanes(even), even.shape[1] // 2
    place = jnp.where(lane < half, lane, lane - half)
    return (lane >= half, place), (lane >= half, place + half)


def in_order(even):
    lane, half = line_lanes(even), even.shape[1] // 2
    return (lane % 2 == 1, lane // 2), (lane % 2 == 1, lane // 2 + half)


def turn_to(layout, even, odd, angles):
    for cosine, sine in angles[:-1]:
        even, odd = cosine * even + sine * odd, cosine * odd - sine * even
        even, odd = move_columns(even, odd)
    by, end = JSTEPS - 1, even.shape[1] - 1
    results = []
    for is_odd, place in layout:
        stayed = place <= end - by
        from_even = jnp.where(stayed, place + by, 2 * end + 1 - by - place)
        from_even = jnp.where(place == 0, 0, from_even)
        source = jnp.where(is_odd, jnp.abs(place - by), from_even)
        is_even = jnp.logical_or(
            jnp.logical_and(is_odd, place < by),
            jnp.logical_and(jnp.logical_not(is_odd), stayed),
        )
        cosine, sine = (take_lanes(x, source) for x in angles[-1])
        by_even = jnp.where(is_even, cosine, -sine)
        by_odd = jnp.where(is_even, sine, cosine)
        results.append(by_even * take_lanes(even, source) + by_odd * take_lanes(odd, source))
    return results


def trim(bands, reach):
    rows = min(bands[0].shape[0], -(-(reach + 1) // 8) * 8)
    return [band[:rows] for band in bands]


def angles_of(bands):
    angles = []
    for step in range(JSTEPS):
        ee, eo, oe, oo = bands = trim(bands, 2 * (JSTEPS - 1 - step))
        angles.append(jacobi_angle(ee[0:1], oo[0:1], eo[0:1]))
        if step < JSTEPS - 1:
            bands = step_bands(*bands, *angles[-1])
    return angles


def carried(bands, angles):
    ahead = 2 * (JSTEPS - 1)
    for step, (cosine, sine) in enumerate(angles):
        bands = turn_bands(*trim(bands, 3 * ahead - 2 * step), cosine, sine)
        if step < JSTEPS - 1:
            bands = move_bands(*bands)
    for step in range(JSTEPS - 1):
        bands = move_bands_back(*trim(bands, 2 * (ahead - step)))
    return bands


def near_starts(width):
    half = width // 2
    reach = REACH - 1
    return (half - 2 * reach, width - WINDOW), (0, half - reach)


def cross_partial(x_even, x_odd, y_even, y_odd, x_second, y_second):
    rows, width = x_even.shape
    x_starts, y_starts = near_starts(width)
    lane = lanes_of(x_even)

    def window(even, odd, flag, starts):
        start = jnp.where(flag, starts[1], starts[0])
        at_zero = pltpu.roll(even, width - start, 1)
        at_next = pltpu.roll(odd, (width - start + WINDOW) % width, 1)
        return jnp.where(lane < WINDOW, at_zero, jnp.where(lane < 2 * WINDOW, at_next, 0.0))

    corner = lax.dot_general(
        window(y_even, y_odd, y_second, y_starts),
        window(x_even, x_odd, x_second, x_starts),
        (((0,), (0,)), ((), ())),
        precision=lax.Precision.HIGHEST,
        preferred_element_type=jnp.float32,
    )
    low = lax.broadcasted_iota(jnp.int32, (WINDOW, width), 1) < 2 * WINDOW
    return jnp.where(low, corner[:WINDOW], right(corner[WINDOW : 2 * WINDOW], 2 * WINDOW))


def own_rotation(angles, second, swapped, first_pair):
    width = angles[0][0].shape[1]
    half = width // 2
    x_starts, y_starts = near_starts(width)
    starts = [jnp.where(first_pair, x, y) for x, y in zip(x_starts, y_starts)]
    shape = (2 * WINDOW, width)
    row = lax.broadcasted_iota(jnp.int32, shape, 0)
    lane = lax.broadcasted_iota(jnp.int32, shape, 1) - jnp.where(second, starts[1], starts[0])
    even, odd = (
        jnp.where(jnp.logical_and(row == lane + at, row // WINDOW == at // WINDOW), 1.0, 0.0)
        for at in (0, WINDOW)
    )
    even, odd = turn_to(in_pair(even, swapped), even, odd, angles)
    low = lax.broadcasted_iota(jnp.int32, shape, 1) < half
    return jnp.where(jnp.logical_xor(low, first_pair), right(odd, half), even)


def cross_bands(packed, x_rotation, y_rotation):
    width = packed.shape[1]
    half = width // 2
    corner = jnp.concatenate((packed[:, :half], right(packed, half)[:, :half]), axis=0)
    highest = dict(precision=lax.Precision.HIGHEST, preferred_element_type=jnp.float32)
    turned_x = jnp.dot(corner, x_rotation, **highest)
    ends = lax.dot_general(turned_x, y_rotation, (((0,), (0,)), ((), ())), **highest)
    even, odd = ends[half - NEAR : half], ends[width - NEAR :]
    quadrants = (even, right(even, half), odd, right(odd, half))
    offset = lanes_of(even) - lax.broadcasted_iota(jnp.int32, even.shape, 0) - (half - NEAR)
    diag = lax.broadcasted_iota(jnp.int32, (DIAGS, width), 0)
    bands = [jnp.zeros((DIAGS, width), jnp.float32) for _ in quadrants]
    for d in range(1, REACH):
        here = offset == d
        for q, quadrant in enumerate(quadrants):
            line = jnp.sum(jnp.where(here, quadrant, 0.0), axis=0, keepdims=True)
            bands[q] = jnp.where(diag == d, line, bands[q])
    return bands


def either(flag, one, other):
    return jnp.logical_or(jnp.logical_and(flag, one), jnp.logical_and(jnp.logical_not(flag), other))


def halves_swapped(is_second):
    return among(is_second[0]), jnp.logical_not(among(is_second[1]))


def on_odd_core():
    return lax.axis_index("row") % 2 == 1


def far_starts(width):
    return REACH - 1, width // 2


def pack_far(bands, flag):
    width = bands[0].shape[1]
    half, count = width // 2, (FAR_DIAGS - DIAGS) // 2
    lane = line_lanes(bands[0])
    packed = []
    for band in bands:
        one, two = band[DIAGS : DIAGS + count], band[DIAGS + count :]
        one, two = (
            jnp.where(flag, left(x, far_starts(width)[1] - at), left(x, far_starts(width)[0] - at))
            for x, at in ((one, 0), (two, half))
        )
        packed.append(jnp.concatenate((band[:DIAGS], jnp.where(lane < half, one, two)), axis=0))
    return packed


def unpack_far(packed, flag):
    width = packed.shape[1]
    half = width // 2
    parts = [packed[:DIAGS]]
    for at in (0, half):
        starts = [start - at for start in far_starts(width)]
        x = packed[DIAGS:]
        parts.append(jnp.where(flag, right(x, starts[1]), right(x, starts[0])))
    return jnp.concatenate(parts, axis=0)


PACKED = DIAGS + (FAR_DIAGS - DIAGS) // 2


def store_part(even, odd, corner, flag, part_ref):
    bands = pack_far(dense_bands(even, odd, FAR_DIAGS), flag)
    for q, band in enumerate(bands):
        part_ref[q * PACKED : (q + 1) * PACKED, :] = band
    part_ref[4 * PACKED :, :] = corner


def open_pairs(is_second, x, y, column_refs, corner_ref, other_ref):
    x_second, y_second = among(is_second[0]), among(is_second[1])
    corner = cross_partial(*x, *y, x_second, y_second)
    flag = on_odd_core()
    mine = [jnp.where(flag, b, a) for a, b in zip(x, y)]
    theirs = [jnp.where(flag, a, b) for a, b in zip(x, y)]
    for ref, value in zip(column_refs, mine + theirs):
        ref[...] = value
    corner_ref[...] = jnp.where(flag, corner[NEAR:], corner[:NEAR])
    store_part(
        *theirs,
        jnp.where(flag, corner[:NEAR], corner[NEAR:]),
        either(flag, x_second, y_second),
        other_ref,
    )


def first_open(own_second, gets_second, is_second, even_ref, odd_ref, payload_ref, *refs):
    *column_refs, corner_ref, other_ref = refs
    own = even_ref[...], odd_ref[...]
    came = unpacked(payload_ref[...], own[0].shape[0], among(gets_second))
    flag = among(own_second)
    x = [jnp.where(flag, b, a) for a, b in zip(own, came)]
    y = [jnp.where(flag, a, b) for a, b in zip(own, came)]
    open_pairs(is_second, x, y, column_refs, corner_ref, other_ref)


def fused_open(picks, is_second, kept_ref, sent_ref, came0_ref, came1_ref, *refs):
    *column_refs, corner_ref, other_ref = refs
    arrays = [ref[...] for ref in (sent_ref, kept_ref, came0_ref, came1_ref)]
    blocks = [choose(pick, arrays) for pick in picks]
    x, y = split_pair(*blocks[:2]), split_pair(*blocks[2:])
    open_pairs(is_second, x, y, column_refs, corner_ref, other_ref)


def swapped_flag(is_second):
    x_swapped, y_swapped = halves_swapped(is_second)
    return either(on_odd_core(), y_swapped, x_swapped)


def own_second_flag(is_second):
    return either(on_odd_core(), among(is_second[1]), among(is_second[0]))


def bands_kernel(is_second, even_ref, odd_ref, corner_ref, part_ref):
    flag = own_second_flag(is_second)
    store_part(even_ref[...], odd_ref[...], corner_ref[...], flag, part_ref)


def angles_kernel(is_second, *refs):
    *part_refs, found_ref = refs
    part = pair_sums([ref[...] for ref in part_refs])
    flag = own_second_flag(is_second)
    quadrants = [unpack_far(part[q * PACKED : (q + 1) * PACKED], flag) for q in range(4)]
    angles = angles_of(quadrants)
    bands = carried(quadrants, angles)
    for step, pair in enumerate(angles):
        for i in (0, 1):
            found_ref[2 * step + i : 2 * step + i + 1, :] = pair[i]
    spare = NEAR - 2 * JSTEPS
    found_ref[2 * JSTEPS : NEAR, :] = jnp.zeros((spare, part.shape[1]), jnp.float32)
    for q in range(4):
        found_ref[NEAR + q * DIAGS : NEAR + (q + 1) * DIAGS, :] = bands[q][:DIAGS]
    found_ref[CORNER:ROTATION, :] = part[4 * PACKED :]
    first_pair = jnp.logical_not(on_odd_core())
    found_ref[ROTATION:, :] = own_rotation(angles, flag, swapped_flag(is_second), first_pair)


CORNER = NEAR + 4 * DIAGS
ROTATION = CORNER + NEAR
FOUND = ROTATION + 2 * WINDOW


def angles_in(found):
    return [(found[2 * i : 2 * i + 1], found[2 * i + 1 : 2 * i + 2]) for i in range(JSTEPS)]


def columns_kernel(is_second, even_ref, odd_ref, found_ref, *out_refs):
    angles = angles_in(found_ref[...])
    layout = in_pair(even_ref, swapped_flag(is_second))
    columns = turn_to(layout, even_ref[...], odd_ref[...], angles)
    for ref, value in zip(out_refs, columns):
        ref[...] = value


def next_bands(x_found, y_found, x_second, y_second):
    corner = jnp.concatenate((x_found[CORNER:ROTATION], y_found[CORNER:ROTATION]), axis=0)
    middle = cross_bands(corner, x_found[ROTATION:], y_found[ROTATION:])
    half = corner.shape[1] // 2
    lane = lanes_of(middle[0])
    diag = lax.broadcasted_iota(jnp.int32, middle[0].shape, 0)
    bands = []
    for q in range(4):
        rows = slice(NEAR + q * DIAGS, NEAR + (q + 1) * DIAGS)
        x, y = x_found[rows], y_found[rows]
        x = jnp.where(x_second, right(x, half), x)
        y = jnp.where(y_second, y, right(y, half))
        crossing = jnp.where(lane - diag < half, middle[q], y)
        bands.append(jnp.where(lane < half, x, crossing))
    return bands


def next_kernel(is_second, sends_first, layout_of, *refs):
    mine_even, mine_odd, even_ref, odd_ref, found_ref, other_ref, kept_ref, sent_ref = refs
    found, other = found_ref[...], other_ref[...]
    flag = on_odd_core()
    x_found, y_found = jnp.where(flag, other, found), jnp.where(flag, found, other)
    bands = next_bands(x_found, y_found, among(is_second[0]), among(is_second[1]))
    x_swapped, y_swapped = halves_swapped(is_second)
    swapped = either(flag, x_swapped, y_swapped)
    layout = in_pair(even_ref, swapped)
    theirs = turn_to(layout, even_ref[...], odd_ref[...], angles_in(other))
    low = line_lanes(found) < found.shape[1] // 2
    from_mine = jnp.logical_xor(low, flag)
    even = jnp.where(from_mine, mine_even[...], theirs[0])
    odd = jnp.where(from_mine, mine_odd[...], theirs[1])
    angles = angles_of(bands)
    first, second = turn_to(layout_of(even), even, odd, angles)
    flag = among(sends_first)
    kept_ref[...] = jnp.where(flag, second, first)
    sent_ref[...] = jnp.where(flag, first, second)


def pair_sums(arrays):
    while len(arrays) > 1:
        arrays = [arrays[i] + arrays[i + 1] for i in range(0, len(arrays), 2)]
    return arrays[0]


def swap(x, axis, mask):
    return lax.ppermute(x, axis, [(i, i ^ mask) for i in range(lax.axis_size(axis))])


def exchange_groups(x, axis, first_bit=0):
    count = lax.axis_size(axis).bit_length() - 1
    bits = [1 << b for b in range(count)]
    groups = [bits[:1]] + [bits[i : i + 2] for i in range(1, count, 2)]
    arrays = [x]
    for group in groups[first_bit:]:
        x = pair_sums(arrays)
        masks = [group[0]] if len(group) == 1 else [group[0], group[1], group[0] | group[1]]
        arrays = [x] + [swap(x, axis, mask) for mask in masks]
    return arrays


def call(kernel, shapes, *args):
    out = [jax.ShapeDtypeStruct(shape, jnp.float32) for shape in shapes]
    return pl.pallas_call(
        kernel,
        out_shape=out,
        compiler_params=pltpu.CompilerParams(vmem_limit_bytes=32 * 1024 * 1024),
    )(*args)


def two_rounds(opened, is_second, sends_first, layout_of):
    *columns, corner, other = opened
    column, width = columns[0].shape, columns[0].shape[1]
    other = swap(other, "row", 1)
    bands = functools.partial(bands_kernel, is_second)
    (mine,) = call(bands, (other.shape,), *columns[:2], corner)
    (found,) = call(
        functools.partial(angles_kernel, is_second),
        ((FOUND, width),),
        *exchange_groups(mine + other, "row", 1),
    )
    other = swap(found, "row", 1)
    turn = functools.partial(columns_kernel, is_second)
    columns[:2] = call(turn, (column, column), *columns[:2], found)
    turn = functools.partial(next_kernel, is_second, sends_first, layout_of)
    return call(turn, (column, column), *columns, found, other)


def per_device(basis):
    rows, cols = basis.shape
    width = cols // 2
    pair_total = lax.axis_size("pair")
    column = (rows, width)
    opened = (column,) * 4 + ((NEAR, width), (4 * PACKED + NEAR, width))
    payload = (rows + rows * 2 * STRIP // width, width)

    sends, sends_second, gets_second, own_second, is_second = first_moves(pair_total)
    opening = functools.partial(open_kernel, sends_second)
    even, odd, sent = call(opening, (column, column, payload), basis)
    came = lax.ppermute(sent, "pair", sends)
    opening = functools.partial(first_open, own_second, gets_second, is_second)
    arrays = call(opening, opened, even, odd, came)
    sends, sends_first, picks, next_second = fused_moves(pair_total)
    kept, sent = two_rounds(arrays, is_second, sends_first, in_blocks)

    came = [lax.ppermute(x, "pair", s) for x, s in zip((sent, kept), sends)]
    opening = functools.partial(fused_open, picks, next_second)
    arrays = call(opening, opened, kept, sent, *came)
    sends, sends_first, gets_first = last_moves(pair_total)
    kept, sent = two_rounds(arrays, next_second, sends_first, in_order)

    came = lax.ppermute(sent, "pair", sends)
    flag = among(gets_first)
    first = jnp.where(flag, came, kept)
    second = jnp.where(flag, kept, came)
    return jnp.concatenate((first, second), axis=1)


def solution(mesh):
    return jax.shard_map(
        per_device,
        mesh=mesh,
        in_specs=(P("row", "pair"),),
        out_specs=P("row", "pair"),
        check_vma=False,
    )
```

```python
import functools

import jax
import jax.numpy as jnp
import numpy as np
from jax import lax
from jax.experimental import pallas as pl
from jax.experimental.pallas import tpu as pltpu
from jax.sharding import PartitionSpec as P

ROUNDS = 4
JSTEPS = 6
REACH = 2 * (JSTEPS - 1) + 1
DIAGS = 16
FAR_DIAGS = 32
WINDOW = 32
NEAR = 16
STRIP = 16
BACK = 3


def tournament_order(pair_count):
    ordering = np.zeros(2 * pair_count, dtype=np.int64)
    ordering[0] = 0
    ordering[2] = 1
    for slot in range(2, pair_count):
        ordering[2 * slot] = 2 * (slot - 1)
    for slot in range(pair_count - 1):
        ordering[2 * slot + 1] = 2 * (slot + 1) + 1
    ordering[2 * pair_count - 1] = 2 * (pair_count - 1)
    return ordering


def host_of(pair, pair_total, round_index):
    if round_index % 2 == 0 or pair == 0:
        return pair
    return min(pair + 1, pair_total - 1) if pair % 2 else pair - 1


def last_moves(pair_total):
    ordering = tournament_order(pair_total)
    sends, sends_first, gets_first = [], set(), set()
    for pair in range(pair_total):
        target = host_of(pair, pair_total, ROUNDS)
        for place in (0, 1):
            old = int(ordering[2 * pair + place])
            source = host_of(old // 2, pair_total, ROUNDS - 1)
            if source == target:
                continue
            sends.append((source, target))
            if old % 2 == 0:
                sends_first.add(source)
            if place == 0:
                gets_first.add(target)
    assert len({s for s, _ in sends}) == len(sends) == len({t for _, t in sends})
    return sends, sends_first, gets_first


def first_moves(pair_total):
    ordering = tournament_order(pair_total)
    sends, sends_second, gets_second, own_second = [], set(), set(), set()
    seconds = (set(), set())
    for pair in range(pair_total):
        here = host_of(pair, pair_total, 1)
        for place in (0, 1):
            old = int(ordering[2 * pair + place])
            if old % 2:
                seconds[place].add(here)
            if old // 2 == here:
                if place:
                    own_second.add(here)
                continue
            sends.append((old // 2, here))
            if old % 2:
                sends_second.add(old // 2)
                gets_second.add(here)
    assert len({s for s, _ in sends}) == len(sends) == len({t for _, t in sends})
    return sends, sends_second, gets_second, own_second, seconds


def fused_moves(pair_total):
    ordering = tournament_order(pair_total)
    before, last = ROUNDS - 3, ROUNDS - 1
    needs, edges, seconds = {}, [], ({}, {})
    for pair in range(pair_total):
        here = host_of(pair, pair_total, last)
        needs[here] = []
        for place in (0, 1):
            source = int(ordering[2 * pair + place])
            seconds[place][here] = source % 2
            for half in (0, 1):
                old = int(ordering[2 * (source // 2) + half])
                there = host_of(old // 2, pair_total, before)
                needs[here].append((there, old % 2))
                if there != here:
                    edges.append((there, old % 2, here))
    turn, left_over = {}, list(edges)
    while left_over:
        source, _, target = left_over[0]
        start = source
        while True:
            for number, one, other in ((0, source, target), (1, target, source)):
                edge = next(e for e in left_over if (e[0], e[2]) == (one, other))
                turn[edge] = number
                left_over.remove(edge)
            if target == start:
                break
            ahead = [e[2] for e in left_over if e[0] == target]
            source, target = target, ahead[0]
    sends = [[(e[0], e[2]) for e in edges if turn[e] == i] for i in (0, 1)]
    for chosen in sends:
        assert len({a for a, _ in chosen}) == len({b for _, b in chosen}) == pair_total
    sends_first = {e[0] for e in edges if turn[e] == 0 and e[1] == 0}
    picks = []
    for slot in range(4):
        pick = {}
        for here in range(pair_total):
            there, half = needs[here][slot]
            if there == here:
                pick[here] = 0 if (half == 0) == (here in sends_first) else 1
            else:
                pick[here] = 2 + turn[(there, half, here)]
        picks.append(pick)
    is_second = [{h for h, place in table.items() if place} for table in seconds]
    return sends, sends_first, picks, is_second


def choose(pick, arrays):
    chosen = arrays[0]
    for number in range(1, len(arrays)):
        members = {here for here, value in pick.items() if value == number}
        if members:
            chosen = jnp.where(among(members), arrays[number], chosen)
    return chosen


def among(members):
    here = lax.axis_index("pair")
    return functools.reduce(
        jnp.logical_or, [here == member for member in sorted(members)], here < 0
    )


def left(x, by):
    width = x.shape[1]
    return pltpu.roll(x, (width - by) % width, 1) if by % width else x


def right(x, by):
    width = x.shape[1]
    return pltpu.roll(x, by % width, 1) if by % width else x


def down(x, by):
    return pltpu.roll(x, by % x.shape[0], 0)


def lanes_of(x):
    return lax.broadcasted_iota(jnp.int32, x.shape, 1)


def split_pair(first, second):
    half = first.shape[1] // 2
    low = lanes_of(first) < half
    even = jnp.where(low, first, right(second, half))
    odd = jnp.where(low, right(first, half), second)
    return even, odd


def take_lanes(x, source):
    if x.shape[0] == 1:
        return take_lanes(jnp.broadcast_to(x, (8, x.shape[1])), source)[:1]
    return jnp.take_along_axis(x, jnp.broadcast_to(source, x.shape), axis=1)


def line_lanes(x):
    return lax.broadcasted_iota(jnp.int32, (1, x.shape[1]), 1)


def separate(first, second):
    lane = line_lanes(first)
    half = first.shape[1] // 2
    low = lane < half
    source = 2 * jnp.where(low, lane, lane - half)
    return tuple(
        jnp.where(low, take_lanes(first, source + odd), take_lanes(second, source + odd))
        for odd in (0, 1)
    )


def backwards(x):
    return jnp.take_along_axis(x, x.shape[1] - 1 - lanes_of(x), axis=1)


def dense_bands(even, odd, diags):
    width = even.shape[1]
    gram = lax.dot_general(
        jnp.concatenate((even, odd), axis=1),
        jnp.concatenate((backwards(even), backwards(odd)), axis=1),
        (((0,), (0,)), ((), ())),
        precision=lax.Precision.HIGHEST,
        preferred_element_type=jnp.float32,
    )
    bands = []
    for near in (0, width):
        for far in (0, width):
            quadrant = gram[far : far + width, near : near + width]
            aligned = pltpu.roll(quadrant, 1, 1, stride=1, stride_axis=0)
            bands.append(jnp.transpose(aligned)[:diags])
    return bands


def store_bands(even, odd, band_ref, diags):
    for q, band in enumerate(dense_bands(even, odd, diags)):
        band_ref[q * diags : (q + 1) * diags, :] = band


def open_kernel(sends_second, basis_ref, even_ref, odd_ref, payload_ref):
    rows, cols = basis_ref.shape
    width = cols // 2
    half = width // 2
    even, odd = separate(basis_ref[:, :width], basis_ref[:, width:])
    even_ref[...] = even
    odd_ref[...] = odd
    flag = among(sends_second)
    even, odd = (jnp.where(flag, left(x, half - STRIP), x) for x in (even, odd))
    payload_ref[:rows] = jnp.where(line_lanes(even) < half, even, right(odd, half))
    group = rows * 2 * STRIP // width
    strips = jnp.zeros((group, width), jnp.float32)
    for i in range(rows // group):
        for j, x in enumerate((even, odd)):
            start = (2 * i + j) * STRIP
            lane = line_lanes(x)
            here = jnp.logical_and(lane >= start, lane < start + STRIP)
            strips = jnp.where(here, left(x[i * group : (i + 1) * group], half - start), strips)
    payload_ref[rows:] = strips


def unpacked(payload, rows, second):
    width = payload.shape[1]
    half = width // 2
    lane = line_lanes(payload)
    main, strips = payload[:rows], payload[rows:]
    group = strips.shape[0]
    columns = []
    for j, x in enumerate((main, left(main, half))):
        ends = [right(strips, half - (2 * i + j) * STRIP) for i in range(rows // group)]
        x = jnp.where(lane < half, x, jnp.where(lane < half + STRIP, jnp.concatenate(ends), 0.0))
        columns.append(jnp.where(second, right(x, half - STRIP), x))
    return columns


def jacobi_angle(diag_even, diag_odd, coupling):
    spread = diag_even - diag_odd
    square = spread * spread + 4.0 * coupling * coupling
    inverse = lax.rsqrt(square)
    larger_square = (square * inverse + jnp.abs(spread)) * (0.5 * inverse)
    larger_inverse = lax.rsqrt(larger_square)
    larger = larger_square * larger_inverse
    smaller = coupling * inverse * larger_inverse
    forward = spread >= 0.0
    sign = jnp.where(coupling > 0.0, 1.0, jnp.where(coupling < 0.0, -1.0, 0.0))
    cosine = jnp.where(forward, larger, jnp.abs(smaller))
    sine_part = jnp.where(forward, smaller, sign * larger)
    return cosine, sine_part


def turn_bands(ee, eo, oe, oo, cosine, sine):
    cl, sl = jnp.broadcast_to(cosine, ee.shape), jnp.broadcast_to(sine, ee.shape)
    ck = pltpu.roll(cl, 0, 1, stride=1, stride_axis=0)
    sk = pltpu.roll(sl, 0, 1, stride=1, stride_axis=0)
    ee, oe = ck * ee + sk * oe, ck * oe - sk * ee
    eo, oo = ck * eo + sk * oo, ck * oo - sk * eo
    ee, eo = cl * ee + sl * eo, cl * eo - sl * ee
    oe, oo = cl * oe + sl * oo, cl * oo - sl * oe
    return ee, eo, oe, oo


def step_bands(ee, eo, oe, oo, cosine, sine):
    lane = lanes_of(ee)
    diag = lax.broadcasted_iota(jnp.int32, ee.shape, 0)
    last = lane == ee.shape[1] - 1
    on, next_on = diag == 0, diag == 1

    def slanted(x, by):
        if by >= 0:
            return pltpu.roll(x, by, 1, stride=1, stride_axis=0)
        return jnp.where(on, left(x, -by), down(slanted(x, 0), -by))

    def rotated(by, wanted):
        cl, sl = (jnp.broadcast_to(x, ee.shape) for x in (cosine, sine))
        ck, sk = (slanted(x, by) for x in (cl, sl))
        cl, sl, a, b, c, d = (right(x, by) for x in (cl, sl, ee, eo, oe, oo))
        a, c = ck * a + sk * c, ck * c - sk * a
        b, d = ck * b + sk * d, ck * d - sk * b
        found = {"ee": (a, b), "eo": (b, a), "oe": (c, d), "oo": (d, c)}
        return [
            cl * one + sl * two if name in ("ee", "oe") else cl * one - sl * two
            for name, (one, two) in found.items()
            if name in wanted
        ]

    ee_0, eo_0, oe_0, oo_0 = rotated(0, ("ee", "eo", "oe", "oo"))
    ee_r, eo_r, oe_r, oo_r = rotated(1, ("ee", "eo", "oe", "oo"))
    eo_l, oo_l = rotated(-1, ("eo", "oo"))

    near = down(jnp.where(on, eo_r, ee_r), 1)
    turned = jnp.where(on, oo_r, oe_r)
    ee_new = jnp.where(lane == diag + 1, turned, jnp.where(lane == diag, near, ee_r))
    ee_new = jnp.where(jnp.logical_and(on, lane == 0), ee_0, ee_new)

    eo_new = down(jnp.where(lane == diag - 1, oo_l, eo_l), -2)
    eo_new = jnp.where(lane == diag, down(eo_l, -1), eo_new)
    eo_new = jnp.where(last, down(ee_0, -1), eo_new)

    oo_new = jnp.where(last, jnp.where(on, ee_0, down(oe_0, 1)), oo_l)

    oe_new = down(oe_r, 2)
    oe_new = jnp.where(next_on, jnp.where(lane == diag, oo_0, eo_0), oe_new)
    oe_new = jnp.where(on, eo_new, oe_new)
    return ee_new, eo_new, oe_new, oo_new


def move_bands(ee, eo, oe, oo):
    lane = lanes_of(ee)
    diag = lax.broadcasted_iota(jnp.int32, ee.shape, 0)
    last = lane == ee.shape[1] - 1
    on, next_on = diag == 0, diag == 1

    near = down(jnp.where(on, eo, ee), 1)
    turned = jnp.where(on, oo, oe)
    mixed = jnp.where(lane == diag, turned, jnp.where(lane == diag - 1, near, ee))
    ee_new = jnp.where(jnp.logical_and(on, lane == 0), ee, right(mixed, 1))

    far = down(jnp.where(last, ee, eo), -1)
    mixed = down(jnp.where(lane == diag, oo, eo), -2)
    mixed = left(jnp.where(lane == diag + 1, far, mixed), 1)
    eo_new = jnp.where(last, far, mixed)

    oo_new = jnp.where(last, jnp.where(on, ee, down(oe, 1)), left(oo, 1))

    oe_new = right(down(oe, 2), 1)
    oe_new = jnp.where(next_on, jnp.where(lane == diag, oo, eo), oe_new)
    oe_new = jnp.where(on, eo_new, oe_new)
    return ee_new, eo_new, oe_new, oo_new


def move_bands_back(views, by):
    ee, eo, oe, oo = views[by]
    ee_left, _, oe_left, _ = views[by - 1]
    _, eo_right, _, oo_right = views[by + 1]
    width = ee.shape[1]
    lane = lanes_of(ee) - by
    lane = jnp.where(lane < 0, lane + width, jnp.where(lane >= width, lane - width, lane))
    diag = lax.broadcasted_iota(jnp.int32, ee.shape, 0)
    last, first = lane == width - 1, lane == diag
    on, next_on = diag == 0, diag == 1
    oo_up, eo_twice = down(oo, -1), down(eo_right, 2)

    far = jnp.where(first, down(ee_left, -1), ee_left)
    ee_old = jnp.where(jnp.logical_and(first, on), ee, far)
    ee_old = jnp.where(last, jnp.where(on, oo, down(eo, 1)), ee_old)

    near = jnp.where(jnp.logical_and(first, diag > 0), ee_left, down(oe_left, -2))
    eo_old = jnp.where(first, down(eo_right, 1), eo_twice)
    eo_old = jnp.where(on, jnp.where(last, oo_up, near), eo_old)
    eo_old = jnp.where(jnp.logical_and(next_on, lane > 1), oe, eo_old)
    eo_old = jnp.where(jnp.logical_and(on, first), far, eo_old)

    oe_old = jnp.where(on, eo_old, jnp.where(last, oo_up, near))

    oo_old = jnp.where(first, eo_twice, oo_right)
    oo_old = jnp.where(jnp.logical_and(next_on, first), oe, oo_old)
    oo_old = jnp.where(jnp.logical_and(on, first), ee_left, oo_old)
    return ee_old, eo_old, oe_old, oo_old


def bands_back(bands, count):
    views = {by: [right(x, by) for x in bands] for by in range(-count, count + 1)}
    for reach in reversed(range(count)):
        views = {by: move_bands_back(views, by) for by in range(-reach, reach + 1)}
    return views[0]


def move_columns(even, odd):
    lane = lanes_of(even)
    first, last = lane == 0, lane == even.shape[1] - 1
    even_new = jnp.where(first, even, right(jnp.where(first, odd, even), 1))
    odd_new = jnp.where(last, even, left(odd, 1))
    return even_new, odd_new


def in_pair(even, shifted=None):
    lane = line_lanes(even)
    if shifted is not None:
        half = even.shape[1] // 2
        lane = jnp.where(shifted, jnp.where(lane < half, lane + half, lane - half), lane)
    return (lane < 0, lane), (lane >= 0, lane)


def in_blocks(even):
    lane, half = line_lanes(even), even.shape[1] // 2
    place = jnp.where(lane < half, lane, lane - half)
    return (lane >= half, place), (lane >= half, place + half)


def in_order(even):
    lane, half = line_lanes(even), even.shape[1] // 2
    return (lane % 2 == 1, lane // 2), (lane % 2 == 1, lane // 2 + half)


def turn_to(layout, even, odd, angles):
    for cosine, sine in angles[:-1]:
        even, odd = cosine * even + sine * odd, cosine * odd - sine * even
        even, odd = move_columns(even, odd)
    by, end = JSTEPS - 1, even.shape[1] - 1
    results = []
    for is_odd, place in layout:
        stayed = place <= end - by
        from_even = jnp.where(stayed, place + by, 2 * end + 1 - by - place)
        from_even = jnp.where(place == 0, 0, from_even)
        source = jnp.where(is_odd, jnp.abs(place - by), from_even)
        is_even = jnp.logical_or(
            jnp.logical_and(is_odd, place < by),
            jnp.logical_and(jnp.logical_not(is_odd), stayed),
        )
        cosine, sine = (take_lanes(x, source) for x in angles[-1])
        by_even = jnp.where(is_even, cosine, -sine)
        by_odd = jnp.where(is_even, sine, cosine)
        results.append(by_even * take_lanes(even, source) + by_odd * take_lanes(odd, source))
    return results


def trim(bands, reach):
    rows = min(bands[0].shape[0], -(-(reach + 1) // 8) * 8)
    return [band[:rows] for band in bands]


def angles_of(bands):
    angles = []
    for step in range(JSTEPS):
        ee, eo, oe, oo = bands = trim(bands, 2 * (JSTEPS - 1 - step))
        angles.append(jacobi_angle(ee[0:1], oo[0:1], eo[0:1]))
        if step < JSTEPS - 1:
            bands = step_bands(*bands, *angles[-1])
    return angles


def carried(bands, angles):
    ahead = 2 * (JSTEPS - 1)
    for step, (cosine, sine) in enumerate(angles):
        bands = turn_bands(*trim(bands, 3 * ahead - 2 * step), cosine, sine)
        if step < JSTEPS - 1:
            bands = move_bands(*bands)
    done = 0
    while done < JSTEPS - 1:
        count = min(BACK, JSTEPS - 1 - done)
        bands = bands_back(trim(bands, 2 * (ahead - done)), count)
        done += count
    return bands


def near_starts(width):
    half = width // 2
    reach = REACH - 1
    return (half - 2 * reach, width - WINDOW), (0, half - reach)


def cross_partial(x_even, x_odd, y_even, y_odd, x_second, y_second):
    rows, width = x_even.shape
    x_starts, y_starts = near_starts(width)
    lane = lanes_of(x_even)

    def window(even, odd, flag, starts):
        start = jnp.where(flag, starts[1], starts[0])
        at_zero = pltpu.roll(even, width - start, 1)
        at_next = pltpu.roll(odd, (width - start + WINDOW) % width, 1)
        return jnp.where(lane < WINDOW, at_zero, jnp.where(lane < 2 * WINDOW, at_next, 0.0))

    corner = lax.dot_general(
        window(y_even, y_odd, y_second, y_starts),
        window(x_even, x_odd, x_second, x_starts),
        (((0,), (0,)), ((), ())),
        precision=lax.Precision.HIGHEST,
        preferred_element_type=jnp.float32,
    )
    low = lax.broadcasted_iota(jnp.int32, (WINDOW, width), 1) < 2 * WINDOW
    return jnp.where(low, corner[:WINDOW], right(corner[WINDOW : 2 * WINDOW], 2 * WINDOW))


def own_rotation(angles, second, swapped, first_pair):
    width = angles[0][0].shape[1]
    half = width // 2
    x_starts, y_starts = near_starts(width)
    starts = [jnp.where(first_pair, x, y) for x, y in zip(x_starts, y_starts)]
    shape = (2 * WINDOW, width)
    row = lax.broadcasted_iota(jnp.int32, shape, 0)
    lane = lax.broadcasted_iota(jnp.int32, shape, 1) - jnp.where(second, starts[1], starts[0])
    even, odd = (
        jnp.where(jnp.logical_and(row == lane + at, row // WINDOW == at // WINDOW), 1.0, 0.0)
        for at in (0, WINDOW)
    )
    even, odd = turn_to(in_pair(even, swapped), even, odd, angles)
    low = lax.broadcasted_iota(jnp.int32, shape, 1) < half
    return jnp.where(jnp.logical_xor(low, first_pair), right(odd, half), even)


def cross_bands(packed, x_rotation, y_rotation):
    width = packed.shape[1]
    half = width // 2
    corner = jnp.concatenate((packed[:, :half], right(packed, half)[:, :half]), axis=0)
    highest = dict(precision=lax.Precision.HIGHEST, preferred_element_type=jnp.float32)
    turned_x = jnp.dot(corner, x_rotation, **highest)
    ends = lax.dot_general(turned_x, y_rotation, (((0,), (0,)), ((), ())), **highest)
    even, odd = ends[half - NEAR : half], ends[width - NEAR :]
    quadrants = (even, right(even, half), odd, right(odd, half))
    offset = lanes_of(even) - lax.broadcasted_iota(jnp.int32, even.shape, 0) - (half - NEAR)
    diag = lax.broadcasted_iota(jnp.int32, (DIAGS, width), 0)
    bands = [jnp.zeros((DIAGS, width), jnp.float32) for _ in quadrants]
    for d in range(1, REACH):
        here = offset == d
        for q, quadrant in enumerate(quadrants):
            line = jnp.sum(jnp.where(here, quadrant, 0.0), axis=0, keepdims=True)
            bands[q] = jnp.where(diag == d, line, bands[q])
    return bands


def either(flag, one, other):
    return jnp.logical_or(jnp.logical_and(flag, one), jnp.logical_and(jnp.logical_not(flag), other))


def halves_swapped(is_second):
    return among(is_second[0]), jnp.logical_not(among(is_second[1]))


def on_odd_core():
    return lax.axis_index("row") % 2 == 1


def far_starts(width):
    return REACH - 1, width // 2


def pack_far(bands, flag):
    width = bands[0].shape[1]
    half, count = width // 2, (FAR_DIAGS - DIAGS) // 2
    lane = line_lanes(bands[0])
    packed = []
    for band in bands:
        one, two = band[DIAGS : DIAGS + count], band[DIAGS + count :]
        one, two = (
            jnp.where(flag, left(x, far_starts(width)[1] - at), left(x, far_starts(width)[0] - at))
            for x, at in ((one, 0), (two, half))
        )
        packed.append(jnp.concatenate((band[:DIAGS], jnp.where(lane < half, one, two)), axis=0))
    return packed


def unpack_far(packed, flag):
    width = packed.shape[1]
    half = width // 2
    parts = [packed[:DIAGS]]
    for at in (0, half):
        starts = [start - at for start in far_starts(width)]
        x = packed[DIAGS:]
        parts.append(jnp.where(flag, right(x, starts[1]), right(x, starts[0])))
    return jnp.concatenate(parts, axis=0)


PACKED = DIAGS + (FAR_DIAGS - DIAGS) // 2


def store_part(even, odd, flag, part_ref):
    bands = pack_far(dense_bands(even, odd, FAR_DIAGS), flag)
    for q, band in enumerate(bands):
        part_ref[q * PACKED : (q + 1) * PACKED, :] = band


def open_pairs(is_second, x, y, column_refs, other_ref):
    flag = on_odd_core()
    mine = [jnp.where(flag, b, a) for a, b in zip(x, y)]
    theirs = [jnp.where(flag, a, b) for a, b in zip(x, y)]
    for ref, value in zip(column_refs, mine + theirs):
        ref[...] = value
    store_part(*theirs, either(flag, among(is_second[0]), among(is_second[1])), other_ref)
    other_ref[4 * PACKED :, :] = jnp.zeros((WINDOW, theirs[0].shape[1]), jnp.float32)


def first_open(own_second, gets_second, is_second, even_ref, odd_ref, payload_ref, *refs):
    *column_refs, other_ref = refs
    own = even_ref[...], odd_ref[...]
    came = unpacked(payload_ref[...], own[0].shape[0], among(gets_second))
    flag = among(own_second)
    x = [jnp.where(flag, b, a) for a, b in zip(own, came)]
    y = [jnp.where(flag, a, b) for a, b in zip(own, came)]
    open_pairs(is_second, x, y, column_refs, other_ref)


def fused_open(picks, is_second, kept_ref, sent_ref, came0_ref, came1_ref, *refs):
    *column_refs, other_ref = refs
    arrays = [ref[...] for ref in (sent_ref, kept_ref, came0_ref, came1_ref)]
    blocks = [choose(pick, arrays) for pick in picks]
    x, y = split_pair(*blocks[:2]), split_pair(*blocks[2:])
    open_pairs(is_second, x, y, column_refs, other_ref)


def swapped_flag(is_second):
    x_swapped, y_swapped = halves_swapped(is_second)
    return either(on_odd_core(), y_swapped, x_swapped)


def own_second_flag(is_second):
    return either(on_odd_core(), among(is_second[1]), among(is_second[0]))


def bands_kernel(is_second, *refs):
    *column_refs, part_ref = refs
    columns = [ref[...] for ref in column_refs]
    store_part(*columns[:2], own_second_flag(is_second), part_ref)
    flag = on_odd_core()
    x = [jnp.where(flag, b, a) for a, b in zip(columns[:2], columns[2:])]
    y = [jnp.where(flag, a, b) for a, b in zip(columns[:2], columns[2:])]
    corner = cross_partial(*x, *y, among(is_second[0]), among(is_second[1]))
    part_ref[4 * PACKED :, :] = corner


def angles_kernel(is_second, *refs):
    *part_refs, found_ref = refs
    part = pair_sums([ref[...] for ref in part_refs])
    flag = own_second_flag(is_second)
    quadrants = [unpack_far(part[q * PACKED : (q + 1) * PACKED], flag) for q in range(4)]
    angles = angles_of(quadrants)
    bands = carried(quadrants, angles)
    for step, pair in enumerate(angles):
        for i in (0, 1):
            found_ref[2 * step + i : 2 * step + i + 1, :] = pair[i]
    spare = NEAR - 2 * JSTEPS
    found_ref[2 * JSTEPS : NEAR, :] = jnp.zeros((spare, part.shape[1]), jnp.float32)
    for q in range(4):
        found_ref[NEAR + q * DIAGS : NEAR + (q + 1) * DIAGS, :] = bands[q][:DIAGS]
    found_ref[CORNER:ROTATION, :] = part[4 * PACKED :]
    first_pair = jnp.logical_not(on_odd_core())
    found_ref[ROTATION:, :] = own_rotation(angles, flag, swapped_flag(is_second), first_pair)


CORNER = NEAR + 4 * DIAGS
ROTATION = CORNER + WINDOW
FOUND = ROTATION + 2 * WINDOW


def angles_in(found):
    return [(found[2 * i : 2 * i + 1], found[2 * i + 1 : 2 * i + 2]) for i in range(JSTEPS)]


def columns_kernel(is_second, even_ref, odd_ref, found_ref, *out_refs):
    angles = angles_in(found_ref[...])
    layout = in_pair(even_ref, swapped_flag(is_second))
    columns = turn_to(layout, even_ref[...], odd_ref[...], angles)
    for ref, value in zip(out_refs, columns):
        ref[...] = value


def next_bands(x_found, y_found, x_second, y_second):
    corner = x_found[CORNER:ROTATION] + y_found[CORNER:ROTATION]
    middle = cross_bands(corner, x_found[ROTATION:], y_found[ROTATION:])
    half = corner.shape[1] // 2
    lane = lanes_of(middle[0])
    diag = lax.broadcasted_iota(jnp.int32, middle[0].shape, 0)
    bands = []
    for q in range(4):
        rows = slice(NEAR + q * DIAGS, NEAR + (q + 1) * DIAGS)
        x, y = x_found[rows], y_found[rows]
        x = jnp.where(x_second, right(x, half), x)
        y = jnp.where(y_second, y, right(y, half))
        crossing = jnp.where(lane - diag < half, middle[q], y)
        bands.append(jnp.where(lane < half, x, crossing))
    return bands


def next_kernel(is_second, sends_first, layout_of, *refs):
    mine_even, mine_odd, even_ref, odd_ref, found_ref, other_ref, kept_ref, sent_ref = refs
    found, other = found_ref[...], other_ref[...]
    flag = on_odd_core()
    x_found, y_found = jnp.where(flag, other, found), jnp.where(flag, found, other)
    bands = next_bands(x_found, y_found, among(is_second[0]), among(is_second[1]))
    x_swapped, y_swapped = halves_swapped(is_second)
    swapped = either(flag, x_swapped, y_swapped)
    layout = in_pair(even_ref, swapped)
    theirs = turn_to(layout, even_ref[...], odd_ref[...], angles_in(other))
    low = line_lanes(found) < found.shape[1] // 2
    from_mine = jnp.logical_xor(low, flag)
    even = jnp.where(from_mine, mine_even[...], theirs[0])
    odd = jnp.where(from_mine, mine_odd[...], theirs[1])
    angles = angles_of(bands)
    first, second = turn_to(layout_of(even), even, odd, angles)
    flag = among(sends_first)
    kept_ref[...] = jnp.where(flag, second, first)
    sent_ref[...] = jnp.where(flag, first, second)


def pair_sums(arrays):
    while len(arrays) > 1:
        arrays = [arrays[i] + arrays[i + 1] for i in range(0, len(arrays), 2)]
    return arrays[0]


def swap(x, axis, mask):
    return lax.ppermute(x, axis, [(i, i ^ mask) for i in range(lax.axis_size(axis))])


def exchange_groups(x, axis, first_bit=0):
    count = lax.axis_size(axis).bit_length() - 1
    bits = [1 << b for b in range(count)]
    groups = [bits[:1]] + [bits[i : i + 2] for i in range(1, count, 2)]
    arrays = [x]
    for group in groups[first_bit:]:
        x = pair_sums(arrays)
        masks = [group[0]] if len(group) == 1 else [group[0], group[1], group[0] | group[1]]
        arrays = [x] + [swap(x, axis, mask) for mask in masks]
    return arrays


def call(kernel, shapes, *args):
    out = [jax.ShapeDtypeStruct(shape, jnp.float32) for shape in shapes]
    return pl.pallas_call(
        kernel,
        out_shape=out,
        compiler_params=pltpu.CompilerParams(vmem_limit_bytes=32 * 1024 * 1024),
    )(*args)


def two_rounds(opened, is_second, sends_first, layout_of):
    *columns, other = opened
    column, width = columns[0].shape, columns[0].shape[1]
    other = swap(other, "row", 1)
    bands = functools.partial(bands_kernel, is_second)
    (mine,) = call(bands, (other.shape,), *columns)
    (found,) = call(
        functools.partial(angles_kernel, is_second),
        ((FOUND, width),),
        *exchange_groups(mine + other, "row", 1),
    )
    other = swap(found, "row", 1)
    turn = functools.partial(columns_kernel, is_second)
    columns[:2] = call(turn, (column, column), *columns[:2], found)
    turn = functools.partial(next_kernel, is_second, sends_first, layout_of)
    return call(turn, (column, column), *columns, found, other)


def per_device(basis):
    rows, cols = basis.shape
    width = cols // 2
    pair_total = lax.axis_size("pair")
    column = (rows, width)
    opened = (column,) * 4 + ((4 * PACKED + WINDOW, width),)
    payload = (rows + rows * 2 * STRIP // width, width)

    sends, sends_second, gets_second, own_second, is_second = first_moves(pair_total)
    opening = functools.partial(open_kernel, sends_second)
    even, odd, sent = call(opening, (column, column, payload), basis)
    came = lax.ppermute(sent, "pair", sends)
    opening = functools.partial(first_open, own_second, gets_second, is_second)
    arrays = call(opening, opened, even, odd, came)
    sends, sends_first, picks, next_second = fused_moves(pair_total)
    kept, sent = two_rounds(arrays, is_second, sends_first, in_blocks)

    came = [lax.ppermute(x, "pair", s) for x, s in zip((sent, kept), sends)]
    opening = functools.partial(fused_open, picks, next_second)
    arrays = call(opening, opened, kept, sent, *came)
    sends, sends_first, gets_first = last_moves(pair_total)
    kept, sent = two_rounds(arrays, next_second, sends_first, in_order)

    came = lax.ppermute(sent, "pair", sends)
    flag = among(gets_first)
    first = jnp.where(flag, came, kept)
    second = jnp.where(flag, kept, came)
    return jnp.concatenate((first, second), axis=1)


def solution(mesh):
    return jax.shard_map(
        per_device,
        mesh=mesh,
        in_specs=(P("row", "pair"),),
        out_specs=P("row", "pair"),
        check_vma=False,
    )
```

```python
import functools

import jax
import jax.numpy as jnp
import numpy as np
from jax import lax
from jax.experimental import pallas as pl
from jax.experimental.pallas import tpu as pltpu
from jax.sharding import PartitionSpec as P

ROUNDS = 4
JSTEPS = 6
REACH = 2 * (JSTEPS - 1) + 1
DIAGS = 16
FAR_DIAGS = 32
WINDOW = 32
NEAR = 16
STRIP = 16
BACK = 3


def tournament_order(pair_count):
    ordering = np.zeros(2 * pair_count, dtype=np.int64)
    ordering[0] = 0
    ordering[2] = 1
    for slot in range(2, pair_count):
        ordering[2 * slot] = 2 * (slot - 1)
    for slot in range(pair_count - 1):
        ordering[2 * slot + 1] = 2 * (slot + 1) + 1
    ordering[2 * pair_count - 1] = 2 * (pair_count - 1)
    return ordering


def host_of(pair, pair_total, round_index):
    if round_index % 2 == 0 or pair == 0:
        return pair
    return min(pair + 1, pair_total - 1) if pair % 2 else pair - 1


def last_moves(pair_total):
    ordering = tournament_order(pair_total)
    sends, sends_first, gets_first = [], set(), set()
    for pair in range(pair_total):
        target = host_of(pair, pair_total, ROUNDS)
        for place in (0, 1):
            old = int(ordering[2 * pair + place])
            source = host_of(old // 2, pair_total, ROUNDS - 1)
            if source == target:
                continue
            sends.append((source, target))
            if old % 2 == 0:
                sends_first.add(source)
            if place == 0:
                gets_first.add(target)
    assert len({s for s, _ in sends}) == len(sends) == len({t for _, t in sends})
    return sends, sends_first, gets_first


def first_moves(pair_total):
    ordering = tournament_order(pair_total)
    sends, sends_second, gets_second, own_second = [], set(), set(), set()
    seconds = (set(), set())
    for pair in range(pair_total):
        here = host_of(pair, pair_total, 1)
        for place in (0, 1):
            old = int(ordering[2 * pair + place])
            if old % 2:
                seconds[place].add(here)
            if old // 2 == here:
                if place:
                    own_second.add(here)
                continue
            sends.append((old // 2, here))
            if old % 2:
                sends_second.add(old // 2)
                gets_second.add(here)
    assert len({s for s, _ in sends}) == len(sends) == len({t for _, t in sends})
    return sends, sends_second, gets_second, own_second, seconds


def fused_moves(pair_total):
    ordering = tournament_order(pair_total)
    before, last = ROUNDS - 3, ROUNDS - 1
    needs, edges, seconds = {}, [], ({}, {})
    for pair in range(pair_total):
        here = host_of(pair, pair_total, last)
        needs[here] = []
        for place in (0, 1):
            source = int(ordering[2 * pair + place])
            seconds[place][here] = source % 2
            for half in (0, 1):
                old = int(ordering[2 * (source // 2) + half])
                there = host_of(old // 2, pair_total, before)
                needs[here].append((there, old % 2))
                if there != here:
                    edges.append((there, old % 2, here))
    turn, left_over = {}, list(edges)
    while left_over:
        source, _, target = left_over[0]
        start = source
        while True:
            for number, one, other in ((0, source, target), (1, target, source)):
                edge = next(e for e in left_over if (e[0], e[2]) == (one, other))
                turn[edge] = number
                left_over.remove(edge)
            if target == start:
                break
            ahead = [e[2] for e in left_over if e[0] == target]
            source, target = target, ahead[0]
    sends = [[(e[0], e[2]) for e in edges if turn[e] == i] for i in (0, 1)]
    for chosen in sends:
        assert len({a for a, _ in chosen}) == len({b for _, b in chosen}) == pair_total
    sends_first = {e[0] for e in edges if turn[e] == 0 and e[1] == 0}
    picks = []
    for slot in range(4):
        pick = {}
        for here in range(pair_total):
            there, half = needs[here][slot]
            if there == here:
                pick[here] = 0 if (half == 0) == (here in sends_first) else 1
            else:
                pick[here] = 2 + turn[(there, half, here)]
        picks.append(pick)
    is_second = [{h for h, place in table.items() if place} for table in seconds]
    return sends, sends_first, picks, is_second


def choose(pick, arrays):
    chosen = arrays[0]
    for number in range(1, len(arrays)):
        members = {here for here, value in pick.items() if value == number}
        if members:
            chosen = jnp.where(among(members), arrays[number], chosen)
    return chosen


def among(members):
    here = lax.axis_index("pair")
    return functools.reduce(
        jnp.logical_or, [here == member for member in sorted(members)], here < 0
    )


def left(x, by):
    width = x.shape[1]
    return pltpu.roll(x, (width - by) % width, 1) if by % width else x


def right(x, by):
    width = x.shape[1]
    return pltpu.roll(x, by % width, 1) if by % width else x


def down(x, by):
    return pltpu.roll(x, by % x.shape[0], 0)


def lanes_of(x):
    return lax.broadcasted_iota(jnp.int32, x.shape, 1)


def split_pair(first, second):
    half = first.shape[1] // 2
    low = lanes_of(first) < half
    even = jnp.where(low, first, right(second, half))
    odd = jnp.where(low, right(first, half), second)
    return even, odd


def take_lanes(x, source):
    if x.shape[0] == 1:
        return take_lanes(jnp.broadcast_to(x, (8, x.shape[1])), source)[:1]
    return jnp.take_along_axis(x, jnp.broadcast_to(source, x.shape), axis=1)


def line_lanes(x):
    return lax.broadcasted_iota(jnp.int32, (1, x.shape[1]), 1)


def separate(first, second):
    lane = line_lanes(first)
    half = first.shape[1] // 2
    low = lane < half
    source = 2 * jnp.where(low, lane, lane - half)
    return tuple(
        jnp.where(low, take_lanes(first, source + odd), take_lanes(second, source + odd))
        for odd in (0, 1)
    )


def backwards(x):
    return jnp.take_along_axis(x, x.shape[1] - 1 - lanes_of(x), axis=1)


def dense_bands(even, odd, diags):
    width = even.shape[1]
    gram = lax.dot_general(
        jnp.concatenate((even, odd), axis=1),
        jnp.concatenate((backwards(even), backwards(odd)), axis=1),
        (((0,), (0,)), ((), ())),
        precision=lax.Precision.HIGHEST,
        preferred_element_type=jnp.float32,
    )
    bands = []
    for near in (0, width):
        for far in (0, width):
            quadrant = gram[far : far + width, near : near + width]
            aligned = pltpu.roll(quadrant, 1, 1, stride=1, stride_axis=0)
            bands.append(jnp.transpose(aligned)[:diags])
    return bands


def store_bands(even, odd, band_ref, diags):
    for q, band in enumerate(dense_bands(even, odd, diags)):
        band_ref[q * diags : (q + 1) * diags, :] = band


def open_kernel(sends_second, basis_ref, even_ref, odd_ref, payload_ref):
    rows, cols = basis_ref.shape
    width = cols // 2
    half = width // 2
    even, odd = separate(basis_ref[:, :width], basis_ref[:, width:])
    even_ref[...] = even
    odd_ref[...] = odd
    flag = among(sends_second)
    even, odd = (jnp.where(flag, left(x, half - STRIP), x) for x in (even, odd))
    payload_ref[:rows] = jnp.where(line_lanes(even) < half, even, right(odd, half))
    group = rows * 2 * STRIP // width
    strips = jnp.zeros((group, width), jnp.float32)
    for i in range(rows // group):
        for j, x in enumerate((even, odd)):
            start = (2 * i + j) * STRIP
            lane = line_lanes(x)
            here = jnp.logical_and(lane >= start, lane < start + STRIP)
            strips = jnp.where(here, left(x[i * group : (i + 1) * group], half - start), strips)
    payload_ref[rows:] = strips


def unpacked(payload, rows, second):
    width = payload.shape[1]
    half = width // 2
    lane = line_lanes(payload)
    main, strips = payload[:rows], payload[rows:]
    group = strips.shape[0]
    columns = []
    for j, x in enumerate((main, left(main, half))):
        ends = [right(strips, half - (2 * i + j) * STRIP) for i in range(rows // group)]
        x = jnp.where(lane < half, x, jnp.where(lane < half + STRIP, jnp.concatenate(ends), 0.0))
        columns.append(jnp.where(second, right(x, half - STRIP), x))
    return columns


def jacobi_angle(diag_even, diag_odd, coupling):
    spread = diag_even - diag_odd
    square = spread * spread + 4.0 * coupling * coupling
    inverse = lax.rsqrt(square)
    larger_square = (square * inverse + jnp.abs(spread)) * (0.5 * inverse)
    larger_inverse = lax.rsqrt(larger_square)
    larger = larger_square * larger_inverse
    smaller = coupling * inverse * larger_inverse
    forward = spread >= 0.0
    sign = jnp.where(coupling > 0.0, 1.0, jnp.where(coupling < 0.0, -1.0, 0.0))
    cosine = jnp.where(forward, larger, jnp.abs(smaller))
    sine_part = jnp.where(forward, smaller, sign * larger)
    return cosine, sine_part


def turn_bands(ee, eo, oe, oo, cosine, sine):
    cl, sl = jnp.broadcast_to(cosine, ee.shape), jnp.broadcast_to(sine, ee.shape)
    ck = pltpu.roll(cl, 0, 1, stride=1, stride_axis=0)
    sk = pltpu.roll(sl, 0, 1, stride=1, stride_axis=0)
    ee, oe = ck * ee + sk * oe, ck * oe - sk * ee
    eo, oo = ck * eo + sk * oo, ck * oo - sk * eo
    ee, eo = cl * ee + sl * eo, cl * eo - sl * ee
    oe, oo = cl * oe + sl * oo, cl * oo - sl * oe
    return ee, eo, oe, oo


def step_bands(ee, eo, oe, oo, cosine, sine):
    lane = lanes_of(ee)
    diag = lax.broadcasted_iota(jnp.int32, ee.shape, 0)
    last = lane == ee.shape[1] - 1
    on, next_on = diag == 0, diag == 1

    def slanted(x, by):
        if by >= 0:
            return pltpu.roll(x, by, 1, stride=1, stride_axis=0)
        return jnp.where(on, left(x, -by), down(slanted(x, 0), -by))

    def rotated(by, wanted):
        cl, sl = (jnp.broadcast_to(x, ee.shape) for x in (cosine, sine))
        ck, sk = (slanted(x, by) for x in (cl, sl))
        cl, sl, a, b, c, d = (right(x, by) for x in (cl, sl, ee, eo, oe, oo))
        a, c = ck * a + sk * c, ck * c - sk * a
        b, d = ck * b + sk * d, ck * d - sk * b
        found = {"ee": (a, b), "eo": (b, a), "oe": (c, d), "oo": (d, c)}
        return [
            cl * one + sl * two if name in ("ee", "oe") else cl * one - sl * two
            for name, (one, two) in found.items()
            if name in wanted
        ]

    ee_0, eo_0, oe_0, oo_0 = rotated(0, ("ee", "eo", "oe", "oo"))
    ee_r, eo_r, oe_r, oo_r = rotated(1, ("ee", "eo", "oe", "oo"))
    eo_l, oo_l = rotated(-1, ("eo", "oo"))

    near = down(jnp.where(on, eo_r, ee_r), 1)
    turned = jnp.where(on, oo_r, oe_r)
    ee_new = jnp.where(lane == diag + 1, turned, jnp.where(lane == diag, near, ee_r))
    ee_new = jnp.where(jnp.logical_and(on, lane == 0), ee_0, ee_new)

    eo_new = down(jnp.where(lane == diag - 1, oo_l, eo_l), -2)
    eo_new = jnp.where(lane == diag, down(eo_l, -1), eo_new)
    eo_new = jnp.where(last, down(ee_0, -1), eo_new)

    oo_new = jnp.where(last, jnp.where(on, ee_0, down(oe_0, 1)), oo_l)

    oe_new = down(oe_r, 2)
    oe_new = jnp.where(next_on, jnp.where(lane == diag, oo_0, eo_0), oe_new)
    oe_new = jnp.where(on, eo_new, oe_new)
    return ee_new, eo_new, oe_new, oo_new


def move_bands(ee, eo, oe, oo):
    lane = lanes_of(ee)
    diag = lax.broadcasted_iota(jnp.int32, ee.shape, 0)
    last = lane == ee.shape[1] - 1
    on, next_on = diag == 0, diag == 1

    near = down(jnp.where(on, eo, ee), 1)
    turned = jnp.where(on, oo, oe)
    mixed = jnp.where(lane == diag, turned, jnp.where(lane == diag - 1, near, ee))
    ee_new = jnp.where(jnp.logical_and(on, lane == 0), ee, right(mixed, 1))

    far = down(jnp.where(last, ee, eo), -1)
    mixed = down(jnp.where(lane == diag, oo, eo), -2)
    mixed = left(jnp.where(lane == diag + 1, far, mixed), 1)
    eo_new = jnp.where(last, far, mixed)

    oo_new = jnp.where(last, jnp.where(on, ee, down(oe, 1)), left(oo, 1))

    oe_new = right(down(oe, 2), 1)
    oe_new = jnp.where(next_on, jnp.where(lane == diag, oo, eo), oe_new)
    oe_new = jnp.where(on, eo_new, oe_new)
    return ee_new, eo_new, oe_new, oo_new


def move_bands_back(views, by):
    ee, eo, oe, oo = views[by]
    ee_left, _, oe_left, _ = views[by - 1]
    _, eo_right, _, oo_right = views[by + 1]
    width = ee.shape[1]
    lane = lanes_of(ee) - by
    lane = jnp.where(lane < 0, lane + width, jnp.where(lane >= width, lane - width, lane))
    diag = lax.broadcasted_iota(jnp.int32, ee.shape, 0)
    last, first = lane == width - 1, lane == diag
    on, next_on = diag == 0, diag == 1
    oo_up, eo_twice = down(oo, -1), down(eo_right, 2)

    far = jnp.where(first, down(ee_left, -1), ee_left)
    ee_old = jnp.where(jnp.logical_and(first, on), ee, far)
    ee_old = jnp.where(last, jnp.where(on, oo, down(eo, 1)), ee_old)

    near = jnp.where(jnp.logical_and(first, diag > 0), ee_left, down(oe_left, -2))
    eo_old = jnp.where(first, down(eo_right, 1), eo_twice)
    eo_old = jnp.where(on, jnp.where(last, oo_up, near), eo_old)
    eo_old = jnp.where(jnp.logical_and(next_on, lane > 1), oe, eo_old)
    eo_old = jnp.where(jnp.logical_and(on, first), far, eo_old)

    oe_old = jnp.where(on, eo_old, jnp.where(last, oo_up, near))

    oo_old = jnp.where(first, eo_twice, oo_right)
    oo_old = jnp.where(jnp.logical_and(next_on, first), oe, oo_old)
    oo_old = jnp.where(jnp.logical_and(on, first), ee_left, oo_old)
    return ee_old, eo_old, oe_old, oo_old


def bands_back(bands, count):
    views = {by: [right(x, by) for x in bands] for by in range(-count, count + 1)}
    for reach in reversed(range(count)):
        views = {by: move_bands_back(views, by) for by in range(-reach, reach + 1)}
    return views[0]


def move_columns(even, odd):
    lane = lanes_of(even)
    first, last = lane == 0, lane == even.shape[1] - 1
    even_new = jnp.where(first, even, right(jnp.where(first, odd, even), 1))
    odd_new = jnp.where(last, even, left(odd, 1))
    return even_new, odd_new


def in_pair(even, shifted=None):
    lane = line_lanes(even)
    if shifted is not None:
        half = even.shape[1] // 2
        lane = jnp.where(shifted, jnp.where(lane < half, lane + half, lane - half), lane)
    return (lane < 0, lane), (lane >= 0, lane)


def in_blocks(even):
    lane, half = line_lanes(even), even.shape[1] // 2
    place = jnp.where(lane < half, lane, lane - half)
    return (lane >= half, place), (lane >= half, place + half)


def in_order(even):
    lane, half = line_lanes(even), even.shape[1] // 2
    return (lane % 2 == 1, lane // 2), (lane % 2 == 1, lane // 2 + half)


def turn_to(layout, even, odd, angles):
    for cosine, sine in angles[:-1]:
        even, odd = cosine * even + sine * odd, cosine * odd - sine * even
        even, odd = move_columns(even, odd)
    by, end = JSTEPS - 1, even.shape[1] - 1
    results = []
    for is_odd, place in layout:
        stayed = place <= end - by
        from_even = jnp.where(stayed, place + by, 2 * end + 1 - by - place)
        from_even = jnp.where(place == 0, 0, from_even)
        source = jnp.where(is_odd, jnp.abs(place - by), from_even)
        is_even = jnp.logical_or(
            jnp.logical_and(is_odd, place < by),
            jnp.logical_and(jnp.logical_not(is_odd), stayed),
        )
        cosine, sine = (take_lanes(x, source) for x in angles[-1])
        by_even = jnp.where(is_even, cosine, -sine)
        by_odd = jnp.where(is_even, sine, cosine)
        results.append(by_even * take_lanes(even, source) + by_odd * take_lanes(odd, source))
    return results


def trim(bands, reach):
    rows = min(bands[0].shape[0], -(-(reach + 1) // 8) * 8)
    return [band[:rows] for band in bands]


def angles_of(bands):
    angles = []
    for step in range(JSTEPS):
        ee, eo, oe, oo = bands = trim(bands, 2 * (JSTEPS - 1 - step))
        angles.append(jacobi_angle(ee[0:1], oo[0:1], eo[0:1]))
        if step < JSTEPS - 1:
            bands = step_bands(*bands, *angles[-1])
    return angles


def carried(bands, angles):
    ahead = 2 * (JSTEPS - 1)
    for step, (cosine, sine) in enumerate(angles):
        bands = turn_bands(*trim(bands, 3 * ahead - 2 * step), cosine, sine)
        if step < JSTEPS - 1:
            bands = move_bands(*bands)
    done = 0
    while done < JSTEPS - 1:
        count = min(BACK, JSTEPS - 1 - done)
        bands = bands_back(trim(bands, 2 * (ahead - done)), count)
        done += count
    return bands


def near_starts(width):
    half = width // 2
    reach = REACH - 1
    return (half - 2 * reach, width - WINDOW), (0, half - reach)


def cross_partial(x_even, x_odd, y_even, y_odd, x_second, y_second):
    rows, width = x_even.shape
    x_starts, y_starts = near_starts(width)
    lane = lanes_of(x_even)

    def window(even, odd, flag, starts):
        start = jnp.where(flag, starts[1], starts[0])
        at_zero = pltpu.roll(even, width - start, 1)
        at_next = pltpu.roll(odd, (width - start + WINDOW) % width, 1)
        return jnp.where(lane < WINDOW, at_zero, jnp.where(lane < 2 * WINDOW, at_next, 0.0))

    corner = lax.dot_general(
        window(y_even, y_odd, y_second, y_starts),
        window(x_even, x_odd, x_second, x_starts),
        (((0,), (0,)), ((), ())),
        precision=lax.Precision.HIGHEST,
        preferred_element_type=jnp.float32,
    )
    low = lax.broadcasted_iota(jnp.int32, (WINDOW, width), 1) < 2 * WINDOW
    return jnp.where(low, corner[:WINDOW], right(corner[WINDOW : 2 * WINDOW], 2 * WINDOW))


def own_rotation(angles, second, swapped, first_pair):
    width = angles[0][0].shape[1]
    half = width // 2
    x_starts, y_starts = near_starts(width)
    starts = [jnp.where(first_pair, x, y) for x, y in zip(x_starts, y_starts)]
    shape = (2 * WINDOW, width)
    row = lax.broadcasted_iota(jnp.int32, shape, 0)
    lane = lax.broadcasted_iota(jnp.int32, shape, 1) - jnp.where(second, starts[1], starts[0])
    even, odd = (
        jnp.where(jnp.logical_and(row == lane + at, row // WINDOW == at // WINDOW), 1.0, 0.0)
        for at in (0, WINDOW)
    )
    even, odd = turn_to(in_pair(even, swapped), even, odd, angles)
    low = lax.broadcasted_iota(jnp.int32, shape, 1) < half
    return jnp.where(jnp.logical_xor(low, first_pair), right(odd, half), even)


def cross_bands(packed, x_rotation, y_rotation):
    width = packed.shape[1]
    half = width // 2
    corner = jnp.concatenate((packed[:, :half], right(packed, half)[:, :half]), axis=0)
    highest = dict(precision=lax.Precision.HIGHEST, preferred_element_type=jnp.float32)
    turned_x = jnp.dot(corner, x_rotation, **highest)
    ends = lax.dot_general(turned_x, y_rotation, (((0,), (0,)), ((), ())), **highest)
    even, odd = ends[half - NEAR : half], ends[width - NEAR :]
    quadrants = (even, right(even, half), odd, right(odd, half))
    offset = lanes_of(even) - lax.broadcasted_iota(jnp.int32, even.shape, 0) - (half - NEAR)
    diag = lax.broadcasted_iota(jnp.int32, (DIAGS, width), 0)
    bands = [jnp.zeros((DIAGS, width), jnp.float32) for _ in quadrants]
    for d in range(1, REACH):
        here = offset == d
        for q, quadrant in enumerate(quadrants):
            line = jnp.sum(jnp.where(here, quadrant, 0.0), axis=0, keepdims=True)
            bands[q] = jnp.where(diag == d, line, bands[q])
    return bands


def either(flag, one, other):
    return jnp.logical_or(jnp.logical_and(flag, one), jnp.logical_and(jnp.logical_not(flag), other))


def halves_swapped(is_second):
    return among(is_second[0]), jnp.logical_not(among(is_second[1]))


def on_odd_core():
    return lax.axis_index("row") % 2 == 1


PLACES = (
    (((16, 16, 80), (60, 16, 108)), ((16, 28, 21), (44, 30, 80))),
    (((68, 16, 24), (112, 16, 0)), ((70, 29, 84), (99, 29, 10))),
)
MIDDLES = (44, 99)


def pick_by(flag, one, other):
    return jnp.where(flag, other, one)


def pack_far(bands, flag):
    width = bands[0].shape[1]
    lane = lax.broadcasted_iota(jnp.int32, (DIAGS, width), 1)
    odd_row = lax.broadcasted_iota(jnp.int32, (DIAGS, width), 0) % 2 == 1
    moves = []
    for parity in (0, 1):
        for part in (0, 1):
            one, other = PLACES[0][parity][part], PLACES[1][parity][part]
            shift = pick_by(flag, (one[2] - one[0]) % width, (other[2] - other[0]) % width)
            start = pick_by(flag, one[2], other[2])
            count = pick_by(flag, one[1], other[1])
            here = jnp.logical_and(lane >= start, lane < start + count)
            moves.append((shift, jnp.logical_and(here, odd_row == (parity == 1))))
    packed = []
    for band in bands:
        near, far = band[:DIAGS], down(band[DIAGS:], -1)
        for shift, here in moves:
            near = jnp.where(here, pltpu.roll(far, shift, 1), near)
        packed.append(near)
    return packed


def unpack_far(packed, flag):
    width = packed.shape[1]
    lane = lanes_of(packed)
    odd_row = lax.broadcasted_iota(jnp.int32, packed.shape, 0) % 2 == 1
    parts = []
    for part in (0, 1):
        rolled = []
        for parity in (0, 1):
            one, other = PLACES[0][parity][part], PLACES[1][parity][part]
            shift = pick_by(flag, (one[0] - one[2]) % width, (other[0] - other[2]) % width)
            rolled.append(pltpu.roll(packed, shift, 1))
        parts.append(jnp.where(odd_row, rolled[1], rolled[0]))
    far = jnp.where(lane < pick_by(flag, *MIDDLES), *parts)
    return jnp.concatenate((packed, down(far, 1)), axis=0)


PACKED = DIAGS


def store_part(even, odd, flag, part_ref):
    bands = pack_far(dense_bands(even, odd, FAR_DIAGS), flag)
    for q, band in enumerate(bands):
        part_ref[q * PACKED : (q + 1) * PACKED, :] = band


def open_pairs(is_second, x, y, column_refs, other_ref):
    flag = on_odd_core()
    mine = [jnp.where(flag, b, a) for a, b in zip(x, y)]
    theirs = [jnp.where(flag, a, b) for a, b in zip(x, y)]
    for ref, value in zip(column_refs, mine + theirs):
        ref[...] = value
    store_part(*theirs, either(flag, among(is_second[0]), among(is_second[1])), other_ref)
    other_ref[4 * PACKED :, :] = jnp.zeros((WINDOW, theirs[0].shape[1]), jnp.float32)


def first_open(own_second, gets_second, is_second, even_ref, odd_ref, payload_ref, *refs):
    *column_refs, other_ref = refs
    own = even_ref[...], odd_ref[...]
    came = unpacked(payload_ref[...], own[0].shape[0], among(gets_second))
    flag = among(own_second)
    x = [jnp.where(flag, b, a) for a, b in zip(own, came)]
    y = [jnp.where(flag, a, b) for a, b in zip(own, came)]
    open_pairs(is_second, x, y, column_refs, other_ref)


def fused_open(picks, is_second, kept_ref, sent_ref, came0_ref, came1_ref, *refs):
    *column_refs, other_ref = refs
    arrays = [ref[...] for ref in (sent_ref, kept_ref, came0_ref, came1_ref)]
    blocks = [choose(pick, arrays) for pick in picks]
    x, y = split_pair(*blocks[:2]), split_pair(*blocks[2:])
    open_pairs(is_second, x, y, column_refs, other_ref)


def swapped_flag(is_second):
    x_swapped, y_swapped = halves_swapped(is_second)
    return either(on_odd_core(), y_swapped, x_swapped)


def own_second_flag(is_second):
    return either(on_odd_core(), among(is_second[1]), among(is_second[0]))


def bands_kernel(is_second, *refs):
    *column_refs, part_ref = refs
    columns = [ref[...] for ref in column_refs]
    store_part(*columns[:2], own_second_flag(is_second), part_ref)
    flag = on_odd_core()
    x = [jnp.where(flag, b, a) for a, b in zip(columns[:2], columns[2:])]
    y = [jnp.where(flag, a, b) for a, b in zip(columns[:2], columns[2:])]
    corner = cross_partial(*x, *y, among(is_second[0]), among(is_second[1]))
    part_ref[4 * PACKED :, :] = corner


def angles_kernel(is_second, *refs):
    *part_refs, found_ref = refs
    part = pair_sums([ref[...] for ref in part_refs])
    flag = own_second_flag(is_second)
    quadrants = [unpack_far(part[q * PACKED : (q + 1) * PACKED], flag) for q in range(4)]
    angles = angles_of(quadrants)
    bands = carried(quadrants, angles)
    for step, pair in enumerate(angles):
        for i in (0, 1):
            found_ref[2 * step + i : 2 * step + i + 1, :] = pair[i]
    spare = NEAR - 2 * JSTEPS
    found_ref[2 * JSTEPS : NEAR, :] = jnp.zeros((spare, part.shape[1]), jnp.float32)
    for q in range(4):
        found_ref[NEAR + q * DIAGS : NEAR + (q + 1) * DIAGS, :] = bands[q][:DIAGS]
    found_ref[CORNER:ROTATION, :] = part[4 * PACKED :]
    first_pair = jnp.logical_not(on_odd_core())
    found_ref[ROTATION:, :] = own_rotation(angles, flag, swapped_flag(is_second), first_pair)


CORNER = NEAR + 4 * DIAGS
ROTATION = CORNER + WINDOW
FOUND = ROTATION + 2 * WINDOW


def angles_in(found):
    return [(found[2 * i : 2 * i + 1], found[2 * i + 1 : 2 * i + 2]) for i in range(JSTEPS)]


def columns_kernel(is_second, even_ref, odd_ref, found_ref, *out_refs):
    angles = angles_in(found_ref[...])
    layout = in_pair(even_ref, swapped_flag(is_second))
    columns = turn_to(layout, even_ref[...], odd_ref[...], angles)
    for ref, value in zip(out_refs, columns):
        ref[...] = value


def next_bands(x_found, y_found, x_second, y_second):
    corner = x_found[CORNER:ROTATION] + y_found[CORNER:ROTATION]
    middle = cross_bands(corner, x_found[ROTATION:], y_found[ROTATION:])
    half = corner.shape[1] // 2
    lane = lanes_of(middle[0])
    diag = lax.broadcasted_iota(jnp.int32, middle[0].shape, 0)
    bands = []
    for q in range(4):
        rows = slice(NEAR + q * DIAGS, NEAR + (q + 1) * DIAGS)
        x, y = x_found[rows], y_found[rows]
        x = jnp.where(x_second, right(x, half), x)
        y = jnp.where(y_second, y, right(y, half))
        crossing = jnp.where(lane - diag < half, middle[q], y)
        bands.append(jnp.where(lane < half, x, crossing))
    return bands


def next_kernel(is_second, sends_first, layout_of, *refs):
    mine_even, mine_odd, even_ref, odd_ref, found_ref, other_ref, kept_ref, sent_ref = refs
    found, other = found_ref[...], other_ref[...]
    flag = on_odd_core()
    x_found, y_found = jnp.where(flag, other, found), jnp.where(flag, found, other)
    bands = next_bands(x_found, y_found, among(is_second[0]), among(is_second[1]))
    x_swapped, y_swapped = halves_swapped(is_second)
    swapped = either(flag, x_swapped, y_swapped)
    layout = in_pair(even_ref, swapped)
    theirs = turn_to(layout, even_ref[...], odd_ref[...], angles_in(other))
    low = line_lanes(found) < found.shape[1] // 2
    from_mine = jnp.logical_xor(low, flag)
    even = jnp.where(from_mine, mine_even[...], theirs[0])
    odd = jnp.where(from_mine, mine_odd[...], theirs[1])
    angles = angles_of(bands)
    first, second = turn_to(layout_of(even), even, odd, angles)
    flag = among(sends_first)
    kept_ref[...] = jnp.where(flag, second, first)
    sent_ref[...] = jnp.where(flag, first, second)


def pair_sums(arrays):
    while len(arrays) > 1:
        arrays = [arrays[i] + arrays[i + 1] for i in range(0, len(arrays), 2)]
    return arrays[0]


def swap(x, axis, mask):
    return lax.ppermute(x, axis, [(i, i ^ mask) for i in range(lax.axis_size(axis))])


def exchange_groups(x, axis, first_bit=0):
    count = lax.axis_size(axis).bit_length() - 1
    bits = [1 << b for b in range(count)]
    groups = [bits[:1]] + [bits[i : i + 2] for i in range(1, count, 2)]
    arrays = [x]
    for group in groups[first_bit:]:
        x = pair_sums(arrays)
        masks = [group[0]] if len(group) == 1 else [group[0], group[1], group[0] | group[1]]
        arrays = [x] + [swap(x, axis, mask) for mask in masks]
    return arrays


def call(kernel, shapes, *args):
    out = [jax.ShapeDtypeStruct(shape, jnp.float32) for shape in shapes]
    return pl.pallas_call(
        kernel,
        out_shape=out,
        compiler_params=pltpu.CompilerParams(vmem_limit_bytes=32 * 1024 * 1024),
    )(*args)


def two_rounds(opened, is_second, sends_first, layout_of):
    *columns, other = opened
    column, width = columns[0].shape, columns[0].shape[1]
    other = swap(other, "row", 1)
    bands = functools.partial(bands_kernel, is_second)
    (mine,) = call(bands, (other.shape,), *columns)
    (found,) = call(
        functools.partial(angles_kernel, is_second),
        ((FOUND, width),),
        *exchange_groups(mine + other, "row", 1),
    )
    other = swap(found, "row", 1)
    turn = functools.partial(columns_kernel, is_second)
    columns[:2] = call(turn, (column, column), *columns[:2], found)
    turn = functools.partial(next_kernel, is_second, sends_first, layout_of)
    return call(turn, (column, column), *columns, found, other)


def per_device(basis):
    rows, cols = basis.shape
    width = cols // 2
    pair_total = lax.axis_size("pair")
    column = (rows, width)
    opened = (column,) * 4 + ((4 * PACKED + WINDOW, width),)
    payload = (rows + rows * 2 * STRIP // width, width)

    sends, sends_second, gets_second, own_second, is_second = first_moves(pair_total)
    opening = functools.partial(open_kernel, sends_second)
    even, odd, sent = call(opening, (column, column, payload), basis)
    came = lax.ppermute(sent, "pair", sends)
    opening = functools.partial(first_open, own_second, gets_second, is_second)
    arrays = call(opening, opened, even, odd, came)
    sends, sends_first, picks, next_second = fused_moves(pair_total)
    kept, sent = two_rounds(arrays, is_second, sends_first, in_blocks)

    came = [lax.ppermute(x, "pair", s) for x, s in zip((sent, kept), sends)]
    opening = functools.partial(fused_open, picks, next_second)
    arrays = call(opening, opened, kept, sent, *came)
    sends, sends_first, gets_first = last_moves(pair_total)
    kept, sent = two_rounds(arrays, next_second, sends_first, in_order)

    came = lax.ppermute(sent, "pair", sends)
    flag = among(gets_first)
    first = jnp.where(flag, came, kept)
    second = jnp.where(flag, kept, came)
    return jnp.concatenate((first, second), axis=1)


def solution(mesh):
    return jax.shard_map(
        per_device,
        mesh=mesh,
        in_specs=(P("row", "pair"),),
        out_specs=P("row", "pair"),
        check_vma=False,
    )
```

```python
import functools

import jax
import jax.numpy as jnp
import numpy as np
from jax import lax
from jax.experimental import pallas as pl
from jax.experimental.pallas import tpu as pltpu
from jax.sharding import PartitionSpec as P

ROUNDS = 4
JSTEPS = 6
REACH = 2 * (JSTEPS - 1) + 1
DIAGS = 16
FAR_DIAGS = 32
WINDOW = 32
NEAR = 16
STRIP = 16
BACK = 3


def tournament_order(pair_count):
    ordering = np.zeros(2 * pair_count, dtype=np.int64)
    ordering[0] = 0
    ordering[2] = 1
    for slot in range(2, pair_count):
        ordering[2 * slot] = 2 * (slot - 1)
    for slot in range(pair_count - 1):
        ordering[2 * slot + 1] = 2 * (slot + 1) + 1
    ordering[2 * pair_count - 1] = 2 * (pair_count - 1)
    return ordering


def host_of(pair, pair_total, round_index):
    if round_index % 2 == 0 or pair == 0:
        return pair
    return min(pair + 1, pair_total - 1) if pair % 2 else pair - 1


def last_moves(pair_total):
    ordering = tournament_order(pair_total)
    sends, sends_first, gets_first = [], set(), set()
    for pair in range(pair_total):
        target = host_of(pair, pair_total, ROUNDS)
        for place in (0, 1):
            old = int(ordering[2 * pair + place])
            source = host_of(old // 2, pair_total, ROUNDS - 1)
            if source == target:
                continue
            sends.append((source, target))
            if old % 2 == 0:
                sends_first.add(source)
            if place == 0:
                gets_first.add(target)
    assert len({s for s, _ in sends}) == len(sends) == len({t for _, t in sends})
    return sends, sends_first, gets_first


def first_moves(pair_total):
    ordering = tournament_order(pair_total)
    sends, sends_second, gets_second, own_second = [], set(), set(), set()
    seconds = (set(), set())
    for pair in range(pair_total):
        here = host_of(pair, pair_total, 1)
        for place in (0, 1):
            old = int(ordering[2 * pair + place])
            if old % 2:
                seconds[place].add(here)
            if old // 2 == here:
                if place:
                    own_second.add(here)
                continue
            sends.append((old // 2, here))
            if old % 2:
                sends_second.add(old // 2)
                gets_second.add(here)
    assert len({s for s, _ in sends}) == len(sends) == len({t for _, t in sends})
    return sends, sends_second, gets_second, own_second, seconds


def fused_moves(pair_total):
    ordering = tournament_order(pair_total)
    before, last = ROUNDS - 3, ROUNDS - 1
    needs, edges, seconds = {}, [], ({}, {})
    for pair in range(pair_total):
        here = host_of(pair, pair_total, last)
        needs[here] = []
        for place in (0, 1):
            source = int(ordering[2 * pair + place])
            seconds[place][here] = source % 2
            for half in (0, 1):
                old = int(ordering[2 * (source // 2) + half])
                there = host_of(old // 2, pair_total, before)
                needs[here].append((there, old % 2))
                if there != here:
                    edges.append((there, old % 2, here))
    turn, left_over = {}, list(edges)
    while left_over:
        source, _, target = left_over[0]
        start = source
        while True:
            for number, one, other in ((0, source, target), (1, target, source)):
                edge = next(e for e in left_over if (e[0], e[2]) == (one, other))
                turn[edge] = number
                left_over.remove(edge)
            if target == start:
                break
            ahead = [e[2] for e in left_over if e[0] == target]
            source, target = target, ahead[0]
    sends = [[(e[0], e[2]) for e in edges if turn[e] == i] for i in (0, 1)]
    for chosen in sends:
        assert len({a for a, _ in chosen}) == len({b for _, b in chosen}) == pair_total
    sends_first = {e[0] for e in edges if turn[e] == 0 and e[1] == 0}
    picks = []
    for slot in range(4):
        pick = {}
        for here in range(pair_total):
            there, half = needs[here][slot]
            if there == here:
                pick[here] = 0 if (half == 0) == (here in sends_first) else 1
            else:
                pick[here] = 2 + turn[(there, half, here)]
        picks.append(pick)
    is_second = [{h for h, place in table.items() if place} for table in seconds]
    return sends, sends_first, picks, is_second


def choose(pick, arrays):
    chosen = arrays[0]
    for number in range(1, len(arrays)):
        members = {here for here, value in pick.items() if value == number}
        if members:
            chosen = jnp.where(among(members), arrays[number], chosen)
    return chosen


def among(members):
    here = lax.axis_index("pair")
    return functools.reduce(
        jnp.logical_or, [here == member for member in sorted(members)], here < 0
    )


def left(x, by):
    width = x.shape[1]
    return pltpu.roll(x, (width - by) % width, 1) if by % width else x


def right(x, by):
    width = x.shape[1]
    return pltpu.roll(x, by % width, 1) if by % width else x


def down(x, by):
    return pltpu.roll(x, by % x.shape[0], 0)


def lanes_of(x):
    return lax.broadcasted_iota(jnp.int32, x.shape, 1)


def split_pair(first, second):
    half = first.shape[1] // 2
    low = lanes_of(first) < half
    even = jnp.where(low, first, right(second, half))
    odd = jnp.where(low, right(first, half), second)
    return even, odd


def take_lanes(x, source):
    if x.shape[0] == 1:
        return take_lanes(jnp.broadcast_to(x, (8, x.shape[1])), source)[:1]
    return jnp.take_along_axis(x, jnp.broadcast_to(source, x.shape), axis=1)


def line_lanes(x):
    return lax.broadcasted_iota(jnp.int32, (1, x.shape[1]), 1)


def separate(first, second):
    lane = line_lanes(first)
    half = first.shape[1] // 2
    low = lane < half
    source = 2 * jnp.where(low, lane, lane - half)
    return tuple(
        jnp.where(low, take_lanes(first, source + odd), take_lanes(second, source + odd))
        for odd in (0, 1)
    )


def backwards(x):
    return jnp.take_along_axis(x, x.shape[1] - 1 - lanes_of(x), axis=1)


def dense_bands(even, odd, diags):
    width = even.shape[1]
    gram = lax.dot_general(
        jnp.concatenate((even, odd), axis=1),
        jnp.concatenate((backwards(even), backwards(odd)), axis=1),
        (((0,), (0,)), ((), ())),
        precision=lax.Precision.HIGHEST,
        preferred_element_type=jnp.float32,
    )
    bands = []
    for near in (0, width):
        for far in (0, width):
            quadrant = gram[far : far + width, near : near + width]
            aligned = pltpu.roll(quadrant, 1, 1, stride=1, stride_axis=0)
            bands.append(jnp.transpose(aligned)[:diags])
    return bands


def store_bands(even, odd, band_ref, diags):
    for q, band in enumerate(dense_bands(even, odd, diags)):
        band_ref[q * diags : (q + 1) * diags, :] = band


def payload_kernel(sends_second, basis_ref, payload_ref):
    rows, cols = basis_ref.shape
    width = cols // 2
    half = width // 2
    first, second = basis_ref[:, :width], basis_ref[:, width:]
    lane = line_lanes(first)
    start = jnp.where(among(sends_second), half - STRIP, 0)
    place = start + jnp.where(lane < half, lane, lane - half)
    odd = jnp.where(lane < half, 0, 1)
    in_first = place < half
    source = 2 * jnp.where(in_first, place, place - half) + odd
    payload_ref[:rows] = jnp.where(in_first, take_lanes(first, source), take_lanes(second, source))
    group = rows * 2 * STRIP // width
    source = 2 * (start + lane % STRIP) + lane // STRIP % 2
    strips = jnp.zeros((group, width), jnp.float32)
    for i in range(rows // group):
        here = lane // (2 * STRIP) == i
        strips = jnp.where(here, take_lanes(second[i * group : (i + 1) * group], source), strips)
    payload_ref[rows:] = strips


def open_kernel(basis_ref, even_ref, odd_ref):
    width = basis_ref.shape[1] // 2
    even_ref[...], odd_ref[...] = separate(basis_ref[:, :width], basis_ref[:, width:])


def unpacked(payload, rows, second):
    width = payload.shape[1]
    half = width // 2
    lane = line_lanes(payload)
    main, strips = payload[:rows], payload[rows:]
    group = strips.shape[0]
    columns = []
    for j, x in enumerate((main, left(main, half))):
        ends = [right(strips, half - (2 * i + j) * STRIP) for i in range(rows // group)]
        x = jnp.where(lane < half, x, jnp.where(lane < half + STRIP, jnp.concatenate(ends), 0.0))
        columns.append(jnp.where(second, right(x, half - STRIP), x))
    return columns


def jacobi_angle(diag_even, diag_odd, coupling):
    spread = diag_even - diag_odd
    square = spread * spread + 4.0 * coupling * coupling
    inverse = lax.rsqrt(square)
    larger_square = (square * inverse + jnp.abs(spread)) * (0.5 * inverse)
    larger_inverse = lax.rsqrt(larger_square)
    larger = larger_square * larger_inverse
    smaller = coupling * inverse * larger_inverse
    forward = spread >= 0.0
    sign = jnp.where(coupling > 0.0, 1.0, jnp.where(coupling < 0.0, -1.0, 0.0))
    cosine = jnp.where(forward, larger, jnp.abs(smaller))
    sine_part = jnp.where(forward, smaller, sign * larger)
    return cosine, sine_part


def turn_bands(ee, eo, oe, oo, cosine, sine):
    cl, sl = jnp.broadcast_to(cosine, ee.shape), jnp.broadcast_to(sine, ee.shape)
    ck = pltpu.roll(cl, 0, 1, stride=1, stride_axis=0)
    sk = pltpu.roll(sl, 0, 1, stride=1, stride_axis=0)
    ee, oe = ck * ee + sk * oe, ck * oe - sk * ee
    eo, oo = ck * eo + sk * oo, ck * oo - sk * eo
    ee, eo = cl * ee + sl * eo, cl * eo - sl * ee
    oe, oo = cl * oe + sl * oo, cl * oo - sl * oe
    return ee, eo, oe, oo


def step_bands(ee, eo, oe, oo, cosine, sine):
    lane = lanes_of(ee)
    diag = lax.broadcasted_iota(jnp.int32, ee.shape, 0)
    last = lane == ee.shape[1] - 1
    on, next_on = diag == 0, diag == 1

    def slanted(x, by):
        if by >= 0:
            return pltpu.roll(x, by, 1, stride=1, stride_axis=0)
        return jnp.where(on, left(x, -by), down(slanted(x, 0), -by))

    def rotated(by, wanted):
        cl, sl = (jnp.broadcast_to(x, ee.shape) for x in (cosine, sine))
        ck, sk = (slanted(x, by) for x in (cl, sl))
        cl, sl, a, b, c, d = (right(x, by) for x in (cl, sl, ee, eo, oe, oo))
        a, c = ck * a + sk * c, ck * c - sk * a
        b, d = ck * b + sk * d, ck * d - sk * b
        found = {"ee": (a, b), "eo": (b, a), "oe": (c, d), "oo": (d, c)}
        return [
            cl * one + sl * two if name in ("ee", "oe") else cl * one - sl * two
            for name, (one, two) in found.items()
            if name in wanted
        ]

    ee_0, eo_0, oe_0, oo_0 = rotated(0, ("ee", "eo", "oe", "oo"))
    ee_r, eo_r, oe_r, oo_r = rotated(1, ("ee", "eo", "oe", "oo"))
    eo_l, oo_l = rotated(-1, ("eo", "oo"))

    near = down(jnp.where(on, eo_r, ee_r), 1)
    turned = jnp.where(on, oo_r, oe_r)
    ee_new = jnp.where(lane == diag + 1, turned, jnp.where(lane == diag, near, ee_r))
    ee_new = jnp.where(jnp.logical_and(on, lane == 0), ee_0, ee_new)

    eo_new = down(jnp.where(lane == diag - 1, oo_l, eo_l), -2)
    eo_new = jnp.where(lane == diag, down(eo_l, -1), eo_new)
    eo_new = jnp.where(last, down(ee_0, -1), eo_new)

    oo_new = jnp.where(last, jnp.where(on, ee_0, down(oe_0, 1)), oo_l)

    oe_new = down(oe_r, 2)
    oe_new = jnp.where(next_on, jnp.where(lane == diag, oo_0, eo_0), oe_new)
    oe_new = jnp.where(on, eo_new, oe_new)
    return ee_new, eo_new, oe_new, oo_new


def move_bands(ee, eo, oe, oo):
    lane = lanes_of(ee)
    diag = lax.broadcasted_iota(jnp.int32, ee.shape, 0)
    last = lane == ee.shape[1] - 1
    on, next_on = diag == 0, diag == 1

    near = down(jnp.where(on, eo, ee), 1)
    turned = jnp.where(on, oo, oe)
    mixed = jnp.where(lane == diag, turned, jnp.where(lane == diag - 1, near, ee))
    ee_new = jnp.where(jnp.logical_and(on, lane == 0), ee, right(mixed, 1))

    far = down(jnp.where(last, ee, eo), -1)
    mixed = down(jnp.where(lane == diag, oo, eo), -2)
    mixed = left(jnp.where(lane == diag + 1, far, mixed), 1)
    eo_new = jnp.where(last, far, mixed)

    oo_new = jnp.where(last, jnp.where(on, ee, down(oe, 1)), left(oo, 1))

    oe_new = right(down(oe, 2), 1)
    oe_new = jnp.where(next_on, jnp.where(lane == diag, oo, eo), oe_new)
    oe_new = jnp.where(on, eo_new, oe_new)
    return ee_new, eo_new, oe_new, oo_new


def move_bands_back(views, by):
    ee, eo, oe, oo = views[by]
    ee_left, _, oe_left, _ = views[by - 1]
    _, eo_right, _, oo_right = views[by + 1]
    width = ee.shape[1]
    lane = lanes_of(ee) - by
    lane = jnp.where(lane < 0, lane + width, jnp.where(lane >= width, lane - width, lane))
    diag = lax.broadcasted_iota(jnp.int32, ee.shape, 0)
    last, first = lane == width - 1, lane == diag
    on, next_on = diag == 0, diag == 1
    oo_up, eo_twice = down(oo, -1), down(eo_right, 2)

    far = jnp.where(first, down(ee_left, -1), ee_left)
    ee_old = jnp.where(jnp.logical_and(first, on), ee, far)
    ee_old = jnp.where(last, jnp.where(on, oo, down(eo, 1)), ee_old)

    near = jnp.where(jnp.logical_and(first, diag > 0), ee_left, down(oe_left, -2))
    eo_old = jnp.where(first, down(eo_right, 1), eo_twice)
    eo_old = jnp.where(on, jnp.where(last, oo_up, near), eo_old)
    eo_old = jnp.where(jnp.logical_and(next_on, lane > 1), oe, eo_old)
    eo_old = jnp.where(jnp.logical_and(on, first), far, eo_old)

    oe_old = jnp.where(on, eo_old, jnp.where(last, oo_up, near))

    oo_old = jnp.where(first, eo_twice, oo_right)
    oo_old = jnp.where(jnp.logical_and(next_on, first), oe, oo_old)
    oo_old = jnp.where(jnp.logical_and(on, first), ee_left, oo_old)
    return ee_old, eo_old, oe_old, oo_old


def bands_back(bands, count):
    views = {by: [right(x, by) for x in bands] for by in range(-count, count + 1)}
    for reach in reversed(range(count)):
        views = {by: move_bands_back(views, by) for by in range(-reach, reach + 1)}
    return views[0]


def move_columns(even, odd):
    lane = lanes_of(even)
    first, last = lane == 0, lane == even.shape[1] - 1
    even_new = jnp.where(first, even, right(jnp.where(first, odd, even), 1))
    odd_new = jnp.where(last, even, left(odd, 1))
    return even_new, odd_new


def in_pair(even, shifted=None):
    lane = line_lanes(even)
    if shifted is not None:
        half = even.shape[1] // 2
        lane = jnp.where(shifted, jnp.where(lane < half, lane + half, lane - half), lane)
    return (lane < 0, lane), (lane >= 0, lane)


def in_blocks(even):
    lane, half = line_lanes(even), even.shape[1] // 2
    place = jnp.where(lane < half, lane, lane - half)
    return (lane >= half, place), (lane >= half, place + half)


def in_order(even):
    lane, half = line_lanes(even), even.shape[1] // 2
    return (lane % 2 == 1, lane // 2), (lane % 2 == 1, lane // 2 + half)


def turn_to(layout, even, odd, angles):
    for cosine, sine in angles[:-1]:
        even, odd = cosine * even + sine * odd, cosine * odd - sine * even
        even, odd = move_columns(even, odd)
    by, end = JSTEPS - 1, even.shape[1] - 1
    results = []
    for is_odd, place in layout:
        stayed = place <= end - by
        from_even = jnp.where(stayed, place + by, 2 * end + 1 - by - place)
        from_even = jnp.where(place == 0, 0, from_even)
        source = jnp.where(is_odd, jnp.abs(place - by), from_even)
        is_even = jnp.logical_or(
            jnp.logical_and(is_odd, place < by),
            jnp.logical_and(jnp.logical_not(is_odd), stayed),
        )
        cosine, sine = (take_lanes(x, source) for x in angles[-1])
        by_even = jnp.where(is_even, cosine, -sine)
        by_odd = jnp.where(is_even, sine, cosine)
        results.append(by_even * take_lanes(even, source) + by_odd * take_lanes(odd, source))
    return results


def trim(bands, reach):
    rows = min(bands[0].shape[0], -(-(reach + 1) // 8) * 8)
    return [band[:rows] for band in bands]


def angles_of(bands):
    angles = []
    for step in range(JSTEPS):
        ee, eo, oe, oo = bands = trim(bands, 2 * (JSTEPS - 1 - step))
        angles.append(jacobi_angle(ee[0:1], oo[0:1], eo[0:1]))
        if step < JSTEPS - 1:
            bands = step_bands(*bands, *angles[-1])
    return angles


def carried(bands, angles):
    ahead = 2 * (JSTEPS - 1)
    for step, (cosine, sine) in enumerate(angles):
        bands = turn_bands(*trim(bands, 3 * ahead - 2 * step), cosine, sine)
        if step < JSTEPS - 1:
            bands = move_bands(*bands)
    done = 0
    while done < JSTEPS - 1:
        count = min(BACK, JSTEPS - 1 - done)
        bands = bands_back(trim(bands, 2 * (ahead - done)), count)
        done += count
    return bands


def near_starts(width):
    half = width // 2
    reach = REACH - 1
    return (half - 2 * reach, width - WINDOW), (0, half - reach)


def cross_partial(x_even, x_odd, y_even, y_odd, x_second, y_second):
    rows, width = x_even.shape
    x_starts, y_starts = near_starts(width)
    lane = lanes_of(x_even)

    def window(even, odd, flag, starts):
        start = jnp.where(flag, starts[1], starts[0])
        at_zero = pltpu.roll(even, (width - start) % width, 1)
        at_next = pltpu.roll(odd, (width - start + WINDOW) % width, 1)
        return jnp.where(lane < WINDOW, at_zero, jnp.where(lane < 2 * WINDOW, at_next, 0.0))

    corner = lax.dot_general(
        window(y_even, y_odd, y_second, y_starts),
        window(x_even, x_odd, x_second, x_starts),
        (((0,), (0,)), ((), ())),
        precision=lax.Precision.HIGHEST,
        preferred_element_type=jnp.float32,
    )
    low = lax.broadcasted_iota(jnp.int32, (WINDOW, width), 1) < 2 * WINDOW
    return jnp.where(low, corner[:WINDOW], right(corner[WINDOW : 2 * WINDOW], 2 * WINDOW))


def own_rotation(angles, second, swapped, first_pair):
    width = angles[0][0].shape[1]
    half = width // 2
    x_starts, y_starts = near_starts(width)
    starts = [jnp.where(first_pair, x, y) for x, y in zip(x_starts, y_starts)]
    shape = (2 * WINDOW, width)
    row = lax.broadcasted_iota(jnp.int32, shape, 0)
    lane = lax.broadcasted_iota(jnp.int32, shape, 1) - jnp.where(second, starts[1], starts[0])
    even, odd = (
        jnp.where(jnp.logical_and(row == lane + at, row // WINDOW == at // WINDOW), 1.0, 0.0)
        for at in (0, WINDOW)
    )
    even, odd = turn_to(in_pair(even, swapped), even, odd, angles)
    low = lax.broadcasted_iota(jnp.int32, shape, 1) < half
    return jnp.where(jnp.logical_xor(low, first_pair), right(odd, half), even)


def cross_bands(packed, x_rotation, y_rotation):
    width = packed.shape[1]
    half = width // 2
    corner = jnp.concatenate((packed[:, :half], right(packed, half)[:, :half]), axis=0)
    highest = dict(precision=lax.Precision.HIGHEST, preferred_element_type=jnp.float32)
    turned_x = jnp.dot(corner, x_rotation, **highest)
    ends = lax.dot_general(turned_x, y_rotation, (((0,), (0,)), ((), ())), **highest)
    even, odd = ends[half - NEAR : half], ends[width - NEAR :]
    quadrants = (even, right(even, half), odd, right(odd, half))
    offset = lanes_of(even) - lax.broadcasted_iota(jnp.int32, even.shape, 0) - (half - NEAR)
    diag = lax.broadcasted_iota(jnp.int32, (DIAGS, width), 0)
    bands = [jnp.zeros((DIAGS, width), jnp.float32) for _ in quadrants]
    for d in range(1, REACH):
        here = offset == d
        for q, quadrant in enumerate(quadrants):
            line = jnp.sum(jnp.where(here, quadrant, 0.0), axis=0, keepdims=True)
            bands[q] = jnp.where(diag == d, line, bands[q])
    return bands


def either(flag, one, other):
    return jnp.logical_or(jnp.logical_and(flag, one), jnp.logical_and(jnp.logical_not(flag), other))


def halves_swapped(is_second):
    return among(is_second[0]), jnp.logical_not(among(is_second[1]))


def on_odd_core():
    return lax.axis_index("row") % 2 == 1


PLACES = (
    (((16, 16, 80), (60, 16, 108)), ((16, 28, 21), (44, 30, 80))),
    (((68, 16, 24), (112, 16, 0)), ((70, 29, 84), (99, 29, 10))),
)
MIDDLES = (44, 99)


def pick_by(flag, one, other):
    return jnp.where(flag, other, one)


def pack_far(bands, flag):
    width = bands[0].shape[1]
    lane = lax.broadcasted_iota(jnp.int32, (DIAGS, width), 1)
    odd_row = lax.broadcasted_iota(jnp.int32, (DIAGS, width), 0) % 2 == 1
    moves = []
    for parity in (0, 1):
        for part in (0, 1):
            one, other = PLACES[0][parity][part], PLACES[1][parity][part]
            shift = pick_by(flag, (one[2] - one[0]) % width, (other[2] - other[0]) % width)
            start = pick_by(flag, one[2], other[2])
            count = pick_by(flag, one[1], other[1])
            here = jnp.logical_and(lane >= start, lane < start + count)
            moves.append((shift, jnp.logical_and(here, odd_row == (parity == 1))))
    packed = []
    for band in bands:
        near, far = band[:DIAGS], down(band[DIAGS:], -1)
        for shift, here in moves:
            near = jnp.where(here, pltpu.roll(far, shift, 1), near)
        packed.append(near)
    return packed


def unpack_far(packed, flag):
    width = packed.shape[1]
    lane = lanes_of(packed)
    odd_row = lax.broadcasted_iota(jnp.int32, packed.shape, 0) % 2 == 1
    parts = []
    for part in (0, 1):
        rolled = []
        for parity in (0, 1):
            one, other = PLACES[0][parity][part], PLACES[1][parity][part]
            shift = pick_by(flag, (one[0] - one[2]) % width, (other[0] - other[2]) % width)
            rolled.append(pltpu.roll(packed, shift, 1))
        parts.append(jnp.where(odd_row, rolled[1], rolled[0]))
    far = jnp.where(lane < pick_by(flag, *MIDDLES), *parts)
    return jnp.concatenate((packed, down(far, 1)), axis=0)


PACKED = DIAGS


def store_part(even, odd, flag, part_ref):
    bands = pack_far(dense_bands(even, odd, FAR_DIAGS), flag)
    for q, band in enumerate(bands):
        part_ref[q * PACKED : (q + 1) * PACKED, :] = band


def open_pairs(is_second, x, y, column_refs, other_ref):
    flag = on_odd_core()
    mine = [jnp.where(flag, b, a) for a, b in zip(x, y)]
    theirs = [jnp.where(flag, a, b) for a, b in zip(x, y)]
    for ref, value in zip(column_refs, mine + theirs):
        ref[...] = value
    store_part(*theirs, either(flag, among(is_second[0]), among(is_second[1])), other_ref)
    other_ref[4 * PACKED :, :] = jnp.zeros((WINDOW, theirs[0].shape[1]), jnp.float32)


def first_open(own_second, gets_second, is_second, even_ref, odd_ref, payload_ref, *refs):
    *column_refs, other_ref = refs
    own = even_ref[...], odd_ref[...]
    came = unpacked(payload_ref[...], own[0].shape[0], among(gets_second))
    flag = among(own_second)
    x = [jnp.where(flag, b, a) for a, b in zip(own, came)]
    y = [jnp.where(flag, a, b) for a, b in zip(own, came)]
    open_pairs(is_second, x, y, column_refs, other_ref)


def fused_open(picks, is_second, kept_ref, sent_ref, came0_ref, came1_ref, *refs):
    *column_refs, other_ref = refs
    arrays = [ref[...] for ref in (sent_ref, kept_ref, came0_ref, came1_ref)]
    blocks = [choose(pick, arrays) for pick in picks]
    x, y = split_pair(*blocks[:2]), split_pair(*blocks[2:])
    open_pairs(is_second, x, y, column_refs, other_ref)


def swapped_flag(is_second):
    x_swapped, y_swapped = halves_swapped(is_second)
    return either(on_odd_core(), y_swapped, x_swapped)


def own_second_flag(is_second):
    return either(on_odd_core(), among(is_second[1]), among(is_second[0]))


def bands_kernel(is_second, *refs):
    *column_refs, part_ref = refs
    columns = [ref[...] for ref in column_refs]
    store_part(*columns[:2], own_second_flag(is_second), part_ref)
    flag = on_odd_core()
    x = [jnp.where(flag, b, a) for a, b in zip(columns[:2], columns[2:])]
    y = [jnp.where(flag, a, b) for a, b in zip(columns[:2], columns[2:])]
    corner = cross_partial(*x, *y, among(is_second[0]), among(is_second[1]))
    part_ref[4 * PACKED :, :] = corner


def angles_kernel(is_second, *refs):
    *part_refs, found_ref = refs
    part = pair_sums([ref[...] for ref in part_refs])
    flag = own_second_flag(is_second)
    quadrants = [unpack_far(part[q * PACKED : (q + 1) * PACKED], flag) for q in range(4)]
    angles = angles_of(quadrants)
    bands = carried(quadrants, angles)
    for step, pair in enumerate(angles):
        for i in (0, 1):
            found_ref[2 * step + i : 2 * step + i + 1, :] = pair[i]
    spare = NEAR - 2 * JSTEPS
    found_ref[2 * JSTEPS : NEAR, :] = jnp.zeros((spare, part.shape[1]), jnp.float32)
    for q in range(4):
        found_ref[NEAR + q * DIAGS : NEAR + (q + 1) * DIAGS, :] = bands[q][:DIAGS]
    found_ref[CORNER:ROTATION, :] = part[4 * PACKED :]
    first_pair = jnp.logical_not(on_odd_core())
    found_ref[ROTATION:, :] = own_rotation(angles, flag, swapped_flag(is_second), first_pair)


CORNER = NEAR + 4 * DIAGS
ROTATION = CORNER + WINDOW
FOUND = ROTATION + 2 * WINDOW


def angles_in(found):
    return [(found[2 * i : 2 * i + 1], found[2 * i + 1 : 2 * i + 2]) for i in range(JSTEPS)]


def columns_kernel(is_second, even_ref, odd_ref, found_ref, *out_refs):
    angles = angles_in(found_ref[...])
    layout = in_pair(even_ref, swapped_flag(is_second))
    columns = turn_to(layout, even_ref[...], odd_ref[...], angles)
    for ref, value in zip(out_refs, columns):
        ref[...] = value


def next_bands(x_found, y_found, x_second, y_second):
    corner = x_found[CORNER:ROTATION] + y_found[CORNER:ROTATION]
    middle = cross_bands(corner, x_found[ROTATION:], y_found[ROTATION:])
    half = corner.shape[1] // 2
    lane = lanes_of(middle[0])
    diag = lax.broadcasted_iota(jnp.int32, middle[0].shape, 0)
    bands = []
    for q in range(4):
        rows = slice(NEAR + q * DIAGS, NEAR + (q + 1) * DIAGS)
        x, y = x_found[rows], y_found[rows]
        x = jnp.where(x_second, right(x, half), x)
        y = jnp.where(y_second, y, right(y, half))
        crossing = jnp.where(lane - diag < half, middle[q], y)
        bands.append(jnp.where(lane < half, x, crossing))
    return bands


def next_kernel(is_second, sends_first, layout_of, *refs):
    mine_even, mine_odd, even_ref, odd_ref, found_ref, other_ref, kept_ref, sent_ref = refs
    found, other = found_ref[...], other_ref[...]
    flag = on_odd_core()
    x_found, y_found = jnp.where(flag, other, found), jnp.where(flag, found, other)
    bands = next_bands(x_found, y_found, among(is_second[0]), among(is_second[1]))
    x_swapped, y_swapped = halves_swapped(is_second)
    swapped = either(flag, x_swapped, y_swapped)
    layout = in_pair(even_ref, swapped)
    theirs = turn_to(layout, even_ref[...], odd_ref[...], angles_in(other))
    low = line_lanes(found) < found.shape[1] // 2
    from_mine = jnp.logical_xor(low, flag)
    even = jnp.where(from_mine, mine_even[...], theirs[0])
    odd = jnp.where(from_mine, mine_odd[...], theirs[1])
    angles = angles_of(bands)
    first, second = turn_to(layout_of(even), even, odd, angles)
    flag = among(sends_first)
    kept_ref[...] = jnp.where(flag, second, first)
    sent_ref[...] = jnp.where(flag, first, second)


def pair_sums(arrays):
    while len(arrays) > 1:
        arrays = [arrays[i] + arrays[i + 1] for i in range(0, len(arrays), 2)]
    return arrays[0]


def swap(x, axis, mask):
    return lax.ppermute(x, axis, [(i, i ^ mask) for i in range(lax.axis_size(axis))])


def exchange_groups(x, axis, first_bit=0):
    count = lax.axis_size(axis).bit_length() - 1
    bits = [1 << b for b in range(count)]
    groups = [bits[:1]] + [bits[i : i + 2] for i in range(1, count, 2)]
    arrays = [x]
    for group in groups[first_bit:]:
        x = pair_sums(arrays)
        masks = [group[0]] if len(group) == 1 else [group[0], group[1], group[0] | group[1]]
        arrays = [x] + [swap(x, axis, mask) for mask in masks]
    return arrays


def call(kernel, shapes, *args):
    out = [jax.ShapeDtypeStruct(shape, jnp.float32) for shape in shapes]
    return pl.pallas_call(
        kernel,
        out_shape=out,
        compiler_params=pltpu.CompilerParams(vmem_limit_bytes=32 * 1024 * 1024),
    )(*args)


def two_rounds(opened, is_second, sends_first, layout_of):
    *columns, other = opened
    column, width = columns[0].shape, columns[0].shape[1]
    other = swap(other, "row", 1)
    bands = functools.partial(bands_kernel, is_second)
    (mine,) = call(bands, (other.shape,), *columns)
    (found,) = call(
        functools.partial(angles_kernel, is_second),
        ((FOUND, width),),
        *exchange_groups(mine + other, "row", 1),
    )
    other = swap(found, "row", 1)
    turn = functools.partial(columns_kernel, is_second)
    columns[:2] = call(turn, (column, column), *columns[:2], found)
    turn = functools.partial(next_kernel, is_second, sends_first, layout_of)
    return call(turn, (column, column), *columns, found, other)


def per_device(basis):
    rows, cols = basis.shape
    width = cols // 2
    pair_total = lax.axis_size("pair")
    column = (rows, width)
    opened = (column,) * 4 + ((4 * PACKED + WINDOW, width),)
    payload = (rows + rows * 2 * STRIP // width, width)

    sends, sends_second, gets_second, own_second, is_second = first_moves(pair_total)
    (sent,) = call(functools.partial(payload_kernel, sends_second), (payload,), basis)
    came = lax.ppermute(sent, "pair", sends)
    even, odd = call(open_kernel, (column, column), basis)
    opening = functools.partial(first_open, own_second, gets_second, is_second)
    arrays = call(opening, opened, even, odd, came)
    sends, sends_first, picks, next_second = fused_moves(pair_total)
    kept, sent = two_rounds(arrays, is_second, sends_first, in_blocks)

    came = [lax.ppermute(x, "pair", s) for x, s in zip((sent, kept), sends)]
    opening = functools.partial(fused_open, picks, next_second)
    arrays = call(opening, opened, kept, sent, *came)
    sends, sends_first, gets_first = last_moves(pair_total)
    kept, sent = two_rounds(arrays, next_second, sends_first, in_order)

    came = lax.ppermute(sent, "pair", sends)
    flag = among(gets_first)
    first = jnp.where(flag, came, kept)
    second = jnp.where(flag, kept, came)
    return jnp.concatenate((first, second), axis=1)


def solution(mesh):
    return jax.shard_map(
        per_device,
        mesh=mesh,
        in_specs=(P("row", "pair"),),
        out_specs=P("row", "pair"),
        check_vma=False,
    )
```

```python
import functools

import jax
import jax.numpy as jnp
import numpy as np
from jax import lax
from jax.experimental import pallas as pl
from jax.experimental.pallas import tpu as pltpu
from jax.sharding import PartitionSpec as P

ROUNDS = 4
JSTEPS = 6
REACH = 2 * (JSTEPS - 1) + 1
DIAGS = 16
FAR_DIAGS = 32
WINDOW = 32
NEAR = 16
STRIP = 16
BACK = 3


def tournament_order(pair_count):
    ordering = np.zeros(2 * pair_count, dtype=np.int64)
    ordering[0] = 0
    ordering[2] = 1
    for slot in range(2, pair_count):
        ordering[2 * slot] = 2 * (slot - 1)
    for slot in range(pair_count - 1):
        ordering[2 * slot + 1] = 2 * (slot + 1) + 1
    ordering[2 * pair_count - 1] = 2 * (pair_count - 1)
    return ordering


def host_of(pair, pair_total, round_index):
    if round_index % 2 == 0 or pair == 0:
        return pair
    return min(pair + 1, pair_total - 1) if pair % 2 else pair - 1


def last_moves(pair_total):
    ordering = tournament_order(pair_total)
    sends, sends_first, gets_first = [], set(), set()
    for pair in range(pair_total):
        target = host_of(pair, pair_total, ROUNDS)
        for place in (0, 1):
            old = int(ordering[2 * pair + place])
            source = host_of(old // 2, pair_total, ROUNDS - 1)
            if source == target:
                continue
            sends.append((source, target))
            if old % 2 == 0:
                sends_first.add(source)
            if place == 0:
                gets_first.add(target)
    assert len({s for s, _ in sends}) == len(sends) == len({t for _, t in sends})
    return sends, sends_first, gets_first


def first_moves(pair_total):
    ordering = tournament_order(pair_total)
    sends, sends_second, gets_second, own_second = [], set(), set(), set()
    seconds = (set(), set())
    for pair in range(pair_total):
        here = host_of(pair, pair_total, 1)
        for place in (0, 1):
            old = int(ordering[2 * pair + place])
            if old % 2:
                seconds[place].add(here)
            if old // 2 == here:
                if place:
                    own_second.add(here)
                continue
            sends.append((old // 2, here))
            if old % 2:
                sends_second.add(old // 2)
                gets_second.add(here)
    assert len({s for s, _ in sends}) == len(sends) == len({t for _, t in sends})
    return sends, sends_second, gets_second, own_second, seconds


def fused_moves(pair_total):
    ordering = tournament_order(pair_total)
    before, last = ROUNDS - 3, ROUNDS - 1
    needs, edges, seconds = {}, [], ({}, {})
    for pair in range(pair_total):
        here = host_of(pair, pair_total, last)
        needs[here] = []
        for place in (0, 1):
            source = int(ordering[2 * pair + place])
            seconds[place][here] = source % 2
            for half in (0, 1):
                old = int(ordering[2 * (source // 2) + half])
                there = host_of(old // 2, pair_total, before)
                needs[here].append((there, old % 2))
                if there != here:
                    edges.append((there, old % 2, here))
    turn, left_over = {}, list(edges)
    while left_over:
        source, _, target = left_over[0]
        start = source
        while True:
            for number, one, other in ((0, source, target), (1, target, source)):
                edge = next(e for e in left_over if (e[0], e[2]) == (one, other))
                turn[edge] = number
                left_over.remove(edge)
            if target == start:
                break
            ahead = [e[2] for e in left_over if e[0] == target]
            source, target = target, ahead[0]
    sends = [[(e[0], e[2]) for e in edges if turn[e] == i] for i in (0, 1)]
    for chosen in sends:
        assert len({a for a, _ in chosen}) == len({b for _, b in chosen}) == pair_total
    sends_first = {e[0] for e in edges if turn[e] == 0 and e[1] == 0}
    picks = []
    for slot in range(4):
        pick = {}
        for here in range(pair_total):
            there, half = needs[here][slot]
            if there == here:
                pick[here] = 0 if (half == 0) == (here in sends_first) else 1
            else:
                pick[here] = 2 + turn[(there, half, here)]
        picks.append(pick)
    is_second = [{h for h, place in table.items() if place} for table in seconds]
    return sends, sends_first, picks, is_second


def choose(pick, arrays):
    chosen = arrays[0]
    for number in range(1, len(arrays)):
        members = {here for here, value in pick.items() if value == number}
        if members:
            chosen = jnp.where(among(members), arrays[number], chosen)
    return chosen


def among(members):
    here = lax.axis_index("pair")
    return functools.reduce(
        jnp.logical_or, [here == member for member in sorted(members)], here < 0
    )


def left(x, by):
    width = x.shape[1]
    return pltpu.roll(x, (width - by) % width, 1) if by % width else x


def right(x, by):
    width = x.shape[1]
    return pltpu.roll(x, by % width, 1) if by % width else x


def down(x, by):
    return pltpu.roll(x, by % x.shape[0], 0)


def lanes_of(x):
    return lax.broadcasted_iota(jnp.int32, x.shape, 1)


def split_pair(first, second):
    half = first.shape[1] // 2
    low = lanes_of(first) < half
    even = jnp.where(low, first, right(second, half))
    odd = jnp.where(low, right(first, half), second)
    return even, odd


def take_lanes(x, source):
    if x.shape[0] == 1:
        return take_lanes(jnp.broadcast_to(x, (8, x.shape[1])), source)[:1]
    return jnp.take_along_axis(x, jnp.broadcast_to(source, x.shape), axis=1)


def line_lanes(x):
    return lax.broadcasted_iota(jnp.int32, (1, x.shape[1]), 1)


def separate(first, second):
    lane = line_lanes(first)
    half = first.shape[1] // 2
    low = lane < half
    source = 2 * jnp.where(low, lane, lane - half)
    return tuple(
        jnp.where(low, take_lanes(first, source + odd), take_lanes(second, source + odd))
        for odd in (0, 1)
    )


def backwards(x):
    return jnp.take_along_axis(x, x.shape[1] - 1 - lanes_of(x), axis=1)


def dense_bands(even, odd, diags):
    width = even.shape[1]
    gram = lax.dot_general(
        jnp.concatenate((even, odd), axis=1),
        jnp.concatenate((backwards(even), backwards(odd)), axis=1),
        (((0,), (0,)), ((), ())),
        precision=lax.Precision.HIGHEST,
        preferred_element_type=jnp.float32,
    )
    bands = []
    for near in (0, width):
        for far in (0, width):
            quadrant = gram[far : far + width, near : near + width]
            aligned = pltpu.roll(quadrant, 1, 1, stride=1, stride_axis=0)
            bands.append(jnp.transpose(aligned)[:diags])
    return bands


def store_bands(even, odd, band_ref, diags):
    for q, band in enumerate(dense_bands(even, odd, diags)):
        band_ref[q * diags : (q + 1) * diags, :] = band


def payload_kernel(sends_second, basis_ref, payload_ref):
    rows, cols = basis_ref.shape
    width = cols // 2
    half = width // 2
    first, second = basis_ref[:, :width], basis_ref[:, width:]
    lane = line_lanes(first)
    start = jnp.where(among(sends_second), half - STRIP, 0)
    place = start + jnp.where(lane < half, lane, lane - half)
    odd = jnp.where(lane < half, 0, 1)
    in_first = place < half
    source = 2 * jnp.where(in_first, place, place - half) + odd
    payload_ref[:rows] = jnp.where(in_first, take_lanes(first, source), take_lanes(second, source))
    group = rows * 2 * STRIP // width
    source = 2 * (start + lane % STRIP) + lane // STRIP % 2
    strips = jnp.zeros((group, width), jnp.float32)
    for i in range(rows // group):
        here = lane // (2 * STRIP) == i
        strips = jnp.where(here, take_lanes(second[i * group : (i + 1) * group], source), strips)
    payload_ref[rows:] = strips


def open_kernel(basis_ref, even_ref, odd_ref):
    width = basis_ref.shape[1] // 2
    even_ref[...], odd_ref[...] = separate(basis_ref[:, :width], basis_ref[:, width:])


def unpacked(payload, rows, second):
    width = payload.shape[1]
    half = width // 2
    lane = line_lanes(payload)
    main, strips = payload[:rows], payload[rows:]
    group = strips.shape[0]
    columns = []
    for j, x in enumerate((main, left(main, half))):
        ends = [right(strips, half - (2 * i + j) * STRIP) for i in range(rows // group)]
        x = jnp.where(lane < half, x, jnp.where(lane < half + STRIP, jnp.concatenate(ends), 0.0))
        columns.append(jnp.where(second, right(x, half - STRIP), x))
    return columns


def jacobi_angle(diag_even, diag_odd, coupling):
    spread = diag_even - diag_odd
    square = spread * spread + 4.0 * coupling * coupling
    inverse = lax.rsqrt(square)
    larger_square = (square * inverse + jnp.abs(spread)) * (0.5 * inverse)
    larger_inverse = lax.rsqrt(larger_square)
    larger = larger_square * larger_inverse
    smaller = coupling * inverse * larger_inverse
    forward = spread >= 0.0
    sign = jnp.where(coupling > 0.0, 1.0, jnp.where(coupling < 0.0, -1.0, 0.0))
    cosine = jnp.where(forward, larger, jnp.abs(smaller))
    sine_part = jnp.where(forward, smaller, sign * larger)
    return cosine, sine_part


def turn_bands(ee, eo, oe, oo, cosine, sine):
    cl, sl = jnp.broadcast_to(cosine, ee.shape), jnp.broadcast_to(sine, ee.shape)
    ck = pltpu.roll(cl, 0, 1, stride=1, stride_axis=0)
    sk = pltpu.roll(sl, 0, 1, stride=1, stride_axis=0)
    ee, oe = ck * ee + sk * oe, ck * oe - sk * ee
    eo, oo = ck * eo + sk * oo, ck * oo - sk * eo
    ee, eo = cl * ee + sl * eo, cl * eo - sl * ee
    oe, oo = cl * oe + sl * oo, cl * oo - sl * oe
    return ee, eo, oe, oo


def step_bands(ee, eo, oe, oo, cosine, sine):
    lane = lanes_of(ee)
    diag = lax.broadcasted_iota(jnp.int32, ee.shape, 0)
    last = lane == ee.shape[1] - 1
    on, next_on = diag == 0, diag == 1

    def slanted(x, by):
        if by >= 0:
            return pltpu.roll(x, by, 1, stride=1, stride_axis=0)
        return jnp.where(on, left(x, -by), down(slanted(x, 0), -by))

    def rotated(by, wanted):
        cl, sl = (jnp.broadcast_to(x, ee.shape) for x in (cosine, sine))
        ck, sk = (slanted(x, by) for x in (cl, sl))
        cl, sl, a, b, c, d = (right(x, by) for x in (cl, sl, ee, eo, oe, oo))
        a, c = ck * a + sk * c, ck * c - sk * a
        b, d = ck * b + sk * d, ck * d - sk * b
        found = {"ee": (a, b), "eo": (b, a), "oe": (c, d), "oo": (d, c)}
        return [
            cl * one + sl * two if name in ("ee", "oe") else cl * one - sl * two
            for name, (one, two) in found.items()
            if name in wanted
        ]

    ee_0, eo_0, oe_0, oo_0 = rotated(0, ("ee", "eo", "oe", "oo"))
    ee_r, eo_r, oe_r, oo_r = rotated(1, ("ee", "eo", "oe", "oo"))
    eo_l, oo_l = rotated(-1, ("eo", "oo"))

    near = down(jnp.where(on, eo_r, ee_r), 1)
    turned = jnp.where(on, oo_r, oe_r)
    ee_new = jnp.where(lane == diag + 1, turned, jnp.where(lane == diag, near, ee_r))
    ee_new = jnp.where(jnp.logical_and(on, lane == 0), ee_0, ee_new)

    eo_new = down(jnp.where(lane == diag - 1, oo_l, eo_l), -2)
    eo_new = jnp.where(lane == diag, down(eo_l, -1), eo_new)
    eo_new = jnp.where(last, down(ee_0, -1), eo_new)

    oo_new = jnp.where(last, jnp.where(on, ee_0, down(oe_0, 1)), oo_l)

    oe_new = down(oe_r, 2)
    oe_new = jnp.where(next_on, jnp.where(lane == diag, oo_0, eo_0), oe_new)
    oe_new = jnp.where(on, eo_new, oe_new)
    return ee_new, eo_new, oe_new, oo_new


def move_bands(ee, eo, oe, oo):
    lane = lanes_of(ee)
    diag = lax.broadcasted_iota(jnp.int32, ee.shape, 0)
    last = lane == ee.shape[1] - 1
    on, next_on = diag == 0, diag == 1

    near = down(jnp.where(on, eo, ee), 1)
    turned = jnp.where(on, oo, oe)
    mixed = jnp.where(lane == diag, turned, jnp.where(lane == diag - 1, near, ee))
    ee_new = jnp.where(jnp.logical_and(on, lane == 0), ee, right(mixed, 1))

    far = down(jnp.where(last, ee, eo), -1)
    mixed = down(jnp.where(lane == diag, oo, eo), -2)
    mixed = left(jnp.where(lane == diag + 1, far, mixed), 1)
    eo_new = jnp.where(last, far, mixed)

    oo_new = jnp.where(last, jnp.where(on, ee, down(oe, 1)), left(oo, 1))

    oe_new = right(down(oe, 2), 1)
    oe_new = jnp.where(next_on, jnp.where(lane == diag, oo, eo), oe_new)
    oe_new = jnp.where(on, eo_new, oe_new)
    return ee_new, eo_new, oe_new, oo_new


def move_bands_back(views, by):
    ee, eo, oe, oo = views[by]
    ee_left, _, oe_left, _ = views[by - 1]
    _, eo_right, _, oo_right = views[by + 1]
    width = ee.shape[1]
    lane = lanes_of(ee) - by
    lane = jnp.where(lane < 0, lane + width, jnp.where(lane >= width, lane - width, lane))
    diag = lax.broadcasted_iota(jnp.int32, ee.shape, 0)
    last, first = lane == width - 1, lane == diag
    on, next_on = diag == 0, diag == 1
    oo_up, eo_twice = down(oo, -1), down(eo_right, 2)

    far = jnp.where(first, down(ee_left, -1), ee_left)
    ee_old = jnp.where(jnp.logical_and(first, on), ee, far)
    ee_old = jnp.where(last, jnp.where(on, oo, down(eo, 1)), ee_old)

    near = jnp.where(jnp.logical_and(first, diag > 0), ee_left, down(oe_left, -2))
    eo_old = jnp.where(first, down(eo_right, 1), eo_twice)
    eo_old = jnp.where(on, jnp.where(last, oo_up, near), eo_old)
    eo_old = jnp.where(jnp.logical_and(next_on, lane > 1), oe, eo_old)
    eo_old = jnp.where(jnp.logical_and(on, first), far, eo_old)

    oe_old = jnp.where(on, eo_old, jnp.where(last, oo_up, near))

    oo_old = jnp.where(first, eo_twice, oo_right)
    oo_old = jnp.where(jnp.logical_and(next_on, first), oe, oo_old)
    oo_old = jnp.where(jnp.logical_and(on, first), ee_left, oo_old)
    return ee_old, eo_old, oe_old, oo_old


def bands_back(bands, count):
    views = {by: [right(x, by) for x in bands] for by in range(-count, count + 1)}
    for reach in reversed(range(count)):
        views = {by: move_bands_back(views, by) for by in range(-reach, reach + 1)}
    return views[0]


def move_columns(even, odd):
    lane = lanes_of(even)
    first, last = lane == 0, lane == even.shape[1] - 1
    even_new = jnp.where(first, even, right(jnp.where(first, odd, even), 1))
    odd_new = jnp.where(last, even, left(odd, 1))
    return even_new, odd_new


def in_pair(even, shifted=None):
    lane = line_lanes(even)
    if shifted is not None:
        half = even.shape[1] // 2
        lane = jnp.where(shifted, jnp.where(lane < half, lane + half, lane - half), lane)
    return (lane < 0, lane), (lane >= 0, lane)


def in_blocks(even):
    lane, half = line_lanes(even), even.shape[1] // 2
    place = jnp.where(lane < half, lane, lane - half)
    return (lane >= half, place), (lane >= half, place + half)


def in_order(even):
    lane, half = line_lanes(even), even.shape[1] // 2
    return (lane % 2 == 1, lane // 2), (lane % 2 == 1, lane // 2 + half)


def turn_to(layout, even, odd, angles):
    for cosine, sine in angles[:-1]:
        even, odd = cosine * even + sine * odd, cosine * odd - sine * even
        even, odd = move_columns(even, odd)
    by, end = JSTEPS - 1, even.shape[1] - 1
    results = []
    for is_odd, place in layout:
        stayed = place <= end - by
        from_even = jnp.where(stayed, place + by, 2 * end + 1 - by - place)
        from_even = jnp.where(place == 0, 0, from_even)
        source = jnp.where(is_odd, jnp.abs(place - by), from_even)
        is_even = jnp.logical_or(
            jnp.logical_and(is_odd, place < by),
            jnp.logical_and(jnp.logical_not(is_odd), stayed),
        )
        cosine, sine = (take_lanes(x, source) for x in angles[-1])
        by_even = jnp.where(is_even, cosine, -sine)
        by_odd = jnp.where(is_even, sine, cosine)
        results.append(by_even * take_lanes(even, source) + by_odd * take_lanes(odd, source))
    return results


def trim(bands, reach):
    rows = min(bands[0].shape[0], -(-(reach + 1) // 8) * 8)
    return [band[:rows] for band in bands]


def angles_of(bands):
    angles = []
    for step in range(JSTEPS):
        ee, eo, oe, oo = bands = trim(bands, 2 * (JSTEPS - 1 - step))
        angles.append(jacobi_angle(ee[0:1], oo[0:1], eo[0:1]))
        if step < JSTEPS - 1:
            bands = step_bands(*bands, *angles[-1])
    return angles


def carried(bands, angles):
    ahead = 2 * (JSTEPS - 1)
    for step, (cosine, sine) in enumerate(angles):
        bands = turn_bands(*trim(bands, 3 * ahead - 2 * step), cosine, sine)
        if step < JSTEPS - 1:
            bands = move_bands(*bands)
    done = 0
    while done < JSTEPS - 1:
        count = min(BACK, JSTEPS - 1 - done)
        bands = bands_back(trim(bands, 2 * (ahead - done)), count)
        done += count
    return bands


def near_starts(width):
    half = width // 2
    reach = REACH - 1
    return (half - 2 * reach, width - WINDOW), (0, half - reach)


def cross_partial(x_even, x_odd, y_even, y_odd, x_second, y_second):
    rows, width = x_even.shape
    x_starts, y_starts = near_starts(width)
    lane = lanes_of(x_even)

    def window(even, odd, flag, starts):
        start = jnp.where(flag, starts[1], starts[0])
        at_zero = pltpu.roll(even, (width - start) % width, 1)
        at_next = pltpu.roll(odd, (width - start + WINDOW) % width, 1)
        return jnp.where(lane < WINDOW, at_zero, jnp.where(lane < 2 * WINDOW, at_next, 0.0))

    corner = lax.dot_general(
        window(y_even, y_odd, y_second, y_starts),
        window(x_even, x_odd, x_second, x_starts),
        (((0,), (0,)), ((), ())),
        precision=lax.Precision.HIGHEST,
        preferred_element_type=jnp.float32,
    )
    low = lax.broadcasted_iota(jnp.int32, (WINDOW, width), 1) < 2 * WINDOW
    return jnp.where(low, corner[:WINDOW], right(corner[WINDOW : 2 * WINDOW], 2 * WINDOW))


def own_rotation(angles, second, swapped, first_pair):
    width = angles[0][0].shape[1]
    half = width // 2
    x_starts, y_starts = near_starts(width)
    starts = [jnp.where(first_pair, x, y) for x, y in zip(x_starts, y_starts)]
    shape = (2 * WINDOW, width)
    row = lax.broadcasted_iota(jnp.int32, shape, 0)
    lane = lax.broadcasted_iota(jnp.int32, shape, 1) - jnp.where(second, starts[1], starts[0])
    even, odd = (
        jnp.where(jnp.logical_and(row == lane + at, row // WINDOW == at // WINDOW), 1.0, 0.0)
        for at in (0, WINDOW)
    )
    even, odd = turn_to(in_pair(even, swapped), even, odd, angles)
    low = lax.broadcasted_iota(jnp.int32, shape, 1) < half
    return jnp.where(jnp.logical_xor(low, first_pair), right(odd, half), even)


def cross_bands(packed, x_rotation, y_rotation):
    width = packed.shape[1]
    half = width // 2
    corner = jnp.concatenate((packed[:, :half], right(packed, half)[:, :half]), axis=0)
    highest = dict(precision=lax.Precision.HIGHEST, preferred_element_type=jnp.float32)
    turned_x = jnp.dot(corner, x_rotation, **highest)
    ends = lax.dot_general(turned_x, y_rotation, (((0,), (0,)), ((), ())), **highest)
    even, odd = ends[half - NEAR : half], ends[width - NEAR :]
    quadrants = (even, right(even, half), odd, right(odd, half))
    offset = lanes_of(even) - lax.broadcasted_iota(jnp.int32, even.shape, 0) - (half - NEAR)
    diag = lax.broadcasted_iota(jnp.int32, (DIAGS, width), 0)
    bands = [jnp.zeros((DIAGS, width), jnp.float32) for _ in quadrants]
    for d in range(1, REACH):
        here = offset == d
        for q, quadrant in enumerate(quadrants):
            line = jnp.sum(jnp.where(here, quadrant, 0.0), axis=0, keepdims=True)
            bands[q] = jnp.where(diag == d, line, bands[q])
    return bands


def either(flag, one, other):
    return jnp.logical_or(jnp.logical_and(flag, one), jnp.logical_and(jnp.logical_not(flag), other))


def halves_swapped(is_second):
    return among(is_second[0]), jnp.logical_not(among(is_second[1]))


def on_odd_core():
    return lax.axis_index("row") % 2 == 1


PLACES = (
    (((16, 16, 80), (60, 16, 108)), ((16, 28, 21), (44, 30, 80))),
    (((68, 16, 24), (112, 16, 0)), ((70, 29, 84), (99, 29, 10))),
)
MIDDLES = (44, 99)


def pick_by(flag, one, other):
    return jnp.where(flag, other, one)


def pack_far(bands, flag):
    width = bands[0].shape[1]
    lane = lax.broadcasted_iota(jnp.int32, (DIAGS, width), 1)
    odd_row = lax.broadcasted_iota(jnp.int32, (DIAGS, width), 0) % 2 == 1
    moves = []
    for parity in (0, 1):
        for part in (0, 1):
            one, other = PLACES[0][parity][part], PLACES[1][parity][part]
            shift = pick_by(flag, (one[2] - one[0]) % width, (other[2] - other[0]) % width)
            start = pick_by(flag, one[2], other[2])
            count = pick_by(flag, one[1], other[1])
            here = jnp.logical_and(lane >= start, lane < start + count)
            moves.append((shift, jnp.logical_and(here, odd_row == (parity == 1))))
    packed = []
    for band in bands:
        near, far = band[:DIAGS], down(band[DIAGS:], -1)
        for shift, here in moves:
            near = jnp.where(here, pltpu.roll(far, shift, 1), near)
        packed.append(near)
    return packed


def unpack_far(packed, flag):
    width = packed.shape[1]
    lane = lanes_of(packed)
    odd_row = lax.broadcasted_iota(jnp.int32, packed.shape, 0) % 2 == 1
    parts = []
    for part in (0, 1):
        rolled = []
        for parity in (0, 1):
            one, other = PLACES[0][parity][part], PLACES[1][parity][part]
            shift = pick_by(flag, (one[0] - one[2]) % width, (other[0] - other[2]) % width)
            rolled.append(pltpu.roll(packed, shift, 1))
        parts.append(jnp.where(odd_row, rolled[1], rolled[0]))
    far = jnp.where(lane < pick_by(flag, *MIDDLES), *parts)
    return jnp.concatenate((packed, down(far, 1)), axis=0)


PACKED = DIAGS


def store_part(even, odd, flag, part_ref):
    bands = pack_far(dense_bands(even, odd, FAR_DIAGS), flag)
    for q, band in enumerate(bands):
        part_ref[q * PACKED : (q + 1) * PACKED, :] = band


def open_pairs(is_second, x, y, column_refs, corner_ref, other_ref):
    corner = cross_partial(*x, *y, among(is_second[0]), among(is_second[1]))
    flag = on_odd_core()
    mine = [jnp.where(flag, b, a) for a, b in zip(x, y)]
    theirs = [jnp.where(flag, a, b) for a, b in zip(x, y)]
    for ref, value in zip(column_refs, mine + theirs):
        ref[...] = value
    store_part(*theirs, either(flag, among(is_second[0]), among(is_second[1])), other_ref)
    corner_ref[...] = jnp.where(flag, corner[NEAR:], corner[:NEAR])
    other_ref[4 * PACKED :, :] = jnp.where(flag, corner[:NEAR], corner[NEAR:])


def first_open(own_second, gets_second, is_second, even_ref, odd_ref, payload_ref, *refs):
    *column_refs, corner_ref, other_ref = refs
    own = even_ref[...], odd_ref[...]
    came = unpacked(payload_ref[...], own[0].shape[0], among(gets_second))
    flag = among(own_second)
    x = [jnp.where(flag, b, a) for a, b in zip(own, came)]
    y = [jnp.where(flag, a, b) for a, b in zip(own, came)]
    open_pairs(is_second, x, y, column_refs, corner_ref, other_ref)


def fused_open(picks, is_second, kept_ref, sent_ref, came0_ref, came1_ref, *refs):
    *column_refs, corner_ref, other_ref = refs
    arrays = [ref[...] for ref in (sent_ref, kept_ref, came0_ref, came1_ref)]
    blocks = [choose(pick, arrays) for pick in picks]
    x, y = split_pair(*blocks[:2]), split_pair(*blocks[2:])
    open_pairs(is_second, x, y, column_refs, corner_ref, other_ref)


def swapped_flag(is_second):
    x_swapped, y_swapped = halves_swapped(is_second)
    return either(on_odd_core(), y_swapped, x_swapped)


def own_second_flag(is_second):
    return either(on_odd_core(), among(is_second[1]), among(is_second[0]))


def bands_kernel(is_second, even_ref, odd_ref, corner_ref, part_ref):
    store_part(even_ref[...], odd_ref[...], own_second_flag(is_second), part_ref)
    part_ref[4 * PACKED :, :] = corner_ref[...]


def angles_kernel(is_second, *refs):
    *part_refs, found_ref = refs
    part = pair_sums([ref[...] for ref in part_refs])
    flag = own_second_flag(is_second)
    quadrants = [unpack_far(part[q * PACKED : (q + 1) * PACKED], flag) for q in range(4)]
    angles = angles_of(quadrants)
    bands = carried(quadrants, angles)
    for step, pair in enumerate(angles):
        for i in (0, 1):
            found_ref[2 * step + i : 2 * step + i + 1, :] = pair[i]
    spare = NEAR - 2 * JSTEPS
    found_ref[2 * JSTEPS : NEAR, :] = jnp.zeros((spare, part.shape[1]), jnp.float32)
    for q in range(4):
        found_ref[NEAR + q * DIAGS : NEAR + (q + 1) * DIAGS, :] = bands[q][:DIAGS]
    found_ref[CORNER:ROTATION, :] = part[4 * PACKED :]
    first_pair = jnp.logical_not(on_odd_core())
    found_ref[ROTATION:, :] = own_rotation(angles, flag, swapped_flag(is_second), first_pair)


CORNER = NEAR + 4 * DIAGS
ROTATION = CORNER + NEAR
FOUND = ROTATION + 2 * WINDOW


def angles_in(found):
    return [(found[2 * i : 2 * i + 1], found[2 * i + 1 : 2 * i + 2]) for i in range(JSTEPS)]


def columns_kernel(is_second, even_ref, odd_ref, found_ref, *out_refs):
    angles = angles_in(found_ref[...])
    layout = in_pair(even_ref, swapped_flag(is_second))
    columns = turn_to(layout, even_ref[...], odd_ref[...], angles)
    for ref, value in zip(out_refs, columns):
        ref[...] = value


def next_bands(x_found, y_found, x_second, y_second):
    corner = jnp.concatenate((x_found[CORNER:ROTATION], y_found[CORNER:ROTATION]), axis=0)
    middle = cross_bands(corner, x_found[ROTATION:], y_found[ROTATION:])
    half = corner.shape[1] // 2
    lane = lanes_of(middle[0])
    diag = lax.broadcasted_iota(jnp.int32, middle[0].shape, 0)
    bands = []
    for q in range(4):
        rows = slice(NEAR + q * DIAGS, NEAR + (q + 1) * DIAGS)
        x, y = x_found[rows], y_found[rows]
        x = jnp.where(x_second, right(x, half), x)
        y = jnp.where(y_second, y, right(y, half))
        crossing = jnp.where(lane - diag < half, middle[q], y)
        bands.append(jnp.where(lane < half, x, crossing))
    return bands


def next_kernel(is_second, sends_first, layout_of, *refs):
    mine_even, mine_odd, even_ref, odd_ref, found_ref, other_ref, kept_ref, sent_ref = refs
    found, other = found_ref[...], other_ref[...]
    flag = on_odd_core()
    x_found, y_found = jnp.where(flag, other, found), jnp.where(flag, found, other)
    bands = next_bands(x_found, y_found, among(is_second[0]), among(is_second[1]))
    x_swapped, y_swapped = halves_swapped(is_second)
    swapped = either(flag, x_swapped, y_swapped)
    layout = in_pair(even_ref, swapped)
    theirs = turn_to(layout, even_ref[...], odd_ref[...], angles_in(other))
    low = line_lanes(found) < found.shape[1] // 2
    from_mine = jnp.logical_xor(low, flag)
    even = jnp.where(from_mine, mine_even[...], theirs[0])
    odd = jnp.where(from_mine, mine_odd[...], theirs[1])
    angles = angles_of(bands)
    first, second = turn_to(layout_of(even), even, odd, angles)
    flag = among(sends_first)
    kept_ref[...] = jnp.where(flag, second, first)
    sent_ref[...] = jnp.where(flag, first, second)


def pair_sums(arrays):
    while len(arrays) > 1:
        arrays = [arrays[i] + arrays[i + 1] for i in range(0, len(arrays), 2)]
    return arrays[0]


def swap(x, axis, mask):
    return lax.ppermute(x, axis, [(i, i ^ mask) for i in range(lax.axis_size(axis))])


def exchange_groups(x, axis, first_bit=0):
    count = lax.axis_size(axis).bit_length() - 1
    bits = [1 << b for b in range(count)]
    groups = [bits[:1]] + [bits[i : i + 2] for i in range(1, count, 2)]
    arrays = [x]
    for group in groups[first_bit:]:
        x = pair_sums(arrays)
        masks = [group[0]] if len(group) == 1 else [group[0], group[1], group[0] | group[1]]
        arrays = [x] + [swap(x, axis, mask) for mask in masks]
    return arrays


def call(kernel, shapes, *args):
    out = [jax.ShapeDtypeStruct(shape, jnp.float32) for shape in shapes]
    return pl.pallas_call(
        kernel,
        out_shape=out,
        compiler_params=pltpu.CompilerParams(vmem_limit_bytes=32 * 1024 * 1024),
    )(*args)


def two_rounds(opened, is_second, sends_first, layout_of):
    *columns, corner, other = opened
    column, width = columns[0].shape, columns[0].shape[1]
    other = swap(other, "row", 1)
    bands = functools.partial(bands_kernel, is_second)
    (mine,) = call(bands, (other.shape,), *columns[:2], corner)
    (found,) = call(
        functools.partial(angles_kernel, is_second),
        ((FOUND, width),),
        *exchange_groups(mine + other, "row", 1),
    )
    other = swap(found, "row", 1)
    turn = functools.partial(columns_kernel, is_second)
    columns[:2] = call(turn, (column, column), *columns[:2], found)
    turn = functools.partial(next_kernel, is_second, sends_first, layout_of)
    return call(turn, (column, column), *columns, found, other)


def per_device(basis):
    rows, cols = basis.shape
    width = cols // 2
    pair_total = lax.axis_size("pair")
    column = (rows, width)
    opened = (column,) * 4 + ((NEAR, width), (4 * PACKED + NEAR, width))
    payload = (rows + rows * 2 * STRIP // width, width)

    sends, sends_second, gets_second, own_second, is_second = first_moves(pair_total)
    (sent,) = call(functools.partial(payload_kernel, sends_second), (payload,), basis)
    came = lax.ppermute(sent, "pair", sends)
    even, odd = call(open_kernel, (column, column), basis)
    opening = functools.partial(first_open, own_second, gets_second, is_second)
    arrays = call(opening, opened, even, odd, came)
    sends, sends_first, picks, next_second = fused_moves(pair_total)
    kept, sent = two_rounds(arrays, is_second, sends_first, in_blocks)

    came = [lax.ppermute(x, "pair", s) for x, s in zip((sent, kept), sends)]
    opening = functools.partial(fused_open, picks, next_second)
    arrays = call(opening, opened, kept, sent, *came)
    sends, sends_first, gets_first = last_moves(pair_total)
    kept, sent = two_rounds(arrays, next_second, sends_first, in_order)

    came = lax.ppermute(sent, "pair", sends)
    flag = among(gets_first)
    first = jnp.where(flag, came, kept)
    second = jnp.where(flag, kept, came)
    return jnp.concatenate((first, second), axis=1)


def solution(mesh):
    return jax.shard_map(
        per_device,
        mesh=mesh,
        in_specs=(P("row", "pair"),),
        out_specs=P("row", "pair"),
        check_vma=False,
    )
```

```python
import functools

import jax
import jax.numpy as jnp
import numpy as np
from jax import lax
from jax.experimental import pallas as pl
from jax.experimental.pallas import tpu as pltpu
from jax.sharding import PartitionSpec as P

ROUNDS = 4
JSTEPS = 6
REACH = 2 * (JSTEPS - 1) + 1
DIAGS = 16
FAR_DIAGS = 32
WINDOW = 32
NEAR = 16
STRIP = 16
BACK = 3


def tournament_order(pair_count):
    ordering = np.zeros(2 * pair_count, dtype=np.int64)
    ordering[0] = 0
    ordering[2] = 1
    for slot in range(2, pair_count):
        ordering[2 * slot] = 2 * (slot - 1)
    for slot in range(pair_count - 1):
        ordering[2 * slot + 1] = 2 * (slot + 1) + 1
    ordering[2 * pair_count - 1] = 2 * (pair_count - 1)
    return ordering


def host_of(pair, pair_total, round_index):
    if round_index % 2 == 0 or pair == 0:
        return pair
    return min(pair + 1, pair_total - 1) if pair % 2 else pair - 1


def last_moves(pair_total):
    ordering = tournament_order(pair_total)
    sends, sends_first, gets_first = [], set(), set()
    for pair in range(pair_total):
        target = host_of(pair, pair_total, ROUNDS)
        for place in (0, 1):
            old = int(ordering[2 * pair + place])
            source = host_of(old // 2, pair_total, ROUNDS - 1)
            if source == target:
                continue
            sends.append((source, target))
            if old % 2 == 0:
                sends_first.add(source)
            if place == 0:
                gets_first.add(target)
    assert len({s for s, _ in sends}) == len(sends) == len({t for _, t in sends})
    return sends, sends_first, gets_first


def first_moves(pair_total):
    ordering = tournament_order(pair_total)
    sends, sends_second, gets_second, own_second = [], set(), set(), set()
    seconds = (set(), set())
    for pair in range(pair_total):
        here = host_of(pair, pair_total, 1)
        for place in (0, 1):
            old = int(ordering[2 * pair + place])
            if old % 2:
                seconds[place].add(here)
            if old // 2 == here:
                if place:
                    own_second.add(here)
                continue
            sends.append((old // 2, here))
            if old % 2:
                sends_second.add(old // 2)
                gets_second.add(here)
    assert len({s for s, _ in sends}) == len(sends) == len({t for _, t in sends})
    return sends, sends_second, gets_second, own_second, seconds


def fused_moves(pair_total):
    ordering = tournament_order(pair_total)
    before, last = ROUNDS - 3, ROUNDS - 1
    needs, edges, seconds = {}, [], ({}, {})
    for pair in range(pair_total):
        here = host_of(pair, pair_total, last)
        needs[here] = []
        for place in (0, 1):
            source = int(ordering[2 * pair + place])
            seconds[place][here] = source % 2
            for half in (0, 1):
                old = int(ordering[2 * (source // 2) + half])
                there = host_of(old // 2, pair_total, before)
                needs[here].append((there, old % 2))
                if there != here:
                    edges.append((there, old % 2, here))
    turn, left_over = {}, list(edges)
    while left_over:
        start = source = min(e[0] for e in left_over)
        target, number = min(e[2] for e in left_over if e[0] == source), 1
        while True:
            for one, other in ((source, target), (target, source)):
                edge = next(e for e in left_over if (e[0], e[2]) == (one, other))
                turn[edge] = number
                left_over.remove(edge)
            if target == start:
                break
            source, number = target, 1 - number
            target = next(e[2] for e in left_over if e[0] == source)
    sends = [[(e[0], e[2]) for e in edges if turn[e] == i] for i in (0, 1)]
    for chosen in sends:
        assert len({a for a, _ in chosen}) == len({b for _, b in chosen}) == pair_total
    sends_first = {e[0] for e in edges if turn[e] == 0 and e[1] == 0}
    picks = []
    for slot in range(4):
        pick = {}
        for here in range(pair_total):
            there, half = needs[here][slot]
            if there == here:
                pick[here] = 0 if (half == 0) == (here in sends_first) else 1
            else:
                pick[here] = 2 + turn[(there, half, here)]
        picks.append(pick)
    is_second = [{h for h, place in table.items() if place} for table in seconds]
    return sends, sends_first, picks, is_second


def choose(pick, arrays):
    chosen = arrays[0]
    for number in range(1, len(arrays)):
        members = {here for here, value in pick.items() if value == number}
        if members:
            chosen = jnp.where(among(members), arrays[number], chosen)
    return chosen


def among(members):
    here = lax.axis_index("pair")
    return functools.reduce(
        jnp.logical_or, [here == member for member in sorted(members)], here < 0
    )


def left(x, by):
    width = x.shape[1]
    return pltpu.roll(x, (width - by) % width, 1) if by % width else x


def right(x, by):
    width = x.shape[1]
    return pltpu.roll(x, by % width, 1) if by % width else x


def down(x, by):
    return pltpu.roll(x, by % x.shape[0], 0)


def lanes_of(x):
    return lax.broadcasted_iota(jnp.int32, x.shape, 1)


def split_pair(first, second):
    half = first.shape[1] // 2
    low = lanes_of(first) < half
    even = jnp.where(low, first, right(second, half))
    odd = jnp.where(low, right(first, half), second)
    return even, odd


def take_lanes(x, source):
    if x.shape[0] == 1:
        return take_lanes(jnp.broadcast_to(x, (8, x.shape[1])), source)[:1]
    return jnp.take_along_axis(x, jnp.broadcast_to(source, x.shape), axis=1)


def line_lanes(x):
    return lax.broadcasted_iota(jnp.int32, (1, x.shape[1]), 1)


def separate(first, second):
    lane = line_lanes(first)
    half = first.shape[1] // 2
    low = lane < half
    source = 2 * jnp.where(low, lane, lane - half)
    return tuple(
        jnp.where(low, take_lanes(first, source + odd), take_lanes(second, source + odd))
        for odd in (0, 1)
    )


def backwards(x):
    return jnp.take_along_axis(x, x.shape[1] - 1 - lanes_of(x), axis=1)


def dense_bands(even, odd, diags):
    width = even.shape[1]
    gram = lax.dot_general(
        jnp.concatenate((even, odd), axis=1),
        jnp.concatenate((backwards(even), backwards(odd)), axis=1),
        (((0,), (0,)), ((), ())),
        precision=lax.Precision.HIGHEST,
        preferred_element_type=jnp.float32,
    )
    bands = []
    for near in (0, width):
        for far in (0, width):
            quadrant = gram[far : far + width, near : near + width]
            aligned = pltpu.roll(quadrant, 1, 1, stride=1, stride_axis=0)
            bands.append(jnp.transpose(aligned)[:diags])
    return bands


def store_bands(even, odd, band_ref, diags):
    for q, band in enumerate(dense_bands(even, odd, diags)):
        band_ref[q * diags : (q + 1) * diags, :] = band


def payload_kernel(sends_second, basis_ref, payload_ref):
    rows, cols = basis_ref.shape
    width = cols // 2
    half = width // 2
    first, second = basis_ref[:, :width], basis_ref[:, width:]
    lane = line_lanes(first)
    start = jnp.where(among(sends_second), half - STRIP, 0)
    place = start + jnp.where(lane < half, lane, lane - half)
    odd = jnp.where(lane < half, 0, 1)
    in_first = place < half
    source = 2 * jnp.where(in_first, place, place - half) + odd
    payload_ref[:rows] = jnp.where(in_first, take_lanes(first, source), take_lanes(second, source))
    group = rows * 2 * STRIP // width
    source = 2 * (start + lane % STRIP) + lane // STRIP % 2
    strips = jnp.zeros((group, width), jnp.float32)
    for i in range(rows // group):
        here = lane // (2 * STRIP) == i
        strips = jnp.where(here, take_lanes(second[i * group : (i + 1) * group], source), strips)
    payload_ref[rows:] = strips


def open_kernel(basis_ref, even_ref, odd_ref):
    width = basis_ref.shape[1] // 2
    even_ref[...], odd_ref[...] = separate(basis_ref[:, :width], basis_ref[:, width:])


def unpacked(payload, rows, second):
    width = payload.shape[1]
    half = width // 2
    lane = line_lanes(payload)
    main, strips = payload[:rows], payload[rows:]
    group = strips.shape[0]
    columns = []
    for j, x in enumerate((main, left(main, half))):
        ends = [right(strips, half - (2 * i + j) * STRIP) for i in range(rows // group)]
        x = jnp.where(lane < half, x, jnp.where(lane < half + STRIP, jnp.concatenate(ends), 0.0))
        columns.append(jnp.where(second, right(x, half - STRIP), x))
    return columns


def jacobi_angle(diag_even, diag_odd, coupling):
    spread = diag_even - diag_odd
    square = spread * spread + 4.0 * coupling * coupling
    inverse = lax.rsqrt(square)
    larger_square = (square * inverse + jnp.abs(spread)) * (0.5 * inverse)
    larger_inverse = lax.rsqrt(larger_square)
    larger = larger_square * larger_inverse
    smaller = coupling * inverse * larger_inverse
    forward = spread >= 0.0
    sign = jnp.where(coupling > 0.0, 1.0, jnp.where(coupling < 0.0, -1.0, 0.0))
    cosine = jnp.where(forward, larger, jnp.abs(smaller))
    sine_part = jnp.where(forward, smaller, sign * larger)
    return cosine, sine_part


def turn_bands(ee, eo, oe, oo, cosine, sine):
    cl, sl = jnp.broadcast_to(cosine, ee.shape), jnp.broadcast_to(sine, ee.shape)
    ck = pltpu.roll(cl, 0, 1, stride=1, stride_axis=0)
    sk = pltpu.roll(sl, 0, 1, stride=1, stride_axis=0)
    ee, oe = ck * ee + sk * oe, ck * oe - sk * ee
    eo, oo = ck * eo + sk * oo, ck * oo - sk * eo
    ee, eo = cl * ee + sl * eo, cl * eo - sl * ee
    oe, oo = cl * oe + sl * oo, cl * oo - sl * oe
    return ee, eo, oe, oo


def step_bands(ee, eo, oe, oo, cosine, sine):
    lane = lanes_of(ee)
    diag = lax.broadcasted_iota(jnp.int32, ee.shape, 0)
    last = lane == ee.shape[1] - 1
    on, next_on = diag == 0, diag == 1

    def slanted(x, by):
        if by >= 0:
            return pltpu.roll(x, by, 1, stride=1, stride_axis=0)
        return jnp.where(on, left(x, -by), down(slanted(x, 0), -by))

    def rotated(by, wanted):
        cl, sl = (jnp.broadcast_to(x, ee.shape) for x in (cosine, sine))
        ck, sk = (slanted(x, by) for x in (cl, sl))
        cl, sl, a, b, c, d = (right(x, by) for x in (cl, sl, ee, eo, oe, oo))
        a, c = ck * a + sk * c, ck * c - sk * a
        b, d = ck * b + sk * d, ck * d - sk * b
        found = {"ee": (a, b), "eo": (b, a), "oe": (c, d), "oo": (d, c)}
        return [
            cl * one + sl * two if name in ("ee", "oe") else cl * one - sl * two
            for name, (one, two) in found.items()
            if name in wanted
        ]

    ee_0, eo_0, oe_0, oo_0 = rotated(0, ("ee", "eo", "oe", "oo"))
    ee_r, eo_r, oe_r, oo_r = rotated(1, ("ee", "eo", "oe", "oo"))
    eo_l, oo_l = rotated(-1, ("eo", "oo"))

    near = down(jnp.where(on, eo_r, ee_r), 1)
    turned = jnp.where(on, oo_r, oe_r)
    ee_new = jnp.where(lane == diag + 1, turned, jnp.where(lane == diag, near, ee_r))
    ee_new = jnp.where(jnp.logical_and(on, lane == 0), ee_0, ee_new)

    eo_new = down(jnp.where(lane == diag - 1, oo_l, eo_l), -2)
    eo_new = jnp.where(lane == diag, down(eo_l, -1), eo_new)
    eo_new = jnp.where(last, down(ee_0, -1), eo_new)

    oo_new = jnp.where(last, jnp.where(on, ee_0, down(oe_0, 1)), oo_l)

    oe_new = down(oe_r, 2)
    oe_new = jnp.where(next_on, jnp.where(lane == diag, oo_0, eo_0), oe_new)
    oe_new = jnp.where(on, eo_new, oe_new)
    return ee_new, eo_new, oe_new, oo_new


def move_bands(ee, eo, oe, oo):
    lane = lanes_of(ee)
    diag = lax.broadcasted_iota(jnp.int32, ee.shape, 0)
    last = lane == ee.shape[1] - 1
    on, next_on = diag == 0, diag == 1

    near = down(jnp.where(on, eo, ee), 1)
    turned = jnp.where(on, oo, oe)
    mixed = jnp.where(lane == diag, turned, jnp.where(lane == diag - 1, near, ee))
    ee_new = jnp.where(jnp.logical_and(on, lane == 0), ee, right(mixed, 1))

    far = down(jnp.where(last, ee, eo), -1)
    mixed = down(jnp.where(lane == diag, oo, eo), -2)
    mixed = left(jnp.where(lane == diag + 1, far, mixed), 1)
    eo_new = jnp.where(last, far, mixed)

    oo_new = jnp.where(last, jnp.where(on, ee, down(oe, 1)), left(oo, 1))

    oe_new = right(down(oe, 2), 1)
    oe_new = jnp.where(next_on, jnp.where(lane == diag, oo, eo), oe_new)
    oe_new = jnp.where(on, eo_new, oe_new)
    return ee_new, eo_new, oe_new, oo_new


def move_bands_back(views, by):
    ee, eo, oe, oo = views[by]
    ee_left, _, oe_left, _ = views[by - 1]
    _, eo_right, _, oo_right = views[by + 1]
    width = ee.shape[1]
    lane = lanes_of(ee) - by
    lane = jnp.where(lane < 0, lane + width, jnp.where(lane >= width, lane - width, lane))
    diag = lax.broadcasted_iota(jnp.int32, ee.shape, 0)
    last, first = lane == width - 1, lane == diag
    on, next_on = diag == 0, diag == 1
    oo_up, eo_twice = down(oo, -1), down(eo_right, 2)

    far = jnp.where(first, down(ee_left, -1), ee_left)
    ee_old = jnp.where(jnp.logical_and(first, on), ee, far)
    ee_old = jnp.where(last, jnp.where(on, oo, down(eo, 1)), ee_old)

    near = jnp.where(jnp.logical_and(first, diag > 0), ee_left, down(oe_left, -2))
    eo_old = jnp.where(first, down(eo_right, 1), eo_twice)
    eo_old = jnp.where(on, jnp.where(last, oo_up, near), eo_old)
    eo_old = jnp.where(jnp.logical_and(next_on, lane > 1), oe, eo_old)
    eo_old = jnp.where(jnp.logical_and(on, first), far, eo_old)

    oe_old = jnp.where(on, eo_old, jnp.where(last, oo_up, near))

    oo_old = jnp.where(first, eo_twice, oo_right)
    oo_old = jnp.where(jnp.logical_and(next_on, first), oe, oo_old)
    oo_old = jnp.where(jnp.logical_and(on, first), ee_left, oo_old)
    return ee_old, eo_old, oe_old, oo_old


def bands_back(bands, count):
    views = {by: [right(x, by) for x in bands] for by in range(-count, count + 1)}
    for reach in reversed(range(count)):
        views = {by: move_bands_back(views, by) for by in range(-reach, reach + 1)}
    return views[0]


def move_columns(even, odd):
    lane = lanes_of(even)
    first, last = lane == 0, lane == even.shape[1] - 1
    even_new = jnp.where(first, even, right(jnp.where(first, odd, even), 1))
    odd_new = jnp.where(last, even, left(odd, 1))
    return even_new, odd_new


def in_pair(even, shifted=None):
    lane = line_lanes(even)
    if shifted is not None:
        half = even.shape[1] // 2
        lane = jnp.where(shifted, jnp.where(lane < half, lane + half, lane - half), lane)
    return (lane < 0, lane), (lane >= 0, lane)


def in_blocks(even):
    lane, half = line_lanes(even), even.shape[1] // 2
    place = jnp.where(lane < half, lane, lane - half)
    return (lane >= half, place), (lane >= half, place + half)


def in_order(even):
    lane, half = line_lanes(even), even.shape[1] // 2
    return (lane % 2 == 1, lane // 2), (lane % 2 == 1, lane // 2 + half)


def turn_to(layout, even, odd, angles):
    for cosine, sine in angles[:-1]:
        even, odd = cosine * even + sine * odd, cosine * odd - sine * even
        even, odd = move_columns(even, odd)
    by, end = JSTEPS - 1, even.shape[1] - 1
    results = []
    for is_odd, place in layout:
        stayed = place <= end - by
        from_even = jnp.where(stayed, place + by, 2 * end + 1 - by - place)
        from_even = jnp.where(place == 0, 0, from_even)
        source = jnp.where(is_odd, jnp.abs(place - by), from_even)
        is_even = jnp.logical_or(
            jnp.logical_and(is_odd, place < by),
            jnp.logical_and(jnp.logical_not(is_odd), stayed),
        )
        cosine, sine = (take_lanes(x, source) for x in angles[-1])
        by_even = jnp.where(is_even, cosine, -sine)
        by_odd = jnp.where(is_even, sine, cosine)
        results.append(by_even * take_lanes(even, source) + by_odd * take_lanes(odd, source))
    return results


def trim(bands, reach):
    rows = min(bands[0].shape[0], -(-(reach + 1) // 8) * 8)
    return [band[:rows] for band in bands]


def angles_of(bands):
    angles = []
    for step in range(JSTEPS):
        ee, eo, oe, oo = bands = trim(bands, 2 * (JSTEPS - 1 - step))
        angles.append(jacobi_angle(ee[0:1], oo[0:1], eo[0:1]))
        if step < JSTEPS - 1:
            bands = step_bands(*bands, *angles[-1])
    return angles


def carried(bands, angles):
    ahead = 2 * (JSTEPS - 1)
    for step, (cosine, sine) in enumerate(angles):
        bands = turn_bands(*trim(bands, 3 * ahead - 2 * step), cosine, sine)
        if step < JSTEPS - 1:
            bands = move_bands(*bands)
    done = 0
    while done < JSTEPS - 1:
        count = min(BACK, JSTEPS - 1 - done)
        bands = bands_back(trim(bands, 2 * (ahead - done)), count)
        done += count
    return bands


def near_starts(width):
    half = width // 2
    reach = REACH - 1
    return (half - 2 * reach, width - WINDOW), (0, half - reach)


def cross_partial(x_even, x_odd, y_even, y_odd, x_second, y_second):
    rows, width = x_even.shape
    x_starts, y_starts = near_starts(width)
    lane = lanes_of(x_even)

    def window(even, odd, flag, starts):
        start = jnp.where(flag, starts[1], starts[0])
        at_zero = pltpu.roll(even, (width - start) % width, 1)
        at_next = pltpu.roll(odd, (width - start + WINDOW) % width, 1)
        return jnp.where(lane < WINDOW, at_zero, jnp.where(lane < 2 * WINDOW, at_next, 0.0))

    corner = lax.dot_general(
        window(y_even, y_odd, y_second, y_starts),
        window(x_even, x_odd, x_second, x_starts),
        (((0,), (0,)), ((), ())),
        precision=lax.Precision.HIGHEST,
        preferred_element_type=jnp.float32,
    )
    low = lax.broadcasted_iota(jnp.int32, (WINDOW, width), 1) < 2 * WINDOW
    return jnp.where(low, corner[:WINDOW], right(corner[WINDOW : 2 * WINDOW], 2 * WINDOW))


def own_rotation(angles, second, swapped, first_pair):
    width = angles[0][0].shape[1]
    half = width // 2
    x_starts, y_starts = near_starts(width)
    starts = [jnp.where(first_pair, x, y) for x, y in zip(x_starts, y_starts)]
    shape = (2 * WINDOW, width)
    row = lax.broadcasted_iota(jnp.int32, shape, 0)
    lane = lax.broadcasted_iota(jnp.int32, shape, 1) - jnp.where(second, starts[1], starts[0])
    even, odd = (
        jnp.where(jnp.logical_and(row == lane + at, row // WINDOW == at // WINDOW), 1.0, 0.0)
        for at in (0, WINDOW)
    )
    even, odd = turn_to(in_pair(even, swapped), even, odd, angles)
    low = lax.broadcasted_iota(jnp.int32, shape, 1) < half
    return jnp.where(jnp.logical_xor(low, first_pair), right(odd, half), even)


def cross_bands(packed, x_rotation, y_rotation):
    width = packed.shape[1]
    half = width // 2
    corner = jnp.concatenate((packed[:, :half], right(packed, half)[:, :half]), axis=0)
    highest = dict(precision=lax.Precision.HIGHEST, preferred_element_type=jnp.float32)
    turned_x = jnp.dot(corner, x_rotation, **highest)
    ends = lax.dot_general(turned_x, y_rotation, (((0,), (0,)), ((), ())), **highest)
    even, odd = ends[half - NEAR : half], ends[width - NEAR :]
    quadrants = (even, right(even, half), odd, right(odd, half))
    offset = lanes_of(even) - lax.broadcasted_iota(jnp.int32, even.shape, 0) - (half - NEAR)
    diag = lax.broadcasted_iota(jnp.int32, (DIAGS, width), 0)
    bands = [jnp.zeros((DIAGS, width), jnp.float32) for _ in quadrants]
    for d in range(1, REACH):
        here = offset == d
        for q, quadrant in enumerate(quadrants):
            line = jnp.sum(jnp.where(here, quadrant, 0.0), axis=0, keepdims=True)
            bands[q] = jnp.where(diag == d, line, bands[q])
    return bands


def either(flag, one, other):
    return jnp.logical_or(jnp.logical_and(flag, one), jnp.logical_and(jnp.logical_not(flag), other))


def halves_swapped(is_second):
    return among(is_second[0]), jnp.logical_not(among(is_second[1]))


def on_odd_core():
    return lax.axis_index("row") % 2 == 1


PLACES = (
    (((16, 16, 80), (60, 16, 108)), ((16, 28, 21), (44, 30, 80))),
    (((68, 16, 24), (112, 16, 0)), ((70, 29, 84), (99, 29, 10))),
)
MIDDLES = (44, 99)


def pick_by(flag, one, other):
    return jnp.where(flag, other, one)


def pack_far(bands, flag):
    width = bands[0].shape[1]
    lane = lax.broadcasted_iota(jnp.int32, (DIAGS, width), 1)
    odd_row = lax.broadcasted_iota(jnp.int32, (DIAGS, width), 0) % 2 == 1
    moves = []
    for parity in (0, 1):
        for part in (0, 1):
            one, other = PLACES[0][parity][part], PLACES[1][parity][part]
            shift = pick_by(flag, (one[2] - one[0]) % width, (other[2] - other[0]) % width)
            start = pick_by(flag, one[2], other[2])
            count = pick_by(flag, one[1], other[1])
            here = jnp.logical_and(lane >= start, lane < start + count)
            moves.append((shift, jnp.logical_and(here, odd_row == (parity == 1))))
    packed = []
    for band in bands:
        near, far = band[:DIAGS], down(band[DIAGS:], -1)
        for shift, here in moves:
            near = jnp.where(here, pltpu.roll(far, shift, 1), near)
        packed.append(near)
    return packed


def unpack_far(packed, flag):
    width = packed.shape[1]
    lane = lanes_of(packed)
    odd_row = lax.broadcasted_iota(jnp.int32, packed.shape, 0) % 2 == 1
    parts = []
    for part in (0, 1):
        rolled = []
        for parity in (0, 1):
            one, other = PLACES[0][parity][part], PLACES[1][parity][part]
            shift = pick_by(flag, (one[0] - one[2]) % width, (other[0] - other[2]) % width)
            rolled.append(pltpu.roll(packed, shift, 1))
        parts.append(jnp.where(odd_row, rolled[1], rolled[0]))
    far = jnp.where(lane < pick_by(flag, *MIDDLES), *parts)
    return jnp.concatenate((packed, down(far, 1)), axis=0)


PACKED = DIAGS


def store_part(even, odd, flag, part_ref):
    bands = pack_far(dense_bands(even, odd, FAR_DIAGS), flag)
    for q, band in enumerate(bands):
        part_ref[q * PACKED : (q + 1) * PACKED, :] = band


def open_pairs(is_second, x, y, column_refs, other_ref):
    flag = on_odd_core()
    mine = [jnp.where(flag, b, a) for a, b in zip(x, y)]
    theirs = [jnp.where(flag, a, b) for a, b in zip(x, y)]
    for ref, value in zip(column_refs, mine + theirs):
        ref[...] = value
    store_part(*theirs, either(flag, among(is_second[0]), among(is_second[1])), other_ref)
    other_ref[4 * PACKED :, :] = jnp.zeros((WINDOW, theirs[0].shape[1]), jnp.float32)


def first_open(own_second, gets_second, is_second, even_ref, odd_ref, payload_ref, *refs):
    *column_refs, other_ref = refs
    own = even_ref[...], odd_ref[...]
    came = unpacked(payload_ref[...], own[0].shape[0], among(gets_second))
    flag = among(own_second)
    x = [jnp.where(flag, b, a) for a, b in zip(own, came)]
    y = [jnp.where(flag, a, b) for a, b in zip(own, came)]
    open_pairs(is_second, x, y, column_refs, other_ref)


def fused_open(picks, is_second, kept_ref, sent_ref, came0_ref, came1_ref, *refs):
    *column_refs, other_ref = refs
    arrays = [ref[...] for ref in (sent_ref, kept_ref, came0_ref, came1_ref)]
    blocks = [choose(pick, arrays) for pick in picks]
    x, y = split_pair(*blocks[:2]), split_pair(*blocks[2:])
    open_pairs(is_second, x, y, column_refs, other_ref)


def swapped_flag(is_second):
    x_swapped, y_swapped = halves_swapped(is_second)
    return either(on_odd_core(), y_swapped, x_swapped)


def own_second_flag(is_second):
    return either(on_odd_core(), among(is_second[1]), among(is_second[0]))


def bands_kernel(is_second, *refs):
    *column_refs, part_ref = refs
    columns = [ref[...] for ref in column_refs]
    store_part(*columns[:2], own_second_flag(is_second), part_ref)
    flag = on_odd_core()
    x = [jnp.where(flag, b, a) for a, b in zip(columns[:2], columns[2:])]
    y = [jnp.where(flag, a, b) for a, b in zip(columns[:2], columns[2:])]
    corner = cross_partial(*x, *y, among(is_second[0]), among(is_second[1]))
    part_ref[4 * PACKED :, :] = corner


def angles_kernel(is_second, *refs):
    *part_refs, found_ref = refs
    part = pair_sums([ref[...] for ref in part_refs])
    flag = own_second_flag(is_second)
    quadrants = [unpack_far(part[q * PACKED : (q + 1) * PACKED], flag) for q in range(4)]
    angles = angles_of(quadrants)
    bands = carried(quadrants, angles)
    for step, pair in enumerate(angles):
        for i in (0, 1):
            found_ref[2 * step + i : 2 * step + i + 1, :] = pair[i]
    spare = NEAR - 2 * JSTEPS
    found_ref[2 * JSTEPS : NEAR, :] = jnp.zeros((spare, part.shape[1]), jnp.float32)
    for q in range(4):
        found_ref[NEAR + q * DIAGS : NEAR + (q + 1) * DIAGS, :] = bands[q][:DIAGS]
    found_ref[CORNER:ROTATION, :] = part[4 * PACKED :]
    first_pair = jnp.logical_not(on_odd_core())
    found_ref[ROTATION:, :] = own_rotation(angles, flag, swapped_flag(is_second), first_pair)


CORNER = NEAR + 4 * DIAGS
ROTATION = CORNER + WINDOW
FOUND = ROTATION + 2 * WINDOW


def angles_in(found):
    return [(found[2 * i : 2 * i + 1], found[2 * i + 1 : 2 * i + 2]) for i in range(JSTEPS)]


def columns_kernel(is_second, even_ref, odd_ref, found_ref, *out_refs):
    angles = angles_in(found_ref[...])
    layout = in_pair(even_ref, swapped_flag(is_second))
    columns = turn_to(layout, even_ref[...], odd_ref[...], angles)
    for ref, value in zip(out_refs, columns):
        ref[...] = value


def next_bands(x_found, y_found, x_second, y_second):
    corner = x_found[CORNER:ROTATION] + y_found[CORNER:ROTATION]
    middle = cross_bands(corner, x_found[ROTATION:], y_found[ROTATION:])
    half = corner.shape[1] // 2
    lane = lanes_of(middle[0])
    diag = lax.broadcasted_iota(jnp.int32, middle[0].shape, 0)
    bands = []
    for q in range(4):
        rows = slice(NEAR + q * DIAGS, NEAR + (q + 1) * DIAGS)
        x, y = x_found[rows], y_found[rows]
        x = jnp.where(x_second, right(x, half), x)
        y = jnp.where(y_second, y, right(y, half))
        crossing = jnp.where(lane - diag < half, middle[q], y)
        bands.append(jnp.where(lane < half, x, crossing))
    return bands


def next_kernel(is_second, sends_first, layout_of, *refs):
    mine_even, mine_odd, even_ref, odd_ref, found_ref, other_ref, kept_ref, sent_ref = refs
    found, other = found_ref[...], other_ref[...]
    flag = on_odd_core()
    x_found, y_found = jnp.where(flag, other, found), jnp.where(flag, found, other)
    bands = next_bands(x_found, y_found, among(is_second[0]), among(is_second[1]))
    x_swapped, y_swapped = halves_swapped(is_second)
    swapped = either(flag, x_swapped, y_swapped)
    layout = in_pair(even_ref, swapped)
    theirs = turn_to(layout, even_ref[...], odd_ref[...], angles_in(other))
    low = line_lanes(found) < found.shape[1] // 2
    from_mine = jnp.logical_xor(low, flag)
    even = jnp.where(from_mine, mine_even[...], theirs[0])
    odd = jnp.where(from_mine, mine_odd[...], theirs[1])
    angles = angles_of(bands)
    first, second = turn_to(layout_of(even), even, odd, angles)
    flag = among(sends_first)
    kept_ref[...] = jnp.where(flag, second, first)
    sent_ref[...] = jnp.where(flag, first, second)


def pair_sums(arrays):
    while len(arrays) > 1:
        arrays = [arrays[i] + arrays[i + 1] for i in range(0, len(arrays), 2)]
    return arrays[0]


def swap(x, axis, mask):
    return lax.ppermute(x, axis, [(i, i ^ mask) for i in range(lax.axis_size(axis))])


def exchange_groups(x, axis, first_bit=0):
    count = lax.axis_size(axis).bit_length() - 1
    bits = [1 << b for b in range(count)]
    groups = [bits[:1]] + [bits[i : i + 2] for i in range(1, count, 2)]
    arrays = [x]
    for group in groups[first_bit:]:
        x = pair_sums(arrays)
        masks = [group[0]] if len(group) == 1 else [group[0], group[1], group[0] | group[1]]
        arrays = [x] + [swap(x, axis, mask) for mask in masks]
    return arrays


def call(kernel, shapes, *args):
    out = [jax.ShapeDtypeStruct(shape, jnp.float32) for shape in shapes]
    return pl.pallas_call(
        kernel,
        out_shape=out,
        compiler_params=pltpu.CompilerParams(vmem_limit_bytes=32 * 1024 * 1024),
    )(*args)


def two_rounds(opened, is_second, sends_first, layout_of):
    *columns, other = opened
    column, width = columns[0].shape, columns[0].shape[1]
    other = swap(other, "row", 1)
    bands = functools.partial(bands_kernel, is_second)
    (mine,) = call(bands, (other.shape,), *columns)
    (found,) = call(
        functools.partial(angles_kernel, is_second),
        ((FOUND, width),),
        *exchange_groups(mine + other, "row", 1),
    )
    other = swap(found, "row", 1)
    turn = functools.partial(columns_kernel, is_second)
    columns[:2] = call(turn, (column, column), *columns[:2], found)
    turn = functools.partial(next_kernel, is_second, sends_first, layout_of)
    return call(turn, (column, column), *columns, found, other)


def per_device(basis):
    rows, cols = basis.shape
    width = cols // 2
    pair_total = lax.axis_size("pair")
    column = (rows, width)
    opened = (column,) * 4 + ((4 * PACKED + WINDOW, width),)
    payload = (rows + rows * 2 * STRIP // width, width)

    sends, sends_second, gets_second, own_second, is_second = first_moves(pair_total)
    (sent,) = call(functools.partial(payload_kernel, sends_second), (payload,), basis)
    came = lax.ppermute(sent, "pair", sends)
    even, odd = call(open_kernel, (column, column), basis)
    opening = functools.partial(first_open, own_second, gets_second, is_second)
    arrays = call(opening, opened, even, odd, came)
    sends, sends_first, picks, next_second = fused_moves(pair_total)
    kept, sent = two_rounds(arrays, is_second, sends_first, in_blocks)

    came = [lax.ppermute(x, "pair", s) for x, s in zip((sent, kept), sends)]
    opening = functools.partial(fused_open, picks, next_second)
    arrays = call(opening, opened, kept, sent, *came)
    sends, sends_first, gets_first = last_moves(pair_total)
    kept, sent = two_rounds(arrays, next_second, sends_first, in_order)

    came = lax.ppermute(sent, "pair", sends)
    flag = among(gets_first)
    first = jnp.where(flag, came, kept)
    second = jnp.where(flag, kept, came)
    return jnp.concatenate((first, second), axis=1)


def solution(mesh):
    return jax.shard_map(
        per_device,
        mesh=mesh,
        in_specs=(P("row", "pair"),),
        out_specs=P("row", "pair"),
        check_vma=False,
    )
```

```python
import functools

import jax
import jax.numpy as jnp
import numpy as np
from jax import lax
from jax.experimental import pallas as pl
from jax.experimental.pallas import tpu as pltpu
from jax.sharding import PartitionSpec as P

ROUNDS = 4
JSTEPS = 6
REACH = 2 * (JSTEPS - 1) + 1
DIAGS = 16
FAR_DIAGS = 32
WINDOW = 32
NEAR = 16
STRIP = REACH - 1
BACK = 3


def tournament_order(pair_count):
    ordering = np.zeros(2 * pair_count, dtype=np.int64)
    ordering[0] = 0
    ordering[2] = 1
    for slot in range(2, pair_count):
        ordering[2 * slot] = 2 * (slot - 1)
    for slot in range(pair_count - 1):
        ordering[2 * slot + 1] = 2 * (slot + 1) + 1
    ordering[2 * pair_count - 1] = 2 * (pair_count - 1)
    return ordering


def host_of(pair, pair_total, round_index):
    if round_index % 2 == 0 or pair == 0:
        return pair
    return min(pair + 1, pair_total - 1) if pair % 2 else pair - 1


def last_moves(pair_total):
    ordering = tournament_order(pair_total)
    sends, sends_first, gets_first = [], set(), set()
    for pair in range(pair_total):
        target = host_of(pair, pair_total, ROUNDS)
        for place in (0, 1):
            old = int(ordering[2 * pair + place])
            source = host_of(old // 2, pair_total, ROUNDS - 1)
            if source == target:
                continue
            sends.append((source, target))
            if old % 2 == 0:
                sends_first.add(source)
            if place == 0:
                gets_first.add(target)
    assert len({s for s, _ in sends}) == len(sends) == len({t for _, t in sends})
    return sends, sends_first, gets_first


def first_moves(pair_total):
    ordering = tournament_order(pair_total)
    sends, sends_second, gets_second, own_second = [], set(), set(), set()
    seconds = (set(), set())
    for pair in range(pair_total):
        here = host_of(pair, pair_total, 1)
        for place in (0, 1):
            old = int(ordering[2 * pair + place])
            if old % 2:
                seconds[place].add(here)
            if old // 2 == here:
                if place:
                    own_second.add(here)
                continue
            sends.append((old // 2, here))
            if old % 2:
                sends_second.add(old // 2)
                gets_second.add(here)
    assert len({s for s, _ in sends}) == len(sends) == len({t for _, t in sends})
    return sends, sends_second, gets_second, own_second, seconds


def fused_moves(pair_total):
    ordering = tournament_order(pair_total)
    before, last = ROUNDS - 3, ROUNDS - 1
    needs, edges, seconds = {}, [], ({}, {})
    for pair in range(pair_total):
        here = host_of(pair, pair_total, last)
        needs[here] = []
        for place in (0, 1):
            source = int(ordering[2 * pair + place])
            seconds[place][here] = source % 2
            for half in (0, 1):
                old = int(ordering[2 * (source // 2) + half])
                there = host_of(old // 2, pair_total, before)
                needs[here].append((there, old % 2))
                if there != here:
                    edges.append((there, old % 2, here))
    turn, left_over = {}, list(edges)
    while left_over:
        source, _, target = left_over[0]
        start = source
        while True:
            for number, one, other in ((0, source, target), (1, target, source)):
                edge = next(e for e in left_over if (e[0], e[2]) == (one, other))
                turn[edge] = number
                left_over.remove(edge)
            if target == start:
                break
            ahead = [e[2] for e in left_over if e[0] == target]
            source, target = target, ahead[0]
    sends = [[(e[0], e[2]) for e in edges if turn[e] == i] for i in (0, 1)]
    for chosen in sends:
        assert len({a for a, _ in chosen}) == len({b for _, b in chosen}) == pair_total
    sends_first = {e[0] for e in edges if turn[e] == 0 and e[1] == 0}
    picks = []
    for slot in range(4):
        pick = {}
        for here in range(pair_total):
            there, half = needs[here][slot]
            if there == here:
                pick[here] = 0 if (half == 0) == (here in sends_first) else 1
            else:
                pick[here] = 2 + turn[(there, half, here)]
        picks.append(pick)
    is_second = [{h for h, place in table.items() if place} for table in seconds]
    return sends, sends_first, picks, is_second


def choose(pick, arrays):
    chosen = arrays[0]
    for number in range(1, len(arrays)):
        members = {here for here, value in pick.items() if value == number}
        if members:
            chosen = jnp.where(among(members), arrays[number], chosen)
    return chosen


def among(members):
    here = lax.axis_index("pair")
    return functools.reduce(
        jnp.logical_or, [here == member for member in sorted(members)], here < 0
    )


def left(x, by):
    width = x.shape[1]
    return pltpu.roll(x, (width - by) % width, 1) if by % width else x


def right(x, by):
    width = x.shape[1]
    return pltpu.roll(x, by % width, 1) if by % width else x


def down(x, by):
    return pltpu.roll(x, by % x.shape[0], 0)


def lanes_of(x):
    return lax.broadcasted_iota(jnp.int32, x.shape, 1)


def split_pair(first, second):
    half = first.shape[1] // 2
    low = lanes_of(first) < half
    even = jnp.where(low, first, right(second, half))
    odd = jnp.where(low, right(first, half), second)
    return even, odd


def take_lanes(x, source):
    if x.shape[0] == 1:
        return take_lanes(jnp.broadcast_to(x, (8, x.shape[1])), source)[:1]
    return jnp.take_along_axis(x, jnp.broadcast_to(source, x.shape), axis=1)


def line_lanes(x):
    return lax.broadcasted_iota(jnp.int32, (1, x.shape[1]), 1)


def separate(first, second):
    lane = line_lanes(first)
    half = first.shape[1] // 2
    low = lane < half
    source = 2 * jnp.where(low, lane, lane - half)
    return tuple(
        jnp.where(low, take_lanes(first, source + odd), take_lanes(second, source + odd))
        for odd in (0, 1)
    )


def backwards(x):
    return jnp.take_along_axis(x, x.shape[1] - 1 - lanes_of(x), axis=1)


def dense_bands(even, odd, diags):
    width = even.shape[1]
    gram = lax.dot_general(
        jnp.concatenate((even, odd), axis=1),
        jnp.concatenate((backwards(even), backwards(odd)), axis=1),
        (((0,), (0,)), ((), ())),
        precision=lax.Precision.HIGHEST,
        preferred_element_type=jnp.float32,
    )
    bands = []
    for near in (0, width):
        for far in (0, width):
            quadrant = gram[far : far + width, near : near + width]
            aligned = pltpu.roll(quadrant, 1, 1, stride=1, stride_axis=0)
            bands.append(jnp.transpose(aligned)[:diags])
    return bands


def store_bands(even, odd, band_ref, diags):
    for q, band in enumerate(dense_bands(even, odd, diags)):
        band_ref[q * diags : (q + 1) * diags, :] = band


def strip_rows(rows, width):
    return -(-rows // (8 * (width // (2 * STRIP)))) * 8


def payload_kernel(sends_second, basis_ref, payload_ref):
    rows, cols = basis_ref.shape
    width = cols // 2
    half = width // 2
    first, second = basis_ref[:, :width], basis_ref[:, width:]
    lane = line_lanes(first)
    start = jnp.where(among(sends_second), half - STRIP, 0)
    place = start + jnp.where(lane < half, lane, lane - half)
    odd = jnp.where(lane < half, 0, 1)
    in_first = place < half
    source = 2 * jnp.where(in_first, place, place - half) + odd
    payload_ref[:rows] = jnp.where(in_first, take_lanes(first, source), take_lanes(second, source))
    places = width // STRIP
    place = lane - STRIP * sum(jnp.where(lane >= STRIP * i, 1, 0) for i in range(1, places))
    odd = sum(jnp.where(lane >= STRIP * i, 1 if i % 2 else -1, 0) for i in range(1, places))
    source = jnp.minimum(2 * (start + place) + odd, width - 1)
    group = strip_rows(rows, width)
    strips = jnp.zeros((group, width), jnp.float32)
    for i, at in enumerate(range(0, rows, group)):
        here = jnp.logical_and(lane >= 2 * STRIP * i, lane < 2 * STRIP * (i + 1))
        part = take_lanes(second[at : at + group], source)
        if part.shape[0] < group:
            spare = jnp.zeros((group - part.shape[0], width), jnp.float32)
            part = jnp.concatenate((part, spare), axis=0)
        strips = jnp.where(here, part, strips)
    payload_ref[rows:] = strips


def open_kernel(basis_ref, even_ref, odd_ref):
    width = basis_ref.shape[1] // 2
    even_ref[...], odd_ref[...] = separate(basis_ref[:, :width], basis_ref[:, width:])


def unpacked(payload, rows, second):
    width = payload.shape[1]
    half = width // 2
    lane = line_lanes(payload)
    main, strips = payload[:rows], payload[rows:]
    group = strips.shape[0]
    columns = []
    for j, x in enumerate((main, left(main, half))):
        ends = [
            right(strips, half - (2 * i + j) * STRIP)[: rows - at]
            for i, at in enumerate(range(0, rows, group))
        ]
        ends = jnp.concatenate(ends, axis=0)
        x = jnp.where(lane < half, x, jnp.where(lane < half + STRIP, ends, 0.0))
        columns.append(jnp.where(second, right(x, half - STRIP), x))
    return columns


def jacobi_angle(diag_even, diag_odd, coupling):
    spread = diag_even - diag_odd
    square = spread * spread + 4.0 * coupling * coupling
    inverse = lax.rsqrt(square)
    larger_square = (square * inverse + jnp.abs(spread)) * (0.5 * inverse)
    larger_inverse = lax.rsqrt(larger_square)
    larger = larger_square * larger_inverse
    smaller = coupling * inverse * larger_inverse
    forward = spread >= 0.0
    sign = jnp.where(coupling > 0.0, 1.0, jnp.where(coupling < 0.0, -1.0, 0.0))
    cosine = jnp.where(forward, larger, jnp.abs(smaller))
    sine_part = jnp.where(forward, smaller, sign * larger)
    return cosine, sine_part


def turn_bands(ee, eo, oe, oo, cosine, sine):
    cl, sl = jnp.broadcast_to(cosine, ee.shape), jnp.broadcast_to(sine, ee.shape)
    ck = pltpu.roll(cl, 0, 1, stride=1, stride_axis=0)
    sk = pltpu.roll(sl, 0, 1, stride=1, stride_axis=0)
    ee, oe = ck * ee + sk * oe, ck * oe - sk * ee
    eo, oo = ck * eo + sk * oo, ck * oo - sk * eo
    ee, eo = cl * ee + sl * eo, cl * eo - sl * ee
    oe, oo = cl * oe + sl * oo, cl * oo - sl * oe
    return ee, eo, oe, oo


def step_bands(ee, eo, oe, oo, cosine, sine):
    lane = lanes_of(ee)
    diag = lax.broadcasted_iota(jnp.int32, ee.shape, 0)
    last = lane == ee.shape[1] - 1
    on, next_on = diag == 0, diag == 1

    def slanted(x, by):
        if by >= 0:
            return pltpu.roll(x, by, 1, stride=1, stride_axis=0)
        return jnp.where(on, left(x, -by), down(slanted(x, 0), -by))

    def rotated(by, wanted):
        cl, sl = (jnp.broadcast_to(x, ee.shape) for x in (cosine, sine))
        ck, sk = (slanted(x, by) for x in (cl, sl))
        cl, sl, a, b, c, d = (right(x, by) for x in (cl, sl, ee, eo, oe, oo))
        a, c = ck * a + sk * c, ck * c - sk * a
        b, d = ck * b + sk * d, ck * d - sk * b
        found = {"ee": (a, b), "eo": (b, a), "oe": (c, d), "oo": (d, c)}
        return [
            cl * one + sl * two if name in ("ee", "oe") else cl * one - sl * two
            for name, (one, two) in found.items()
            if name in wanted
        ]

    ee_0, eo_0, oe_0, oo_0 = rotated(0, ("ee", "eo", "oe", "oo"))
    ee_r, eo_r, oe_r, oo_r = rotated(1, ("ee", "eo", "oe", "oo"))
    eo_l, oo_l = rotated(-1, ("eo", "oo"))

    near = down(jnp.where(on, eo_r, ee_r), 1)
    turned = jnp.where(on, oo_r, oe_r)
    ee_new = jnp.where(lane == diag + 1, turned, jnp.where(lane == diag, near, ee_r))
    ee_new = jnp.where(jnp.logical_and(on, lane == 0), ee_0, ee_new)

    eo_new = down(jnp.where(lane == diag - 1, oo_l, eo_l), -2)
    eo_new = jnp.where(lane == diag, down(eo_l, -1), eo_new)
    eo_new = jnp.where(last, down(ee_0, -1), eo_new)

    oo_new = jnp.where(last, jnp.where(on, ee_0, down(oe_0, 1)), oo_l)

    oe_new = down(oe_r, 2)
    oe_new = jnp.where(next_on, jnp.where(lane == diag, oo_0, eo_0), oe_new)
    oe_new = jnp.where(on, eo_new, oe_new)
    return ee_new, eo_new, oe_new, oo_new


def move_bands(ee, eo, oe, oo):
    lane = lanes_of(ee)
    diag = lax.broadcasted_iota(jnp.int32, ee.shape, 0)
    last = lane == ee.shape[1] - 1
    on, next_on = diag == 0, diag == 1

    near = down(jnp.where(on, eo, ee), 1)
    turned = jnp.where(on, oo, oe)
    mixed = jnp.where(lane == diag, turned, jnp.where(lane == diag - 1, near, ee))
    ee_new = jnp.where(jnp.logical_and(on, lane == 0), ee, right(mixed, 1))

    far = down(jnp.where(last, ee, eo), -1)
    mixed = down(jnp.where(lane == diag, oo, eo), -2)
    mixed = left(jnp.where(lane == diag + 1, far, mixed), 1)
    eo_new = jnp.where(last, far, mixed)

    oo_new = jnp.where(last, jnp.where(on, ee, down(oe, 1)), left(oo, 1))

    oe_new = right(down(oe, 2), 1)
    oe_new = jnp.where(next_on, jnp.where(lane == diag, oo, eo), oe_new)
    oe_new = jnp.where(on, eo_new, oe_new)
    return ee_new, eo_new, oe_new, oo_new


def move_bands_back(views, by):
    ee, eo, oe, oo = views[by]
    ee_left, _, oe_left, _ = views[by - 1]
    _, eo_right, _, oo_right = views[by + 1]
    width = ee.shape[1]
    lane = lanes_of(ee) - by
    lane = jnp.where(lane < 0, lane + width, jnp.where(lane >= width, lane - width, lane))
    diag = lax.broadcasted_iota(jnp.int32, ee.shape, 0)
    last, first = lane == width - 1, lane == diag
    on, next_on = diag == 0, diag == 1
    oo_up, eo_twice = down(oo, -1), down(eo_right, 2)

    far = jnp.where(first, down(ee_left, -1), ee_left)
    ee_old = jnp.where(jnp.logical_and(first, on), ee, far)
    ee_old = jnp.where(last, jnp.where(on, oo, down(eo, 1)), ee_old)

    near = jnp.where(jnp.logical_and(first, diag > 0), ee_left, down(oe_left, -2))
    eo_old = jnp.where(first, down(eo_right, 1), eo_twice)
    eo_old = jnp.where(on, jnp.where(last, oo_up, near), eo_old)
    eo_old = jnp.where(jnp.logical_and(next_on, lane > 1), oe, eo_old)
    eo_old = jnp.where(jnp.logical_and(on, first), far, eo_old)

    oe_old = jnp.where(on, eo_old, jnp.where(last, oo_up, near))

    oo_old = jnp.where(first, eo_twice, oo_right)
    oo_old = jnp.where(jnp.logical_and(next_on, first), oe, oo_old)
    oo_old = jnp.where(jnp.logical_and(on, first), ee_left, oo_old)
    return ee_old, eo_old, oe_old, oo_old


def bands_back(bands, count):
    views = {by: [right(x, by) for x in bands] for by in range(-count, count + 1)}
    for reach in reversed(range(count)):
        views = {by: move_bands_back(views, by) for by in range(-reach, reach + 1)}
    return views[0]


def move_columns(even, odd):
    lane = lanes_of(even)
    first, last = lane == 0, lane == even.shape[1] - 1
    even_new = jnp.where(first, even, right(jnp.where(first, odd, even), 1))
    odd_new = jnp.where(last, even, left(odd, 1))
    return even_new, odd_new


def in_pair(even, shifted=None):
    lane = line_lanes(even)
    if shifted is not None:
        half = even.shape[1] // 2
        lane = jnp.where(shifted, jnp.where(lane < half, lane + half, lane - half), lane)
    return (lane < 0, lane), (lane >= 0, lane)


def in_blocks(even):
    lane, half = line_lanes(even), even.shape[1] // 2
    place = jnp.where(lane < half, lane, lane - half)
    return (lane >= half, place), (lane >= half, place + half)


def in_order(even):
    lane, half = line_lanes(even), even.shape[1] // 2
    return (lane % 2 == 1, lane // 2), (lane % 2 == 1, lane // 2 + half)


def turn_to(layout, even, odd, angles):
    for cosine, sine in angles[:-1]:
        even, odd = cosine * even + sine * odd, cosine * odd - sine * even
        even, odd = move_columns(even, odd)
    by, end = JSTEPS - 1, even.shape[1] - 1
    results = []
    for is_odd, place in layout:
        stayed = place <= end - by
        from_even = jnp.where(stayed, place + by, 2 * end + 1 - by - place)
        from_even = jnp.where(place == 0, 0, from_even)
        source = jnp.where(is_odd, jnp.abs(place - by), from_even)
        is_even = jnp.logical_or(
            jnp.logical_and(is_odd, place < by),
            jnp.logical_and(jnp.logical_not(is_odd), stayed),
        )
        cosine, sine = (take_lanes(x, source) for x in angles[-1])
        by_even = jnp.where(is_even, cosine, -sine)
        by_odd = jnp.where(is_even, sine, cosine)
        results.append(by_even * take_lanes(even, source) + by_odd * take_lanes(odd, source))
    return results


def trim(bands, reach):
    rows = min(bands[0].shape[0], -(-(reach + 1) // 8) * 8)
    return [band[:rows] for band in bands]


def angles_of(bands):
    angles = []
    for step in range(JSTEPS):
        ee, eo, oe, oo = bands = trim(bands, 2 * (JSTEPS - 1 - step))
        angles.append(jacobi_angle(ee[0:1], oo[0:1], eo[0:1]))
        if step < JSTEPS - 1:
            bands = step_bands(*bands, *angles[-1])
    return angles


def carried(bands, angles):
    ahead = 2 * (JSTEPS - 1)
    for step, (cosine, sine) in enumerate(angles):
        bands = turn_bands(*trim(bands, 3 * ahead - 2 * step), cosine, sine)
        if step < JSTEPS - 1:
            bands = move_bands(*bands)
    done = 0
    while done < JSTEPS - 1:
        count = min(BACK, JSTEPS - 1 - done)
        bands = bands_back(trim(bands, 2 * (ahead - done)), count)
        done += count
    return bands


def near_starts(width):
    half = width // 2
    reach = REACH - 1
    return (half - 2 * reach, width - WINDOW), (0, half - reach)


def cross_partial(x_even, x_odd, y_even, y_odd, x_second, y_second):
    rows, width = x_even.shape
    x_starts, y_starts = near_starts(width)
    lane = lanes_of(x_even)

    def window(even, odd, flag, starts):
        start = jnp.where(flag, starts[1], starts[0])
        at_zero = pltpu.roll(even, (width - start) % width, 1)
        at_next = pltpu.roll(odd, (width - start + WINDOW) % width, 1)
        return jnp.where(lane < WINDOW, at_zero, jnp.where(lane < 2 * WINDOW, at_next, 0.0))

    corner = lax.dot_general(
        window(y_even, y_odd, y_second, y_starts),
        window(x_even, x_odd, x_second, x_starts),
        (((0,), (0,)), ((), ())),
        precision=lax.Precision.HIGHEST,
        preferred_element_type=jnp.float32,
    )
    low = lax.broadcasted_iota(jnp.int32, (WINDOW, width), 1) < 2 * WINDOW
    return jnp.where(low, corner[:WINDOW], right(corner[WINDOW : 2 * WINDOW], 2 * WINDOW))


def own_rotation(angles, second, swapped, first_pair):
    width = angles[0][0].shape[1]
    half = width // 2
    x_starts, y_starts = near_starts(width)
    starts = [jnp.where(first_pair, x, y) for x, y in zip(x_starts, y_starts)]
    shape = (2 * WINDOW, width)
    row = lax.broadcasted_iota(jnp.int32, shape, 0)
    lane = lax.broadcasted_iota(jnp.int32, shape, 1) - jnp.where(second, starts[1], starts[0])
    even, odd = (
        jnp.where(jnp.logical_and(row == lane + at, row // WINDOW == at // WINDOW), 1.0, 0.0)
        for at in (0, WINDOW)
    )
    even, odd = turn_to(in_pair(even, swapped), even, odd, angles)
    low = lax.broadcasted_iota(jnp.int32, shape, 1) < half
    return jnp.where(jnp.logical_xor(low, first_pair), right(odd, half), even)


def cross_bands(packed, x_rotation, y_rotation):
    width = packed.shape[1]
    half = width // 2
    corner = jnp.concatenate((packed[:, :half], right(packed, half)[:, :half]), axis=0)
    highest = dict(precision=lax.Precision.HIGHEST, preferred_element_type=jnp.float32)
    turned_x = jnp.dot(corner, x_rotation, **highest)
    ends = lax.dot_general(turned_x, y_rotation, (((0,), (0,)), ((), ())), **highest)
    even, odd = ends[half - NEAR : half], ends[width - NEAR :]
    quadrants = (even, right(even, half), odd, right(odd, half))
    offset = lanes_of(even) - lax.broadcasted_iota(jnp.int32, even.shape, 0) - (half - NEAR)
    diag = lax.broadcasted_iota(jnp.int32, (DIAGS, width), 0)
    bands = [jnp.zeros((DIAGS, width), jnp.float32) for _ in quadrants]
    for d in range(1, REACH):
        here = offset == d
        for q, quadrant in enumerate(quadrants):
            line = jnp.sum(jnp.where(here, quadrant, 0.0), axis=0, keepdims=True)
            bands[q] = jnp.where(diag == d, line, bands[q])
    return bands


def either(flag, one, other):
    return jnp.logical_or(jnp.logical_and(flag, one), jnp.logical_and(jnp.logical_not(flag), other))


def halves_swapped(is_second):
    return among(is_second[0]), jnp.logical_not(among(is_second[1]))


def on_odd_core():
    return lax.axis_index("row") % 2 == 1


PLACES = (
    (((16, 16, 80), (60, 16, 108)), ((16, 28, 21), (44, 30, 80))),
    (((68, 16, 24), (112, 16, 0)), ((70, 29, 84), (99, 29, 10))),
)
MIDDLES = (44, 99)


def pick_by(flag, one, other):
    return jnp.where(flag, other, one)


def pack_far(bands, flag):
    width = bands[0].shape[1]
    lane = lax.broadcasted_iota(jnp.int32, (DIAGS, width), 1)
    odd_row = lax.broadcasted_iota(jnp.int32, (DIAGS, width), 0) % 2 == 1
    moves = []
    for parity in (0, 1):
        for part in (0, 1):
            one, other = PLACES[0][parity][part], PLACES[1][parity][part]
            shift = pick_by(flag, (one[2] - one[0]) % width, (other[2] - other[0]) % width)
            start = pick_by(flag, one[2], other[2])
            count = pick_by(flag, one[1], other[1])
            here = jnp.logical_and(lane >= start, lane < start + count)
            moves.append((shift, jnp.logical_and(here, odd_row == (parity == 1))))
    packed = []
    for band in bands:
        near, far = band[:DIAGS], down(band[DIAGS:], -1)
        for shift, here in moves:
            near = jnp.where(here, pltpu.roll(far, shift, 1), near)
        packed.append(near)
    return packed


def unpack_far(packed, flag):
    width = packed.shape[1]
    lane = lanes_of(packed)
    odd_row = lax.broadcasted_iota(jnp.int32, packed.shape, 0) % 2 == 1
    parts = []
    for part in (0, 1):
        rolled = []
        for parity in (0, 1):
            one, other = PLACES[0][parity][part], PLACES[1][parity][part]
            shift = pick_by(flag, (one[0] - one[2]) % width, (other[0] - other[2]) % width)
            rolled.append(pltpu.roll(packed, shift, 1))
        parts.append(jnp.where(odd_row, rolled[1], rolled[0]))
    far = jnp.where(lane < pick_by(flag, *MIDDLES), *parts)
    return jnp.concatenate((packed, down(far, 1)), axis=0)


PACKED = DIAGS


def store_part(even, odd, flag, part_ref):
    bands = pack_far(dense_bands(even, odd, FAR_DIAGS), flag)
    for q, band in enumerate(bands):
        part_ref[q * PACKED : (q + 1) * PACKED, :] = band


def open_pairs(is_second, x, y, column_refs, other_ref):
    flag = on_odd_core()
    mine = [jnp.where(flag, b, a) for a, b in zip(x, y)]
    theirs = [jnp.where(flag, a, b) for a, b in zip(x, y)]
    for ref, value in zip(column_refs, mine + theirs):
        ref[...] = value
    store_part(*theirs, either(flag, among(is_second[0]), among(is_second[1])), other_ref)
    other_ref[4 * PACKED :, :] = jnp.zeros((WINDOW, theirs[0].shape[1]), jnp.float32)


def first_open(own_second, gets_second, is_second, even_ref, odd_ref, payload_ref, *refs):
    *column_refs, other_ref = refs
    own = even_ref[...], odd_ref[...]
    came = unpacked(payload_ref[...], own[0].shape[0], among(gets_second))
    flag = among(own_second)
    x = [jnp.where(flag, b, a) for a, b in zip(own, came)]
    y = [jnp.where(flag, a, b) for a, b in zip(own, came)]
    open_pairs(is_second, x, y, column_refs, other_ref)


def fused_open(picks, is_second, kept_ref, sent_ref, came0_ref, came1_ref, *refs):
    *column_refs, other_ref = refs
    arrays = [ref[...] for ref in (sent_ref, kept_ref, came0_ref, came1_ref)]
    blocks = [choose(pick, arrays) for pick in picks]
    x, y = split_pair(*blocks[:2]), split_pair(*blocks[2:])
    open_pairs(is_second, x, y, column_refs, other_ref)


def swapped_flag(is_second):
    x_swapped, y_swapped = halves_swapped(is_second)
    return either(on_odd_core(), y_swapped, x_swapped)


def own_second_flag(is_second):
    return either(on_odd_core(), among(is_second[1]), among(is_second[0]))


def bands_kernel(is_second, *refs):
    *column_refs, part_ref = refs
    columns = [ref[...] for ref in column_refs]
    store_part(*columns[:2], own_second_flag(is_second), part_ref)
    flag = on_odd_core()
    x = [jnp.where(flag, b, a) for a, b in zip(columns[:2], columns[2:])]
    y = [jnp.where(flag, a, b) for a, b in zip(columns[:2], columns[2:])]
    corner = cross_partial(*x, *y, among(is_second[0]), among(is_second[1]))
    part_ref[4 * PACKED :, :] = corner


def angles_kernel(is_second, *refs):
    *part_refs, found_ref = refs
    part = pair_sums([ref[...] for ref in part_refs])
    flag = own_second_flag(is_second)
    quadrants = [unpack_far(part[q * PACKED : (q + 1) * PACKED], flag) for q in range(4)]
    angles = angles_of(quadrants)
    bands = carried(quadrants, angles)
    for step, pair in enumerate(angles):
        for i in (0, 1):
            found_ref[2 * step + i : 2 * step + i + 1, :] = pair[i]
    spare = NEAR - 2 * JSTEPS
    found_ref[2 * JSTEPS : NEAR, :] = jnp.zeros((spare, part.shape[1]), jnp.float32)
    for q in range(4):
        found_ref[NEAR + q * DIAGS : NEAR + (q + 1) * DIAGS, :] = bands[q][:DIAGS]
    found_ref[CORNER:ROTATION, :] = part[4 * PACKED :]
    first_pair = jnp.logical_not(on_odd_core())
    found_ref[ROTATION:, :] = own_rotation(angles, flag, swapped_flag(is_second), first_pair)


CORNER = NEAR + 4 * DIAGS
ROTATION = CORNER + WINDOW
FOUND = ROTATION + 2 * WINDOW


def angles_in(found):
    return [(found[2 * i : 2 * i + 1], found[2 * i + 1 : 2 * i + 2]) for i in range(JSTEPS)]


def columns_kernel(is_second, even_ref, odd_ref, found_ref, *out_refs):
    angles = angles_in(found_ref[...])
    layout = in_pair(even_ref, swapped_flag(is_second))
    columns = turn_to(layout, even_ref[...], odd_ref[...], angles)
    for ref, value in zip(out_refs, columns):
        ref[...] = value


def next_bands(x_found, y_found, x_second, y_second):
    corner = x_found[CORNER:ROTATION] + y_found[CORNER:ROTATION]
    middle = cross_bands(corner, x_found[ROTATION:], y_found[ROTATION:])
    half = corner.shape[1] // 2
    lane = lanes_of(middle[0])
    diag = lax.broadcasted_iota(jnp.int32, middle[0].shape, 0)
    bands = []
    for q in range(4):
        rows = slice(NEAR + q * DIAGS, NEAR + (q + 1) * DIAGS)
        x, y = x_found[rows], y_found[rows]
        x = jnp.where(x_second, right(x, half), x)
        y = jnp.where(y_second, y, right(y, half))
        crossing = jnp.where(lane - diag < half, middle[q], y)
        bands.append(jnp.where(lane < half, x, crossing))
    return bands


def next_kernel(is_second, sends_first, layout_of, *refs):
    mine_even, mine_odd, even_ref, odd_ref, found_ref, other_ref, kept_ref, sent_ref = refs
    found, other = found_ref[...], other_ref[...]
    flag = on_odd_core()
    x_found, y_found = jnp.where(flag, other, found), jnp.where(flag, found, other)
    bands = next_bands(x_found, y_found, among(is_second[0]), among(is_second[1]))
    x_swapped, y_swapped = halves_swapped(is_second)
    swapped = either(flag, x_swapped, y_swapped)
    layout = in_pair(even_ref, swapped)
    theirs = turn_to(layout, even_ref[...], odd_ref[...], angles_in(other))
    low = line_lanes(found) < found.shape[1] // 2
    from_mine = jnp.logical_xor(low, flag)
    even = jnp.where(from_mine, mine_even[...], theirs[0])
    odd = jnp.where(from_mine, mine_odd[...], theirs[1])
    angles = angles_of(bands)
    first, second = turn_to(layout_of(even), even, odd, angles)
    flag = among(sends_first)
    kept_ref[...] = jnp.where(flag, second, first)
    sent_ref[...] = jnp.where(flag, first, second)


def pair_sums(arrays):
    while len(arrays) > 1:
        arrays = [arrays[i] + arrays[i + 1] for i in range(0, len(arrays), 2)]
    return arrays[0]


def swap(x, axis, mask):
    return lax.ppermute(x, axis, [(i, i ^ mask) for i in range(lax.axis_size(axis))])


def exchange_groups(x, axis, first_bit=0):
    count = lax.axis_size(axis).bit_length() - 1
    bits = [1 << b for b in range(count)]
    groups = [bits[:1]] + [bits[i : i + 2] for i in range(1, count, 2)]
    arrays = [x]
    for group in groups[first_bit:]:
        x = pair_sums(arrays)
        masks = [group[0]] if len(group) == 1 else [group[0], group[1], group[0] | group[1]]
        arrays = [x] + [swap(x, axis, mask) for mask in masks]
    return arrays


def call(kernel, shapes, *args):
    out = [jax.ShapeDtypeStruct(shape, jnp.float32) for shape in shapes]
    return pl.pallas_call(
        kernel,
        out_shape=out,
        compiler_params=pltpu.CompilerParams(vmem_limit_bytes=32 * 1024 * 1024),
    )(*args)


def two_rounds(opened, is_second, sends_first, layout_of):
    *columns, other = opened
    column, width = columns[0].shape, columns[0].shape[1]
    other = swap(other, "row", 1)
    bands = functools.partial(bands_kernel, is_second)
    (mine,) = call(bands, (other.shape,), *columns)
    (found,) = call(
        functools.partial(angles_kernel, is_second),
        ((FOUND, width),),
        *exchange_groups(mine + other, "row", 1),
    )
    other = swap(found, "row", 1)
    turn = functools.partial(columns_kernel, is_second)
    columns[:2] = call(turn, (column, column), *columns[:2], found)
    turn = functools.partial(next_kernel, is_second, sends_first, layout_of)
    return call(turn, (column, column), *columns, found, other)


def per_device(basis):
    rows, cols = basis.shape
    width = cols // 2
    pair_total = lax.axis_size("pair")
    column = (rows, width)
    opened = (column,) * 4 + ((4 * PACKED + WINDOW, width),)
    payload = (rows + strip_rows(rows, width), width)

    sends, sends_second, gets_second, own_second, is_second = first_moves(pair_total)
    (sent,) = call(functools.partial(payload_kernel, sends_second), (payload,), basis)
    came = lax.ppermute(sent, "pair", sends)
    even, odd = call(open_kernel, (column, column), basis)
    opening = functools.partial(first_open, own_second, gets_second, is_second)
    arrays = call(opening, opened, even, odd, came)
    sends, sends_first, picks, next_second = fused_moves(pair_total)
    kept, sent = two_rounds(arrays, is_second, sends_first, in_blocks)

    came = [lax.ppermute(x, "pair", s) for x, s in zip((sent, kept), sends)]
    opening = functools.partial(fused_open, picks, next_second)
    arrays = call(opening, opened, kept, sent, *came)
    sends, sends_first, gets_first = last_moves(pair_total)
    kept, sent = two_rounds(arrays, next_second, sends_first, in_order)

    came = lax.ppermute(sent, "pair", sends)
    flag = among(gets_first)
    first = jnp.where(flag, came, kept)
    second = jnp.where(flag, kept, came)
    return jnp.concatenate((first, second), axis=1)


def solution(mesh):
    return jax.shard_map(
        per_device,
        mesh=mesh,
        in_specs=(P("row", "pair"),),
        out_specs=P("row", "pair"),
        check_vma=False,
    )
```

```python
import functools

import jax
import jax.numpy as jnp
import numpy as np
from jax import lax
from jax.experimental import pallas as pl
from jax.experimental.pallas import tpu as pltpu
from jax.sharding import PartitionSpec as P

ROUNDS = 4
JSTEPS = 6
REACH = 2 * (JSTEPS - 1) + 1
DIAGS = 16
FAR_DIAGS = 32
WINDOW = 32
NEAR = 16
STRIP = REACH - 1
BACK = 3


def tournament_order(pair_count):
    ordering = np.zeros(2 * pair_count, dtype=np.int64)
    ordering[0] = 0
    ordering[2] = 1
    for slot in range(2, pair_count):
        ordering[2 * slot] = 2 * (slot - 1)
    for slot in range(pair_count - 1):
        ordering[2 * slot + 1] = 2 * (slot + 1) + 1
    ordering[2 * pair_count - 1] = 2 * (pair_count - 1)
    return ordering


def host_of(pair, pair_total, round_index):
    if round_index % 2 == 0 or pair == 0:
        return pair
    return min(pair + 1, pair_total - 1) if pair % 2 else pair - 1


def last_moves(pair_total):
    ordering = tournament_order(pair_total)
    sends, sends_first, gets_first = [], set(), set()
    for pair in range(pair_total):
        target = host_of(pair, pair_total, ROUNDS)
        for place in (0, 1):
            old = int(ordering[2 * pair + place])
            source = host_of(old // 2, pair_total, ROUNDS - 1)
            if source == target:
                continue
            sends.append((source, target))
            if old % 2 == 0:
                sends_first.add(source)
            if place == 0:
                gets_first.add(target)
    assert len({s for s, _ in sends}) == len(sends) == len({t for _, t in sends})
    return sends, sends_first, gets_first


def first_moves(pair_total):
    ordering = tournament_order(pair_total)
    sends, sends_second, gets_second, own_second = [], set(), set(), set()
    seconds = (set(), set())
    for pair in range(pair_total):
        here = host_of(pair, pair_total, 1)
        for place in (0, 1):
            old = int(ordering[2 * pair + place])
            if old % 2:
                seconds[place].add(here)
            if old // 2 == here:
                if place:
                    own_second.add(here)
                continue
            sends.append((old // 2, here))
            if old % 2:
                sends_second.add(old // 2)
                gets_second.add(here)
    assert len({s for s, _ in sends}) == len(sends) == len({t for _, t in sends})
    return sends, sends_second, gets_second, own_second, seconds


def fused_moves(pair_total):
    ordering = tournament_order(pair_total)
    before, last = ROUNDS - 3, ROUNDS - 1
    needs, edges, seconds = {}, [], ({}, {})
    for pair in range(pair_total):
        here = host_of(pair, pair_total, last)
        needs[here] = []
        for place in (0, 1):
            source = int(ordering[2 * pair + place])
            seconds[place][here] = source % 2
            for half in (0, 1):
                old = int(ordering[2 * (source // 2) + half])
                there = host_of(old // 2, pair_total, before)
                needs[here].append((there, old % 2))
                if there != here:
                    edges.append((there, old % 2, here))
    turn, left_over = {}, list(edges)
    while left_over:
        source, _, target = left_over[0]
        start = source
        while True:
            for number, one, other in ((0, source, target), (1, target, source)):
                edge = next(e for e in left_over if (e[0], e[2]) == (one, other))
                turn[edge] = number
                left_over.remove(edge)
            if target == start:
                break
            ahead = [e[2] for e in left_over if e[0] == target]
            source, target = target, ahead[0]
    sends = [[(e[0], e[2]) for e in edges if turn[e] == i] for i in (0, 1)]
    for chosen in sends:
        assert len({a for a, _ in chosen}) == len({b for _, b in chosen}) == pair_total
    sends_first = {e[0] for e in edges if turn[e] == 0 and e[1] == 0}
    picks = []
    for slot in range(4):
        pick = {}
        for here in range(pair_total):
            there, half = needs[here][slot]
            if there == here:
                pick[here] = 0 if (half == 0) == (here in sends_first) else 1
            else:
                pick[here] = 2 + turn[(there, half, here)]
        picks.append(pick)
    is_second = [{h for h, place in table.items() if place} for table in seconds]
    return sends, sends_first, picks, is_second


def choose(pick, arrays):
    chosen = arrays[0]
    for number in range(1, len(arrays)):
        members = {here for here, value in pick.items() if value == number}
        if members:
            chosen = jnp.where(among(members), arrays[number], chosen)
    return chosen


def among(members):
    here = lax.axis_index("pair")
    return functools.reduce(
        jnp.logical_or, [here == member for member in sorted(members)], here < 0
    )


def left(x, by):
    width = x.shape[1]
    return pltpu.roll(x, (width - by) % width, 1) if by % width else x


def right(x, by):
    width = x.shape[1]
    return pltpu.roll(x, by % width, 1) if by % width else x


def down(x, by):
    return pltpu.roll(x, by % x.shape[0], 0)


def lanes_of(x):
    return lax.broadcasted_iota(jnp.int32, x.shape, 1)


def split_pair(first, second):
    half = first.shape[1] // 2
    low = lanes_of(first) < half
    even = jnp.where(low, first, right(second, half))
    odd = jnp.where(low, right(first, half), second)
    return even, odd


def take_lanes(x, source):
    if x.shape[0] == 1:
        return take_lanes(jnp.broadcast_to(x, (8, x.shape[1])), source)[:1]
    return jnp.take_along_axis(x, jnp.broadcast_to(source, x.shape), axis=1)


def line_lanes(x):
    return lax.broadcasted_iota(jnp.int32, (1, x.shape[1]), 1)


def separate(first, second):
    lane = line_lanes(first)
    half = first.shape[1] // 2
    low = lane < half
    source = 2 * jnp.where(low, lane, lane - half)
    return tuple(
        jnp.where(low, take_lanes(first, source + odd), take_lanes(second, source + odd))
        for odd in (0, 1)
    )


def backwards(x):
    return jnp.take_along_axis(x, x.shape[1] - 1 - lanes_of(x), axis=1)


def dense_bands(even, odd, diags):
    width = even.shape[1]
    gram = lax.dot_general(
        jnp.concatenate((even, odd), axis=1),
        jnp.concatenate((backwards(even), backwards(odd)), axis=1),
        (((0,), (0,)), ((), ())),
        precision=lax.Precision.HIGHEST,
        preferred_element_type=jnp.float32,
    )
    bands = []
    for near in (0, width):
        for far in (0, width):
            quadrant = gram[far : far + width, near : near + width]
            aligned = pltpu.roll(quadrant, 1, 1, stride=1, stride_axis=0)
            bands.append(jnp.transpose(aligned)[:diags])
    return bands


def store_bands(even, odd, band_ref, diags):
    for q, band in enumerate(dense_bands(even, odd, diags)):
        band_ref[q * diags : (q + 1) * diags, :] = band


def strip_rows(rows, width):
    return -(-rows // (8 * (width // (2 * STRIP)))) * 8


def payload_kernel(sends_second, basis_ref, payload_ref):
    rows, cols = basis_ref.shape
    width = cols // 2
    half = width // 2
    first, second = basis_ref[:, :width], basis_ref[:, width:]
    lane = line_lanes(first)
    start = jnp.where(among(sends_second), half - STRIP, 0)
    place = start + jnp.where(lane < half, lane, lane - half)
    odd = jnp.where(lane < half, 0, 1)
    in_first = place < half
    source = 2 * jnp.where(in_first, place, place - half) + odd
    payload_ref[:rows] = jnp.where(in_first, take_lanes(first, source), take_lanes(second, source))
    places = width // STRIP
    place = lane - STRIP * sum(jnp.where(lane >= STRIP * i, 1, 0) for i in range(1, places))
    odd = sum(jnp.where(lane >= STRIP * i, 1 if i % 2 else -1, 0) for i in range(1, places))
    source = jnp.minimum(2 * (start + place) + odd, width - 1)
    group = strip_rows(rows, width)
    strips = jnp.zeros((group, width), jnp.float32)
    for i, at in enumerate(range(0, rows, group)):
        here = jnp.logical_and(lane >= 2 * STRIP * i, lane < 2 * STRIP * (i + 1))
        part = take_lanes(second[at : at + group], source)
        if part.shape[0] < group:
            spare = jnp.zeros((group - part.shape[0], width), jnp.float32)
            part = jnp.concatenate((part, spare), axis=0)
        strips = jnp.where(here, part, strips)
    payload_ref[rows:] = strips


def open_kernel(basis_ref, even_ref, odd_ref):
    width = basis_ref.shape[1] // 2
    even_ref[...], odd_ref[...] = separate(basis_ref[:, :width], basis_ref[:, width:])


def unpacked(payload, rows, second):
    width = payload.shape[1]
    half = width // 2
    lane = line_lanes(payload)
    main, strips = payload[:rows], payload[rows:]
    group = strips.shape[0]
    columns = []
    for j, x in enumerate((main, left(main, half))):
        ends = [
            right(strips, half - (2 * i + j) * STRIP)[: rows - at]
            for i, at in enumerate(range(0, rows, group))
        ]
        ends = jnp.concatenate(ends, axis=0)
        x = jnp.where(lane < half, x, jnp.where(lane < half + STRIP, ends, 0.0))
        columns.append(jnp.where(second, right(x, half - STRIP), x))
    return columns


def jacobi_angle(diag_even, diag_odd, coupling):
    spread = diag_even - diag_odd
    square = spread * spread + 4.0 * coupling * coupling
    inverse = lax.rsqrt(square)
    larger_square = (square * inverse + jnp.abs(spread)) * (0.5 * inverse)
    larger_inverse = lax.rsqrt(larger_square)
    larger = larger_square * larger_inverse
    smaller = coupling * inverse * larger_inverse
    forward = spread >= 0.0
    sign = jnp.where(coupling > 0.0, 1.0, jnp.where(coupling < 0.0, -1.0, 0.0))
    cosine = jnp.where(forward, larger, jnp.abs(smaller))
    sine_part = jnp.where(forward, smaller, sign * larger)
    return cosine, sine_part


def turn_bands(ee, eo, oe, oo, cosine, sine):
    cl, sl = jnp.broadcast_to(cosine, ee.shape), jnp.broadcast_to(sine, ee.shape)
    ck = pltpu.roll(cl, 0, 1, stride=1, stride_axis=0)
    sk = pltpu.roll(sl, 0, 1, stride=1, stride_axis=0)
    ee, oe = ck * ee + sk * oe, ck * oe - sk * ee
    eo, oo = ck * eo + sk * oo, ck * oo - sk * eo
    ee, eo = cl * ee + sl * eo, cl * eo - sl * ee
    oe, oo = cl * oe + sl * oo, cl * oo - sl * oe
    return ee, eo, oe, oo


def step_bands(ee, eo, oe, oo, cosine, sine):
    lane = lanes_of(ee)
    diag = lax.broadcasted_iota(jnp.int32, ee.shape, 0)
    last = lane == ee.shape[1] - 1
    on, next_on = diag == 0, diag == 1

    def slanted(x, by):
        if by >= 0:
            return pltpu.roll(x, by, 1, stride=1, stride_axis=0)
        return jnp.where(on, left(x, -by), down(slanted(x, 0), -by))

    def rotated(by, wanted):
        cl, sl = (jnp.broadcast_to(x, ee.shape) for x in (cosine, sine))
        ck, sk = (slanted(x, by) for x in (cl, sl))
        cl, sl, a, b, c, d = (right(x, by) for x in (cl, sl, ee, eo, oe, oo))
        a, c = ck * a + sk * c, ck * c - sk * a
        b, d = ck * b + sk * d, ck * d - sk * b
        found = {"ee": (a, b), "eo": (b, a), "oe": (c, d), "oo": (d, c)}
        return [
            cl * one + sl * two if name in ("ee", "oe") else cl * one - sl * two
            for name, (one, two) in found.items()
            if name in wanted
        ]

    ee_0, eo_0, oe_0, oo_0 = rotated(0, ("ee", "eo", "oe", "oo"))
    ee_r, eo_r, oe_r, oo_r = rotated(1, ("ee", "eo", "oe", "oo"))
    eo_l, oo_l = rotated(-1, ("eo", "oo"))

    near = down(jnp.where(on, eo_r, ee_r), 1)
    turned = jnp.where(on, oo_r, oe_r)
    ee_new = jnp.where(lane == diag + 1, turned, jnp.where(lane == diag, near, ee_r))
    ee_new = jnp.where(jnp.logical_and(on, lane == 0), ee_0, ee_new)

    eo_new = down(jnp.where(lane == diag - 1, oo_l, eo_l), -2)
    eo_new = jnp.where(lane == diag, down(eo_l, -1), eo_new)
    eo_new = jnp.where(last, down(ee_0, -1), eo_new)

    oo_new = jnp.where(last, jnp.where(on, ee_0, down(oe_0, 1)), oo_l)

    oe_new = down(oe_r, 2)
    oe_new = jnp.where(next_on, jnp.where(lane == diag, oo_0, eo_0), oe_new)
    oe_new = jnp.where(on, eo_new, oe_new)
    return ee_new, eo_new, oe_new, oo_new


def move_bands(ee, eo, oe, oo):
    lane = lanes_of(ee)
    diag = lax.broadcasted_iota(jnp.int32, ee.shape, 0)
    last = lane == ee.shape[1] - 1
    on, next_on = diag == 0, diag == 1

    near = down(jnp.where(on, eo, ee), 1)
    turned = jnp.where(on, oo, oe)
    mixed = jnp.where(lane == diag, turned, jnp.where(lane == diag - 1, near, ee))
    ee_new = jnp.where(jnp.logical_and(on, lane == 0), ee, right(mixed, 1))

    far = down(jnp.where(last, ee, eo), -1)
    mixed = down(jnp.where(lane == diag, oo, eo), -2)
    mixed = left(jnp.where(lane == diag + 1, far, mixed), 1)
    eo_new = jnp.where(last, far, mixed)

    oo_new = jnp.where(last, jnp.where(on, ee, down(oe, 1)), left(oo, 1))

    oe_new = right(down(oe, 2), 1)
    oe_new = jnp.where(next_on, jnp.where(lane == diag, oo, eo), oe_new)
    oe_new = jnp.where(on, eo_new, oe_new)
    return ee_new, eo_new, oe_new, oo_new


def move_bands_back(views, by):
    ee, eo, oe, oo = views[by]
    ee_left, _, oe_left, _ = views[by - 1]
    _, eo_right, _, oo_right = views[by + 1]
    width = ee.shape[1]
    lane = lanes_of(ee) - by
    lane = jnp.where(lane < 0, lane + width, jnp.where(lane >= width, lane - width, lane))
    diag = lax.broadcasted_iota(jnp.int32, ee.shape, 0)
    last, first = lane == width - 1, lane == diag
    on, next_on = diag == 0, diag == 1
    oo_up, eo_twice = down(oo, -1), down(eo_right, 2)

    far = jnp.where(first, down(ee_left, -1), ee_left)
    ee_old = jnp.where(jnp.logical_and(first, on), ee, far)
    ee_old = jnp.where(last, jnp.where(on, oo, down(eo, 1)), ee_old)

    near = jnp.where(jnp.logical_and(first, diag > 0), ee_left, down(oe_left, -2))
    eo_old = jnp.where(first, down(eo_right, 1), eo_twice)
    eo_old = jnp.where(on, jnp.where(last, oo_up, near), eo_old)
    eo_old = jnp.where(jnp.logical_and(next_on, lane > 1), oe, eo_old)
    eo_old = jnp.where(jnp.logical_and(on, first), far, eo_old)

    oe_old = jnp.where(on, eo_old, jnp.where(last, oo_up, near))

    oo_old = jnp.where(first, eo_twice, oo_right)
    oo_old = jnp.where(jnp.logical_and(next_on, first), oe, oo_old)
    oo_old = jnp.where(jnp.logical_and(on, first), ee_left, oo_old)
    return ee_old, eo_old, oe_old, oo_old


def bands_back(bands, count):
    views = {by: [right(x, by) for x in bands] for by in range(-count, count + 1)}
    for reach in reversed(range(count)):
        views = {by: move_bands_back(views, by) for by in range(-reach, reach + 1)}
    return views[0]


def move_columns(even, odd):
    lane = lanes_of(even)
    first, last = lane == 0, lane == even.shape[1] - 1
    even_new = jnp.where(first, even, right(jnp.where(first, odd, even), 1))
    odd_new = jnp.where(last, even, left(odd, 1))
    return even_new, odd_new


def in_pair(even, shifted=None):
    lane = line_lanes(even)
    if shifted is not None:
        half = even.shape[1] // 2
        lane = jnp.where(shifted, jnp.where(lane < half, lane + half, lane - half), lane)
    return (lane < 0, lane), (lane >= 0, lane)


def in_blocks(even):
    lane, half = line_lanes(even), even.shape[1] // 2
    place = jnp.where(lane < half, lane, lane - half)
    return (lane >= half, place), (lane >= half, place + half)


def in_order(even):
    lane, half = line_lanes(even), even.shape[1] // 2
    return (lane % 2 == 1, lane // 2), (lane % 2 == 1, lane // 2 + half)


def turn_to(layout, even, odd, angles):
    for cosine, sine in angles[:-1]:
        even, odd = cosine * even + sine * odd, cosine * odd - sine * even
        even, odd = move_columns(even, odd)
    by, end = JSTEPS - 1, even.shape[1] - 1
    results = []
    for is_odd, place in layout:
        stayed = place <= end - by
        from_even = jnp.where(stayed, place + by, 2 * end + 1 - by - place)
        from_even = jnp.where(place == 0, 0, from_even)
        source = jnp.where(is_odd, jnp.abs(place - by), from_even)
        is_even = jnp.logical_or(
            jnp.logical_and(is_odd, place < by),
            jnp.logical_and(jnp.logical_not(is_odd), stayed),
        )
        cosine, sine = (take_lanes(x, source) for x in angles[-1])
        by_even = jnp.where(is_even, cosine, -sine)
        by_odd = jnp.where(is_even, sine, cosine)
        results.append(by_even * take_lanes(even, source) + by_odd * take_lanes(odd, source))
    return results


def trim(bands, reach):
    rows = min(bands[0].shape[0], -(-(reach + 1) // 8) * 8)
    return [band[:rows] for band in bands]


def angles_of(bands):
    angles = []
    for step in range(JSTEPS):
        ee, eo, oe, oo = bands = trim(bands, 2 * (JSTEPS - 1 - step))
        angles.append(jacobi_angle(ee[0:1], oo[0:1], eo[0:1]))
        if step < JSTEPS - 1:
            bands = step_bands(*bands, *angles[-1])
    return angles


def carried(bands, angles):
    ahead = 2 * (JSTEPS - 1)
    for step, (cosine, sine) in enumerate(angles):
        bands = turn_bands(*trim(bands, 3 * ahead - 2 * step), cosine, sine)
        if step < JSTEPS - 1:
            bands = move_bands(*bands)
    done = 0
    while done < JSTEPS - 1:
        count = min(BACK, JSTEPS - 1 - done)
        bands = bands_back(trim(bands, 2 * (ahead - done)), count)
        done += count
    return bands


def near_starts(width):
    half = width // 2
    reach = REACH - 1
    return (half - 2 * reach, width - WINDOW), (0, half - reach)


def cross_partial(x_even, x_odd, y_even, y_odd, x_second, y_second):
    width = x_even.shape[1]
    half = width // 2
    x_starts, y_starts = near_starts(width)
    lane = line_lanes(x_even)

    def window(even, odd, start):
        here = jnp.logical_and(lane >= start, lane < start + WINDOW)
        return jnp.where(here, even, right(odd, half))

    x_start = jnp.where(x_second, x_starts[1], x_starts[0])
    y_start = jnp.where(y_second, y_starts[1], y_starts[0])
    product = lax.dot_general(
        window(y_even, y_odd, y_start),
        window(x_even, x_odd, x_start),
        (((0,), (0,)), ((), ())),
        precision=lax.Precision.HIGHEST,
        preferred_element_type=jnp.float32,
    )
    product = pltpu.roll(product, (width - y_start) % width, 0)
    product = pltpu.roll(product, (width - x_start) % width, 1)
    upper, lower = product[:WINDOW], product[half : half + WINDOW]
    upper = jnp.where(lane < WINDOW, upper, left(upper, half - WINDOW))
    lower = jnp.where(lane < half + WINDOW, right(lower, half), right(lower, WINDOW))
    return jnp.where(lane < half, upper, lower)


def own_rotation(angles, second, swapped, first_pair):
    width = angles[0][0].shape[1]
    half = width // 2
    x_starts, y_starts = near_starts(width)
    starts = [jnp.where(first_pair, x, y) for x, y in zip(x_starts, y_starts)]
    shape = (2 * WINDOW, width)
    row = lax.broadcasted_iota(jnp.int32, shape, 0)
    lane = lax.broadcasted_iota(jnp.int32, shape, 1) - jnp.where(second, starts[1], starts[0])
    even, odd = (
        jnp.where(jnp.logical_and(row == lane + at, row // WINDOW == at // WINDOW), 1.0, 0.0)
        for at in (0, WINDOW)
    )
    even, odd = turn_to(in_pair(even, swapped), even, odd, angles)
    low = lax.broadcasted_iota(jnp.int32, shape, 1) < half
    return jnp.where(jnp.logical_xor(low, first_pair), right(odd, half), even)


def cross_bands(packed, x_rotation, y_rotation):
    width = packed.shape[1]
    half = width // 2
    corner = jnp.concatenate((packed[:, :half], right(packed, half)[:, :half]), axis=0)
    highest = dict(precision=lax.Precision.HIGHEST, preferred_element_type=jnp.float32)
    turned_x = jnp.dot(corner, x_rotation, **highest)
    ends = lax.dot_general(turned_x, y_rotation, (((0,), (0,)), ((), ())), **highest)
    even, odd = ends[half - NEAR : half], ends[width - NEAR :]
    quadrants = (even, right(even, half), odd, right(odd, half))
    offset = lanes_of(even) - lax.broadcasted_iota(jnp.int32, even.shape, 0) - (half - NEAR)
    diag = lax.broadcasted_iota(jnp.int32, (DIAGS, width), 0)
    bands = [jnp.zeros((DIAGS, width), jnp.float32) for _ in quadrants]
    for d in range(1, REACH):
        here = offset == d
        for q, quadrant in enumerate(quadrants):
            line = jnp.sum(jnp.where(here, quadrant, 0.0), axis=0, keepdims=True)
            bands[q] = jnp.where(diag == d, line, bands[q])
    return bands


def either(flag, one, other):
    return jnp.logical_or(jnp.logical_and(flag, one), jnp.logical_and(jnp.logical_not(flag), other))


def halves_swapped(is_second):
    return among(is_second[0]), jnp.logical_not(among(is_second[1]))


def on_odd_core():
    return lax.axis_index("row") % 2 == 1


PLACES = (
    (((16, 16, 80), (60, 16, 108)), ((16, 28, 21), (44, 30, 80))),
    (((68, 16, 24), (112, 16, 0)), ((70, 29, 84), (99, 29, 10))),
)
MIDDLES = (44, 99)


def pick_by(flag, one, other):
    return jnp.where(flag, other, one)


def pack_far(bands, flag):
    width = bands[0].shape[1]
    lane = lax.broadcasted_iota(jnp.int32, (DIAGS, width), 1)
    odd_row = lax.broadcasted_iota(jnp.int32, (DIAGS, width), 0) % 2 == 1
    moves = []
    for parity in (0, 1):
        for part in (0, 1):
            one, other = PLACES[0][parity][part], PLACES[1][parity][part]
            shift = pick_by(flag, (one[2] - one[0]) % width, (other[2] - other[0]) % width)
            start = pick_by(flag, one[2], other[2])
            count = pick_by(flag, one[1], other[1])
            here = jnp.logical_and(lane >= start, lane < start + count)
            moves.append((shift, jnp.logical_and(here, odd_row == (parity == 1))))
    packed = []
    for band in bands:
        near, far = band[:DIAGS], down(band[DIAGS:], -1)
        for shift, here in moves:
            near = jnp.where(here, pltpu.roll(far, shift, 1), near)
        packed.append(near)
    return packed


def unpack_far(packed, flag):
    width = packed.shape[1]
    lane = lanes_of(packed)
    odd_row = lax.broadcasted_iota(jnp.int32, packed.shape, 0) % 2 == 1
    parts = []
    for part in (0, 1):
        rolled = []
        for parity in (0, 1):
            one, other = PLACES[0][parity][part], PLACES[1][parity][part]
            shift = pick_by(flag, (one[0] - one[2]) % width, (other[0] - other[2]) % width)
            rolled.append(pltpu.roll(packed, shift, 1))
        parts.append(jnp.where(odd_row, rolled[1], rolled[0]))
    far = jnp.where(lane < pick_by(flag, *MIDDLES), *parts)
    return jnp.concatenate((packed, down(far, 1)), axis=0)


PACKED = DIAGS


def store_part(even, odd, flag, part_ref):
    bands = pack_far(dense_bands(even, odd, FAR_DIAGS), flag)
    for q, band in enumerate(bands):
        part_ref[q * PACKED : (q + 1) * PACKED, :] = band


def open_pairs(is_second, x, y, column_refs, corner_ref, other_ref):
    corner = cross_partial(*x, *y, among(is_second[0]), among(is_second[1]))
    flag = on_odd_core()
    mine = [jnp.where(flag, b, a) for a, b in zip(x, y)]
    theirs = [jnp.where(flag, a, b) for a, b in zip(x, y)]
    for ref, value in zip(column_refs, mine + theirs):
        ref[...] = value
    store_part(*theirs, either(flag, among(is_second[0]), among(is_second[1])), other_ref)
    corner_ref[...] = jnp.where(flag, corner[NEAR:], corner[:NEAR])
    other_ref[4 * PACKED :, :] = jnp.where(flag, corner[:NEAR], corner[NEAR:])


def first_open(own_second, gets_second, is_second, even_ref, odd_ref, payload_ref, *refs):
    *column_refs, corner_ref, other_ref = refs
    own = even_ref[...], odd_ref[...]
    came = unpacked(payload_ref[...], own[0].shape[0], among(gets_second))
    flag = among(own_second)
    x = [jnp.where(flag, b, a) for a, b in zip(own, came)]
    y = [jnp.where(flag, a, b) for a, b in zip(own, came)]
    open_pairs(is_second, x, y, column_refs, corner_ref, other_ref)


def fused_open(picks, is_second, kept_ref, sent_ref, came0_ref, came1_ref, *refs):
    *column_refs, corner_ref, other_ref = refs
    arrays = [ref[...] for ref in (sent_ref, kept_ref, came0_ref, came1_ref)]
    blocks = [choose(pick, arrays) for pick in picks]
    x, y = split_pair(*blocks[:2]), split_pair(*blocks[2:])
    open_pairs(is_second, x, y, column_refs, corner_ref, other_ref)


def swapped_flag(is_second):
    x_swapped, y_swapped = halves_swapped(is_second)
    return either(on_odd_core(), y_swapped, x_swapped)


def own_second_flag(is_second):
    return either(on_odd_core(), among(is_second[1]), among(is_second[0]))


def bands_kernel(is_second, even_ref, odd_ref, corner_ref, part_ref):
    store_part(even_ref[...], odd_ref[...], own_second_flag(is_second), part_ref)
    part_ref[4 * PACKED :, :] = corner_ref[...]


def angles_kernel(is_second, *refs):
    *part_refs, found_ref = refs
    part = pair_sums([ref[...] for ref in part_refs])
    flag = own_second_flag(is_second)
    quadrants = [unpack_far(part[q * PACKED : (q + 1) * PACKED], flag) for q in range(4)]
    angles = angles_of(quadrants)
    bands = carried(quadrants, angles)
    for step, pair in enumerate(angles):
        for i in (0, 1):
            found_ref[2 * step + i : 2 * step + i + 1, :] = pair[i]
    spare = NEAR - 2 * JSTEPS
    found_ref[2 * JSTEPS : NEAR, :] = jnp.zeros((spare, part.shape[1]), jnp.float32)
    for q in range(4):
        found_ref[NEAR + q * DIAGS : NEAR + (q + 1) * DIAGS, :] = bands[q][:DIAGS]
    found_ref[CORNER:ROTATION, :] = part[4 * PACKED :]
    first_pair = jnp.logical_not(on_odd_core())
    found_ref[ROTATION:, :] = own_rotation(angles, flag, swapped_flag(is_second), first_pair)


CORNER = NEAR + 4 * DIAGS
ROTATION = CORNER + NEAR
FOUND = ROTATION + 2 * WINDOW


def angles_in(found):
    return [(found[2 * i : 2 * i + 1], found[2 * i + 1 : 2 * i + 2]) for i in range(JSTEPS)]


def columns_kernel(is_second, even_ref, odd_ref, found_ref, *out_refs):
    angles = angles_in(found_ref[...])
    layout = in_pair(even_ref, swapped_flag(is_second))
    columns = turn_to(layout, even_ref[...], odd_ref[...], angles)
    for ref, value in zip(out_refs, columns):
        ref[...] = value


def next_bands(x_found, y_found, x_second, y_second):
    corner = jnp.concatenate((x_found[CORNER:ROTATION], y_found[CORNER:ROTATION]), axis=0)
    middle = cross_bands(corner, x_found[ROTATION:], y_found[ROTATION:])
    half = corner.shape[1] // 2
    lane = lanes_of(middle[0])
    diag = lax.broadcasted_iota(jnp.int32, middle[0].shape, 0)
    bands = []
    for q in range(4):
        rows = slice(NEAR + q * DIAGS, NEAR + (q + 1) * DIAGS)
        x, y = x_found[rows], y_found[rows]
        x = jnp.where(x_second, right(x, half), x)
        y = jnp.where(y_second, y, right(y, half))
        crossing = jnp.where(lane - diag < half, middle[q], y)
        bands.append(jnp.where(lane < half, x, crossing))
    return bands


def next_kernel(is_second, sends_first, layout_of, *refs):
    mine_even, mine_odd, even_ref, odd_ref, found_ref, other_ref, kept_ref, sent_ref = refs
    found, other = found_ref[...], other_ref[...]
    flag = on_odd_core()
    x_found, y_found = jnp.where(flag, other, found), jnp.where(flag, found, other)
    bands = next_bands(x_found, y_found, among(is_second[0]), among(is_second[1]))
    x_swapped, y_swapped = halves_swapped(is_second)
    swapped = either(flag, x_swapped, y_swapped)
    layout = in_pair(even_ref, swapped)
    theirs = turn_to(layout, even_ref[...], odd_ref[...], angles_in(other))
    low = line_lanes(found) < found.shape[1] // 2
    from_mine = jnp.logical_xor(low, flag)
    even = jnp.where(from_mine, mine_even[...], theirs[0])
    odd = jnp.where(from_mine, mine_odd[...], theirs[1])
    angles = angles_of(bands)
    first, second = turn_to(layout_of(even), even, odd, angles)
    flag = among(sends_first)
    kept_ref[...] = jnp.where(flag, second, first)
    sent_ref[...] = jnp.where(flag, first, second)


def pair_sums(arrays):
    while len(arrays) > 1:
        arrays = [arrays[i] + arrays[i + 1] for i in range(0, len(arrays), 2)]
    return arrays[0]


def swap(x, axis, mask):
    return lax.ppermute(x, axis, [(i, i ^ mask) for i in range(lax.axis_size(axis))])


def exchange_groups(x, axis, first_bit=0):
    count = lax.axis_size(axis).bit_length() - 1
    bits = [1 << b for b in range(count)]
    groups = [bits[:1]] + [bits[i : i + 2] for i in range(1, count, 2)]
    arrays = [x]
    for group in groups[first_bit:]:
        x = pair_sums(arrays)
        masks = [group[0]] if len(group) == 1 else [group[0], group[1], group[0] | group[1]]
        arrays = [x] + [swap(x, axis, mask) for mask in masks]
    return arrays


def call(kernel, shapes, *args):
    out = [jax.ShapeDtypeStruct(shape, jnp.float32) for shape in shapes]
    return pl.pallas_call(
        kernel,
        out_shape=out,
        compiler_params=pltpu.CompilerParams(vmem_limit_bytes=32 * 1024 * 1024),
    )(*args)


def two_rounds(opened, is_second, sends_first, layout_of):
    *columns, corner, other = opened
    column, width = columns[0].shape, columns[0].shape[1]
    other = swap(other, "row", 1)
    bands = functools.partial(bands_kernel, is_second)
    (mine,) = call(bands, (other.shape,), *columns[:2], corner)
    (found,) = call(
        functools.partial(angles_kernel, is_second),
        ((FOUND, width),),
        *exchange_groups(mine + other, "row", 1),
    )
    other = swap(found, "row", 1)
    turn = functools.partial(columns_kernel, is_second)
    columns[:2] = call(turn, (column, column), *columns[:2], found)
    turn = functools.partial(next_kernel, is_second, sends_first, layout_of)
    return call(turn, (column, column), *columns, found, other)


def per_device(basis):
    rows, cols = basis.shape
    width = cols // 2
    pair_total = lax.axis_size("pair")
    column = (rows, width)
    opened = (column,) * 4 + ((NEAR, width), (4 * PACKED + NEAR, width))
    payload = (rows + strip_rows(rows, width), width)

    sends, sends_second, gets_second, own_second, is_second = first_moves(pair_total)
    (sent,) = call(functools.partial(payload_kernel, sends_second), (payload,), basis)
    came = lax.ppermute(sent, "pair", sends)
    even, odd = call(open_kernel, (column, column), basis)
    opening = functools.partial(first_open, own_second, gets_second, is_second)
    arrays = call(opening, opened, even, odd, came)
    sends, sends_first, picks, next_second = fused_moves(pair_total)
    kept, sent = two_rounds(arrays, is_second, sends_first, in_blocks)

    came = [lax.ppermute(x, "pair", s) for x, s in zip((sent, kept), sends)]
    opening = functools.partial(fused_open, picks, next_second)
    arrays = call(opening, opened, kept, sent, *came)
    sends, sends_first, gets_first = last_moves(pair_total)
    kept, sent = two_rounds(arrays, next_second, sends_first, in_order)

    came = lax.ppermute(sent, "pair", sends)
    flag = among(gets_first)
    first = jnp.where(flag, came, kept)
    second = jnp.where(flag, kept, came)
    return jnp.concatenate((first, second), axis=1)


def solution(mesh):
    return jax.shard_map(
        per_device,
        mesh=mesh,
        in_specs=(P("row", "pair"),),
        out_specs=P("row", "pair"),
        check_vma=False,
    )
```

```python
import functools

import jax
import jax.numpy as jnp
import numpy as np
from jax import lax
from jax.experimental import pallas as pl
from jax.experimental.pallas import tpu as pltpu
from jax.sharding import PartitionSpec as P

ROUNDS = 4
JSTEPS = 6
REACH = 2 * (JSTEPS - 1) + 1
DIAGS = 16
FAR_DIAGS = 32
WINDOW = 32
NEAR = 16
STRIP = REACH - 1
BACK = 3


def tournament_order(pair_count):
    ordering = np.zeros(2 * pair_count, dtype=np.int64)
    ordering[0] = 0
    ordering[2] = 1
    for slot in range(2, pair_count):
        ordering[2 * slot] = 2 * (slot - 1)
    for slot in range(pair_count - 1):
        ordering[2 * slot + 1] = 2 * (slot + 1) + 1
    ordering[2 * pair_count - 1] = 2 * (pair_count - 1)
    return ordering


def host_of(pair, pair_total, round_index):
    if round_index % 2 == 0 or pair == 0:
        return pair
    return min(pair + 1, pair_total - 1) if pair % 2 else pair - 1


def last_moves(pair_total):
    ordering = tournament_order(pair_total)
    sends, sends_first, gets_first = [], set(), set()
    for pair in range(pair_total):
        target = host_of(pair, pair_total, ROUNDS)
        for place in (0, 1):
            old = int(ordering[2 * pair + place])
            source = host_of(old // 2, pair_total, ROUNDS - 1)
            if source == target:
                continue
            sends.append((source, target))
            if old % 2 == 0:
                sends_first.add(source)
            if place == 0:
                gets_first.add(target)
    assert len({s for s, _ in sends}) == len(sends) == len({t for _, t in sends})
    return sends, sends_first, gets_first


def first_moves(pair_total):
    ordering = tournament_order(pair_total)
    sends, sends_second, gets_second, own_second = [], set(), set(), set()
    seconds = (set(), set())
    for pair in range(pair_total):
        here = host_of(pair, pair_total, 1)
        for place in (0, 1):
            old = int(ordering[2 * pair + place])
            if old % 2:
                seconds[place].add(here)
            if old // 2 == here:
                if place:
                    own_second.add(here)
                continue
            sends.append((old // 2, here))
            if old % 2:
                sends_second.add(old // 2)
                gets_second.add(here)
    assert len({s for s, _ in sends}) == len(sends) == len({t for _, t in sends})
    return sends, sends_second, gets_second, own_second, seconds


def fused_moves(pair_total):
    ordering = tournament_order(pair_total)
    before, last = ROUNDS - 3, ROUNDS - 1
    needs, edges, seconds = {}, [], ({}, {})
    for pair in range(pair_total):
        here = host_of(pair, pair_total, last)
        needs[here] = []
        for place in (0, 1):
            source = int(ordering[2 * pair + place])
            seconds[place][here] = source % 2
            for half in (0, 1):
                old = int(ordering[2 * (source // 2) + half])
                there = host_of(old // 2, pair_total, before)
                needs[here].append((there, old % 2))
                if there != here:
                    edges.append((there, old % 2, here))
    turn, left_over = {}, list(edges)
    while left_over:
        source, _, target = left_over[0]
        start = source
        while True:
            for number, one, other in ((0, source, target), (1, target, source)):
                edge = next(e for e in left_over if (e[0], e[2]) == (one, other))
                turn[edge] = number
                left_over.remove(edge)
            if target == start:
                break
            ahead = [e[2] for e in left_over if e[0] == target]
            source, target = target, ahead[0]
    sends = [[(e[0], e[2]) for e in edges if turn[e] == i] for i in (0, 1)]
    for chosen in sends:
        assert len({a for a, _ in chosen}) == len({b for _, b in chosen}) == pair_total
    sends_first = {e[0] for e in edges if turn[e] == 0 and e[1] == 0}
    picks = []
    for slot in range(4):
        pick = {}
        for here in range(pair_total):
            there, half = needs[here][slot]
            if there == here:
                pick[here] = 0 if (half == 0) == (here in sends_first) else 1
            else:
                pick[here] = 2 + turn[(there, half, here)]
        picks.append(pick)
    is_second = [{h for h, place in table.items() if place} for table in seconds]
    return sends, sends_first, picks, is_second


def choose(pick, arrays):
    chosen = arrays[0]
    for number in range(1, len(arrays)):
        members = {here for here, value in pick.items() if value == number}
        if members:
            chosen = jnp.where(among(members), arrays[number], chosen)
    return chosen


def among(members):
    here = lax.axis_index("pair")
    return functools.reduce(
        jnp.logical_or, [here == member for member in sorted(members)], here < 0
    )


def left(x, by):
    width = x.shape[1]
    return pltpu.roll(x, (width - by) % width, 1) if by % width else x


def right(x, by):
    width = x.shape[1]
    return pltpu.roll(x, by % width, 1) if by % width else x


def down(x, by):
    return pltpu.roll(x, by % x.shape[0], 0)


def lanes_of(x):
    return lax.broadcasted_iota(jnp.int32, x.shape, 1)


def split_pair(first, second):
    half = first.shape[1] // 2
    low = lanes_of(first) < half
    even = jnp.where(low, first, right(second, half))
    odd = jnp.where(low, right(first, half), second)
    return even, odd


def take_lanes(x, source):
    if x.shape[0] == 1:
        return take_lanes(jnp.broadcast_to(x, (8, x.shape[1])), source)[:1]
    return jnp.take_along_axis(x, jnp.broadcast_to(source, x.shape), axis=1)


def line_lanes(x):
    return lax.broadcasted_iota(jnp.int32, (1, x.shape[1]), 1)


def separate(first, second):
    lane = line_lanes(first)
    half = first.shape[1] // 2
    low = lane < half
    source = 2 * jnp.where(low, lane, lane - half)
    return tuple(
        jnp.where(low, take_lanes(first, source + odd), take_lanes(second, source + odd))
        for odd in (0, 1)
    )


def backwards(x):
    return jnp.take_along_axis(x, x.shape[1] - 1 - lanes_of(x), axis=1)


def dense_bands(even, odd, diags):
    width = even.shape[1]
    gram = lax.dot_general(
        jnp.concatenate((even, odd), axis=1),
        jnp.concatenate((backwards(even), backwards(odd)), axis=1),
        (((0,), (0,)), ((), ())),
        precision=lax.Precision.HIGHEST,
        preferred_element_type=jnp.float32,
    )
    bands = []
    for near in (0, width):
        for far in (0, width):
            quadrant = gram[far : far + width, near : near + width]
            aligned = pltpu.roll(quadrant, 1, 1, stride=1, stride_axis=0)
            bands.append(jnp.transpose(aligned)[:diags])
    return bands


def store_bands(even, odd, band_ref, diags):
    for q, band in enumerate(dense_bands(even, odd, diags)):
        band_ref[q * diags : (q + 1) * diags, :] = band


def strip_rows(rows, width):
    return -(-rows // (8 * (width // (2 * STRIP)))) * 8


def payload_kernel(sends_second, basis_ref, payload_ref):
    rows, cols = basis_ref.shape
    width = cols // 2
    half = width // 2
    first, second = basis_ref[:, :width], basis_ref[:, width:]
    lane = line_lanes(first)
    start = jnp.where(among(sends_second), half - STRIP, 0)
    place = start + jnp.where(lane < half, lane, lane - half)
    odd = jnp.where(lane < half, 0, 1)
    in_first = place < half
    source = 2 * jnp.where(in_first, place, place - half) + odd
    payload_ref[:rows] = jnp.where(in_first, take_lanes(first, source), take_lanes(second, source))
    places = width // STRIP
    place = lane - STRIP * sum(jnp.where(lane >= STRIP * i, 1, 0) for i in range(1, places))
    odd = sum(jnp.where(lane >= STRIP * i, 1 if i % 2 else -1, 0) for i in range(1, places))
    source = jnp.minimum(2 * (start + place) + odd, width - 1)
    group = strip_rows(rows, width)
    strips = jnp.zeros((group, width), jnp.float32)
    for i, at in enumerate(range(0, rows, group)):
        here = jnp.logical_and(lane >= 2 * STRIP * i, lane < 2 * STRIP * (i + 1))
        part = take_lanes(second[at : at + group], source)
        if part.shape[0] < group:
            spare = jnp.zeros((group - part.shape[0], width), jnp.float32)
            part = jnp.concatenate((part, spare), axis=0)
        strips = jnp.where(here, part, strips)
    payload_ref[rows:] = strips


def open_kernel(basis_ref, even_ref, odd_ref):
    width = basis_ref.shape[1] // 2
    even_ref[...], odd_ref[...] = separate(basis_ref[:, :width], basis_ref[:, width:])


def unpacked(payload, rows, second):
    width = payload.shape[1]
    half = width // 2
    lane = line_lanes(payload)
    main, strips = payload[:rows], payload[rows:]
    group = strips.shape[0]
    columns = []
    for j, x in enumerate((main, left(main, half))):
        ends = [
            right(strips, half - (2 * i + j) * STRIP)[: rows - at]
            for i, at in enumerate(range(0, rows, group))
        ]
        ends = jnp.concatenate(ends, axis=0)
        x = jnp.where(lane < half, x, jnp.where(lane < half + STRIP, ends, 0.0))
        columns.append(jnp.where(second, right(x, half - STRIP), x))
    return columns


def jacobi_angle(diag_even, diag_odd, coupling):
    spread = diag_even - diag_odd
    square = spread * spread + 4.0 * coupling * coupling
    inverse = lax.rsqrt(square)
    larger_square = (square * inverse + jnp.abs(spread)) * (0.5 * inverse)
    larger_inverse = lax.rsqrt(larger_square)
    larger = larger_square * larger_inverse
    smaller = coupling * inverse * larger_inverse
    forward = spread >= 0.0
    sign = jnp.where(coupling > 0.0, 1.0, jnp.where(coupling < 0.0, -1.0, 0.0))
    cosine = jnp.where(forward, larger, jnp.abs(smaller))
    sine_part = jnp.where(forward, smaller, sign * larger)
    return cosine, sine_part


def turn_bands(ee, eo, oe, oo, cosine, sine):
    cl, sl = jnp.broadcast_to(cosine, ee.shape), jnp.broadcast_to(sine, ee.shape)
    ck = pltpu.roll(cl, 0, 1, stride=1, stride_axis=0)
    sk = pltpu.roll(sl, 0, 1, stride=1, stride_axis=0)
    ee, oe = ck * ee + sk * oe, ck * oe - sk * ee
    eo, oo = ck * eo + sk * oo, ck * oo - sk * eo
    ee, eo = cl * ee + sl * eo, cl * eo - sl * ee
    oe, oo = cl * oe + sl * oo, cl * oo - sl * oe
    return ee, eo, oe, oo


def step_bands(ee, eo, oe, oo, cosine, sine):
    lane = lanes_of(ee)
    diag = lax.broadcasted_iota(jnp.int32, ee.shape, 0)
    last = lane == ee.shape[1] - 1
    on, next_on = diag == 0, diag == 1

    def slanted(x, by):
        if by >= 0:
            return pltpu.roll(x, by, 1, stride=1, stride_axis=0)
        return jnp.where(on, left(x, -by), down(slanted(x, 0), -by))

    def rotated(by, wanted):
        cl, sl = (jnp.broadcast_to(x, ee.shape) for x in (cosine, sine))
        ck, sk = (slanted(x, by) for x in (cl, sl))
        cl, sl, a, b, c, d = (right(x, by) for x in (cl, sl, ee, eo, oe, oo))
        a, c = ck * a + sk * c, ck * c - sk * a
        b, d = ck * b + sk * d, ck * d - sk * b
        found = {"ee": (a, b), "eo": (b, a), "oe": (c, d), "oo": (d, c)}
        return [
            cl * one + sl * two if name in ("ee", "oe") else cl * one - sl * two
            for name, (one, two) in found.items()
            if name in wanted
        ]

    ee_0, eo_0, oe_0, oo_0 = rotated(0, ("ee", "eo", "oe", "oo"))
    ee_r, eo_r, oe_r, oo_r = rotated(1, ("ee", "eo", "oe", "oo"))
    eo_l, oo_l = rotated(-1, ("eo", "oo"))

    near = down(jnp.where(on, eo_r, ee_r), 1)
    turned = jnp.where(on, oo_r, oe_r)
    ee_new = jnp.where(lane == diag + 1, turned, jnp.where(lane == diag, near, ee_r))
    ee_new = jnp.where(jnp.logical_and(on, lane == 0), ee_0, ee_new)

    eo_new = down(jnp.where(lane == diag - 1, oo_l, eo_l), -2)
    eo_new = jnp.where(lane == diag, down(eo_l, -1), eo_new)
    eo_new = jnp.where(last, down(ee_0, -1), eo_new)

    oo_new = jnp.where(last, jnp.where(on, ee_0, down(oe_0, 1)), oo_l)

    oe_new = down(oe_r, 2)
    oe_new = jnp.where(next_on, jnp.where(lane == diag, oo_0, eo_0), oe_new)
    oe_new = jnp.where(on, eo_new, oe_new)
    return ee_new, eo_new, oe_new, oo_new


def move_bands(ee, eo, oe, oo):
    lane = lanes_of(ee)
    diag = lax.broadcasted_iota(jnp.int32, ee.shape, 0)
    last = lane == ee.shape[1] - 1
    on, next_on = diag == 0, diag == 1

    near = down(jnp.where(on, eo, ee), 1)
    turned = jnp.where(on, oo, oe)
    mixed = jnp.where(lane == diag, turned, jnp.where(lane == diag - 1, near, ee))
    ee_new = jnp.where(jnp.logical_and(on, lane == 0), ee, right(mixed, 1))

    far = down(jnp.where(last, ee, eo), -1)
    mixed = down(jnp.where(lane == diag, oo, eo), -2)
    mixed = left(jnp.where(lane == diag + 1, far, mixed), 1)
    eo_new = jnp.where(last, far, mixed)

    oo_new = jnp.where(last, jnp.where(on, ee, down(oe, 1)), left(oo, 1))

    oe_new = right(down(oe, 2), 1)
    oe_new = jnp.where(next_on, jnp.where(lane == diag, oo, eo), oe_new)
    oe_new = jnp.where(on, eo_new, oe_new)
    return ee_new, eo_new, oe_new, oo_new


def move_bands_back(views, by):
    ee, eo, oe, oo = views[by]
    ee_left, _, oe_left, _ = views[by - 1]
    _, eo_right, _, oo_right = views[by + 1]
    width = ee.shape[1]
    lane = lanes_of(ee) - by
    lane = jnp.where(lane < 0, lane + width, jnp.where(lane >= width, lane - width, lane))
    diag = lax.broadcasted_iota(jnp.int32, ee.shape, 0)
    last, first = lane == width - 1, lane == diag
    on, next_on = diag == 0, diag == 1
    oo_up, eo_twice = down(oo, -1), down(eo_right, 2)

    far = jnp.where(first, down(ee_left, -1), ee_left)
    ee_old = jnp.where(jnp.logical_and(first, on), ee, far)
    ee_old = jnp.where(last, jnp.where(on, oo, down(eo, 1)), ee_old)

    near = jnp.where(jnp.logical_and(first, diag > 0), ee_left, down(oe_left, -2))
    eo_old = jnp.where(first, down(eo_right, 1), eo_twice)
    eo_old = jnp.where(on, jnp.where(last, oo_up, near), eo_old)
    eo_old = jnp.where(jnp.logical_and(next_on, lane > 1), oe, eo_old)
    eo_old = jnp.where(jnp.logical_and(on, first), far, eo_old)

    oe_old = jnp.where(on, eo_old, jnp.where(last, oo_up, near))

    oo_old = jnp.where(first, eo_twice, oo_right)
    oo_old = jnp.where(jnp.logical_and(next_on, first), oe, oo_old)
    oo_old = jnp.where(jnp.logical_and(on, first), ee_left, oo_old)
    return ee_old, eo_old, oe_old, oo_old


def bands_back(bands, count):
    views = {by: [right(x, by) for x in bands] for by in range(-count, count + 1)}
    for reach in reversed(range(count)):
        views = {by: move_bands_back(views, by) for by in range(-reach, reach + 1)}
    return views[0]


def move_columns(even, odd):
    lane = lanes_of(even)
    first, last = lane == 0, lane == even.shape[1] - 1
    even_new = jnp.where(first, even, right(jnp.where(first, odd, even), 1))
    odd_new = jnp.where(last, even, left(odd, 1))
    return even_new, odd_new


def in_pair(even, shifted=None):
    lane = line_lanes(even)
    if shifted is not None:
        half = even.shape[1] // 2
        lane = jnp.where(shifted, jnp.where(lane < half, lane + half, lane - half), lane)
    return (lane < 0, lane), (lane >= 0, lane)


def in_blocks(even):
    lane, half = line_lanes(even), even.shape[1] // 2
    place = jnp.where(lane < half, lane, lane - half)
    return (lane >= half, place), (lane >= half, place + half)


def in_order(even):
    lane, half = line_lanes(even), even.shape[1] // 2
    return (lane % 2 == 1, lane // 2), (lane % 2 == 1, lane // 2 + half)


def turn_to(layout, even, odd, angles):
    for cosine, sine in angles[:-1]:
        even, odd = cosine * even + sine * odd, cosine * odd - sine * even
        even, odd = move_columns(even, odd)
    by, end = JSTEPS - 1, even.shape[1] - 1
    results = []
    for is_odd, place in layout:
        stayed = place <= end - by
        from_even = jnp.where(stayed, place + by, 2 * end + 1 - by - place)
        from_even = jnp.where(place == 0, 0, from_even)
        source = jnp.where(is_odd, jnp.abs(place - by), from_even)
        is_even = jnp.logical_or(
            jnp.logical_and(is_odd, place < by),
            jnp.logical_and(jnp.logical_not(is_odd), stayed),
        )
        cosine, sine = (take_lanes(x, source) for x in angles[-1])
        by_even = jnp.where(is_even, cosine, -sine)
        by_odd = jnp.where(is_even, sine, cosine)
        results.append(by_even * take_lanes(even, source) + by_odd * take_lanes(odd, source))
    return results


def trim(bands, reach):
    rows = min(bands[0].shape[0], -(-(reach + 1) // 8) * 8)
    return [band[:rows] for band in bands]


def angles_of(bands):
    angles = []
    for step in range(JSTEPS):
        ee, eo, oe, oo = bands = trim(bands, 2 * (JSTEPS - 1 - step))
        angles.append(jacobi_angle(ee[0:1], oo[0:1], eo[0:1]))
        if step < JSTEPS - 1:
            bands = step_bands(*bands, *angles[-1])
    return angles


def carried(bands, angles):
    ahead = 2 * (JSTEPS - 1)
    for step, (cosine, sine) in enumerate(angles):
        bands = turn_bands(*trim(bands, 3 * ahead - 2 * step), cosine, sine)
        if step < JSTEPS - 1:
            bands = move_bands(*bands)
    done = 0
    while done < JSTEPS - 1:
        count = min(BACK, JSTEPS - 1 - done)
        bands = bands_back(trim(bands, 2 * (ahead - done)), count)
        done += count
    return bands


def near_starts(width):
    half = width // 2
    reach = REACH - 1
    return (half - 2 * reach, width - WINDOW), (0, half - reach)


def cross_partial(x_even, x_odd, y_even, y_odd, x_second, y_second):
    rows, width = x_even.shape
    x_starts, y_starts = near_starts(width)
    lane = lanes_of(x_even)

    def window(even, odd, flag, starts):
        start = jnp.where(flag, starts[1], starts[0])
        at_zero = pltpu.roll(even, (width - start) % width, 1)
        at_next = pltpu.roll(odd, (width - start + WINDOW) % width, 1)
        return jnp.where(lane < WINDOW, at_zero, jnp.where(lane < 2 * WINDOW, at_next, 0.0))

    corner = lax.dot_general(
        window(y_even, y_odd, y_second, y_starts),
        window(x_even, x_odd, x_second, x_starts),
        (((0,), (0,)), ((), ())),
        precision=lax.Precision.HIGHEST,
        preferred_element_type=jnp.float32,
    )
    low = lax.broadcasted_iota(jnp.int32, (WINDOW, width), 1) < 2 * WINDOW
    return jnp.where(low, corner[:WINDOW], right(corner[WINDOW : 2 * WINDOW], 2 * WINDOW))


def own_rotation(angles, second, swapped, first_pair):
    width = angles[0][0].shape[1]
    half = width // 2
    x_starts, y_starts = near_starts(width)
    starts = [jnp.where(first_pair, x, y) for x, y in zip(x_starts, y_starts)]
    shape = (2 * WINDOW, width)
    row = lax.broadcasted_iota(jnp.int32, shape, 0)
    lane = lax.broadcasted_iota(jnp.int32, shape, 1) - jnp.where(second, starts[1], starts[0])
    even, odd = (
        jnp.where(jnp.logical_and(row == lane + at, row // WINDOW == at // WINDOW), 1.0, 0.0)
        for at in (0, WINDOW)
    )
    even, odd = turn_to(in_pair(even, swapped), even, odd, angles)
    low = lax.broadcasted_iota(jnp.int32, shape, 1) < half
    return jnp.where(jnp.logical_xor(low, first_pair), right(odd, half), even)


def cross_bands(packed, x_rotation, y_rotation):
    width = packed.shape[1]
    half = width // 2
    corner = jnp.concatenate((packed[:, :half], right(packed, half)[:, :half]), axis=0)
    highest = dict(precision=lax.Precision.HIGHEST, preferred_element_type=jnp.float32)
    turned_x = jnp.dot(corner, x_rotation, **highest)
    ends = lax.dot_general(turned_x, y_rotation, (((0,), (0,)), ((), ())), **highest)
    even, odd = ends[half - NEAR : half], ends[width - NEAR :]
    quadrants = (even, right(even, half), odd, right(odd, half))
    offset = lanes_of(even) - lax.broadcasted_iota(jnp.int32, even.shape, 0) - (half - NEAR)
    diag = lax.broadcasted_iota(jnp.int32, (DIAGS, width), 0)
    bands = [jnp.zeros((DIAGS, width), jnp.float32) for _ in quadrants]
    for d in range(1, REACH):
        here = offset == d
        for q, quadrant in enumerate(quadrants):
            line = jnp.sum(jnp.where(here, quadrant, 0.0), axis=0, keepdims=True)
            bands[q] = jnp.where(diag == d, line, bands[q])
    return bands


def either(flag, one, other):
    return jnp.logical_or(jnp.logical_and(flag, one), jnp.logical_and(jnp.logical_not(flag), other))


def halves_swapped(is_second):
    return among(is_second[0]), jnp.logical_not(among(is_second[1]))


def on_odd_core():
    return lax.axis_index("row") % 2 == 1


PLACES = (
    (((16, 16, 80), (60, 16, 108)), ((16, 28, 21), (44, 30, 80))),
    (((68, 16, 24), (112, 16, 0)), ((70, 29, 84), (99, 29, 10))),
)
MIDDLES = (44, 99)


def pick_by(flag, one, other):
    return jnp.where(flag, other, one)


def pack_far(bands, flag):
    width = bands[0].shape[1]
    lane = lax.broadcasted_iota(jnp.int32, (DIAGS, width), 1)
    odd_row = lax.broadcasted_iota(jnp.int32, (DIAGS, width), 0) % 2 == 1
    moves = []
    for parity in (0, 1):
        for part in (0, 1):
            one, other = PLACES[0][parity][part], PLACES[1][parity][part]
            shift = pick_by(flag, (one[2] - one[0]) % width, (other[2] - other[0]) % width)
            start = pick_by(flag, one[2], other[2])
            count = pick_by(flag, one[1], other[1])
            here = jnp.logical_and(lane >= start, lane < start + count)
            moves.append((shift, jnp.logical_and(here, odd_row == (parity == 1))))
    packed = []
    for band in bands:
        near, far = band[:DIAGS], down(band[DIAGS:], -1)
        for shift, here in moves:
            near = jnp.where(here, pltpu.roll(far, shift, 1), near)
        packed.append(near)
    return packed


def unpack_far(packed, flag):
    width = packed.shape[1]
    lane = lanes_of(packed)
    odd_row = lax.broadcasted_iota(jnp.int32, packed.shape, 0) % 2 == 1
    parts = []
    for part in (0, 1):
        rolled = []
        for parity in (0, 1):
            one, other = PLACES[0][parity][part], PLACES[1][parity][part]
            shift = pick_by(flag, (one[0] - one[2]) % width, (other[0] - other[2]) % width)
            rolled.append(pltpu.roll(packed, shift, 1))
        parts.append(jnp.where(odd_row, rolled[1], rolled[0]))
    far = jnp.where(lane < pick_by(flag, *MIDDLES), *parts)
    return jnp.concatenate((packed, down(far, 1)), axis=0)


PACKED = DIAGS


def store_part(even, odd, flag, part_ref):
    bands = pack_far(dense_bands(even, odd, FAR_DIAGS), flag)
    for q, band in enumerate(bands):
        part_ref[q * PACKED : (q + 1) * PACKED, :] = band


def open_pairs(is_second, x, y, column_refs, other_ref):
    flag = on_odd_core()
    mine = [jnp.where(flag, b, a) for a, b in zip(x, y)]
    theirs = [jnp.where(flag, a, b) for a, b in zip(x, y)]
    for ref, value in zip(column_refs, mine + theirs):
        ref[...] = value
    store_part(*theirs, either(flag, among(is_second[0]), among(is_second[1])), other_ref)
    other_ref[4 * PACKED :, :] = jnp.zeros((WINDOW, theirs[0].shape[1]), jnp.float32)


def first_open(own_second, gets_second, is_second, even_ref, odd_ref, payload_ref, *refs):
    *column_refs, other_ref = refs
    own = even_ref[...], odd_ref[...]
    came = unpacked(payload_ref[...], own[0].shape[0], among(gets_second))
    flag = among(own_second)
    x = [jnp.where(flag, b, a) for a, b in zip(own, came)]
    y = [jnp.where(flag, a, b) for a, b in zip(own, came)]
    open_pairs(is_second, x, y, column_refs, other_ref)


def fused_open(picks, is_second, kept_ref, sent_ref, came0_ref, came1_ref, *refs):
    *column_refs, other_ref = refs
    arrays = [ref[...] for ref in (sent_ref, kept_ref, came0_ref, came1_ref)]
    blocks = [choose(pick, arrays) for pick in picks]
    x, y = split_pair(*blocks[:2]), split_pair(*blocks[2:])
    open_pairs(is_second, x, y, column_refs, other_ref)


def swapped_flag(is_second):
    x_swapped, y_swapped = halves_swapped(is_second)
    return either(on_odd_core(), y_swapped, x_swapped)


def own_second_flag(is_second):
    return either(on_odd_core(), among(is_second[1]), among(is_second[0]))


def bands_kernel(is_second, *refs):
    *column_refs, part_ref = refs
    columns = [ref[...] for ref in column_refs]
    store_part(*columns[:2], own_second_flag(is_second), part_ref)
    flag = on_odd_core()
    x = [jnp.where(flag, b, a) for a, b in zip(columns[:2], columns[2:])]
    y = [jnp.where(flag, a, b) for a, b in zip(columns[:2], columns[2:])]
    corner = cross_partial(*x, *y, among(is_second[0]), among(is_second[1]))
    part_ref[4 * PACKED :, :] = corner


def angles_kernel(is_second, *refs):
    *part_refs, found_ref = refs
    part = pair_sums([ref[...] for ref in part_refs])
    flag = own_second_flag(is_second)
    quadrants = [unpack_far(part[q * PACKED : (q + 1) * PACKED], flag) for q in range(4)]
    angles = angles_of(quadrants)
    first_pair = jnp.logical_not(on_odd_core())
    found_ref[ROTATION:, :] = own_rotation(angles, flag, swapped_flag(is_second), first_pair)
    bands = carried(quadrants, angles)
    for step, pair in enumerate(angles):
        for i in (0, 1):
            found_ref[2 * step + i : 2 * step + i + 1, :] = pair[i]
    spare = NEAR - 2 * JSTEPS
    found_ref[2 * JSTEPS : NEAR, :] = jnp.zeros((spare, part.shape[1]), jnp.float32)
    for q in range(4):
        found_ref[NEAR + q * DIAGS : NEAR + (q + 1) * DIAGS, :] = bands[q][:DIAGS]
    found_ref[CORNER:ROTATION, :] = part[4 * PACKED :]


CORNER = NEAR + 4 * DIAGS
ROTATION = CORNER + WINDOW
FOUND = ROTATION + 2 * WINDOW


def angles_in(found):
    return [(found[2 * i : 2 * i + 1], found[2 * i + 1 : 2 * i + 2]) for i in range(JSTEPS)]


def columns_kernel(is_second, even_ref, odd_ref, found_ref, *out_refs):
    angles = angles_in(found_ref[...])
    layout = in_pair(even_ref, swapped_flag(is_second))
    columns = turn_to(layout, even_ref[...], odd_ref[...], angles)
    for ref, value in zip(out_refs, columns):
        ref[...] = value


def next_bands(x_found, y_found, x_second, y_second):
    corner = x_found[CORNER:ROTATION] + y_found[CORNER:ROTATION]
    middle = cross_bands(corner, x_found[ROTATION:], y_found[ROTATION:])
    half = corner.shape[1] // 2
    lane = lanes_of(middle[0])
    diag = lax.broadcasted_iota(jnp.int32, middle[0].shape, 0)
    bands = []
    for q in range(4):
        rows = slice(NEAR + q * DIAGS, NEAR + (q + 1) * DIAGS)
        x, y = x_found[rows], y_found[rows]
        x = jnp.where(x_second, right(x, half), x)
        y = jnp.where(y_second, y, right(y, half))
        crossing = jnp.where(lane - diag < half, middle[q], y)
        bands.append(jnp.where(lane < half, x, crossing))
    return bands


def next_kernel(is_second, sends_first, layout_of, *refs):
    mine_even, mine_odd, even_ref, odd_ref, found_ref, other_ref, kept_ref, sent_ref = refs
    found, other = found_ref[...], other_ref[...]
    flag = on_odd_core()
    x_found, y_found = jnp.where(flag, other, found), jnp.where(flag, found, other)
    bands = next_bands(x_found, y_found, among(is_second[0]), among(is_second[1]))
    x_swapped, y_swapped = halves_swapped(is_second)
    swapped = either(flag, x_swapped, y_swapped)
    layout = in_pair(even_ref, swapped)
    theirs = turn_to(layout, even_ref[...], odd_ref[...], angles_in(other))
    low = line_lanes(found) < found.shape[1] // 2
    from_mine = jnp.logical_xor(low, flag)
    even = jnp.where(from_mine, mine_even[...], theirs[0])
    odd = jnp.where(from_mine, mine_odd[...], theirs[1])
    angles = angles_of(bands)
    first, second = turn_to(layout_of(even), even, odd, angles)
    flag = among(sends_first)
    kept_ref[...] = jnp.where(flag, second, first)
    sent_ref[...] = jnp.where(flag, first, second)


def pair_sums(arrays):
    while len(arrays) > 1:
        arrays = [arrays[i] + arrays[i + 1] for i in range(0, len(arrays), 2)]
    return arrays[0]


def swap(x, axis, mask):
    return lax.ppermute(x, axis, [(i, i ^ mask) for i in range(lax.axis_size(axis))])


def exchange_groups(x, axis, first_bit=0):
    count = lax.axis_size(axis).bit_length() - 1
    bits = [1 << b for b in range(count)]
    groups = [bits[:1]] + [bits[i : i + 2] for i in range(1, count, 2)]
    arrays = [x]
    for group in groups[first_bit:]:
        x = pair_sums(arrays)
        masks = [group[0]] if len(group) == 1 else [group[0], group[1], group[0] | group[1]]
        came = {mask: swap(x, axis, mask) for mask in reversed(masks)}
        arrays = [x] + [came[mask] for mask in masks]
    return arrays


def call(kernel, shapes, *args):
    out = [jax.ShapeDtypeStruct(shape, jnp.float32) for shape in shapes]
    return pl.pallas_call(
        kernel,
        out_shape=out,
        compiler_params=pltpu.CompilerParams(vmem_limit_bytes=32 * 1024 * 1024),
    )(*args)


def two_rounds(opened, is_second, sends_first, layout_of):
    *columns, other = opened
    column, width = columns[0].shape, columns[0].shape[1]
    other = swap(other, "row", 1)
    bands = functools.partial(bands_kernel, is_second)
    (mine,) = call(bands, (other.shape,), *columns)
    (found,) = call(
        functools.partial(angles_kernel, is_second),
        ((FOUND, width),),
        *exchange_groups(mine + other, "row", 1),
    )
    other = swap(found, "row", 1)
    turn = functools.partial(columns_kernel, is_second)
    columns[:2] = call(turn, (column, column), *columns[:2], found)
    turn = functools.partial(next_kernel, is_second, sends_first, layout_of)
    return call(turn, (column, column), *columns, found, other)


def per_device(basis):
    rows, cols = basis.shape
    width = cols // 2
    pair_total = lax.axis_size("pair")
    column = (rows, width)
    opened = (column,) * 4 + ((4 * PACKED + WINDOW, width),)
    payload = (rows + strip_rows(rows, width), width)

    sends, sends_second, gets_second, own_second, is_second = first_moves(pair_total)
    (sent,) = call(functools.partial(payload_kernel, sends_second), (payload,), basis)
    came = lax.ppermute(sent, "pair", sends)
    even, odd = call(open_kernel, (column, column), basis)
    opening = functools.partial(first_open, own_second, gets_second, is_second)
    arrays = call(opening, opened, even, odd, came)
    sends, sends_first, picks, next_second = fused_moves(pair_total)
    kept, sent = two_rounds(arrays, is_second, sends_first, in_blocks)

    came = [lax.ppermute(x, "pair", s) for x, s in zip((sent, kept), sends)]
    opening = functools.partial(fused_open, picks, next_second)
    arrays = call(opening, opened, kept, sent, *came)
    sends, sends_first, gets_first = last_moves(pair_total)
    kept, sent = two_rounds(arrays, next_second, sends_first, in_order)

    came = lax.ppermute(sent, "pair", sends)
    flag = among(gets_first)
    first = jnp.where(flag, came, kept)
    second = jnp.where(flag, kept, came)
    return jnp.concatenate((first, second), axis=1)


def solution(mesh):
    return jax.shard_map(
        per_device,
        mesh=mesh,
        in_specs=(P("row", "pair"),),
        out_specs=P("row", "pair"),
        check_vma=False,
    )
```

```python
import functools

import jax
import jax.numpy as jnp
import numpy as np
from jax import lax
from jax.experimental import pallas as pl
from jax.experimental.pallas import tpu as pltpu
from jax.sharding import PartitionSpec as P

ROUNDS = 4
JSTEPS = 6
REACH = 2 * (JSTEPS - 1) + 1
DIAGS = 16
FAR_DIAGS = 32
WINDOW = 32
NEAR = 16
STRIP = REACH - 1
BACK = 3


def tournament_order(pair_count):
    ordering = np.zeros(2 * pair_count, dtype=np.int64)
    ordering[0] = 0
    ordering[2] = 1
    for slot in range(2, pair_count):
        ordering[2 * slot] = 2 * (slot - 1)
    for slot in range(pair_count - 1):
        ordering[2 * slot + 1] = 2 * (slot + 1) + 1
    ordering[2 * pair_count - 1] = 2 * (pair_count - 1)
    return ordering


def host_of(pair, pair_total, round_index):
    if round_index % 2 == 0 or pair == 0:
        return pair
    return min(pair + 1, pair_total - 1) if pair % 2 else pair - 1


def last_moves(pair_total):
    ordering = tournament_order(pair_total)
    sends, sends_first, gets_first = [], set(), set()
    for pair in range(pair_total):
        target = host_of(pair, pair_total, ROUNDS)
        for place in (0, 1):
            old = int(ordering[2 * pair + place])
            source = host_of(old // 2, pair_total, ROUNDS - 1)
            if source == target:
                continue
            sends.append((source, target))
            if old % 2 == 0:
                sends_first.add(source)
            if place == 0:
                gets_first.add(target)
    assert len({s for s, _ in sends}) == len(sends) == len({t for _, t in sends})
    return sends, sends_first, gets_first


def first_moves(pair_total):
    ordering = tournament_order(pair_total)
    sends, sends_second, gets_second, own_second = [], set(), set(), set()
    seconds = (set(), set())
    for pair in range(pair_total):
        here = host_of(pair, pair_total, 1)
        for place in (0, 1):
            old = int(ordering[2 * pair + place])
            if old % 2:
                seconds[place].add(here)
            if old // 2 == here:
                if place:
                    own_second.add(here)
                continue
            sends.append((old // 2, here))
            if old % 2:
                sends_second.add(old // 2)
                gets_second.add(here)
    assert len({s for s, _ in sends}) == len(sends) == len({t for _, t in sends})
    return sends, sends_second, gets_second, own_second, seconds


def fused_moves(pair_total):
    ordering = tournament_order(pair_total)
    before, last = ROUNDS - 3, ROUNDS - 1
    needs, edges, seconds = {}, [], ({}, {})
    for pair in range(pair_total):
        here = host_of(pair, pair_total, last)
        needs[here] = []
        for place in (0, 1):
            source = int(ordering[2 * pair + place])
            seconds[place][here] = source % 2
            for half in (0, 1):
                old = int(ordering[2 * (source // 2) + half])
                there = host_of(old // 2, pair_total, before)
                needs[here].append((there, old % 2))
                if there != here:
                    edges.append((there, old % 2, here))
    turn, left_over = {}, list(edges)
    while left_over:
        source, _, target = left_over[0]
        start = source
        while True:
            for number, one, other in ((0, source, target), (1, target, source)):
                edge = next(e for e in left_over if (e[0], e[2]) == (one, other))
                turn[edge] = number
                left_over.remove(edge)
            if target == start:
                break
            ahead = [e[2] for e in left_over if e[0] == target]
            source, target = target, ahead[0]
    sends = [[(e[0], e[2]) for e in edges if turn[e] == i] for i in (0, 1)]
    for chosen in sends:
        assert len({a for a, _ in chosen}) == len({b for _, b in chosen}) == pair_total
    sends_first = {e[0] for e in edges if turn[e] == 0 and e[1] == 0}
    picks = []
    for slot in range(4):
        pick = {}
        for here in range(pair_total):
            there, half = needs[here][slot]
            if there == here:
                pick[here] = 0 if (half == 0) == (here in sends_first) else 1
            else:
                pick[here] = 2 + turn[(there, half, here)]
        picks.append(pick)
    is_second = [{h for h, place in table.items() if place} for table in seconds]
    return sends, sends_first, picks, is_second


def choose(pick, arrays):
    chosen = arrays[0]
    for number in range(1, len(arrays)):
        members = {here for here, value in pick.items() if value == number}
        if members:
            chosen = jnp.where(among(members), arrays[number], chosen)
    return chosen


def among(members):
    here = lax.axis_index("pair")
    return functools.reduce(
        jnp.logical_or, [here == member for member in sorted(members)], here < 0
    )


def left(x, by):
    width = x.shape[1]
    return pltpu.roll(x, (width - by) % width, 1) if by % width else x


def right(x, by):
    width = x.shape[1]
    return pltpu.roll(x, by % width, 1) if by % width else x


def down(x, by):
    return pltpu.roll(x, by % x.shape[0], 0)


def lanes_of(x):
    return lax.broadcasted_iota(jnp.int32, x.shape, 1)


def split_pair(first, second):
    half = first.shape[1] // 2
    low = lanes_of(first) < half
    even = jnp.where(low, first, right(second, half))
    odd = jnp.where(low, right(first, half), second)
    return even, odd


def take_lanes(x, source):
    if x.shape[0] == 1:
        return take_lanes(jnp.broadcast_to(x, (8, x.shape[1])), source)[:1]
    return jnp.take_along_axis(x, jnp.broadcast_to(source, x.shape), axis=1)


def line_lanes(x):
    return lax.broadcasted_iota(jnp.int32, (1, x.shape[1]), 1)


def separate(first, second):
    lane = line_lanes(first)
    half = first.shape[1] // 2
    low = lane < half
    source = 2 * jnp.where(low, lane, lane - half)
    return tuple(
        jnp.where(low, take_lanes(first, source + odd), take_lanes(second, source + odd))
        for odd in (0, 1)
    )


def backwards(x):
    return jnp.take_along_axis(x, x.shape[1] - 1 - lanes_of(x), axis=1)


def dense_bands(even, odd, diags):
    width = even.shape[1]
    gram = lax.dot_general(
        jnp.concatenate((even, odd), axis=1),
        jnp.concatenate((backwards(even), backwards(odd)), axis=1),
        (((0,), (0,)), ((), ())),
        precision=lax.Precision.HIGHEST,
        preferred_element_type=jnp.float32,
    )
    bands = []
    for near in (0, width):
        for far in (0, width):
            quadrant = gram[far : far + width, near : near + width]
            aligned = pltpu.roll(quadrant, 1, 1, stride=1, stride_axis=0)
            bands.append(jnp.transpose(aligned)[:diags])
    return bands


def store_bands(even, odd, band_ref, diags):
    for q, band in enumerate(dense_bands(even, odd, diags)):
        band_ref[q * diags : (q + 1) * diags, :] = band


def strip_rows(rows, width):
    return -(-rows // (8 * (width // (2 * STRIP)))) * 8


def payload_kernel(sends_second, basis_ref, payload_ref):
    rows, cols = basis_ref.shape
    width = cols // 2
    half = width // 2
    first, second = basis_ref[:, :width], basis_ref[:, width:]
    lane = line_lanes(first)
    start = jnp.where(among(sends_second), half - STRIP, 0)
    place = start + jnp.where(lane < half, lane, lane - half)
    odd = jnp.where(lane < half, 0, 1)
    in_first = place < half
    source = 2 * jnp.where(in_first, place, place - half) + odd
    payload_ref[:rows] = jnp.where(in_first, take_lanes(first, source), take_lanes(second, source))
    places = width // STRIP
    place = lane - STRIP * sum(jnp.where(lane >= STRIP * i, 1, 0) for i in range(1, places))
    odd = sum(jnp.where(lane >= STRIP * i, 1 if i % 2 else -1, 0) for i in range(1, places))
    source = jnp.minimum(2 * (start + place) + odd, width - 1)
    group = strip_rows(rows, width)
    strips = jnp.zeros((group, width), jnp.float32)
    for i, at in enumerate(range(0, rows, group)):
        here = jnp.logical_and(lane >= 2 * STRIP * i, lane < 2 * STRIP * (i + 1))
        part = take_lanes(second[at : at + group], source)
        if part.shape[0] < group:
            spare = jnp.zeros((group - part.shape[0], width), jnp.float32)
            part = jnp.concatenate((part, spare), axis=0)
        strips = jnp.where(here, part, strips)
    payload_ref[rows:] = strips


def open_kernel(basis_ref, even_ref, odd_ref):
    width = basis_ref.shape[1] // 2
    even_ref[...], odd_ref[...] = separate(basis_ref[:, :width], basis_ref[:, width:])


def unpacked(payload, rows, second):
    width = payload.shape[1]
    half = width // 2
    lane = line_lanes(payload)
    main, strips = payload[:rows], payload[rows:]
    group = strips.shape[0]
    columns = []
    for j, x in enumerate((main, left(main, half))):
        ends = [
            right(strips, half - (2 * i + j) * STRIP)[: rows - at]
            for i, at in enumerate(range(0, rows, group))
        ]
        ends = jnp.concatenate(ends, axis=0)
        x = jnp.where(lane < half, x, jnp.where(lane < half + STRIP, ends, 0.0))
        columns.append(jnp.where(second, right(x, half - STRIP), x))
    return columns


def jacobi_angle(diag_even, diag_odd, coupling):
    spread = diag_even - diag_odd
    square = spread * spread + 4.0 * coupling * coupling
    inverse = lax.rsqrt(square)
    larger_square = (square * inverse + jnp.abs(spread)) * (0.5 * inverse)
    larger_inverse = lax.rsqrt(larger_square)
    larger = larger_square * larger_inverse
    smaller = coupling * inverse * larger_inverse
    forward = spread >= 0.0
    sign = jnp.where(coupling > 0.0, 1.0, jnp.where(coupling < 0.0, -1.0, 0.0))
    cosine = jnp.where(forward, larger, jnp.abs(smaller))
    sine_part = jnp.where(forward, smaller, sign * larger)
    return cosine, sine_part


def turn_bands(ee, eo, oe, oo, cosine, sine):
    cl, sl = jnp.broadcast_to(cosine, ee.shape), jnp.broadcast_to(sine, ee.shape)
    ck = pltpu.roll(cl, 0, 1, stride=1, stride_axis=0)
    sk = pltpu.roll(sl, 0, 1, stride=1, stride_axis=0)
    ee, oe = ck * ee + sk * oe, ck * oe - sk * ee
    eo, oo = ck * eo + sk * oo, ck * oo - sk * eo
    ee, eo = cl * ee + sl * eo, cl * eo - sl * ee
    oe, oo = cl * oe + sl * oo, cl * oo - sl * oe
    return ee, eo, oe, oo


def step_bands(ee, eo, oe, oo, cosine, sine):
    lane = lanes_of(ee)
    diag = lax.broadcasted_iota(jnp.int32, ee.shape, 0)
    last = lane == ee.shape[1] - 1
    on, next_on = diag == 0, diag == 1

    def slanted(x, by):
        if by >= 0:
            return pltpu.roll(x, by, 1, stride=1, stride_axis=0)
        return jnp.where(on, left(x, -by), down(slanted(x, 0), -by))

    def rotated(by, wanted):
        cl, sl = (jnp.broadcast_to(x, ee.shape) for x in (cosine, sine))
        ck, sk = (slanted(x, by) for x in (cl, sl))
        cl, sl, a, b, c, d = (right(x, by) for x in (cl, sl, ee, eo, oe, oo))
        a, c = ck * a + sk * c, ck * c - sk * a
        b, d = ck * b + sk * d, ck * d - sk * b
        found = {"ee": (a, b), "eo": (b, a), "oe": (c, d), "oo": (d, c)}
        return [
            cl * one + sl * two if name in ("ee", "oe") else cl * one - sl * two
            for name, (one, two) in found.items()
            if name in wanted
        ]

    ee_0, eo_0, oe_0, oo_0 = rotated(0, ("ee", "eo", "oe", "oo"))
    ee_r, eo_r, oe_r, oo_r = rotated(1, ("ee", "eo", "oe", "oo"))
    eo_l, oo_l = rotated(-1, ("eo", "oo"))

    near = down(jnp.where(on, eo_r, ee_r), 1)
    turned = jnp.where(on, oo_r, oe_r)
    ee_new = jnp.where(lane == diag + 1, turned, jnp.where(lane == diag, near, ee_r))
    ee_new = jnp.where(jnp.logical_and(on, lane == 0), ee_0, ee_new)

    eo_new = down(jnp.where(lane == diag - 1, oo_l, eo_l), -2)
    eo_new = jnp.where(lane == diag, down(eo_l, -1), eo_new)
    eo_new = jnp.where(last, down(ee_0, -1), eo_new)

    oo_new = jnp.where(last, jnp.where(on, ee_0, down(oe_0, 1)), oo_l)

    oe_new = down(oe_r, 2)
    oe_new = jnp.where(next_on, jnp.where(lane == diag, oo_0, eo_0), oe_new)
    oe_new = jnp.where(on, eo_new, oe_new)
    return ee_new, eo_new, oe_new, oo_new


def move_bands(ee, eo, oe, oo):
    lane = lanes_of(ee)
    diag = lax.broadcasted_iota(jnp.int32, ee.shape, 0)
    last = lane == ee.shape[1] - 1
    on, next_on = diag == 0, diag == 1

    near = down(jnp.where(on, eo, ee), 1)
    turned = jnp.where(on, oo, oe)
    mixed = jnp.where(lane == diag, turned, jnp.where(lane == diag - 1, near, ee))
    ee_new = jnp.where(jnp.logical_and(on, lane == 0), ee, right(mixed, 1))

    far = down(jnp.where(last, ee, eo), -1)
    mixed = down(jnp.where(lane == diag, oo, eo), -2)
    mixed = left(jnp.where(lane == diag + 1, far, mixed), 1)
    eo_new = jnp.where(last, far, mixed)

    oo_new = jnp.where(last, jnp.where(on, ee, down(oe, 1)), left(oo, 1))

    oe_new = right(down(oe, 2), 1)
    oe_new = jnp.where(next_on, jnp.where(lane == diag, oo, eo), oe_new)
    oe_new = jnp.where(on, eo_new, oe_new)
    return ee_new, eo_new, oe_new, oo_new


def move_bands_back(views, by):
    ee, eo, oe, oo = views[by]
    ee_left, _, oe_left, _ = views[by - 1]
    _, eo_right, _, oo_right = views[by + 1]
    width = ee.shape[1]
    lane = lanes_of(ee) - by
    lane = jnp.where(lane < 0, lane + width, jnp.where(lane >= width, lane - width, lane))
    diag = lax.broadcasted_iota(jnp.int32, ee.shape, 0)
    last, first = lane == width - 1, lane == diag
    on, next_on = diag == 0, diag == 1
    oo_up, eo_twice = down(oo, -1), down(eo_right, 2)

    far = jnp.where(first, down(ee_left, -1), ee_left)
    ee_old = jnp.where(jnp.logical_and(first, on), ee, far)
    ee_old = jnp.where(last, jnp.where(on, oo, down(eo, 1)), ee_old)

    near = jnp.where(jnp.logical_and(first, diag > 0), ee_left, down(oe_left, -2))
    eo_old = jnp.where(first, down(eo_right, 1), eo_twice)
    eo_old = jnp.where(on, jnp.where(last, oo_up, near), eo_old)
    eo_old = jnp.where(jnp.logical_and(next_on, lane > 1), oe, eo_old)
    eo_old = jnp.where(jnp.logical_and(on, first), far, eo_old)

    oe_old = jnp.where(on, eo_old, jnp.where(last, oo_up, near))

    oo_old = jnp.where(first, eo_twice, oo_right)
    oo_old = jnp.where(jnp.logical_and(next_on, first), oe, oo_old)
    oo_old = jnp.where(jnp.logical_and(on, first), ee_left, oo_old)
    return ee_old, eo_old, oe_old, oo_old


def bands_back(bands, count):
    views = {by: [right(x, by) for x in bands] for by in range(-count, count + 1)}
    for reach in reversed(range(count)):
        views = {by: move_bands_back(views, by) for by in range(-reach, reach + 1)}
    return views[0]


def move_columns(even, odd):
    lane = lanes_of(even)
    first, last = lane == 0, lane == even.shape[1] - 1
    even_new = jnp.where(first, even, right(jnp.where(first, odd, even), 1))
    odd_new = jnp.where(last, even, left(odd, 1))
    return even_new, odd_new


def in_pair(even, shifted=None):
    lane = line_lanes(even)
    if shifted is not None:
        half = even.shape[1] // 2
        lane = jnp.where(shifted, jnp.where(lane < half, lane + half, lane - half), lane)
    return (lane < 0, lane), (lane >= 0, lane)


def in_blocks(even):
    lane, half = line_lanes(even), even.shape[1] // 2
    place = jnp.where(lane < half, lane, lane - half)
    return (lane >= half, place), (lane >= half, place + half)


def in_order(even):
    lane, half = line_lanes(even), even.shape[1] // 2
    return (lane % 2 == 1, lane // 2), (lane % 2 == 1, lane // 2 + half)


def turn_to(layout, even, odd, angles):
    for cosine, sine in angles[:-1]:
        even, odd = cosine * even + sine * odd, cosine * odd - sine * even
        even, odd = move_columns(even, odd)
    by, end = JSTEPS - 1, even.shape[1] - 1
    results = []
    for is_odd, place in layout:
        stayed = place <= end - by
        from_even = jnp.where(stayed, place + by, 2 * end + 1 - by - place)
        from_even = jnp.where(place == 0, 0, from_even)
        source = jnp.where(is_odd, jnp.abs(place - by), from_even)
        is_even = jnp.logical_or(
            jnp.logical_and(is_odd, place < by),
            jnp.logical_and(jnp.logical_not(is_odd), stayed),
        )
        cosine, sine = (take_lanes(x, source) for x in angles[-1])
        by_even = jnp.where(is_even, cosine, -sine)
        by_odd = jnp.where(is_even, sine, cosine)
        results.append(by_even * take_lanes(even, source) + by_odd * take_lanes(odd, source))
    return results


def trim(bands, reach):
    rows = min(bands[0].shape[0], -(-(reach + 1) // 8) * 8)
    return [band[:rows] for band in bands]


def angles_of(bands):
    angles = []
    for step in range(JSTEPS):
        ee, eo, oe, oo = bands = trim(bands, 2 * (JSTEPS - 1 - step))
        angles.append(jacobi_angle(ee[0:1], oo[0:1], eo[0:1]))
        if step < JSTEPS - 1:
            bands = step_bands(*bands, *angles[-1])
    return angles


def carried(bands, angles):
    ahead = 2 * (JSTEPS - 1)
    for step, (cosine, sine) in enumerate(angles):
        bands = turn_bands(*trim(bands, 3 * ahead - 2 * step), cosine, sine)
        if step < JSTEPS - 1:
            bands = move_bands(*bands)
    done = 0
    while done < JSTEPS - 1:
        count = min(BACK, JSTEPS - 1 - done)
        bands = bands_back(trim(bands, 2 * (ahead - done)), count)
        done += count
    return bands


def near_starts(width):
    half = width // 2
    reach = REACH - 1
    return (half - 2 * reach, width - WINDOW), (0, half - reach)


def cross_partial(x_even, x_odd, y_even, y_odd, x_second, y_second):
    rows, width = x_even.shape
    x_starts, y_starts = near_starts(width)
    lane = lanes_of(x_even)

    def window(even, odd, flag, starts):
        start = jnp.where(flag, starts[1], starts[0])
        at_zero = pltpu.roll(even, (width - start) % width, 1)
        at_next = pltpu.roll(odd, (width - start + WINDOW) % width, 1)
        return jnp.where(lane < WINDOW, at_zero, jnp.where(lane < 2 * WINDOW, at_next, 0.0))

    corner = lax.dot_general(
        window(y_even, y_odd, y_second, y_starts),
        window(x_even, x_odd, x_second, x_starts),
        (((0,), (0,)), ((), ())),
        precision=lax.Precision.HIGHEST,
        preferred_element_type=jnp.float32,
    )
    low = lax.broadcasted_iota(jnp.int32, (WINDOW, width), 1) < 2 * WINDOW
    return jnp.where(low, corner[:WINDOW], right(corner[WINDOW : 2 * WINDOW], 2 * WINDOW))


def own_rotation(angles, second, swapped, first_pair):
    width = angles[0][0].shape[1]
    half = width // 2
    x_starts, y_starts = near_starts(width)
    starts = [jnp.where(first_pair, x, y) for x, y in zip(x_starts, y_starts)]
    shape = (2 * WINDOW, width)
    row = lax.broadcasted_iota(jnp.int32, shape, 0)
    lane = lax.broadcasted_iota(jnp.int32, shape, 1) - jnp.where(second, starts[1], starts[0])
    even, odd = (
        jnp.where(jnp.logical_and(row == lane + at, row // WINDOW == at // WINDOW), 1.0, 0.0)
        for at in (0, WINDOW)
    )
    even, odd = turn_to(in_pair(even, swapped), even, odd, angles)
    low = lax.broadcasted_iota(jnp.int32, shape, 1) < half
    return jnp.where(jnp.logical_xor(low, first_pair), right(odd, half), even)


def cross_bands(packed, x_rotation, y_rotation):
    width = packed.shape[1]
    half = width // 2
    corner = jnp.concatenate((packed[:, :half], right(packed, half)[:, :half]), axis=0)
    highest = dict(precision=lax.Precision.HIGHEST, preferred_element_type=jnp.float32)
    turned_x = jnp.dot(corner, x_rotation, **highest)
    ends = lax.dot_general(turned_x, y_rotation, (((0,), (0,)), ((), ())), **highest)
    even, odd = ends[half - NEAR : half], ends[width - NEAR :]
    quadrants = (even, right(even, half), odd, right(odd, half))
    offset = lanes_of(even) - lax.broadcasted_iota(jnp.int32, even.shape, 0) - (half - NEAR)
    diag = lax.broadcasted_iota(jnp.int32, (DIAGS, width), 0)
    bands = [jnp.zeros((DIAGS, width), jnp.float32) for _ in quadrants]
    for d in range(1, REACH):
        here = offset == d
        for q, quadrant in enumerate(quadrants):
            line = jnp.sum(jnp.where(here, quadrant, 0.0), axis=0, keepdims=True)
            bands[q] = jnp.where(diag == d, line, bands[q])
    return bands


def either(flag, one, other):
    return jnp.logical_or(jnp.logical_and(flag, one), jnp.logical_and(jnp.logical_not(flag), other))


def halves_swapped(is_second):
    return among(is_second[0]), jnp.logical_not(among(is_second[1]))


def on_odd_core():
    return lax.axis_index("row") % 2 == 1


PLACES = (
    (((16, 16, 80), (60, 16, 108)), ((16, 28, 21), (44, 30, 80))),
    (((68, 16, 24), (112, 16, 0)), ((70, 29, 84), (99, 29, 10))),
)
MIDDLES = (44, 99)


def pick_by(flag, one, other):
    return jnp.where(flag, other, one)


def pack_far(bands, flag):
    width = bands[0].shape[1]
    lane = lax.broadcasted_iota(jnp.int32, (DIAGS, width), 1)
    odd_row = lax.broadcasted_iota(jnp.int32, (DIAGS, width), 0) % 2 == 1
    moves = []
    for parity in (0, 1):
        for part in (0, 1):
            one, other = PLACES[0][parity][part], PLACES[1][parity][part]
            shift = pick_by(flag, (one[2] - one[0]) % width, (other[2] - other[0]) % width)
            start = pick_by(flag, one[2], other[2])
            count = pick_by(flag, one[1], other[1])
            here = jnp.logical_and(lane >= start, lane < start + count)
            moves.append((shift, jnp.logical_and(here, odd_row == (parity == 1))))
    packed = []
    for band in bands:
        near, far = band[:DIAGS], down(band[DIAGS:], -1)
        for shift, here in moves:
            near = jnp.where(here, pltpu.roll(far, shift, 1), near)
        packed.append(near)
    return packed


def unpack_far(packed, flag):
    width = packed.shape[1]
    lane = lanes_of(packed)
    odd_row = lax.broadcasted_iota(jnp.int32, packed.shape, 0) % 2 == 1
    parts = []
    for part in (0, 1):
        rolled = []
        for parity in (0, 1):
            one, other = PLACES[0][parity][part], PLACES[1][parity][part]
            shift = pick_by(flag, (one[0] - one[2]) % width, (other[0] - other[2]) % width)
            rolled.append(pltpu.roll(packed, shift, 1))
        parts.append(jnp.where(odd_row, rolled[1], rolled[0]))
    far = jnp.where(lane < pick_by(flag, *MIDDLES), *parts)
    return jnp.concatenate((packed, down(far, 1)), axis=0)


PACKED = DIAGS


def store_part(even, odd, flag, part_ref):
    bands = pack_far(dense_bands(even, odd, FAR_DIAGS), flag)
    for q, band in enumerate(bands):
        part_ref[q * PACKED : (q + 1) * PACKED, :] = band


def open_pairs(is_second, theirs, mine, column_refs, other_ref):
    second = either(on_odd_core(), among(is_second[0]), among(is_second[1]))
    store_part(*theirs, second, other_ref)
    other_ref[4 * PACKED :, :] = jnp.zeros((WINDOW, theirs[0].shape[1]), jnp.float32)
    for ref, value in zip(column_refs, mine() + theirs):
        ref[...] = value


def first_open(own_second, gets_second, is_second, even_ref, odd_ref, payload_ref, *refs):
    *column_refs, other_ref = refs
    own = even_ref[...], odd_ref[...]
    came = unpacked(payload_ref[...], own[0].shape[0], among(gets_second))
    flag = jnp.logical_xor(among(own_second), jnp.logical_not(on_odd_core()))
    theirs = [jnp.where(flag, b, a) for a, b in zip(own, came)]

    def mine():
        return [jnp.where(flag, a, b) for a, b in zip(own, came)]

    open_pairs(is_second, theirs, mine, column_refs, other_ref)


def fused_open(picks, is_second, kept_ref, sent_ref, came0_ref, came1_ref, *refs):
    *column_refs, other_ref = refs
    arrays = [ref[...] for ref in (sent_ref, kept_ref, came0_ref, came1_ref)]
    blocks = [choose(pick, arrays) for pick in picks]
    flag = on_odd_core()
    theirs = split_pair(*(jnp.where(flag, a, b) for a, b in zip(blocks[:2], blocks[2:])))

    def mine():
        own = split_pair(*(jnp.where(flag, b, a) for a, b in zip(blocks[:2], blocks[2:])))
        return list(own)

    open_pairs(is_second, list(theirs), mine, column_refs, other_ref)


def swapped_flag(is_second):
    x_swapped, y_swapped = halves_swapped(is_second)
    return either(on_odd_core(), y_swapped, x_swapped)


def own_second_flag(is_second):
    return either(on_odd_core(), among(is_second[1]), among(is_second[0]))


def bands_kernel(is_second, *refs):
    *column_refs, part_ref = refs
    columns = [ref[...] for ref in column_refs]
    store_part(*columns[:2], own_second_flag(is_second), part_ref)
    flag = on_odd_core()
    x = [jnp.where(flag, b, a) for a, b in zip(columns[:2], columns[2:])]
    y = [jnp.where(flag, a, b) for a, b in zip(columns[:2], columns[2:])]
    corner = cross_partial(*x, *y, among(is_second[0]), among(is_second[1]))
    part_ref[4 * PACKED :, :] = corner


def angles_kernel(is_second, *refs):
    *part_refs, found_ref = refs
    part = pair_sums([ref[...] for ref in part_refs])
    flag = own_second_flag(is_second)
    quadrants = [unpack_far(part[q * PACKED : (q + 1) * PACKED], flag) for q in range(4)]
    angles = angles_of(quadrants)
    first_pair = jnp.logical_not(on_odd_core())
    found_ref[ROTATION:, :] = own_rotation(angles, flag, swapped_flag(is_second), first_pair)
    bands = carried(quadrants, angles)
    for step, pair in enumerate(angles):
        for i in (0, 1):
            found_ref[2 * step + i : 2 * step + i + 1, :] = pair[i]
    spare = NEAR - 2 * JSTEPS
    found_ref[2 * JSTEPS : NEAR, :] = jnp.zeros((spare, part.shape[1]), jnp.float32)
    for q in range(4):
        found_ref[NEAR + q * DIAGS : NEAR + (q + 1) * DIAGS, :] = bands[q][:DIAGS]
    found_ref[CORNER:ROTATION, :] = part[4 * PACKED :]


CORNER = NEAR + 4 * DIAGS
ROTATION = CORNER + WINDOW
FOUND = ROTATION + 2 * WINDOW


def angles_in(found):
    return [(found[2 * i : 2 * i + 1], found[2 * i + 1 : 2 * i + 2]) for i in range(JSTEPS)]


def columns_kernel(is_second, even_ref, odd_ref, found_ref, *out_refs):
    angles = angles_in(found_ref[...])
    layout = in_pair(even_ref, swapped_flag(is_second))
    columns = turn_to(layout, even_ref[...], odd_ref[...], angles)
    for ref, value in zip(out_refs, columns):
        ref[...] = value


def next_bands(x_found, y_found, x_second, y_second):
    corner = x_found[CORNER:ROTATION] + y_found[CORNER:ROTATION]
    middle = cross_bands(corner, x_found[ROTATION:], y_found[ROTATION:])
    half = corner.shape[1] // 2
    lane = lanes_of(middle[0])
    diag = lax.broadcasted_iota(jnp.int32, middle[0].shape, 0)
    bands = []
    for q in range(4):
        rows = slice(NEAR + q * DIAGS, NEAR + (q + 1) * DIAGS)
        x, y = x_found[rows], y_found[rows]
        x = jnp.where(x_second, right(x, half), x)
        y = jnp.where(y_second, y, right(y, half))
        crossing = jnp.where(lane - diag < half, middle[q], y)
        bands.append(jnp.where(lane < half, x, crossing))
    return bands


def next_kernel(is_second, sends_first, layout_of, *refs):
    mine_even, mine_odd, even_ref, odd_ref, found_ref, other_ref, kept_ref, sent_ref = refs
    found, other = found_ref[...], other_ref[...]
    flag = on_odd_core()
    x_found, y_found = jnp.where(flag, other, found), jnp.where(flag, found, other)
    bands = next_bands(x_found, y_found, among(is_second[0]), among(is_second[1]))
    x_swapped, y_swapped = halves_swapped(is_second)
    swapped = either(flag, x_swapped, y_swapped)
    layout = in_pair(even_ref, swapped)
    theirs = turn_to(layout, even_ref[...], odd_ref[...], angles_in(other))
    low = line_lanes(found) < found.shape[1] // 2
    from_mine = jnp.logical_xor(low, flag)
    even = jnp.where(from_mine, mine_even[...], theirs[0])
    odd = jnp.where(from_mine, mine_odd[...], theirs[1])
    angles = angles_of(bands)
    first, second = turn_to(layout_of(even), even, odd, angles)
    flag = among(sends_first)
    kept_ref[...] = jnp.where(flag, second, first)
    sent_ref[...] = jnp.where(flag, first, second)


def pair_sums(arrays):
    while len(arrays) > 1:
        arrays = [arrays[i] + arrays[i + 1] for i in range(0, len(arrays), 2)]
    return arrays[0]


def swap(x, axis, mask):
    return lax.ppermute(x, axis, [(i, i ^ mask) for i in range(lax.axis_size(axis))])


def exchange_groups(x, axis, first_bit=0):
    count = lax.axis_size(axis).bit_length() - 1
    bits = [1 << b for b in range(count)]
    groups = [bits[:1]] + [bits[i : i + 2] for i in range(1, count, 2)]
    arrays = [x]
    for group in groups[first_bit:]:
        x = pair_sums(arrays)
        masks = [group[0]] if len(group) == 1 else [group[0], group[1], group[0] | group[1]]
        came = {mask: swap(x, axis, mask) for mask in reversed(masks)}
        arrays = [x] + [came[mask] for mask in masks]
    return arrays


def call(kernel, shapes, *args):
    out = [jax.ShapeDtypeStruct(shape, jnp.float32) for shape in shapes]
    return pl.pallas_call(
        kernel,
        out_shape=out,
        compiler_params=pltpu.CompilerParams(vmem_limit_bytes=32 * 1024 * 1024),
    )(*args)


def two_rounds(opened, is_second, sends_first, layout_of):
    *columns, other = opened
    column, width = columns[0].shape, columns[0].shape[1]
    other = swap(other, "row", 1)
    bands = functools.partial(bands_kernel, is_second)
    (mine,) = call(bands, (other.shape,), *columns)
    (found,) = call(
        functools.partial(angles_kernel, is_second),
        ((FOUND, width),),
        *exchange_groups(mine + other, "row", 1),
    )
    other = swap(found, "row", 1)
    turn = functools.partial(columns_kernel, is_second)
    columns[:2] = call(turn, (column, column), *columns[:2], found)
    turn = functools.partial(next_kernel, is_second, sends_first, layout_of)
    return call(turn, (column, column), *columns, found, other)


def per_device(basis):
    rows, cols = basis.shape
    width = cols // 2
    pair_total = lax.axis_size("pair")
    column = (rows, width)
    opened = (column,) * 4 + ((4 * PACKED + WINDOW, width),)
    payload = (rows + strip_rows(rows, width), width)

    sends, sends_second, gets_second, own_second, is_second = first_moves(pair_total)
    (sent,) = call(functools.partial(payload_kernel, sends_second), (payload,), basis)
    came = lax.ppermute(sent, "pair", sends)
    even, odd = call(open_kernel, (column, column), basis)
    opening = functools.partial(first_open, own_second, gets_second, is_second)
    arrays = call(opening, opened, even, odd, came)
    sends, sends_first, picks, next_second = fused_moves(pair_total)
    kept, sent = two_rounds(arrays, is_second, sends_first, in_blocks)

    came = [lax.ppermute(x, "pair", s) for x, s in zip((sent, kept), sends)]
    opening = functools.partial(fused_open, picks, next_second)
    arrays = call(opening, opened, kept, sent, *came)
    sends, sends_first, gets_first = last_moves(pair_total)
    kept, sent = two_rounds(arrays, next_second, sends_first, in_order)

    came = lax.ppermute(sent, "pair", sends)
    flag = among(gets_first)
    first = jnp.where(flag, came, kept)
    second = jnp.where(flag, kept, came)
    return jnp.concatenate((first, second), axis=1)


def solution(mesh):
    return jax.shard_map(
        per_device,
        mesh=mesh,
        in_specs=(P("row", "pair"),),
        out_specs=P("row", "pair"),
        check_vma=False,
    )
```
